32 devices in a mesh: dp: 4 (over y, x), expert: 8 (over z, core).
Axes of the slice: x: 2, y: 2, z: 4, core: 2. Of those that a mesh axis runs over, the one named last changes fastest.
Arguments:
- tokens: bfloat16 [16384, 1024], P(('dp', 'expert')), may hold values from -6 to 6
- routes: int32 [16384, 2], P(('dp', 'expert')), may hold values from 0 to 7, all different within a row
- rel_bucket: int32 [1023], replicated, may hold values from 0 to 31
- norm_gain1: float32 [1024], replicated, may hold values from 0.25 to 1.75
- w_qkv: bfloat16 [1024, 3072], P(('dp', 'expert')), may hold values from -0.1875 to 0.1875
- w_out_proj: bfloat16 [1024, 1024], P(('dp', 'expert')), may hold values from -1.5 to 1.5
- bias_table: float32 [32, 16], replicated, may hold values from -4 to 4
- norm_gain2: float32 [1024], replicated, may hold values from 0.25 to 1.75
- w_router: float32 [1024, 8], replicated, may hold values from -0.125 to 0.125
- w_expert_in: bfloat16 [8, 2, 1024, 2816], P('expert'), may hold values from -0.1875 to 0.1875
- w_expert_out: bfloat16 [8, 2816, 1024], P('expert'), may hold values from -0.15625 to 0.15625
- grad_out: bfloat16 [16384, 1024], P(('dp', 'expert')), may hold values from -6 to 6
Outputs:
- block_out: bfloat16 [16384, 1024], P(('dp', 'expert'))
- grad_tokens: float32 [16384, 1024], P(('dp', 'expert'))
- grad_norm1: float32 [1024], replicated
- grad_qkv: float32 [1024, 3072], P(('dp', 'expert'))
- grad_out_proj: float32 [1024, 1024], P(('dp', 'expert'))
- grad_bias: float32 [32, 16], replicated
- grad_norm2: float32 [1024], replicated
- grad_router: float32 [1024, 8], replicated
- grad_expert_in: float32 [8, 2, 1024, 2816], P('expert', None, 'dp')
- grad_expert_out: float32 [8, 2816, 1024], P('expert', None, 'dp')
The draws below stay inside these ranges and needn't reach their ends.
Inputs may be any that keep to these rules, and one draw needn't show every extreme that they name: `routes`: each token names two different experts, and every expert is named by some token.
All inputs are finite; a program needn't handle non-finite values.
Results may differ from the reference program's by a relative error of at most 0.015.
Values may be sent and summed in bfloat16 or wider, within the bound.
A program may use at most 256 MiB of HBM per device.

```python
import jax
import jax.numpy as jnp
from jax import lax

D = 1024
HEADS = 16
HEAD_DIM = 64
FF = 2816
BUCKETS = 32
LENGTH = 512
TOK_DEV = 512
TOKENS = 16384
EXPERTS = 8
CAPACITY = 160
N_DP = 4
N_EXPERT = 8


def set_ends(entries, rng, least, top_value):
    index_at = [jax.random.randint(jax.random.fold_in(rng, axis), (), 0, length) for axis, length in enumerate(entries.shape)]
    widest = entries.shape.index(max(entries.shape))
    beside = index_at[:widest] + [(index_at[widest] + 1) % entries.shape[widest]] + index_at[widest + 1:]
    return entries.at[tuple(index_at)].set(least).at[tuple(beside)].set(top_value)


def levels(key, shape, pieces, least, top_value):
    factor_of, own = 1.0, jax.random.fold_in(key, 6)
    for axis_at, parts in pieces:
        draws = jnp.exp(jax.random.uniform(jax.random.fold_in(own, axis_at), (parts,), jnp.float32, least / len(pieces), top_value / len(pieces)))
        factor_of = factor_of * jnp.repeat(draws, shape[axis_at] // parts).reshape([-1 if axis == axis_at else 1 for axis in range(len(shape))])
    return factor_of


def choose_distinct(key, rows, number_of, top, lift):
    ranking = jax.random.permutation(jax.random.fold_in(key, 1), number_of)
    pull = ranking
    for power in range(3):
        pull = pull * pull // number_of
    pull = pull * lift // number_of
    tickets = jax.random.randint(jax.random.fold_in(key, 2), (rows, number_of), 0, 4096) + pull
    holders = jax.random.permutation(jax.random.fold_in(key, 3), rows)[jnp.arange(number_of) % rows]
    tickets = jnp.where(jnp.arange(rows)[:, None] == holders[None, :], 1 << 14, tickets)
    score = tickets * number_of + jnp.arange(number_of)
    return lax.top_k(score.astype(jnp.int32), top)[1].astype(jnp.int32)


def centred(own_key, shape, deviation, reach, split=(), kind=jnp.bfloat16):
    values = jax.random.normal(own_key, shape, jnp.float32) * deviation
    if len(split) > 0:
        values = levels(own_key, shape, split, -0.22, 0.18) * values
    return jnp.clip(values, min=-reach, max=reach).astype(kind)


def setup_inputs(seed: int = 0) -> dict:
    keys = jax.random.split(jax.random.key(seed), 13)
    return {
        "tokens": centred(keys[0], (TOKENS, D), 1.0, 6.0, ((0, 32),)),
        "routes": choose_distinct(keys[1], TOKENS, EXPERTS, 2, 2048),
        "rel_bucket": set_ends(jax.random.randint(keys[2], (2 * LENGTH - 1,), 0, BUCKETS), jax.random.fold_in(keys[2], 1), 0, BUCKETS - 1).astype(jnp.int32),
        "norm_gain1": jnp.clip(1.0 + 0.15 * jax.random.normal(keys[3], (D,), jnp.float32), 0.25, 1.75),
        "w_qkv": centred(keys[4], (D, 3 * D), D ** -0.5, 0.1875, ((0, 32),)),
        "w_out_proj": centred(keys[5], (D, D), (D * 8 // LENGTH) ** -0.5, 1.5, ((0, 32),)),
        "bias_table": centred(keys[6], (BUCKETS, HEADS), 1.0, 4.0, (), jnp.float32),
        "norm_gain2": jnp.clip(1.0 + 0.15 * jax.random.normal(keys[7], (D,), jnp.float32), 0.25, 1.75),
        "w_router": centred(keys[8], (D, EXPERTS), (2 * D) ** -0.5, 0.125, (), jnp.float32),
        "w_expert_in": centred(keys[9], (EXPERTS, 2, D, FF), D ** -0.5, 0.1875, ((0, 8),)),
        "w_expert_out": centred(keys[10], (EXPERTS, FF, D), (FF // 2) ** -0.5, 0.15625, ((0, 8),)),
        "grad_out": centred(keys[11], (TOKENS, D), 1.0, 6.0, ((0, 32),)),
    }


EPS = 1e-06

@jax.custom_vjp
def low(v):
    return lax.optimization_barrier(v.astype(jnp.bfloat16)).astype(jnp.float32)

@jax.custom_vjp
def low_back(v):
    return v

def low_keep(v):
    return (low(v), None)

def low_pass(kept, grad):
    return (grad,)

def back_keep(v):
    return (v, None)

def back_low(kept, grad):
    return (low(grad),)
low.defvjp(low_keep, low_pass)
low_back.defvjp(back_keep, back_low)

def rms_norm(values, norm_gain):
    inv_rms = lax.rsqrt(lax.optimization_barrier(jnp.mean(values * values, axis=-1, keepdims=True)) + EPS)
    return values * inv_rms * norm_gain

def reference(tokens, routes, rel_bucket, norm_gain1, w_qkv, w_out_proj, bias_table, norm_gain2, w_router, w_expert_in, w_expert_out, grad_out):
    highest = lax.Precision.HIGHEST
    dev_count = N_DP * N_EXPERT
    seq_total = TOKENS // LENGTH
    scale_factor = HEAD_DIM ** (-0.5)
    expert_ids = jnp.arange(EXPERTS, dtype=jnp.int32)
    pair_expert = routes.reshape(dev_count, TOK_DEV, 2).transpose(0, 2, 1).reshape(dev_count, 2 * TOK_DEV)
    pair_hot = (pair_expert[:, :, None] == expert_ids[None, None, :]).astype(jnp.int32)
    slot_place = lax.optimization_barrier(jnp.sum((jnp.cumsum(pair_hot, axis=1) - 1) * pair_hot, axis=2))
    kept_mask = slot_place < CAPACITY
    dev_ids = jnp.arange(dev_count, dtype=jnp.int32)[:, None]
    slot_total = dev_count * EXPERTS * CAPACITY
    slot_index = jnp.where(kept_mask, (dev_ids * EXPERTS + pair_expert) * CAPACITY + slot_place, slot_total).reshape(-1).astype(jnp.int32)
    fetch_index = jnp.minimum(slot_index, slot_total - 1)
    tok_pos = jnp.tile(jnp.arange(TOK_DEV, dtype=jnp.int32), 2)[None, :]
    tok_index = (dev_ids * TOK_DEV + tok_pos).reshape(-1).astype(jnp.int32)
    kept_f = kept_mask.reshape(-1).astype(jnp.float32)[:, None]
    positions = jnp.arange(LENGTH, dtype=jnp.int32)
    distance = positions[:, None] - positions[None, :] + LENGTH - 1
    bucket_full = jnp.take(rel_bucket, distance)

    def forward(inputs_f, qkv_weight, out_weight, table, gain_one, gain_two, router, expert_in, expert_out):
        normed1 = low(rms_norm(inputs_f, gain_one))
        qkv_all = low(low_back(jnp.dot(normed1, qkv_weight, precision=highest)))
        bias_full = jnp.transpose(table[bucket_full], (2, 0, 1))

        def one_seq(seq_block):
            query_rows = seq_block[:, :D].reshape(LENGTH, HEADS, HEAD_DIM)
            key_rows = seq_block[:, D:2 * D].reshape(LENGTH, HEADS, HEAD_DIM)
            value_rows = seq_block[:, 2 * D:].reshape(LENGTH, HEADS, HEAD_DIM)
            scores = low_back(jnp.einsum('qhd,khd->hqk', query_rows, key_rows, precision=highest) * scale_factor + bias_full)
            attn_probs = jax.nn.softmax(scores, axis=-1)
            mixed_out = jnp.einsum('hqk,khd->qhd', low(attn_probs), value_rows, precision=highest)
            return mixed_out.reshape(LENGTH, D)
        mixed_all = lax.map(jax.checkpoint(one_seq), qkv_all.reshape(seq_total, LENGTH, 3 * D)).reshape(TOKENS, D)
        mixed_all = low(low_back(mixed_all))
        attn_out = low_back(jnp.dot(mixed_all, out_weight, precision=highest))
        residual = inputs_f + attn_out
        normed2 = low(rms_norm(residual, gain_two))
        logits = jnp.dot(normed2, router, precision=highest)
        chosen = jnp.take_along_axis(logits, routes, axis=1)
        gate_probs = jax.nn.softmax(chosen, axis=-1)
        slot_rows = jnp.zeros((slot_total, D), jnp.float32).at[slot_index].set(normed2[tok_index], mode='drop')
        slot_rows = low_back(slot_rows)
        slot_rows = slot_rows.reshape(N_DP, N_EXPERT, EXPERTS, CAPACITY, D).transpose(2, 0, 1, 3, 4).reshape(EXPERTS, N_DP * N_EXPERT * CAPACITY, D)

        def one_expert(packed):
            rows_in, weight_in, weight_out = packed
            gate_pre = low_back(jnp.dot(rows_in, weight_in[0], precision=highest))
            up_pre = low_back(jnp.dot(rows_in, weight_in[1], precision=highest))
            hidden = low(jax.nn.gelu(gate_pre) * up_pre)
            return low(low_back(jnp.dot(hidden, weight_out, precision=highest)))
        produced = lax.map(jax.checkpoint(one_expert), (slot_rows, expert_in, expert_out))
        produced = produced.reshape(EXPERTS, N_DP, N_EXPERT, CAPACITY, D).transpose(1, 2, 0, 3, 4).reshape(slot_total, D)
        paired = (produced[fetch_index] * kept_f).reshape(dev_count, 2, TOK_DEV, D)
        first_out = paired[:, 0].reshape(TOKENS, D)
        second_out = paired[:, 1].reshape(TOKENS, D)
        return residual + gate_probs[:, 0:1] * first_out + gate_probs[:, 1:2] * second_out
    primals = (tokens.astype(jnp.float32), w_qkv.astype(jnp.float32), w_out_proj.astype(jnp.float32), bias_table, norm_gain1, norm_gain2, w_router, w_expert_in.astype(jnp.float32), w_expert_out.astype(jnp.float32))
    result, pullback = jax.vjp(forward, *primals)
    grads = pullback(grad_out.astype(jnp.float32))
    return (result.astype(jnp.bfloat16), grads[0], grads[4], grads[1], grads[2], grads[3], grads[5], grads[6], grads[7], grads[8])
```

```python
import functools

import jax
import jax.numpy as jnp
from jax import lax
from jax.experimental import pallas as pl
from jax.experimental.pallas import tpu as pltpu
from jax.sharding import PartitionSpec as P

LENGTH = 512
EPS = 1e-06
HIGHEST = lax.Precision.HIGHEST
F32 = jnp.float32
BF16 = jnp.bfloat16


def dot_nt(a, b):
    return lax.dot_general(a, b, (((1,), (1,)), ((), ())), preferred_element_type=F32)


def dot_nn(a, b):
    return jnp.dot(a, b, preferred_element_type=F32)


def iota(shape, axis):
    return lax.broadcasted_iota(jnp.int32, shape, axis)


def spread_bias(row):
    values = jnp.broadcast_to(row, (8, 1024))
    lift = 7 - iota((8, 1024), 0)
    for bit in (1, 2, 4):
        values = jnp.where((lift // bit) % 2 == 1, pltpu.roll(values, 1024 - bit, 1), values)
    return jnp.concatenate(
        [pltpu.roll(values, (904 + 8 * block) % 1024, 1) for block in range(16)], axis=0
    )


def fold_bias(parts):
    total = parts[0:8]
    total = pltpu.roll(total, 120, 1)
    for block in range(1, 16):
        piece = parts[8 * block : 8 * block + 8]
        total = total + (pltpu.roll(piece, 120 - 8 * block, 1) if block < 15 else piece)
    lift = 7 - iota((8, 1024), 0)
    for bit in (1, 2, 4):
        total = jnp.where((lift // bit) % 2 == 1, pltpu.roll(total, bit, 1), total)
    return jnp.sum(total, axis=0, keepdims=True)


def attend_pair(pair, q_ref, k_ref, v_ref, table_ref, o_ref, p_ref):
    query = q_ref[...] * jnp.asarray(0.125, BF16)
    values_t = v_ref[...].T
    half = iota((512, 128), 1) // 64
    halves = []
    for t in range(2):
        shifted = spread_bias(table_ref[pl.ds(2 * pair + t, 1), :])
        query_t = jnp.where(half == t, query, jnp.zeros_like(query))
        scores = [
            dot_nt(k_ref[128 * c : 128 * c + 128, :], query_t)
            + shifted[:, 384 - 128 * c : 896 - 128 * c]
            for c in range(4)
        ]
        top = functools.reduce(jnp.maximum, [jnp.max(s, axis=0, keepdims=True) for s in scores])
        exps = [jnp.exp(s - top) for s in scores]
        total = functools.reduce(jnp.add, [jnp.sum(e, axis=0, keepdims=True) for e in exps])
        inverse = 1.0 / total
        for c in range(4):
            p_ref[t, 128 * c : 128 * c + 128, :] = (exps[c] * inverse).astype(BF16)
        halves.append(dot_nn(values_t, p_ref[t]))
    mixed = jnp.where(iota((128, 512), 0) < 64, halves[0], halves[1])
    o_ref[...] = mixed.T.astype(BF16)


def attend_back_pair(pair, q_ref, k_ref, v_ref, p_ref, do_ref, dq_ref, dk_ref, dv_ref, fold_ref):
    query = q_ref[...] * jnp.asarray(0.125, BF16)
    keys_t = k_ref[...].T
    values = v_ref[...]
    grads = do_ref[...]
    half = iota((512, 128), 1) // 64
    dq_halves, dk_halves, dv_halves = [], [], []
    for t in range(2):
        values_t = jnp.where(half == t, values, jnp.zeros_like(values))
        probs = [p_ref[t, 128 * c : 128 * c + 128, :].astype(F32) for c in range(4)]
        grad_probs = [dot_nt(values_t[128 * c : 128 * c + 128], grads) for c in range(4)]
        delta = functools.reduce(
            jnp.add,
            [jnp.sum(p * g, axis=0, keepdims=True) for p, g in zip(probs, grad_probs)],
        )
        scores = [(p * (g - delta)).astype(BF16) for p, g in zip(probs, grad_probs)]
        padded = [
            jnp.concatenate(
                ([jnp.zeros((128, 384 - 128 * c), F32)] if c < 3 else [])
                + [scores[c].astype(F32), jnp.zeros((128, 128 + 128 * c), F32)],
                axis=1,
            )
            for c in range(4)
        ]
        fold_ref[pl.ds(2 * pair + t, 1), :] = fold_bias(functools.reduce(jnp.add, padded))
        grad_scores = jnp.concatenate(scores, axis=0)
        dv_halves.append(dot_nn(p_ref[t], grads))
        dk_halves.append(dot_nn(grad_scores, query))
        dq_halves.append(dot_nn(keys_t, grad_scores))
    dq = jnp.where(iota((128, 512), 0) < 64, dq_halves[0], dq_halves[1]) * 0.125
    dq_ref[...] = dq.T.astype(BF16)
    dk_ref[...] = jnp.where(half == 0, dk_halves[0], dk_halves[1]).astype(BF16)
    dv_ref[...] = jnp.where(half == 0, dv_halves[0], dv_halves[1]).astype(BF16)


def pair_spec(offset):
    return pl.BlockSpec((512, 128), lambda pair: (0, offset + pair))


WHOLE = pl.BlockSpec((16, 1024), lambda pair: (0, 0))
PROBS = pl.BlockSpec((2, 512, 512), lambda pair: (pair, 0, 0))
PARAMS = pltpu.CompilerParams(vmem_limit_bytes=48 * 1024 * 1024)


def attend(qkv, table):
    def body(*refs):
        attend_pair(pl.program_id(0), *refs)

    return pl.pallas_call(
        body,
        grid=(8,),
        in_specs=[pair_spec(0), pair_spec(8), pair_spec(16), WHOLE],
        out_specs=[pair_spec(0), PROBS],
        out_shape=[
            jax.ShapeDtypeStruct((512, 1024), BF16),
            jax.ShapeDtypeStruct((16, 512, 512), BF16),
        ],
        compiler_params=PARAMS,
    )(qkv, qkv, qkv, table)


def attend_back(qkv, probs, grad_mixed):
    def body(*refs):
        attend_back_pair(pl.program_id(0), *refs)

    return pl.pallas_call(
        body,
        grid=(8,),
        in_specs=[pair_spec(0), pair_spec(8), pair_spec(16), PROBS, pair_spec(0)],
        out_specs=[pair_spec(0), pair_spec(0), pair_spec(0), WHOLE],
        out_shape=[
            jax.ShapeDtypeStruct((512, 1024), BF16),
            jax.ShapeDtypeStruct((512, 1024), BF16),
            jax.ShapeDtypeStruct((512, 1024), BF16),
            jax.ShapeDtypeStruct((16, 1024), F32),
        ],
        compiler_params=PARAMS,
    )(qkv, qkv, qkv, probs, grad_mixed)


def rms_forward(values, norm_gain):
    inv_rms = lax.rsqrt(jnp.mean(values * values, axis=-1, keepdims=True) + EPS)
    return (values * inv_rms * norm_gain, inv_rms)


def rms_backward(values, inv_rms, norm_gain, grad_norm):
    normed = values * inv_rms
    scaled = grad_norm * norm_gain
    grad_gain = jnp.sum(grad_norm * normed, axis=0)
    grad_values = inv_rms * (scaled - normed * jnp.mean(scaled * normed, axis=-1, keepdims=True))
    return (grad_values, grad_gain)


def shards(
    tokens,
    routes,
    rel_bucket,
    norm_gain1,
    w_qkv,
    w_out_proj,
    bias_table,
    norm_gain2,
    w_router,
    w_expert_in,
    w_expert_out,
    grad_out,
):
    row_count, model_width = tokens.shape
    bucket_count, head_count = bias_table.shape
    expert_count = lax.axis_size("expert")
    capacity = 10 * row_count // (4 * expert_count)
    slot_total = expert_count * capacity
    qkv_full = lax.all_gather(w_qkv, ("dp", "expert"), axis=0, tiled=True)
    out_full = lax.all_gather(w_out_proj, ("dp", "expert"), axis=0, tiled=True)

    def exchange(rows):
        return lax.all_to_all(
            rows.reshape(expert_count, capacity, model_width),
            "expert",
            split_axis=0,
            concat_axis=0,
            tiled=True,
        ).reshape(slot_total, model_width)

    expert_ids = jnp.arange(expert_count, dtype=jnp.int32)
    pair_expert = routes.T.reshape(2 * row_count)
    pair_hot = pair_expert[:, None] == expert_ids[None, :]
    pair_ids = jnp.arange(2 * row_count, dtype=jnp.int32)
    earlier = (pair_ids[:, None] > pair_ids[None, :]).astype(BF16)
    counts = dot_nn(earlier, pair_hot.astype(BF16))
    slot_place = jnp.sum(jnp.where(pair_hot, counts, 0.0), axis=1).astype(jnp.int32)
    slot_index = jnp.where(
        slot_place < capacity, pair_expert * capacity + slot_place, slot_total
    ).reshape(2, row_count)
    slot_ids = jnp.arange(slot_total, dtype=jnp.int32)
    hot0 = (slot_ids[:, None] == slot_index[0][None, :]).astype(BF16)
    hot1 = (slot_ids[:, None] == slot_index[1][None, :]).astype(BF16)
    hot = hot0 + hot1

    bucket_ids = jnp.arange(bucket_count, dtype=jnp.int32)
    bucket_hot = jnp.concatenate(
        [bucket_ids[:, None] == rel_bucket[None, :], jnp.zeros((bucket_count, 1), bool)], axis=1
    ).astype(F32)
    table = jnp.dot(bias_table.T, bucket_hot, precision=HIGHEST)

    inputs_f = tokens.astype(F32)
    normed1, inv_rms1 = rms_forward(inputs_f, norm_gain1)
    normed1_r = normed1.astype(BF16)
    qkv_r = dot_nn(normed1_r, qkv_full).astype(BF16)
    mixed_r, probs = attend(qkv_r, table)
    residual = inputs_f + dot_nn(mixed_r, out_full)
    normed2, inv_rms2 = rms_forward(residual, norm_gain2)
    normed2_r = normed2.astype(BF16)
    normed2_f = normed2_r.astype(F32)
    arrived = exchange(dot_nn(hot, normed2_r).astype(BF16))
    logits = jnp.dot(normed2_f, w_router, precision=HIGHEST)
    route_hot = (routes[:, :, None] == expert_ids[None, None, :]).astype(F32)
    chosen = jnp.sum(logits[:, None, :] * route_hot, axis=-1)
    gate_probs = jax.nn.softmax(chosen, axis=-1)
    grad_y = grad_out.astype(F32)
    back0 = (gate_probs[:, 0:1] * grad_y).astype(BF16)
    back1 = (gate_probs[:, 1:2] * grad_y).astype(BF16)
    grad_produced = exchange((dot_nn(hot0, back0) + dot_nn(hot1, back1)).astype(BF16))

    w_in = w_expert_in[0]
    w_out = w_expert_out[0]
    gate_pre = dot_nn(arrived, w_in[0])
    up_pre = dot_nn(arrived, w_in[1])
    gelu_val, gelu_back = jax.vjp(jax.nn.gelu, gate_pre)
    hidden_r = (gelu_val * up_pre).astype(BF16)
    produced = dot_nn(hidden_r, w_out).astype(BF16)
    returned = exchange(produced)
    grad_hidden = dot_nt(grad_produced, w_out)
    grad_gate_r = gelu_back(grad_hidden * up_pre)[0].astype(BF16)
    grad_up_r = (grad_hidden * gelu_val).astype(BF16)
    grad_arrived = (dot_nt(grad_gate_r, w_in[0]) + dot_nt(grad_up_r, w_in[1])).astype(BF16)
    grad_returned = exchange(grad_arrived)
    grad_w_out = dot_nn(hidden_r.T, grad_produced)
    grad_w_in = jnp.stack(
        [dot_nn(arrived.T, grad_gate_r), dot_nn(arrived.T, grad_up_r)], axis=0
    )
    grad_expert_out = lax.psum_scatter(
        grad_w_out[None].astype(BF16), "dp", scatter_dimension=2, tiled=True
    ).astype(F32)
    grad_expert_in = lax.psum_scatter(
        grad_w_in[None].astype(BF16), "dp", scatter_dimension=2, tiled=True
    ).astype(F32)

    first_out = dot_nn(hot0.T, returned)
    second_out = dot_nn(hot1.T, returned)
    block_out = (
        residual + gate_probs[:, 0:1] * first_out + gate_probs[:, 1:2] * second_out
    ).astype(BF16)
    grad_gates = jnp.stack(
        [jnp.sum(grad_y * first_out, axis=-1), jnp.sum(grad_y * second_out, axis=-1)], axis=1
    )
    grad_chosen = gate_probs * (
        grad_gates - jnp.sum(gate_probs * grad_gates, axis=-1, keepdims=True)
    )
    grad_logits = jnp.sum(grad_chosen[:, :, None] * route_hot, axis=1)
    grad_router = jnp.dot(normed2_f.T, grad_logits, precision=HIGHEST)
    grad_normed2 = jnp.dot(grad_logits, w_router.T, precision=HIGHEST) + dot_nn(
        hot.T, grad_returned
    )
    grad_res_norm, grad_gain2 = rms_backward(residual, inv_rms2, norm_gain2, grad_normed2)
    grad_residual = grad_y + grad_res_norm
    grad_attn_r = grad_residual.astype(BF16)
    grad_out_w = dot_nn(mixed_r.T, grad_attn_r)
    grad_mixed_r = dot_nt(grad_attn_r, out_full).astype(BF16)
    grad_q, grad_k, grad_v, folded = attend_back(qkv_r, probs, grad_mixed_r)
    grad_qkv_r = jnp.concatenate([grad_q, grad_k, grad_v], axis=1)
    grad_qkv_w = dot_nn(normed1_r.T, grad_qkv_r)
    grad_normed1 = dot_nt(grad_qkv_r, qkv_full)
    grad_in_norm, grad_gain1 = rms_backward(inputs_f, inv_rms1, norm_gain1, grad_normed1)
    grad_tokens = grad_residual + grad_in_norm
    grad_bias_local = lax.dot_general(
        bucket_hot, folded, (((1,), (1,)), ((), ())), precision=HIGHEST
    )
    grad_bias, grad_norm1, grad_norm2, grad_router_all = lax.psum(
        (grad_bias_local, grad_gain1, grad_gain2, grad_router), ("dp", "expert")
    )
    grad_out_proj = lax.psum_scatter(
        grad_out_w.astype(BF16), ("dp", "expert"), scatter_dimension=0, tiled=True
    ).astype(F32)
    grad_qkv = lax.psum_scatter(
        grad_qkv_w.astype(BF16), ("dp", "expert"), scatter_dimension=0, tiled=True
    ).astype(F32)
    return (
        block_out,
        grad_tokens,
        grad_norm1,
        grad_qkv,
        grad_out_proj,
        grad_bias,
        grad_norm2,
        grad_router_all,
        grad_expert_in,
        grad_expert_out,
    )


def solution(mesh):
    split = P(("dp", "expert"), None)
    in_specs = (
        split,
        split,
        P(),
        P(),
        split,
        split,
        P(),
        P(),
        P(),
        P("expert", None, None, None),
        P("expert", None, None),
        split,
    )
    out_specs = (
        split,
        split,
        P(),
        split,
        split,
        P(),
        P(),
        P(),
        P("expert", None, "dp", None),
        P("expert", None, "dp"),
    )
    return jax.shard_map(shards, mesh=mesh, in_specs=in_specs, out_specs=out_specs, check_vma=False)
```

```python
import functools

import jax
import jax.numpy as jnp
from jax import lax
from jax.experimental import pallas as pl
from jax.experimental.pallas import tpu as pltpu
from jax.sharding import PartitionSpec as P

LENGTH = 512
EPS = 1e-06
HIGHEST = lax.Precision.HIGHEST
F32 = jnp.float32
BF16 = jnp.bfloat16


def dot_nt(a, b):
    return lax.dot_general(a, b, (((1,), (1,)), ((), ())), preferred_element_type=F32)


def dot_nn(a, b):
    return jnp.dot(a, b, preferred_element_type=F32)


def iota(shape, axis):
    return lax.broadcasted_iota(jnp.int32, shape, axis)


def spread_bias(row):
    values = jnp.broadcast_to(row, (8, 1024))
    lift = 7 - iota((8, 1024), 0)
    for bit in (1, 2, 4):
        values = jnp.where((lift // bit) % 2 == 1, pltpu.roll(values, 1024 - bit, 1), values)
    return jnp.concatenate(
        [pltpu.roll(values, (904 + 8 * block) % 1024, 1) for block in range(16)], axis=0
    )


def fold_bias(parts):
    total = parts[0:8]
    total = pltpu.roll(total, 120, 1)
    for block in range(1, 16):
        piece = parts[8 * block : 8 * block + 8]
        total = total + (pltpu.roll(piece, 120 - 8 * block, 1) if block < 15 else piece)
    lift = 7 - iota((8, 1024), 0)
    for bit in (1, 2, 4):
        total = jnp.where((lift // bit) % 2 == 1, pltpu.roll(total, bit, 1), total)
    return jnp.sum(total, axis=0, keepdims=True)


def attend_pair(pair, q_ref, k_ref, v_ref, table_ref, o_ref, p_ref):
    query = q_ref[...] * jnp.asarray(0.125, BF16)
    values_t = v_ref[...].T
    half = iota((512, 128), 1) // 64
    halves = []
    for t in range(2):
        shifted = spread_bias(table_ref[pl.ds(2 * pair + t, 1), :])
        query_t = jnp.where(half == t, query, jnp.zeros_like(query))
        scores = [
            dot_nt(k_ref[128 * c : 128 * c + 128, :], query_t)
            + shifted[:, 384 - 128 * c : 896 - 128 * c]
            for c in range(4)
        ]
        top = functools.reduce(jnp.maximum, [jnp.max(s, axis=0, keepdims=True) for s in scores])
        exps = [jnp.exp(s - top) for s in scores]
        total = functools.reduce(jnp.add, [jnp.sum(e, axis=0, keepdims=True) for e in exps])
        inverse = 1.0 / total
        for c in range(4):
            p_ref[t, 128 * c : 128 * c + 128, :] = (exps[c] * inverse).astype(BF16)
        halves.append(dot_nn(values_t, p_ref[t]))
    mixed = jnp.where(iota((128, 512), 0) < 64, halves[0], halves[1])
    o_ref[...] = mixed.T.astype(BF16)


def attend_back_pair(pair, q_ref, k_ref, v_ref, p_ref, do_ref, dq_ref, dk_ref, dv_ref, fold_ref):
    query = q_ref[...] * jnp.asarray(0.125, BF16)
    keys_t = k_ref[...].T
    values = v_ref[...]
    grads = do_ref[...]
    half = iota((512, 128), 1) // 64
    dq_halves, dk_halves, dv_halves = [], [], []
    for t in range(2):
        values_t = jnp.where(half == t, values, jnp.zeros_like(values))
        probs = [p_ref[t, 128 * c : 128 * c + 128, :].astype(F32) for c in range(4)]
        grad_probs = [dot_nt(values_t[128 * c : 128 * c + 128], grads) for c in range(4)]
        delta = functools.reduce(
            jnp.add,
            [jnp.sum(p * g, axis=0, keepdims=True) for p, g in zip(probs, grad_probs)],
        )
        scores = [(p * (g - delta)).astype(BF16) for p, g in zip(probs, grad_probs)]
        padded = [
            jnp.concatenate(
                ([jnp.zeros((128, 384 - 128 * c), F32)] if c < 3 else [])
                + [scores[c].astype(F32), jnp.zeros((128, 128 + 128 * c), F32)],
                axis=1,
            )
            for c in range(4)
        ]
        fold_ref[pl.ds(2 * pair + t, 1), :] = fold_bias(functools.reduce(jnp.add, padded))
        grad_scores = jnp.concatenate(scores, axis=0)
        dv_halves.append(dot_nn(p_ref[t], grads))
        dk_halves.append(dot_nn(grad_scores, query))
        dq_halves.append(dot_nn(keys_t, grad_scores))
    dq = jnp.where(iota((128, 512), 0) < 64, dq_halves[0], dq_halves[1]) * 0.125
    dq_ref[...] = dq.T.astype(BF16)
    dk_ref[...] = jnp.where(half == 0, dk_halves[0], dk_halves[1]).astype(BF16)
    dv_ref[...] = jnp.where(half == 0, dv_halves[0], dv_halves[1]).astype(BF16)


def pair_spec(offset):
    return pl.BlockSpec((512, 128), lambda pair: (0, offset + pair))


WHOLE = pl.BlockSpec((16, 1024), lambda pair: (0, 0))
PROBS = pl.BlockSpec((2, 512, 512), lambda pair: (pair, 0, 0))
PARAMS = pltpu.CompilerParams(vmem_limit_bytes=48 * 1024 * 1024)


def attend(qkv, table):
    def body(*refs):
        attend_pair(pl.program_id(0), *refs)

    return pl.pallas_call(
        body,
        grid=(8,),
        in_specs=[pair_spec(0), pair_spec(8), pair_spec(16), WHOLE],
        out_specs=[pair_spec(0), PROBS],
        out_shape=[
            jax.ShapeDtypeStruct((512, 1024), BF16),
            jax.ShapeDtypeStruct((16, 512, 512), BF16),
        ],
        compiler_params=PARAMS,
    )(qkv, qkv, qkv, table)


def attend_back(qkv, probs, grad_mixed):
    def body(*refs):
        attend_back_pair(pl.program_id(0), *refs)

    return pl.pallas_call(
        body,
        grid=(8,),
        in_specs=[pair_spec(0), pair_spec(8), pair_spec(16), PROBS, pair_spec(0)],
        out_specs=[pair_spec(0), pair_spec(0), pair_spec(0), WHOLE],
        out_shape=[
            jax.ShapeDtypeStruct((512, 1024), BF16),
            jax.ShapeDtypeStruct((512, 1024), BF16),
            jax.ShapeDtypeStruct((512, 1024), BF16),
            jax.ShapeDtypeStruct((16, 1024), F32),
        ],
        compiler_params=PARAMS,
    )(qkv, qkv, qkv, probs, grad_mixed)


MESH = pl.DeviceIdType.MESH
ANY = pl.BlockSpec(memory_space=pl.ANY)
GROUPS = 4
TILE = 256


def flip(index, mask):
    bit = 1
    while bit <= mask:
        if mask & bit:
            index = index + bit - 2 * bit * ((index // bit) % 2)
        bit *= 2
    return index


def remote(src, dst, send_sem, recv_sem, **axes):
    return pltpu.make_async_remote_copy(
        src_ref=src,
        dst_ref=dst,
        send_sem=send_sem,
        recv_sem=recv_sem,
        device_id=axes,
        device_id_type=MESH,
    )


def greet(partners):
    barrier = pltpu.get_barrier_semaphore()
    for axes in partners:
        pl.semaphore_signal(barrier, inc=1, device_id=axes, device_id_type=MESH)
    pl.semaphore_wait(barrier, len(partners))


def gelu_parts(x):
    root = 0.7978845608028654
    square = x * x
    t = jnp.tanh(root * x * (1.0 + 0.044715 * square))
    half = 0.5 * (1.0 + t)
    slope = half + 0.5 * x * (1.0 - t * t) * (root * (1.0 + 3 * 0.044715 * square))
    return x * half, slope


def experts_kernel(
    xs_ref,
    dys_ref,
    w_in_ref,
    w_out_ref,
    y_back_ref,
    dx_back_ref,
    dw_ref,
    w_in_v,
    w_out_v,
    x_v,
    dy_v,
    hid_v,
    dgate_v,
    dup_v,
    y_v,
    dx_v,
    y_sum,
    dx_sum,
    stage,
    local_sem,
    stage_sem,
    x_send,
    x_recv,
    dy_send,
    dy_recv,
    y_send,
    y_recv,
    dx_send,
    dx_recv,
):
    expert_count, capacity, width = xs_ref.shape
    hidden = w_out_ref.shape[0]
    tiles = hidden // TILE
    size = expert_count // GROUPS
    rows = size * capacity
    me = lax.axis_index("expert")
    my_group, my_place = me // size, me % size

    def others(c):
        group = flip(my_group, c)
        return [group * size + (my_place + s) % size for s in range(1 if c == 0 else 0, size)]

    greet([{"expert": (me + d) % expert_count} for d in range(1, expert_count)])
    for c in (2, 3, 1, 0):
        for peer in others(c):
            remote(
                xs_ref.at[peer], x_v.at[me], x_send.at[peer], x_recv.at[me], expert=peer
            ).start()
            remote(
                dys_ref.at[peer], dy_v.at[me], dy_send.at[peer], dy_recv.at[me], expert=peer
            ).start()
    own = [
        pltpu.make_async_copy(xs_ref.at[me], x_v.at[me], local_sem.at[0]),
        pltpu.make_async_copy(dys_ref.at[me], dy_v.at[me], local_sem.at[1]),
        pltpu.make_async_copy(w_in_ref, w_in_v, local_sem.at[2]),
        pltpu.make_async_copy(w_out_ref, w_out_v, local_sem.at[3]),
    ]
    for copy in own:
        copy.start()
    for copy in own:
        copy.wait()

    for c in range(GROUPS):
        group = flip(my_group, c)
        span = pl.ds(group * size, size)
        for peer in others(c):
            remote(
                xs_ref.at[peer], x_v.at[peer], x_send.at[peer], x_recv.at[peer], expert=peer
            ).wait_recv()
            remote(
                dys_ref.at[peer], dy_v.at[peer], dy_send.at[peer], dy_recv.at[peer], expert=peer
            ).wait_recv()
        y_sum[...] = jnp.zeros_like(y_sum)
        dx_sum[...] = jnp.zeros_like(dx_sum)

        def step(f, carry, group=group, span=span):
            cols = pl.ds(pl.multiple_of(f * TILE, TILE), TILE)
            x = x_v[span].reshape(rows, width)
            dy = dy_v[span].reshape(rows, width)
            w_gate, w_up, w_down = w_in_v[0, :, cols], w_in_v[1, :, cols], w_out_v[cols, :]
            gate, up, dhid = dot_nn(x, w_gate), dot_nn(x, w_up), dot_nt(dy, w_down)
            gelu, slope = gelu_parts(gate)
            hid = (gelu * up).astype(BF16)
            dgate = (dhid * up * slope).astype(BF16)
            dup = (dhid * gelu).astype(BF16)
            hid_v[group, :, cols] = hid
            dgate_v[group, :, cols] = dgate
            dup_v[group, :, cols] = dup
            y_sum[...] += dot_nn(hid, w_down)
            dx_sum[...] += dot_nt(dgate, w_gate) + dot_nt(dup, w_up)
            return carry

        lax.fori_loop(0, tiles, step, 0)
        y_v[span] = y_sum[...].astype(BF16).reshape(size, capacity, width)
        dx_v[span] = dx_sum[...].astype(BF16).reshape(size, capacity, width)
        for peer in others(c):
            remote(
                dx_v.at[peer], dx_back_ref.at[me], dx_send.at[peer], dx_recv.at[me], expert=peer
            ).start()
    own = [
        pltpu.make_async_copy(dx_v.at[me], dx_back_ref.at[me], local_sem.at[0]),
        pltpu.make_async_copy(y_v.at[me], y_back_ref.at[me], local_sem.at[1]),
    ]
    for copy in own:
        copy.start()
    for c in (2, 3, 1, 0):
        for peer in others(c):
            remote(
                y_v.at[peer], y_back_ref.at[me], y_send.at[peer], y_recv.at[me], expert=peer
            ).start()

    slots = expert_count * capacity
    w_in_v[0, :, 0:slots] = x_v[...].reshape(slots, width).T
    w_in_v[1, :, 0:slots] = dy_v[...].reshape(slots, width).T

    def put(m, f):
        return pltpu.make_async_copy(stage.at[m], dw_ref.at[m * tiles + f], stage_sem.at[m])

    def grads(f, carry):
        cols = pl.ds(pl.multiple_of(f * TILE, TILE), TILE)
        for m, (side, right) in enumerate(((0, dgate_v), (0, dup_v), (1, hid_v))):

            @pl.when(f > 0)
            def _():
                put(m, f - 1).wait()

            block = dot_nn(w_in_v[side, :, 0:slots], right[:, :, cols].reshape(slots, TILE))
            stage[m] = block.astype(BF16).reshape(stage.shape[1:])
            put(m, f).start()
        return carry

    lax.fori_loop(0, tiles, grads, 0)
    for m in range(3):
        put(m, tiles - 1).wait()
    for copy in own:
        copy.wait()
    for c in range(GROUPS):
        for peer in others(c):
            for src, dst, send_sem, recv_sem in (
                (xs_ref, x_v, x_send, x_recv),
                (dys_ref, dy_v, dy_send, dy_recv),
            ):
                remote(
                    src.at[peer], dst.at[me], send_sem.at[peer], recv_sem.at[me], expert=peer
                ).wait_send()
            for src, dst, send_sem, recv_sem in (
                (dx_v, dx_back_ref, dx_send, dx_recv),
                (y_v, y_back_ref, y_send, y_recv),
            ):
                remote(
                    src.at[peer], dst.at[me], send_sem.at[peer], recv_sem.at[me], expert=peer
                ).wait_send()
                remote(
                    src.at[peer], dst.at[peer], send_sem.at[peer], recv_sem.at[peer], expert=peer
                ).wait_recv()


def experts(xs, dys, w_in, w_out, dp_count):
    expert_count, capacity, width = xs.shape
    hidden = w_out.shape[0]
    size = expert_count // GROUPS
    tiles = hidden // TILE
    rows = size * capacity
    slots = jax.ShapeDtypeStruct(xs.shape, BF16)
    parts = (dp_count, width // dp_count, TILE)
    peers = pltpu.SemaphoreType.DMA((expert_count,))
    return pl.pallas_call(
        experts_kernel,
        in_specs=[ANY] * 4,
        out_specs=[ANY] * 3,
        out_shape=[slots, slots, jax.ShapeDtypeStruct((3 * tiles, *parts), BF16)],
        scratch_shapes=[
            pltpu.VMEM(w_in.shape, BF16),
            pltpu.VMEM(w_out.shape, BF16),
            pltpu.VMEM(xs.shape, BF16),
            pltpu.VMEM(xs.shape, BF16),
            pltpu.VMEM((GROUPS, rows, hidden), BF16),
            pltpu.VMEM((GROUPS, rows, hidden), BF16),
            pltpu.VMEM((GROUPS, rows, hidden), BF16),
            pltpu.VMEM(xs.shape, BF16),
            pltpu.VMEM(xs.shape, BF16),
            pltpu.VMEM((rows, width), F32),
            pltpu.VMEM((rows, width), F32),
            pltpu.VMEM((3, *parts), BF16),
            pltpu.SemaphoreType.DMA((4,)),
            pltpu.SemaphoreType.DMA((3,)),
        ]
        + [peers] * 8,
        compiler_params=pltpu.CompilerParams(
            collective_id=1, has_side_effects=True, vmem_limit_bytes=61 * 1024 * 1024
        ),
        name="experts",
    )(xs, dys, w_in, w_out)


def reduce_kernel(part_count, *refs):
    dw_ref, small_ref = refs[:2]
    parts_in = refs[2 : 2 + part_count]
    refs = refs[2 + part_count :]
    g_in_ref, g_out_ref, small_out_ref = refs[:3]
    parts_out = refs[3 : 3 + part_count]
    (
        own_v,
        first_v,
        second_v,
        small_v,
        part_v,
        core_v,
        step1_v,
        step2_v,
        last_v,
        own_sem,
        first_send,
        first_recv,
        second_send,
        second_recv,
        small_send,
        small_recv,
        part_sem,
        core_send,
        core_recv,
        step1_send,
        step1_recv,
        step2_send,
        step2_recv,
        last_send,
        last_recv,
    ) = refs[3 + part_count :]
    expert_count = lax.axis_size("expert")
    chips = expert_count // 2
    me, dp = lax.axis_index("expert"), lax.axis_index("dp")
    core, chip = me % 2, me // 2
    x, y = dp % 2, dp // 2
    core_peer = me + 1 - 2 * core
    x_peer, y_peer = dp + 1 - 2 * x, dp + 2 - 4 * y
    chip_peers = [(chip + d) % chips for d in range(1, chips)]
    greet(
        [{"expert": core_peer}, {"dp": x_peer}, {"dp": y_peer}]
        + [{"expert": peer * 2 + core} for peer in chip_peers]
    )

    tile_count = dw_ref.shape[0]

    def way(t):
        q = t % 2
        sent = [(1 - q) * (2 * i + 1 - x) + q * (2 * (1 - y) + i) for i in range(2)]
        held = [(1 - q) * (2 * i + x) + q * (2 * y + i) for i in range(2)]
        peer1 = (1 - q) * x_peer + q * y_peer
        peer2 = (1 - q) * y_peer + q * x_peer
        keep = (1 - q) * y + q * x
        return sent, held, peer1, peer2, keep

    def first_copy(t, i, sent, peer):
        return remote(
            dw_ref.at[t, sent[i]], first_v.at[t, i], first_send.at[t, i], first_recv.at[t, i], dp=peer
        )

    def own_copy(t, i, held):
        return pltpu.make_async_copy(dw_ref.at[t, held[i]], own_v.at[t, i], own_sem.at[t, i])

    def second_copy(t, keep, peer):
        return remote(own_v.at[t, 1 - keep], second_v.at[t], second_send.at[t], second_recv.at[t], dp=peer)

    def begin(t, carry):
        sent, held, peer1, _, _ = way(t)
        for i in range(2):
            first_copy(t, i, sent, peer1).start()
        for i in range(2):
            own_copy(t, i, held).start()
        return carry

    def relay(t, carry):
        sent, held, peer1, peer2, keep = way(t)
        for i in range(2):
            own_copy(t, i, held).wait()
            first_copy(t, i, sent, peer1).wait_recv()
        pass_on = own_v[t, 1 - keep].astype(F32) + first_v[t, 1 - keep].astype(F32)
        own_v[t, 1 - keep] = pass_on.astype(BF16)
        second_copy(t, keep, peer2).start()
        return carry

    def finish(m, out_ref):
        tiles = tile_count // 3

        def body(f, carry):
            t = m * tiles + f
            sent, held, peer1, peer2, keep = way(t)
            second_copy(t, keep, peer2).wait()
            for i in range(2):
                first_copy(t, i, sent, peer1).wait_send()
            total = own_v[t, keep].astype(F32) + first_v[t, keep].astype(F32)
            cols = pl.ds(pl.multiple_of(f * TILE, TILE), TILE)
            out_ref[:, cols] = total + second_v[t].astype(F32)
            return carry

        lax.fori_loop(0, tiles, body, 0)

    half = parts_in[0].shape[-1] // 2

    def part_core(p):
        return remote(
            parts_in[p].at[:, :, :, 1 - core], core_v.at[p], core_send.at[p], core_recv.at[p], expert=core_peer
        )

    def part_own(p):
        return pltpu.make_async_copy(parts_in[p].at[:, :, :, core], part_v.at[p], part_sem.at[p])

    def part_step1(p, b):
        src = (
            part_v.at[p, :, 1 - x, :, :, 0:half]
            if b == 0
            else part_v.at[p, 1 - y, :, :, :, half : 2 * half]
        )
        return remote(
            src, step1_v.at[p, b], step1_send.at[p, b], step1_recv.at[p, b], dp=(x_peer, y_peer)[b]
        )

    def part_step2(p, b):
        src = step1_v.at[p, b, (1 - y, 1 - x)[b]]
        return remote(
            src, step2_v.at[p, b], step2_send.at[p, b], step2_recv.at[p, b], dp=(y_peer, x_peer)[b]
        )

    def part_last(p, peer):
        return remote(
            part_v.at[p, 0, 0, peer],
            last_v.at[p, chip],
            last_send.at[p, peer],
            last_recv.at[p, chip],
            expert=peer * 2 + core,
        )

    def part_arrival(p, peer):
        return remote(
            part_v.at[p, 0, 0, peer],
            last_v.at[p, peer],
            last_send.at[p, peer],
            last_recv.at[p, peer],
            expert=peer * 2 + core,
        )

    def part_a(p):
        part_core(p).start()
        part_own(p).start()

    def part_b(p):
        part_own(p).wait()
        part_core(p).wait()
        part_v[p] = (part_v[p].astype(F32) + core_v[p].astype(F32)).astype(BF16)
        for b in range(2):
            part_step1(p, b).start()

    def part_held(p, b, i):
        return part_v[p, i, x, :, :, 0:half] if b == 0 else part_v[p, y, i, :, :, half : 2 * half]

    def part_c(p):
        for b in range(2):
            part_step1(p, b).wait()
            for i in range(2):
                total = part_held(p, b, i).astype(F32) + step1_v[p, b, i].astype(F32)
                step1_v[p, b, i] = total.astype(BF16)
            part_step2(p, b).start()

    def part_d(p):
        for b in range(2):
            part_step2(p, b).wait()
            total = step1_v[p, b, (y, x)[b]].astype(F32) + step2_v[p, b].astype(F32)
            part_v[p, 0, 0, :, :, b * half : b * half + half] = total.astype(BF16)
        for peer in chip_peers:
            part_last(p, peer).start()

    def part_e(p):
        total = part_v[p, 0, 0, chip].astype(F32)
        for peer in chip_peers:
            part_arrival(p, peer).wait_recv()
            total = total + last_v[p, peer].astype(F32)
        parts_out[p][...] = total
        for peer in chip_peers:
            part_last(p, peer).wait_send()

    bits = []
    bit = 1
    while bit < expert_count:
        bits.append({"expert": flip(me, bit)})
        bit *= 2
    bits += [{"dp": x_peer}, {"dp": y_peer}]

    def small_stage(s):
        src = small_v.at[s]
        copy = remote(
            src, small_v.at[len(bits) + 1 + s], small_send.at[s], small_recv.at[s], **bits[s]
        )
        copy.start()
        copy.wait()
        small_v[s + 1] = small_v[s] + small_v[len(bits) + 1 + s]

    for p in range(part_count):
        part_a(p)
    lax.fori_loop(0, tile_count, begin, 0)
    small_v[0] = small_ref[...]
    for p in range(part_count):
        part_b(p)
    for s in range(len(bits)):
        small_stage(s)
    small_out_ref[...] = small_v[len(bits)]
    lax.fori_loop(0, tile_count // 2, relay, 0)
    for p in range(part_count):
        part_c(p)
    lax.fori_loop(tile_count // 2, tile_count, relay, 0)
    for p in range(part_count):
        part_d(p)
    for m in range(2):
        finish(m, g_in_ref.at[m])
    for p in range(part_count):
        part_e(p)
    finish(2, g_out_ref)


def reduce_all(dw, small, parts):
    count = len(parts)
    tile_count, dp_count, deep, _ = dw.shape
    expert_count = lax.axis_size("expert")
    chips = expert_count // 2
    rows, cols = parts[0].shape
    own = rows // (dp_count * expert_count)
    parts = [p.reshape(2, 2, chips, 2, own, cols) for p in parts]
    bits = expert_count.bit_length() + 1
    vmem = pl.BlockSpec(memory_space=pltpu.VMEM)
    sem = pltpu.SemaphoreType.DMA
    return pl.pallas_call(
        functools.partial(reduce_kernel, count),
        in_specs=[ANY, vmem] + [ANY] * count,
        out_specs=[vmem] * (3 + count),
        out_shape=[
            jax.ShapeDtypeStruct((2, deep, tile_count // 3 * TILE), F32),
            jax.ShapeDtypeStruct((deep, tile_count // 3 * TILE), F32),
            jax.ShapeDtypeStruct(small.shape, F32),
        ]
        + [jax.ShapeDtypeStruct((own, cols), F32)] * count,
        scratch_shapes=[
            pltpu.VMEM((tile_count, 2, deep, TILE), BF16),
            pltpu.VMEM((tile_count, 2, deep, TILE), BF16),
            pltpu.VMEM((tile_count, deep, TILE), BF16),
            pltpu.VMEM((2 * bits + 1, *small.shape), F32),
            pltpu.VMEM((count, 2, 2, chips, own, cols), BF16),
            pltpu.VMEM((count, 2, 2, chips, own, cols), BF16),
            pltpu.VMEM((count, 2, 2, chips, own, cols // 2), BF16),
            pltpu.VMEM((count, 2, chips, own, cols // 2), BF16),
            pltpu.VMEM((count, chips, own, cols), BF16),
            sem((tile_count, 2)),
            sem((tile_count, 2)),
            sem((tile_count, 2)),
            sem((tile_count,)),
            sem((tile_count,)),
            sem((bits,)),
            sem((bits,)),
            sem((count,)),
            sem((count,)),
            sem((count,)),
            sem((count, 2)),
            sem((count, 2)),
            sem((count, 2)),
            sem((count, 2)),
            sem((count, chips)),
            sem((count, chips)),
        ],
        compiler_params=pltpu.CompilerParams(
            collective_id=2, has_side_effects=True, vmem_limit_bytes=60 * 1024 * 1024
        ),
        name="reduce",
    )(dw, small, *parts)


def rms_forward(values, norm_gain):
    inv_rms = lax.rsqrt(jnp.mean(values * values, axis=-1, keepdims=True) + EPS)
    return (values * inv_rms * norm_gain, inv_rms)


def rms_backward(values, inv_rms, norm_gain, grad_norm):
    normed = values * inv_rms
    scaled = grad_norm * norm_gain
    grad_gain = jnp.sum(grad_norm * normed, axis=0)
    grad_values = inv_rms * (scaled - normed * jnp.mean(scaled * normed, axis=-1, keepdims=True))
    return (grad_values, grad_gain)


def shards(
    tokens,
    routes,
    rel_bucket,
    norm_gain1,
    w_qkv,
    w_out_proj,
    bias_table,
    norm_gain2,
    w_router,
    w_expert_in,
    w_expert_out,
    grad_out,
):
    row_count, model_width = tokens.shape
    bucket_count, head_count = bias_table.shape
    expert_count = lax.axis_size("expert")
    capacity = 10 * row_count // (4 * expert_count)
    slot_total = expert_count * capacity
    qkv_full = lax.all_gather(w_qkv, ("dp", "expert"), axis=0, tiled=True)
    out_full = lax.all_gather(w_out_proj, ("dp", "expert"), axis=0, tiled=True)

    expert_ids = jnp.arange(expert_count, dtype=jnp.int32)
    pair_expert = routes.T.reshape(2 * row_count)
    pair_hot = pair_expert[:, None] == expert_ids[None, :]
    pair_ids = jnp.arange(2 * row_count, dtype=jnp.int32)
    earlier = (pair_ids[:, None] > pair_ids[None, :]).astype(BF16)
    counts = dot_nn(earlier, pair_hot.astype(BF16))
    slot_place = jnp.sum(jnp.where(pair_hot, counts, 0.0), axis=1).astype(jnp.int32)
    slot_index = jnp.where(
        slot_place < capacity, pair_expert * capacity + slot_place, slot_total
    ).reshape(2, row_count)
    slot_ids = jnp.arange(slot_total, dtype=jnp.int32)
    hot0 = (slot_ids[:, None] == slot_index[0][None, :]).astype(BF16)
    hot1 = (slot_ids[:, None] == slot_index[1][None, :]).astype(BF16)
    hot = hot0 + hot1

    bucket_ids = jnp.arange(bucket_count, dtype=jnp.int32)
    bucket_hot = jnp.concatenate(
        [bucket_ids[:, None] == rel_bucket[None, :], jnp.zeros((bucket_count, 1), bool)], axis=1
    ).astype(F32)
    table = jnp.dot(bias_table.T, bucket_hot, precision=HIGHEST)

    inputs_f = tokens.astype(F32)
    normed1, inv_rms1 = rms_forward(inputs_f, norm_gain1)
    normed1_r = normed1.astype(BF16)
    qkv_r = dot_nn(normed1_r, qkv_full).astype(BF16)
    mixed_r, probs = attend(qkv_r, table)
    residual = inputs_f + dot_nn(mixed_r, out_full)
    normed2, inv_rms2 = rms_forward(residual, norm_gain2)
    normed2_r = normed2.astype(BF16)
    normed2_f = normed2_r.astype(F32)
    outgoing = dot_nn(hot, normed2_r).astype(BF16)
    logits = jnp.dot(normed2_f, w_router, precision=HIGHEST)
    route_hot = (routes[:, :, None] == expert_ids[None, None, :]).astype(F32)
    chosen = jnp.sum(logits[:, None, :] * route_hot, axis=-1)
    gate_probs = jax.nn.softmax(chosen, axis=-1)
    grad_y = grad_out.astype(F32)
    back0 = (gate_probs[:, 0:1] * grad_y).astype(BF16)
    back1 = (gate_probs[:, 1:2] * grad_y).astype(BF16)
    back_slots = (dot_nn(hot0, back0) + dot_nn(hot1, back1)).astype(BF16)
    slot_shape = (expert_count, capacity, model_width)
    returned, grad_returned, grad_w = experts(
        outgoing.reshape(slot_shape),
        back_slots.reshape(slot_shape),
        w_expert_in[0],
        w_expert_out[0],
        lax.axis_size("dp"),
    )
    returned = returned.reshape(slot_total, model_width)
    grad_returned = grad_returned.reshape(slot_total, model_width)
    first_out = dot_nn(hot0.T, returned)
    second_out = dot_nn(hot1.T, returned)
    block_out = (
        residual + gate_probs[:, 0:1] * first_out + gate_probs[:, 1:2] * second_out
    ).astype(BF16)
    grad_gates = jnp.stack(
        [jnp.sum(grad_y * first_out, axis=-1), jnp.sum(grad_y * second_out, axis=-1)], axis=1
    )
    grad_chosen = gate_probs * (
        grad_gates - jnp.sum(gate_probs * grad_gates, axis=-1, keepdims=True)
    )
    grad_logits = jnp.sum(grad_chosen[:, :, None] * route_hot, axis=1)
    grad_router = jnp.dot(normed2_f.T, grad_logits, precision=HIGHEST)
    grad_normed2 = jnp.dot(grad_logits, w_router.T, precision=HIGHEST) + dot_nn(
        hot.T, grad_returned
    )
    grad_res_norm, grad_gain2 = rms_backward(residual, inv_rms2, norm_gain2, grad_normed2)
    grad_residual = grad_y + grad_res_norm
    grad_attn_r = grad_residual.astype(BF16)
    grad_mixed_r = dot_nt(grad_attn_r, out_full).astype(BF16)
    grad_q, grad_k, grad_v, folded = attend_back(qkv_r, probs, grad_mixed_r)
    grad_qkv_r = jnp.concatenate([grad_q, grad_k, grad_v], axis=1)
    grad_normed1 = dot_nt(grad_qkv_r, qkv_full)
    grad_in_norm, grad_gain1 = rms_backward(inputs_f, inv_rms1, norm_gain1, grad_normed1)
    grad_tokens = grad_residual + grad_in_norm
    grad_bias_local = lax.dot_general(
        bucket_hot, folded, (((1,), (1,)), ((), ())), precision=HIGHEST
    )
    small = jnp.concatenate(
        [
            grad_router.T,
            grad_gain1[None],
            grad_gain2[None],
            jnp.pad(grad_bias_local.reshape(1, -1), ((0, 0), (0, model_width - bucket_count * head_count))),
        ],
        axis=0,
    )
    small = jnp.pad(small, ((0, -small.shape[0] % 8), (0, 0)))
    parts = [
        dot_nn(left.T, right).astype(BF16)
        for left, right in (
            (mixed_r, grad_attn_r),
            (normed1_r, grad_q),
            (normed1_r, grad_k),
            (normed1_r, grad_v),
        )
    ]
    grad_in, grad_out_t, small, grad_out_proj, *grad_qkv = reduce_all(grad_w, small, parts)
    grad_expert_in, grad_expert_out = grad_in[None], grad_out_t.T[None]
    grad_qkv = jnp.concatenate(grad_qkv, axis=1)
    grad_router_all = small[:expert_count].T
    grad_norm1, grad_norm2 = small[expert_count], small[expert_count + 1]
    grad_bias = small[expert_count + 2, : bucket_count * head_count].reshape(
        bucket_count, head_count
    )
    return (
        block_out,
        grad_tokens,
        grad_norm1,
        grad_qkv,
        grad_out_proj,
        grad_bias,
        grad_norm2,
        grad_router_all,
        grad_expert_in,
        grad_expert_out,
    )


def solution(mesh):
    split = P(("dp", "expert"), None)
    in_specs = (
        split,
        split,
        P(),
        P(),
        split,
        split,
        P(),
        P(),
        P(),
        P("expert", None, None, None),
        P("expert", None, None),
        split,
    )
    out_specs = (
        split,
        split,
        P(),
        split,
        split,
        P(),
        P(),
        P(),
        P("expert", None, "dp", None),
        P("expert", None, "dp"),
    )
    return jax.shard_map(shards, mesh=mesh, in_specs=in_specs, out_specs=out_specs, check_vma=False)
```

```python
import functools

import jax
import jax.numpy as jnp
from jax import lax
from jax.experimental import pallas as pl
from jax.experimental.pallas import tpu as pltpu
from jax.sharding import PartitionSpec as P

LENGTH = 512
EPS = 1e-06
HIGHEST = lax.Precision.HIGHEST
F32 = jnp.float32
BF16 = jnp.bfloat16


def dot_nt(a, b):
    return lax.dot_general(a, b, (((1,), (1,)), ((), ())), preferred_element_type=F32)


def dot_nn(a, b):
    return jnp.dot(a, b, preferred_element_type=F32)


def iota(shape, axis):
    return lax.broadcasted_iota(jnp.int32, shape, axis)


def spread_bias(row):
    values = jnp.broadcast_to(row, (8, 1024))
    lift = 7 - iota((8, 1024), 0)
    for bit in (1, 2, 4):
        values = jnp.where((lift // bit) % 2 == 1, pltpu.roll(values, 1024 - bit, 1), values)
    return jnp.concatenate(
        [pltpu.roll(values, (904 + 8 * block) % 1024, 1) for block in range(16)], axis=0
    )


def fold_bias(parts):
    total = parts[0:8]
    total = pltpu.roll(total, 120, 1)
    for block in range(1, 16):
        piece = parts[8 * block : 8 * block + 8]
        total = total + (pltpu.roll(piece, 120 - 8 * block, 1) if block < 15 else piece)
    lift = 7 - iota((8, 1024), 0)
    for bit in (1, 2, 4):
        total = jnp.where((lift // bit) % 2 == 1, pltpu.roll(total, bit, 1), total)
    return jnp.sum(total, axis=0, keepdims=True)


MESH = pl.DeviceIdType.MESH
ANY = pl.BlockSpec(memory_space=pl.ANY)
GROUPS = 4
TILE = 256


def flip(index, mask):
    bit = 1
    while bit <= mask:
        if mask & bit:
            index = index + bit - 2 * bit * ((index // bit) % 2)
        bit *= 2
    return index


def remote(src, dst, send_sem, recv_sem, **axes):
    return pltpu.make_async_remote_copy(
        src_ref=src,
        dst_ref=dst,
        send_sem=send_sem,
        recv_sem=recv_sem,
        device_id=axes,
        device_id_type=MESH,
    )


def greet(partners):
    barrier = pltpu.get_barrier_semaphore()
    for axes in partners:
        pl.semaphore_signal(barrier, inc=1, device_id=axes, device_id_type=MESH)
    pl.semaphore_wait(barrier, len(partners))


def gelu_parts(x):
    root = 0.7978845608028654
    square = x * x
    t = jnp.tanh(root * x * (1.0 + 0.044715 * square))
    half = 0.5 * (1.0 + t)
    slope = half + 0.5 * x * (1.0 - t * t) * (root * (1.0 + 3 * 0.044715 * square))
    return x * half, slope


def experts_kernel(
    xs_ref,
    gates_ref,
    g_ref,
    w_in_ref,
    w_out_ref,
    y_ref,
    dx_back_ref,
    dgates_back_ref,
    dw_ref,
    w_in_v,
    w_out_v,
    x_v,
    gates_v,
    dgates_v,
    g_v,
    dy_v,
    hid_v,
    dgate_v,
    dup_v,
    y_v,
    dx_v,
    y_sum,
    dx_sum,
    stage,
    local_sem,
    stage_sem,
    x_send,
    x_recv,
    gates_send,
    gates_recv,
    dgates_send,
    dgates_recv,
    dx_send,
    dx_recv,
    y_sem,
):
    expert_count, capacity, width = xs_ref.shape
    hidden = w_out_ref.shape[0]
    tiles = hidden // TILE
    size = expert_count // GROUPS
    rows = size * capacity
    me = lax.axis_index("expert")
    my_group, my_place = me // size, me % size

    def others(c):
        group = flip(my_group, c)
        return [group * size + (my_place + s) % size for s in range(1 if c == 0 else 0, size)]

    greet([{"expert": (me + d) % expert_count} for d in range(1, expert_count)])
    for c in (2, 3, 1, 0):
        for peer in others(c):
            remote(
                xs_ref.at[peer], x_v.at[me], x_send.at[peer], x_recv.at[me], expert=peer
            ).start()
            remote(
                gates_ref.at[peer], gates_v.at[me], gates_send.at[peer], gates_recv.at[me], expert=peer
            ).start()
    own = [
        pltpu.make_async_copy(xs_ref.at[me], x_v.at[me], local_sem.at[0]),
        pltpu.make_async_copy(gates_ref.at[me], gates_v.at[me], local_sem.at[1]),
        pltpu.make_async_copy(g_ref, g_v, local_sem.at[4]),
        pltpu.make_async_copy(w_in_ref, w_in_v, local_sem.at[2]),
        pltpu.make_async_copy(w_out_ref, w_out_v, local_sem.at[3]),
    ]
    for copy in own:
        copy.start()
    for copy in own:
        copy.wait()

    def y_copy(c):
        span = pl.ds(flip(my_group, c) * size, size)
        return pltpu.make_async_copy(y_v.at[span], y_ref.at[span], y_sem.at[c])

    def back_copies(peer, at):
        return [
            remote(
                dx_v.at[peer], dx_back_ref.at[at], dx_send.at[peer], dx_recv.at[at], expert=peer
            ),
            remote(
                dgates_v.at[peer],
                dgates_back_ref.at[at],
                dgates_send.at[peer],
                dgates_recv.at[at],
                expert=peer,
            ),
        ]

    dgates_v[...] = jnp.zeros_like(dgates_v)
    for c in range(GROUPS):
        group = flip(my_group, c)
        span = pl.ds(group * size, size)
        for peer in others(c):
            remote(
                xs_ref.at[peer], x_v.at[peer], x_send.at[peer], x_recv.at[peer], expert=peer
            ).wait_recv()
            remote(
                gates_ref.at[peer], gates_v.at[peer], gates_send.at[peer], gates_recv.at[peer], expert=peer
            ).wait_recv()
        for s in range(size):
            src = group * size + s
            gate_col = gates_v[src].T[0:capacity, 0:1]
            dy_v[src] = (g_v[src].astype(F32) * gate_col).astype(BF16)
        y_sum[...] = jnp.zeros_like(y_sum)
        dx_sum[...] = jnp.zeros_like(dx_sum)

        def step(f, carry, group=group, span=span):
            cols = pl.ds(pl.multiple_of(f * TILE, TILE), TILE)
            x = x_v[span].reshape(rows, width)
            dy = dy_v[span].reshape(rows, width)
            w_gate, w_up, w_down = w_in_v[0, :, cols], w_in_v[1, :, cols], w_out_v[cols, :]
            gate, up, dhid = dot_nn(x, w_gate), dot_nn(x, w_up), dot_nt(dy, w_down)
            gelu, slope = gelu_parts(gate)
            hid = (gelu * up).astype(BF16)
            dgate = (dhid * up * slope).astype(BF16)
            dup = (dhid * gelu).astype(BF16)
            hid_v[group, :, cols] = hid
            dgate_v[group, :, cols] = dgate
            dup_v[group, :, cols] = dup
            y_sum[...] += dot_nn(hid, w_down)
            dx_sum[...] += dot_nt(dgate, w_gate) + dot_nt(dup, w_up)
            return carry

        lax.fori_loop(0, tiles, step, 0)
        y_v[span] = y_sum[...].astype(BF16).reshape(size, capacity, width)
        dx_v[span] = dx_sum[...].astype(BF16).reshape(size, capacity, width)
        y_copy(c).start()
        for s in range(size):
            src = group * size + s
            product = g_v[src].astype(F32) * y_v[src].astype(F32)
            dgate = jnp.sum(product, axis=1, keepdims=True)
            dgates_v[src, :, 0:capacity] = jnp.broadcast_to(dgate, (capacity, 128)).T[0:8]
        for peer in others(c):
            for copy in back_copies(peer, me):
                copy.start()
    own = [
        pltpu.make_async_copy(dx_v.at[me], dx_back_ref.at[me], local_sem.at[0]),
        pltpu.make_async_copy(dgates_v.at[me], dgates_back_ref.at[me], local_sem.at[1]),
    ]
    for copy in own:
        copy.start()

    slots = expert_count * capacity
    w_in_v[0, :, 0:slots] = x_v[...].reshape(slots, width).T
    w_in_v[1, :, 0:slots] = dy_v[...].reshape(slots, width).T

    def put(m, f):
        return pltpu.make_async_copy(stage.at[m], dw_ref.at[m * tiles + f], stage_sem.at[m])

    def grads(f, carry):
        cols = pl.ds(pl.multiple_of(f * TILE, TILE), TILE)
        for m, (side, right) in enumerate(((0, dgate_v), (0, dup_v), (1, hid_v))):

            @pl.when(f > 0)
            def _():
                put(m, f - 1).wait()

            block = dot_nn(w_in_v[side, :, 0:slots], right[:, :, cols].reshape(slots, TILE))
            stage[m] = block.astype(BF16).reshape(stage.shape[1:])
            put(m, f).start()
        return carry

    lax.fori_loop(0, tiles, grads, 0)
    for m in range(3):
        put(m, tiles - 1).wait()
    for copy in own:
        copy.wait()
    for c in range(GROUPS):
        for peer in others(c):
            for src, dst, send_sem, recv_sem in (
                (xs_ref, x_v, x_send, x_recv),
                (gates_ref, gates_v, gates_send, gates_recv),
            ):
                remote(
                    src.at[peer], dst.at[me], send_sem.at[peer], recv_sem.at[me], expert=peer
                ).wait_send()
            for copy in back_copies(peer, me):
                copy.wait_send()
            for copy in back_copies(peer, peer):
                copy.wait_recv()
        y_copy(c).wait()


def experts(xs, gates, g, w_in, w_out, dp_count):
    expert_count, capacity, width = xs.shape
    hidden = w_out.shape[0]
    size = expert_count // GROUPS
    tiles = hidden // TILE
    rows = size * capacity
    slots = jax.ShapeDtypeStruct(xs.shape, BF16)
    parts = (dp_count, width // dp_count, TILE)
    peers = pltpu.SemaphoreType.DMA((expert_count,))
    return pl.pallas_call(
        experts_kernel,
        in_specs=[ANY] * 5,
        out_specs=[ANY] * 4,
        out_shape=[slots, slots, jax.ShapeDtypeStruct(gates.shape, F32), jax.ShapeDtypeStruct((3 * tiles, *parts), BF16)],
        scratch_shapes=[
            pltpu.VMEM(w_in.shape, BF16),
            pltpu.VMEM(w_out.shape, BF16),
            pltpu.VMEM(xs.shape, BF16),
            pltpu.VMEM(gates.shape, F32),
            pltpu.VMEM(gates.shape, F32),
            pltpu.VMEM(xs.shape, BF16),
            pltpu.VMEM(xs.shape, BF16),
            pltpu.VMEM((GROUPS, rows, hidden), BF16),
            pltpu.VMEM((GROUPS, rows, hidden), BF16),
            pltpu.VMEM((GROUPS, rows, hidden), BF16),
            pltpu.VMEM(xs.shape, BF16),
            pltpu.VMEM(xs.shape, BF16),
            pltpu.VMEM((rows, width), F32),
            pltpu.VMEM((rows, width), F32),
            pltpu.VMEM((3, *parts), BF16),
            pltpu.SemaphoreType.DMA((5,)),
            pltpu.SemaphoreType.DMA((3,)),
        ]
        + [peers] * 8
        + [pltpu.SemaphoreType.DMA((GROUPS,))],
        compiler_params=pltpu.CompilerParams(
            collective_id=1, has_side_effects=True, vmem_limit_bytes=61 * 1024 * 1024
        ),
        name="experts",
    )(xs, gates, g, w_in, w_out)


def column(values, k):
    return values[:, k : k + 1]


def attend_pair(j, a, qkv_v, table_ref, p_ref):
    def lanes(part):
        return pl.ds(pl.multiple_of(256 * part + 128 * a, 128), 128)

    query = qkv_v[j, :, lanes(0)] * jnp.asarray(0.125, BF16)
    values_t = qkv_v[j, :, lanes(2)].T
    half = iota((512, 128), 1) // 64
    halves = []
    for t in range(2):
        shifted = spread_bias(table_ref[pl.ds(4 * j + 2 * a + t, 1), :])
        query_t = jnp.where(half == t, query, jnp.zeros_like(query))
        scores = [
            dot_nt(qkv_v[j, 128 * c : 128 * c + 128, lanes(1)], query_t)
            + shifted[:, 384 - 128 * c : 896 - 128 * c]
            for c in range(4)
        ]
        top = functools.reduce(jnp.maximum, [jnp.max(s, axis=0, keepdims=True) for s in scores])
        exps = [jnp.exp(s - top) for s in scores]
        total = functools.reduce(jnp.add, [jnp.sum(e, axis=0, keepdims=True) for e in exps])
        inverse = 1.0 / total
        for c in range(4):
            p_ref[t, 128 * c : 128 * c + 128, :] = (exps[c] * inverse).astype(BF16)
        halves.append(dot_nn(values_t, p_ref[t]))
    return jnp.where(iota((128, 512), 0) < 64, halves[0], halves[1])


def front_kernel(
    tokens_ref,
    gain1_ref,
    gain2_ref,
    table_ref,
    routes_ref,
    grad_ref,
    router_ref,
    ws_ref,
    wo_ref,
    wq_out,
    wo_out,
    qkv_out,
    p_out,
    g_back,
    mixed_t_ref,
    normed_t_ref,
    resid_ref,
    normed2_ref,
    xs_ref,
    gates_ref,
    cols_ref,
    wq_v,
    wo_v,
    qkv_v,
    p_v,
    mixed_v,
    normed_v,
    hot_v,
    g_v,
    own_sem,
    z_send,
    z_recv,
    xy_send,
    xy_recv,
    core_send,
    core_recv,
    g_send,
    g_recv,
    out_sem,
    p_sem,
):
    expert_count, capacity, width = xs_ref.shape
    lane_count = gates_ref.shape[2]
    slots = expert_count * capacity
    size = expert_count // GROUPS
    chips = expert_count // 2
    me, dp = lax.axis_index("expert"), lax.axis_index("dp")
    core, chip = me % 2, me // 2
    x, y = dp % 2, dp // 2
    core_peer = me + 1 - 2 * core
    x_peer, y_peer = dp + 1 - 2 * x, dp + 2 - 4 * y
    my_group, my_place = me // size, me % size
    chip_peers = [(chip + d) % chips for d in range(1, chips)]
    greet(
        [{"expert": (me + d) % expert_count} for d in range(1, expert_count)]
        + [{"dp": x_peer}, {"dp": y_peer}]
    )

    groups = ws_ref.shape[0]
    count = groups + 1
    srcs = [ws_ref.at[j] for j in range(groups)] + [wo_ref]
    bufs = [wq_v.at[j] for j in range(groups)] + [wo_v]
    widths = [ws_ref.shape[2]] * groups + [wo_ref.shape[1]]
    places = ((y, x), (y, 1 - x), (1 - y, x), (1 - y, 1 - x))

    def z_copy(j, peer, at):
        return remote(
            srcs[j], bufs[j].at[y, x, at, core], z_send.at[j, peer], z_recv.at[j, at], expert=peer * 2 + core
        )

    def own_copy(j):
        return pltpu.make_async_copy(srcs[j], bufs[j].at[y, x, chip, core], own_sem.at[j])

    def xy_copy(j, k):
        half = widths[j] // 2
        src = (
            bufs[j].at[y, x, :, core],
            bufs[j].at[y, x, :, core],
            bufs[j].at[1 - y, x, :, core, :, half : 2 * half],
            bufs[j].at[y, 1 - x, :, core, :, 0:half],
        )[k]
        return remote(src, src, xy_send.at[j, k], xy_recv.at[j, k], dp=(x_peer, y_peer)[k % 2])

    def core_copy(j, k):
        src = bufs[j].at[places[k][0], places[k][1], :, core]
        return remote(src, src, core_send.at[j, k], core_recv.at[j, k], expert=core_peer)

    def spread(j):
        own_copy(j).wait()
        for peer in chip_peers:
            z_copy(j, peer, peer).wait_recv()
        for k in range(2):
            xy_copy(j, k).start()
        core_copy(j, 0).start()

    def forward(j):
        for k in range(2):
            xy_copy(j, k).wait_recv()
            xy_copy(j, 3 - k).start()
            core_copy(j, 1 + k).start()

    def complete(j):
        for k in (2, 3):
            xy_copy(j, k).wait_recv()
        core_copy(j, 3).start()

    def out_copy(j):
        src, dst = (wq_v.at[j], wq_out.at[j]) if j < groups else (wo_v, wo_out)
        return pltpu.make_async_copy(src, dst, out_sem.at[j])

    def gathered(j):
        for k in range(4):
            core_copy(j, k).wait_recv()
        out_copy(j).start()

    for j in range(count):
        own_copy(j).start()
        for peer in chip_peers:
            z_copy(j, peer, chip).start()

    inputs = tokens_ref[...].astype(F32)
    inv_rms = lax.rsqrt(jnp.mean(inputs * inputs, axis=1, keepdims=True) + EPS)
    normed = (inputs * inv_rms * gain1_ref[...]).astype(BF16)
    normed_v[...] = normed
    normed_t_ref[...] = normed.T
    spread(0)
    spread(1)

    routes = routes_ref[...]
    rows = routes.shape[0]
    lane = iota((rows, 128), 1)
    hots = [lane == column(routes, k) for k in range(2)]
    earlier = (iota((rows, rows), 0) > iota((rows, rows), 1)).astype(BF16)
    ones = [jnp.where(h, 1.0, 0.0) for h in hots]
    counts = [dot_nn(earlier, o.astype(BF16)) for o in ones]
    counts[1] = counts[1] + jnp.sum(ones[0], axis=0, keepdims=True)
    slot = []
    for k in range(2):
        place = jnp.sum(counts[k] * ones[k], axis=1, keepdims=True)
        at = column(routes, k).astype(F32) * capacity + place
        slot.append(jnp.where(place < capacity, at, float(slots)))
    slot_rows = jnp.where(lane == 0, slot[0], slot[1]).T
    slot_ids = iota((slots, rows), 0).astype(F32)
    hot = (slot_ids == slot_rows[0:1]) | (slot_ids == slot_rows[1:2])
    hot_v[...] = jnp.where(hot, 1.0, 0.0).astype(BF16)
    g_v[...] = dot_nn(hot_v[...], grad_ref[...]).astype(BF16).reshape(g_v.shape)

    def g_copy(peer, at):
        return remote(g_v.at[peer], g_back.at[at], g_send.at[peer], g_recv.at[at], expert=peer)

    def others(c):
        group = flip(my_group, c)
        return [group * size + (my_place + s) % size for s in range(1 if c == 0 else 0, size)]

    peers = [peer for c in (2, 3, 1, 0) for peer in others(c)]
    for peer in peers:
        g_copy(peer, me).start()
    g_own = pltpu.make_async_copy(g_v.at[me], g_back.at[me], own_sem.at[count])
    g_own.start()

    def p_copy(j, a):
        return pltpu.make_async_copy(p_v.at[a], p_out.at[pl.ds(4 * j + 2 * a, 2)], p_sem.at[a])

    def group(j):
        gathered(j)
        qkv_v[j] = dot_nn(normed_v[...], wq_v[j].reshape(width, widths[j])).astype(BF16)

        def pair(a, carry):
            if j > 0:
                p_copy(j - 1, a).wait()
            mixed = attend_pair(j, a, qkv_v, table_ref, p_v.at[a])
            p_copy(j, a).start()
            span = pl.ds(pl.multiple_of(256 * j + 128 * a, 128), 128)
            mixed_t_ref[span, :] = mixed.astype(BF16)
            mixed_v[:, span] = mixed.T.astype(BF16)
            return carry

        lax.fori_loop(0, 2, pair, 0)

    forward(0)
    spread(2)
    spread(3)
    forward(1)
    complete(0)
    spread(4)
    forward(2)
    complete(1)
    group(0)
    forward(3)
    complete(2)
    group(1)
    forward(4)
    complete(3)
    group(2)
    complete(4)
    group(3)
    qkv_copy = pltpu.make_async_copy(qkv_v, qkv_out, own_sem.at[count + 1])
    qkv_copy.start()
    gathered(groups)

    resid = tokens_ref[...].astype(F32) + dot_nn(mixed_v[...], wo_v[...].reshape(width, width))
    resid_ref[...] = resid
    inv_rms2 = lax.rsqrt(jnp.mean(resid * resid, axis=1, keepdims=True) + EPS)
    normed2 = (resid * inv_rms2 * gain2_ref[...]).astype(BF16)
    normed2_ref[...] = normed2
    xs_ref[...] = dot_nn(hot_v[...], normed2).astype(BF16).reshape(xs_ref.shape)
    rest = router_ref[...]
    logits = jnp.zeros((rows, expert_count), F32)
    for _ in range(3):
        piece = rest.astype(BF16)
        rest = rest - piece.astype(F32)
        logits = logits + dot_nn(normed2, piece)
    ids = iota((rows, expert_count), 1)
    chosen = [
        jnp.sum(jnp.where(ids == column(routes, k), logits, 0.0), axis=1, keepdims=True)
        for k in range(2)
    ]
    top = jnp.maximum(chosen[0], chosen[1])
    exps = [jnp.exp(c - top) for c in chosen]
    gates = [e / (exps[0] + exps[1]) for e in exps]
    cols = jnp.where(lane == 2, gates[0], jnp.where(lane == 3, gates[1], 0.0))
    cols_ref[...] = jnp.where(lane == 0, slot[0], jnp.where(lane == 1, slot[1], cols))
    wide = iota((rows, lane_count), 1)

    def gate_row(e, carry):
        base = (e * capacity).astype(F32)
        total = jnp.zeros((rows, lane_count), F32)
        for k in range(2):
            here = (wide.astype(F32) == slot[k] - base) & (wide < capacity)
            total = total + jnp.where(here, gates[k], 0.0)
        row = jnp.sum(total, axis=0, keepdims=True)
        gates_ref[pl.ds(e, 1)] = jnp.broadcast_to(row, (8, lane_count))[None]
        return carry

    lax.fori_loop(0, expert_count, gate_row, 0)

    for a in range(2):
        p_copy(groups - 1, a).wait()
    qkv_copy.wait()
    g_own.wait()
    for j in range(count):
        out_copy(j).wait()
        for peer in chip_peers:
            z_copy(j, peer, chip).wait_send()
        for k in range(4):
            xy_copy(j, k).wait_send()
            core_copy(j, k).wait_send()
    for peer in peers:
        g_copy(peer, me).wait_send()
        g_copy(peer, peer).wait_recv()


def front(tokens, gain1, gain2, table, routes, grad_out, router, ws, wo, dp_count, capacity):
    rows, width = tokens.shape
    expert_count = router.shape[1]
    chips = expert_count // 2
    groups, own, part = ws.shape
    heads = table.shape[0]
    lane_count = -(-capacity // 128) * 128
    vmem = pl.BlockSpec(memory_space=pltpu.VMEM)
    sem = pltpu.SemaphoreType.DMA
    shape = jax.ShapeDtypeStruct
    slots = (expert_count, capacity, width)
    spread = (2, 2, chips, 2, own)
    return pl.pallas_call(
        front_kernel,
        in_specs=[vmem] * 9,
        out_specs=[ANY] * 5 + [vmem] * 7,
        out_shape=[
            shape((groups, *spread, part), BF16),
            shape((*spread, width), BF16),
            shape((groups, rows, part), BF16),
            shape((heads, rows, rows), BF16),
            shape(slots, BF16),
            shape((width, rows), BF16),
            shape((width, rows), BF16),
            shape((rows, width), F32),
            shape((rows, width), BF16),
            shape(slots, BF16),
            shape((expert_count, 8, lane_count), F32),
            shape((rows, 128), F32),
        ],
        scratch_shapes=[
            pltpu.VMEM((groups, *spread, part), BF16),
            pltpu.VMEM((*spread, width), BF16),
            pltpu.VMEM((groups, rows, part), BF16),
            pltpu.VMEM((2, 2, rows, rows), BF16),
            pltpu.VMEM((rows, width), BF16),
            pltpu.VMEM((rows, width), BF16),
            pltpu.VMEM((expert_count * capacity, rows), BF16),
            pltpu.VMEM(slots, BF16),
            sem((groups + 3,)),
            sem((groups + 1, chips)),
            sem((groups + 1, chips)),
            sem((groups + 1, 4)),
            sem((groups + 1, 4)),
            sem((groups + 1, 4)),
            sem((groups + 1, 4)),
            sem((expert_count,)),
            sem((expert_count,)),
            sem((groups + 1,)),
            sem((2,)),
        ],
        compiler_params=pltpu.CompilerParams(
            collective_id=3, has_side_effects=True, vmem_limit_bytes=60 * 1024 * 1024
        ),
        name="front",
    )(tokens, gain1, gain2, table, routes, grad_out, router, ws, wo)


def attend_back_pair(j, a, qkv_v, p_ref, grads_v, dqkv_v, fold_ref):
    def lanes(part):
        return pl.ds(pl.multiple_of(256 * part + 128 * a, 128), 128)

    query = qkv_v[j, :, lanes(0)] * jnp.asarray(0.125, BF16)
    keys_t = qkv_v[j, :, lanes(1)].T
    values = qkv_v[j, :, lanes(2)]
    grads = grads_v[:, pl.ds(pl.multiple_of(256 * j + 128 * a, 128), 128)]
    half = iota((512, 128), 1) // 64
    dq_halves, dk_halves, dv_halves = [], [], []
    for t in range(2):
        values_t = jnp.where(half == t, values, jnp.zeros_like(values))
        probs = [p_ref[t, 128 * c : 128 * c + 128, :].astype(F32) for c in range(4)]
        grad_probs = [dot_nt(values_t[128 * c : 128 * c + 128], grads) for c in range(4)]
        delta = functools.reduce(
            jnp.add,
            [jnp.sum(p * g, axis=0, keepdims=True) for p, g in zip(probs, grad_probs)],
        )
        scores = [(p * (g - delta)).astype(BF16) for p, g in zip(probs, grad_probs)]
        padded = [
            jnp.concatenate(
                ([jnp.zeros((128, 384 - 128 * c), F32)] if c < 3 else [])
                + [scores[c].astype(F32), jnp.zeros((128, 128 + 128 * c), F32)],
                axis=1,
            )
            for c in range(4)
        ]
        fold_ref[pl.ds(4 * j + 2 * a + t, 1), :] = fold_bias(functools.reduce(jnp.add, padded))
        grad_scores = jnp.concatenate(scores, axis=0)
        dv_halves.append(dot_nn(p_ref[t], grads))
        dk_halves.append(dot_nn(grad_scores, query))
        dq_halves.append(dot_nn(keys_t, grad_scores))
    dq = jnp.where(iota((128, 512), 0) < 64, dq_halves[0], dq_halves[1]) * 0.125
    dqkv_v[:, lanes(0)] = dq.T.astype(BF16)
    dqkv_v[:, lanes(1)] = jnp.where(half == 0, dk_halves[0], dk_halves[1]).astype(BF16)
    dqkv_v[:, lanes(2)] = jnp.where(half == 0, dv_halves[0], dv_halves[1]).astype(BF16)


def dot_exact(a, b, dot=dot_nn):
    total = None
    for _ in range(3):
        piece = a.astype(BF16)
        a = a - piece.astype(F32)
        term = dot(piece, b)
        total = term if total is None else total + term
    return total


def dot_f32(a, b):
    total = None
    for _ in range(3):
        piece = b.astype(BF16)
        b = b - piece.astype(F32)
        term = dot_exact(a, piece)
        total = term if total is None else total + term
    return total


BATCH = 3


def back_kernel(
    dw_ref,
    ys_ref,
    dx_ref,
    dgates_ref,
    cols_ref,
    routes_ref,
    tokens_ref,
    grad_ref,
    resid_ref,
    normed2_ref,
    normed_t_ref,
    mixed_t_ref,
    gain1_ref,
    gain2_ref,
    router_t_ref,
    bucket_hot_ref,
    wq_ref,
    wo_ref,
    qkv_ref,
    p_ref,
    w_out_ref,
    first_ref,
    second_ref,
    small_out_ref,
    gq_out_ref,
    go_out_ref,
    block_ref,
    grad_tokens_ref,
    y_v,
    grads_q,
    grads_o,
    core_q,
    core_o,
    step1_q,
    step1_o,
    step2_q,
    step2_o,
    last_q,
    last_o,
    qkv_v,
    p_v,
    wq_v,
    dqkv_v,
    dmix_v,
    dn1_v,
    fold_v,
    small_v,
    own_v,
    first_v,
    second_v,
    pass_v,
    total_v,
    y_send,
    y_recv,
    first_send,
    first_recv,
    second_send,
    second_recv,
    ring_sem,
    total_sem,
    small_send,
    small_recv,
    core_send,
    core_recv,
    step1_send,
    step1_recv,
    step2_send,
    step2_recv,
    last_send,
    last_recv,
    local_sem,
    p_sem,
    wq_sem,
):
    expert_count, capacity, width = ys_ref.shape
    slots = expert_count * capacity
    rows = tokens_ref.shape[0]
    chips = expert_count // 2
    size = expert_count // GROUPS
    me, dp = lax.axis_index("expert"), lax.axis_index("dp")
    core, chip = me % 2, me // 2
    x, y = dp % 2, dp // 2
    core_peer = me + 1 - 2 * core
    x_peer, y_peer = dp + 1 - 2 * x, dp + 2 - 4 * y
    my_group, my_place = me // size, me % size
    chip_peers = [(chip + d) % chips for d in range(1, chips)]
    greet(
        [{"expert": (me + d) % expert_count} for d in range(1, expert_count)]
        + [{"dp": x_peer}, {"dp": y_peer}]
    )

    tile_count = dw_ref.shape[0]
    tiles = tile_count // 3
    batches = tile_count // BATCH

    def way(t):
        q = t % 2
        sent = [(1 - q) * (2 * i + 1 - x) + q * (2 * (1 - y) + i) for i in range(2)]
        peer1 = (1 - q) * x_peer + q * y_peer
        peer2 = (1 - q) * y_peer + q * x_peer
        keep = (1 - q) * y + q * x
        held = [(1 - q) * (2 * k + x) + q * (2 * y + k) for k in (keep, 1 - keep)]
        return sent, held, peer1, peer2, keep

    def first_copy(t, i):
        sent, _, peer, _, _ = way(t)
        return remote(
            dw_ref.at[t, sent[i]], first_ref.at[t, i], first_send.at[t, i], first_recv.at[t, i], dp=peer
        )

    def second_copy(t, n):
        peer = way(t)[3]
        return remote(
            pass_v.at[n % 2, t % BATCH], second_ref.at[t], second_send.at[t], second_recv.at[t], dp=peer
        )

    def ring(src, dst, slot, q, k):
        return pltpu.make_async_copy(src, dst.at[slot, q], ring_sem.at[slot, q, k])

    def relay_loads(t, b):
        _, held, _, _, keep = way(t)
        q = t % BATCH
        return [
            ring(dw_ref.at[t, held[1]], own_v, b % 2, q, 0),
            ring(first_ref.at[t, 1 - keep], first_v, b % 2, q, 1),
        ]

    def finish_loads(t, b):
        _, held, _, _, keep = way(t)
        q = t % BATCH
        return [
            ring(dw_ref.at[t, held[0]], own_v, b % 2, q, 0),
            ring(first_ref.at[t, keep], first_v, b % 2, q, 1),
            ring(second_ref.at[t], second_v, b % 2, q, 2),
        ]

    def over(b, body):
        def step(t, carry):
            body(t)
            return carry

        lax.fori_loop(BATCH * b, BATCH * b + BATCH, step, 0)

    def issue(b):
        def body(t):
            for i in range(2):
                first_copy(t, i).start()

        over(b, body)

    def relay_begin(b):
        def body(t):
            for i in range(2):
                first_copy(t, i).wait_recv()
            for load in relay_loads(t, b):
                load.start()

        over(b, body)

    def relay_end(b):
        def body(t):
            for load in relay_loads(t, b):
                load.wait()
            if b >= 2:
                second_copy(t - 2 * BATCH, b).wait_send()
            q = t % BATCH
            pass_v[b % 2, q] = (
                own_v[b % 2, q].astype(F32) + first_v[b % 2, q].astype(F32)
            ).astype(BF16)
            second_copy(t, b).start()

        over(b, body)

    def finish_begin(b):
        def body(t):
            second_copy(t, b).wait_recv()
            for load in finish_loads(t, b):
                load.start()

        over(b, body)

    def total_copy(t, b):
        span = pl.ds(pl.multiple_of((t % tiles) * TILE, TILE), TILE)
        q = t % BATCH
        return pltpu.make_async_copy(
            total_v.at[b % 2, q], w_out_ref.at[t // tiles, :, span], total_sem.at[b % 2, q]
        )

    def finish_end(b):
        def body(t):
            for load in finish_loads(t, b):
                load.wait()
            if b >= 2:
                total_copy(t - 2 * BATCH, b).wait()
            q = t % BATCH
            total = own_v[b % 2, q].astype(F32) + first_v[b % 2, q].astype(F32)
            total_v[b % 2, q] = total + second_v[b % 2, q].astype(F32)
            total_copy(t, b).start()

        over(b, body)

    groups = grads_q.shape[0]
    count = groups + 1

    def pick(many, one, p):
        return many.at[p] if p < groups else one

    grads = [pick(grads_q, grads_o, p) for p in range(count)]
    cores = [pick(core_q, core_o, p) for p in range(count)]
    step1 = [pick(step1_q, step1_o, p) for p in range(count)]
    step2 = [pick(step2_q, step2_o, p) for p in range(count)]
    lasts = [pick(last_q, last_o, p) for p in range(count)]
    outs = [pick(gq_out_ref, go_out_ref, p) for p in range(count)]
    widths = [grads_q.shape[-1]] * groups + [grads_o.shape[-1]]

    def part_core(p):
        return remote(
            grads[p].at[:, :, :, 1 - core], cores[p], core_send.at[p], core_recv.at[p], expert=core_peer
        )

    def part_step1(p, b):
        half = widths[p] // 2
        src = (
            grads[p].at[:, 1 - x, :, core, :, 0:half]
            if b == 0
            else grads[p].at[1 - y, :, :, core, :, half : 2 * half]
        )
        return remote(
            src, step1[p].at[b], step1_send.at[p, b], step1_recv.at[p, b], dp=(x_peer, y_peer)[b]
        )

    def part_step2(p, b):
        src = step1[p].at[b, (1 - y, 1 - x)[b]]
        return remote(
            src, step2[p].at[b], step2_send.at[p, b], step2_recv.at[p, b], dp=(y_peer, x_peer)[b]
        )

    def part_last(p, peer, at):
        return remote(
            cores[p].at[0, 0, peer], lasts[p].at[at], last_send.at[p, peer], last_recv.at[p, at],
            expert=peer * 2 + core,
        )

    def part_a(p):
        part_core(p).start()

    def part_b(p):
        part_core(p).wait()
        total = grads[p][:, :, :, core].astype(F32) + cores[p][...].astype(F32)
        grads[p][:, :, :, core] = total.astype(BF16)
        for b in range(2):
            part_step1(p, b).start()

    def part_c(p):
        half = widths[p] // 2
        for b in range(2):
            part_step1(p, b).wait()
            for i in range(2):
                held = (
                    grads[p][i, x, :, core, :, 0:half]
                    if b == 0
                    else grads[p][y, i, :, core, :, half : 2 * half]
                )
                total = held.astype(F32) + step1[p][b, i].astype(F32)
                step1[p][b, i] = total.astype(BF16)
            part_step2(p, b).start()

    def part_d(p):
        half = widths[p] // 2
        for b in range(2):
            part_step2(p, b).wait()
            total = step1[p][b, (y, x)[b]].astype(F32) + step2[p][b].astype(F32)
            cores[p][0, 0, :, :, b * half : b * half + half] = total.astype(BF16)
        for peer in chip_peers:
            part_last(p, peer, chip).start()

    def part_e(p):
        total = cores[p][0, 0, chip].astype(F32)
        for peer in chip_peers:
            part_last(p, peer, peer).wait_recv()
            total = total + lasts[p][peer].astype(F32)
        outs[p][...] = total
        for peer in chip_peers:
            part_last(p, peer, chip).wait_send()

    partners = []
    bit = 1
    while bit < expert_count:
        partners.append({"expert": flip(me, bit)})
        bit *= 2
    partners += [{"dp": x_peer}, {"dp": y_peer}]
    stages = len(partners)

    def small_copy(s):
        return remote(
            small_v.at[0], small_v.at[1 + s], small_send.at[s], small_recv.at[s], **partners[s]
        )

    def small_next(s):
        small_copy(s).wait()
        small_v[0] = small_v[0] + small_v[1 + s]
        if s + 1 < stages:
            small_copy(s + 1).start()

    def y_copy(peer, at):
        return remote(ys_ref.at[peer], y_v.at[at], y_send.at[peer], y_recv.at[at], expert=peer)

    def others(c):
        group = flip(my_group, c)
        return [group * size + (my_place + s) % size for s in range(1 if c == 0 else 0, size)]

    peers = [peer for c in (2, 3, 1, 0) for peer in others(c)]

    def p_copy(j, a):
        return pltpu.make_async_copy(p_ref.at[pl.ds(4 * j + 2 * a, 2)], p_v.at[a], p_sem.at[a])

    def wq_copy(j):
        return pltpu.make_async_copy(wq_ref.at[j], wq_v.at[j % 2], wq_sem.at[j % 2])

    lane = iota((rows, 128), 1)
    slot = [column(cols_ref[...], k) for k in range(2)]
    gates = [column(cols_ref[...], 2 + k) for k in range(2)]

    def hots():
        at = iota((rows, slots), 1).astype(F32)
        return [at == s for s in slot]

    def dense():
        lanes = dgates_ref.shape[2]
        wide = iota((rows, lanes), 1)

        def step(e, totals):
            base = (e * capacity).astype(F32)
            row = dgates_ref[pl.ds(e, 1)][0][0:1]
            return tuple(
                totals[k]
                + jnp.where((wide.astype(F32) == slot[k] - base) & (wide < capacity), row, 0.0)
                for k in range(2)
            )

        zero = jnp.zeros((rows, lanes), F32)
        sums = lax.fori_loop(0, expert_count, step, (zero, zero))
        dgates = [jnp.sum(s, axis=1, keepdims=True) for s in sums]
        mean = gates[0] * dgates[0] + gates[1] * dgates[1]
        dchosen = [gates[k] * (dgates[k] - mean) for k in range(2)]
        routes = routes_ref[...]
        dlogits = jnp.zeros((rows, 128), F32)
        for k in range(2):
            dlogits = dlogits + jnp.where(lane == column(routes, k), dchosen[k], 0.0)
        small_rows = dot_exact(dlogits.T[0:expert_count], normed2_ref[...])
        small_v[0, 0:expert_count] = small_rows
        hot0, hot1 = hots()
        hot = jnp.where(hot0 | hot1, 1.0, 0.0).astype(BF16)
        dnormed = dot_f32(dlogits, router_t_ref[...])
        dnormed = dnormed + dot_nn(hot, dx_ref[...].reshape(slots, width))
        resid = resid_ref[...]
        inv_rms = lax.rsqrt(jnp.mean(resid * resid, axis=1, keepdims=True) + EPS)
        normed = resid * inv_rms
        scaled = dnormed * gain2_ref[...]
        small_v[0, expert_count + 1 : expert_count + 2] = jnp.sum(
            dnormed * normed, axis=0, keepdims=True
        )
        inner = jnp.mean(scaled * normed, axis=1, keepdims=True)
        dresid = grad_ref[...].astype(F32) + inv_rms * (scaled - normed * inner)
        grad_tokens_ref[...] = dresid
        dresid_r = dresid.astype(BF16)
        grads_o[...] = dot_nn(mixed_t_ref[...], dresid_r).astype(BF16).reshape(grads_o.shape)
        part_a(groups)
        dmix_v[...] = dot_nt(dresid_r, wo_ref[...]).astype(BF16)

    def group(j):
        if j + 1 < groups:
            wq_copy(j + 1).start()

        def pair(a, carry):
            p_copy(j, a).wait()
            attend_back_pair(j, a, qkv_v, p_v.at[a], dmix_v, dqkv_v, fold_v)
            if j + 1 < groups:
                p_copy(j + 1, a).start()
            return carry

        lax.fori_loop(0, 2, pair, 0)
        block = dot_nn(normed_t_ref[...], dqkv_v[...])
        grads_q[j] = block.astype(BF16).reshape(grads_q.shape[1:])
        part_a(j)
        wq_copy(j).wait()
        term = dot_nt(dqkv_v[...], wq_v[j % 2])
        dn1_v[...] = term if j == 0 else dn1_v[...] + term

    def norm_back():
        inputs = tokens_ref[...].astype(F32)
        inv_rms = lax.rsqrt(jnp.mean(inputs * inputs, axis=1, keepdims=True) + EPS)
        normed = inputs * inv_rms
        dnormed = dn1_v[...]
        scaled = dnormed * gain1_ref[...]
        small_v[0, expert_count : expert_count + 1] = jnp.sum(
            dnormed * normed, axis=0, keepdims=True
        )
        inner = jnp.mean(scaled * normed, axis=1, keepdims=True)
        grad_tokens_ref[...] += inv_rms * (scaled - normed * inner)
        buckets = dot_exact(fold_v[...], bucket_hot_ref[...], dot_nt)
        base = expert_count + 2
        heads = fold_v.shape[0]
        small_v[0, base : base + heads, 0 : buckets.shape[1]] = buckets
        small_copy(0).start()

    def outputs():
        for peer in peers:
            y_copy(peer, peer).wait_recv()
        y_own.wait()
        values = y_v[...].reshape(slots, width)
        total = resid_ref[...]
        for k, hot in enumerate(hots()):
            total = total + gates[k] * dot_nn(jnp.where(hot, 1.0, 0.0).astype(BF16), values)
        block_ref[...] = total.astype(BF16)

    small_v[0] = jnp.zeros(small_v.shape[1:], F32)
    for peer in peers:
        y_copy(peer, me).start()
    y_own = pltpu.make_async_copy(ys_ref.at[me], y_v.at[me], local_sem.at[0])
    y_own.start()
    qkv_copy = pltpu.make_async_copy(qkv_ref, qkv_v, local_sem.at[1])
    qkv_copy.start()
    wq_copy(0).start()
    for a in range(2):
        p_copy(0, a).start()
    ahead = 5
    for b in range(ahead):
        issue(b)
    dense()
    qkv_copy.wait()
    relay_begin(0)
    group(0)
    relay_end(0)
    issue(ahead)
    relay_begin(1)
    group(1)
    part_b(groups)
    relay_end(1)
    issue(ahead + 1)
    relay_begin(2)
    group(2)
    part_b(0)
    relay_end(2)
    issue(ahead + 2)
    relay_begin(3)
    group(3)
    part_b(1)
    relay_end(3)
    issue(ahead + 3)
    norm_back()
    part_b(2)
    relay_begin(4)
    relay_end(4)
    issue(ahead + 4)
    small_next(0)
    part_b(3)
    small_next(1)
    outputs()
    part_c(groups)
    relay_begin(5)
    relay_end(5)
    issue(ahead + 5)
    small_next(2)
    part_c(0)
    small_next(3)
    relay_begin(6)
    relay_end(6)
    part_c(1)
    part_d(groups)
    for s in range(4, stages):
        small_next(s)
    small_out_ref[...] = small_v[0]
    relay_begin(7)
    relay_end(7)
    part_c(2)
    part_d(0)
    part_c(3)
    part_d(1)
    relay_begin(8)
    relay_end(8)
    part_d(2)
    part_e(groups)
    relay_begin(9)
    relay_end(9)
    part_d(3)
    part_e(0)
    relay_begin(10)
    relay_end(10)
    part_e(1)
    part_e(2)
    part_e(3)
    for b in range(2):
        over(batches - 2 + b, lambda t, b=b: second_copy(t, batches - 2 + b).wait_send())
    for b in range(batches):
        finish_begin(b)
        if b > 0:
            finish_end(b - 1)
    finish_end(batches - 1)
    for b in (batches - 2, batches - 1):
        over(b, lambda t, b=b: total_copy(t, b).wait())

    def drain(t, carry):
        for i in range(2):
            first_copy(t, i).wait_send()
        return carry

    lax.fori_loop(0, tile_count, drain, 0)
    for peer in peers:
        y_copy(peer, me).wait_send()


def back(
    dw, ys, dx, dgates, cols, routes, tokens, grad_out, resid, normed2, normed_t, mixed_t,
    gain1, gain2, router_t, bucket_hot, wq, wo, qkv, probs,
):
    tile_count, dp_count, deep, _ = dw.shape
    expert_count, capacity, width = ys.shape
    chips = expert_count // 2
    rows = tokens.shape[0]
    groups, _, part = qkv.shape
    own = width // (dp_count * expert_count)
    heads = probs.shape[0]
    small_rows = -(-(expert_count + 2 + heads) // 8) * 8
    stages = expert_count.bit_length() + 1
    vmem = pl.BlockSpec(memory_space=pltpu.VMEM)
    sem = pltpu.SemaphoreType.DMA
    shape = jax.ShapeDtypeStruct
    ring = (2, BATCH, deep, TILE)

    def pairs(make):
        return [pltpu.VMEM((groups, *make(part)), BF16), pltpu.VMEM(make(width), BF16)]

    return pl.pallas_call(
        back_kernel,
        in_specs=[ANY] * 2 + [vmem] * 14 + [ANY, vmem, ANY, ANY],
        out_specs=[ANY] * 3 + [vmem] * 5,
        out_shape=[
            shape((3, deep, tile_count // 3 * TILE), F32),
            shape((tile_count, 2, deep, TILE), BF16),
            shape((tile_count, deep, TILE), BF16),
            shape((small_rows, width), F32),
            shape((groups, own, part), F32),
            shape((own, width), F32),
            shape((rows, width), BF16),
            shape((rows, width), F32),
        ],
        scratch_shapes=[pltpu.VMEM(ys.shape, BF16)]
        + pairs(lambda w: (2, 2, chips, 2, own, w))
        + pairs(lambda w: (2, 2, chips, own, w))
        + pairs(lambda w: (2, 2, chips, own, w // 2))
        + pairs(lambda w: (2, chips, own, w // 2))
        + pairs(lambda w: (chips, own, w))
        + [
            pltpu.VMEM(qkv.shape, BF16),
            pltpu.VMEM((2, 2, rows, rows), BF16),
            pltpu.VMEM((2, *wq.shape[1:]), BF16),
            pltpu.VMEM((rows, part), BF16),
            pltpu.VMEM((rows, width), BF16),
            pltpu.VMEM((rows, width), F32),
            pltpu.VMEM((heads, bucket_hot.shape[1]), F32),
            pltpu.VMEM((stages + 1, small_rows, width), F32),
            pltpu.VMEM(ring, BF16),
            pltpu.VMEM(ring, BF16),
            pltpu.VMEM(ring, BF16),
            pltpu.VMEM(ring, BF16),
            pltpu.VMEM(ring, F32),
            sem((expert_count,)),
            sem((expert_count,)),
            sem((tile_count, 2)),
            sem((tile_count, 2)),
            sem((tile_count,)),
            sem((tile_count,)),
            sem((2, BATCH, 3)),
            sem((2, BATCH)),
            sem((stages,)),
            sem((stages,)),
            sem((groups + 1,)),
            sem((groups + 1,)),
            sem((groups + 1, 2)),
            sem((groups + 1, 2)),
            sem((groups + 1, 2)),
            sem((groups + 1, 2)),
            sem((groups + 1, chips)),
            sem((groups + 1, chips)),
            sem((2,)),
            sem((2,)),
            sem((2,)),
        ],
        compiler_params=pltpu.CompilerParams(
            collective_id=2, has_side_effects=True, vmem_limit_bytes=61 * 1024 * 1024
        ),
        name="back",
    )(
        dw, ys, dx, dgates, cols, routes, tokens, grad_out, resid, normed2, normed_t, mixed_t,
        gain1, gain2, router_t, bucket_hot, wq, wo, qkv, probs,
    )


def shards(
    tokens,
    routes,
    rel_bucket,
    norm_gain1,
    w_qkv,
    w_out_proj,
    bias_table,
    norm_gain2,
    w_router,
    w_expert_in,
    w_expert_out,
    grad_out,
):
    row_count, model_width = tokens.shape
    bucket_count, head_count = bias_table.shape
    expert_count = lax.axis_size("expert")
    capacity = 10 * row_count // (4 * expert_count)
    slot_total = expert_count * capacity
    hidden_groups = 4
    shard_rows = w_qkv.shape[0]
    ws = w_qkv.reshape(shard_rows, 3, hidden_groups, -1).transpose(2, 0, 1, 3)
    ws = ws.reshape(hidden_groups, shard_rows, -1)

    bucket_ids = jnp.arange(bucket_count, dtype=jnp.int32)
    bucket_hot = jnp.concatenate(
        [bucket_ids[:, None] == rel_bucket[None, :], jnp.zeros((bucket_count, 1), bool)], axis=1
    ).astype(F32)
    table = jnp.dot(bias_table.T, bucket_hot, precision=HIGHEST)

    wq_full, out_full, qkv, probs, g_rows, mixed_t, normed1_t, residual, normed2_r, xs, gates, cols = front(
        tokens,
        norm_gain1[None],
        norm_gain2[None],
        table,
        routes,
        grad_out,
        w_router,
        ws,
        w_out_proj,
        lax.axis_size("dp"),
        capacity,
    )
    produced, grad_rows, grad_gates, grad_w = experts(
        xs, gates, g_rows, w_expert_in[0], w_expert_out[0], lax.axis_size("dp")
    )
    grad_w, _, _, small, grad_qkv, grad_out_proj, block_out, grad_tokens = back(
        grad_w,
        produced,
        grad_rows,
        grad_gates,
        cols,
        routes,
        tokens,
        grad_out,
        residual,
        normed2_r,
        normed1_t,
        mixed_t,
        norm_gain1[None],
        norm_gain2[None],
        jnp.pad(w_router.T, ((0, 128 - expert_count), (0, 0))),
        bucket_hot.astype(BF16),
        wq_full.reshape(hidden_groups, model_width, -1),
        out_full.reshape(model_width, model_width),
        qkv,
        probs,
    )
    grad_expert_in, grad_expert_out = grad_w[None, :2], grad_w[2].T[None]
    grad_qkv = grad_qkv.reshape(hidden_groups, shard_rows, 3, -1).transpose(1, 2, 0, 3)
    grad_qkv = grad_qkv.reshape(shard_rows, 3 * model_width)
    grad_router_all = small[:expert_count].T
    grad_norm1, grad_norm2 = small[expert_count], small[expert_count + 1]
    grad_bias = small[expert_count + 2 : expert_count + 2 + head_count, :bucket_count].T
    return (
        block_out,
        grad_tokens,
        grad_norm1,
        grad_qkv,
        grad_out_proj,
        grad_bias,
        grad_norm2,
        grad_router_all,
        grad_expert_in,
        grad_expert_out,
    )


def solution(mesh):
    split = P(("dp", "expert"), None)
    in_specs = (
        split,
        split,
        P(),
        P(),
        split,
        split,
        P(),
        P(),
        P(),
        P("expert", None, None, None),
        P("expert", None, None),
        split,
    )
    out_specs = (
        split,
        split,
        P(),
        split,
        split,
        P(),
        P(),
        P(),
        P("expert", None, "dp", None),
        P("expert", None, "dp"),
    )
    return jax.shard_map(shards, mesh=mesh, in_specs=in_specs, out_specs=out_specs, check_vma=False)
```

```python
import functools

import jax
import jax.numpy as jnp
from jax import lax
from jax.experimental import pallas as pl
from jax.experimental.pallas import tpu as pltpu
from jax.sharding import PartitionSpec as P

LENGTH = 512
EPS = 1e-06
HIGHEST = lax.Precision.HIGHEST
F32 = jnp.float32
BF16 = jnp.bfloat16


def dot_nt(a, b):
    return lax.dot_general(a, b, (((1,), (1,)), ((), ())), preferred_element_type=F32)


def dot_nn(a, b):
    return jnp.dot(a, b, preferred_element_type=F32)


def iota(shape, axis):
    return lax.broadcasted_iota(jnp.int32, shape, axis)


def spread_bias(row):
    values = jnp.broadcast_to(row, (8, 1024))
    lift = 7 - iota((8, 1024), 0)
    for bit in (1, 2, 4):
        values = jnp.where((lift // bit) % 2 == 1, pltpu.roll(values, 1024 - bit, 1), values)
    return jnp.concatenate(
        [pltpu.roll(values, (904 + 8 * block) % 1024, 1) for block in range(16)], axis=0
    )


def fold_bias(parts):
    total = parts[0:8]
    total = pltpu.roll(total, 120, 1)
    for block in range(1, 16):
        piece = parts[8 * block : 8 * block + 8]
        total = total + (pltpu.roll(piece, 120 - 8 * block, 1) if block < 15 else piece)
    lift = 7 - iota((8, 1024), 0)
    for bit in (1, 2, 4):
        total = jnp.where((lift // bit) % 2 == 1, pltpu.roll(total, bit, 1), total)
    return jnp.sum(total, axis=0, keepdims=True)


MESH = pl.DeviceIdType.MESH
ANY = pl.BlockSpec(memory_space=pl.ANY)
GROUPS = 4
TILE = 256
WIDE = 512


def flip(index, mask):
    bit = 1
    while bit <= mask:
        if mask & bit:
            index = index + bit - 2 * bit * ((index // bit) % 2)
        bit *= 2
    return index


def remote(src, dst, send_sem, recv_sem, **axes):
    return pltpu.make_async_remote_copy(
        src_ref=src,
        dst_ref=dst,
        send_sem=send_sem,
        recv_sem=recv_sem,
        device_id=axes,
        device_id_type=MESH,
    )


def greet(partners):
    barrier = pltpu.get_barrier_semaphore()
    for axes in partners:
        pl.semaphore_signal(barrier, inc=1, device_id=axes, device_id_type=MESH)
    pl.semaphore_wait(barrier, len(partners))


def gelu_parts(x):
    root = 0.7978845608028654
    square = x * x
    t = jnp.tanh(root * x * (1.0 + 0.044715 * square))
    half = 0.5 * (1.0 + t)
    slope = half + 0.5 * x * (1.0 - t * t) * (root * (1.0 + 3 * 0.044715 * square))
    return x * half, slope


BATCH = 3
AHEAD = 4


def ways(dp, t):
    x, y = dp % 2, dp // 2
    x_peer, y_peer = dp + 1 - 2 * x, dp + 2 - 4 * y
    q = t % 2
    sent = [(1 - q) * (2 * i + 1 - x) + q * (2 * (1 - y) + i) for i in range(2)]
    keep = (1 - q) * y + q * x
    held = [(1 - q) * (2 * k + x) + q * (2 * y + k) for k in (keep, 1 - keep)]
    return sent, held, (1 - q) * x_peer + q * y_peer, (1 - q) * y_peer + q * x_peer, keep


def experts_kernel(
    xs_ref,
    gates_ref,
    g_ref,
    w_in_ref,
    w_out_ref,
    y_ref,
    dx_back_ref,
    dgates_back_ref,
    dw_ref,
    head_ref,
    w_in_v,
    w_out_v,
    x_v,
    gates_v,
    dgates_v,
    g_v,
    dy_v,
    hid_v,
    dgate_v,
    dup_v,
    y_v,
    dx_v,
    pre_v,
    stage,
    local_sem,
    stage_sem,
    x_send,
    x_recv,
    gates_send,
    gates_recv,
    dgates_send,
    dgates_recv,
    dx_send,
    dx_recv,
    y_sem,
    head_send,
    head_recv,
):
    expert_count, capacity, width = xs_ref.shape
    hidden = w_out_ref.shape[0]
    tiles = hidden // TILE
    size = expert_count // GROUPS
    rows = size * capacity
    me = lax.axis_index("expert")
    my_group, my_place = me // size, me % size

    def others(c):
        group = flip(my_group, c)
        return [group * size + (my_place + s) % size for s in range(1 if c == 0 else 0, size)]

    dp = lax.axis_index("dp")
    greet(
        [{"expert": (me + d) % expert_count} for d in range(1, expert_count)]
        + [{"dp": flip(dp, 1)}, {"dp": flip(dp, 2)}]
    )
    for c in (2, 3, 1, 0):
        for peer in others(c):
            remote(
                xs_ref.at[peer], x_v.at[me], x_send.at[peer], x_recv.at[me], expert=peer
            ).start()
            remote(
                gates_ref.at[peer], gates_v.at[me], gates_send.at[peer], gates_recv.at[me], expert=peer
            ).start()
    own = [
        pltpu.make_async_copy(xs_ref.at[me], x_v.at[me], local_sem.at[0]),
        pltpu.make_async_copy(gates_ref.at[me], gates_v.at[me], local_sem.at[1]),
        pltpu.make_async_copy(g_ref, g_v, local_sem.at[4]),
        pltpu.make_async_copy(w_in_ref, w_in_v, local_sem.at[2]),
        pltpu.make_async_copy(w_out_ref, w_out_v, local_sem.at[3]),
    ]
    for copy in own:
        copy.start()
    for copy in own:
        copy.wait()

    def y_copy(c):
        span = pl.ds(flip(my_group, c) * size, size)
        return pltpu.make_async_copy(y_v.at[span], y_ref.at[span], y_sem.at[c])

    def back_copies(peer, at):
        return [
            remote(
                dx_v.at[peer], dx_back_ref.at[at], dx_send.at[peer], dx_recv.at[at], expert=peer
            ),
            remote(
                dgates_v.at[peer],
                dgates_back_ref.at[at],
                dgates_send.at[peer],
                dgates_recv.at[at],
                expert=peer,
            ),
        ]

    dgates_v[...] = jnp.zeros_like(dgates_v)
    for c in range(GROUPS):
        group = flip(my_group, c)
        span = pl.ds(group * size, size)
        for peer in others(c):
            remote(
                xs_ref.at[peer], x_v.at[peer], x_send.at[peer], x_recv.at[peer], expert=peer
            ).wait_recv()
            remote(
                gates_ref.at[peer], gates_v.at[peer], gates_send.at[peer], gates_recv.at[peer], expert=peer
            ).wait_recv()
        for s in range(size):
            src = group * size + s
            gate_col = gates_v[src].T[0:capacity, 0:1]
            dy_v[src] = (g_v[src].astype(F32) * gate_col).astype(BF16)

        def before(f, slot, span=span):
            cols = pl.ds(pl.multiple_of(f * TILE, TILE), TILE)
            x = x_v[span].reshape(rows, width)
            pre_v[slot, 0] = dot_nn(x, w_in_v[0, :, cols])
            pre_v[slot, 1] = dot_nn(x, w_in_v[1, :, cols])
            pre_v[slot, 2] = dot_nt(dy_v[span].reshape(rows, width), w_out_v[cols, :])

        def after(f, slot, group=group):
            cols = pl.ds(pl.multiple_of(f * TILE, TILE), TILE)
            gate, up, dhid = pre_v[slot, 0], pre_v[slot, 1], pre_v[slot, 2]
            gelu, slope = gelu_parts(gate)
            hid_v[group, :, cols] = (gelu * up).astype(BF16)
            dgate_v[group, :, cols] = (dhid * up * slope).astype(BF16)
            dup_v[group, :, cols] = (dhid * gelu).astype(BF16)

        def two(h, carry):
            before(2 * h + 1, 1)
            after(2 * h, 0)
            before(jnp.minimum(2 * h + 2, tiles - 1), 0)
            after(2 * h + 1, 1)
            return carry

        def backs(n, carry, group=group, span=span):
            cols = pl.ds(pl.multiple_of(n * WIDE, WIDE), WIDE)
            out = dot_nn(hid_v[group], w_out_v[:, cols])
            y_v[span, :, cols] = out.astype(BF16).reshape(size, capacity, WIDE)
            back = dot_nt(dgate_v[group], w_in_v[0, cols, :])
            back = back + dot_nt(dup_v[group], w_in_v[1, cols, :])
            dx_v[span, :, cols] = back.astype(BF16).reshape(size, capacity, WIDE)
            return carry

        before(0, 0)
        lax.fori_loop(0, tiles // 2, two, 0)
        if tiles % 2:
            after(tiles - 1, 0)
        lax.fori_loop(0, width // WIDE, backs, 0)
        y_copy(c).start()
        for s in range(size):
            src = group * size + s
            product = g_v[src].astype(F32) * y_v[src].astype(F32)
            dgate = jnp.sum(product, axis=1, keepdims=True)
            dgates_v[src, :, 0:capacity] = jnp.broadcast_to(dgate, (capacity, 128)).T[0:8]
        for peer in others(c):
            for copy in back_copies(peer, me):
                copy.start()
    own = [
        pltpu.make_async_copy(dx_v.at[me], dx_back_ref.at[me], local_sem.at[0]),
        pltpu.make_async_copy(dgates_v.at[me], dgates_back_ref.at[me], local_sem.at[1]),
    ]
    for copy in own:
        copy.start()

    slots = expert_count * capacity
    w_in_v[0, :, 0:slots] = x_v[...].reshape(slots, width).T
    w_in_v[1, :, 0:slots] = dy_v[...].reshape(slots, width).T

    def put(f, m):
        return pltpu.make_async_copy(stage.at[m], dw_ref.at[BATCH * f + m], stage_sem.at[m])

    def head_copy(f, m, i):
        t = BATCH * f + m
        sent, _, peer, _, _ = ways(dp, t)
        return remote(
            dw_ref.at[t, sent[i]], head_ref.at[t, i], head_send.at[t, i], head_recv.at[t, i], dp=peer
        )

    parts, deep = stage.shape[1:3]

    def grads(f, carry):
        cols = pl.ds(pl.multiple_of(f * TILE, TILE), TILE)
        for m, (side, right) in enumerate(((0, dgate_v), (0, dup_v), (1, hid_v))):

            @pl.when(f > 0)
            def _():
                put(f - 1, m).wait()

            @pl.when((f > 0) & (f <= AHEAD))
            def _():
                for i in range(2):
                    head_copy(f - 1, m, i).start()

            across = right[:, :, cols].reshape(slots, TILE)
            for r in range(0, parts, 2):
                span = slice(r * deep, (r + 2) * deep)
                block = dot_nn(w_in_v[side, span, 0:slots], across)
                stage[m, r : r + 2] = block.astype(BF16).reshape(2, deep, TILE)
            put(f, m).start()
        return carry

    lax.fori_loop(0, tiles, grads, 0)
    for m in range(BATCH):
        put(tiles - 1, m).wait()

    def heads(t, carry):
        for i in range(2):
            head_copy(t // BATCH, t % BATCH, i).wait()
        return carry

    lax.fori_loop(0, BATCH * AHEAD, heads, 0)
    for copy in own:
        copy.wait()
    for c in range(GROUPS):
        for peer in others(c):
            for src, dst, send_sem, recv_sem in (
                (xs_ref, x_v, x_send, x_recv),
                (gates_ref, gates_v, gates_send, gates_recv),
            ):
                remote(
                    src.at[peer], dst.at[me], send_sem.at[peer], recv_sem.at[me], expert=peer
                ).wait_send()
            for copy in back_copies(peer, me):
                copy.wait_send()
            for copy in back_copies(peer, peer):
                copy.wait_recv()
        y_copy(c).wait()


def experts(xs, gates, g, w_in, w_out, dp_count):
    expert_count, capacity, width = xs.shape
    hidden = w_out.shape[0]
    size = expert_count // GROUPS
    tiles = hidden // TILE
    rows = size * capacity
    slots = jax.ShapeDtypeStruct(xs.shape, BF16)
    parts = (dp_count, width // dp_count, TILE)
    peers = pltpu.SemaphoreType.DMA((expert_count,))
    return pl.pallas_call(
        experts_kernel,
        in_specs=[ANY] * 5,
        out_specs=[ANY] * 5,
        out_shape=[slots, slots, jax.ShapeDtypeStruct(gates.shape, F32), jax.ShapeDtypeStruct((BATCH * tiles, *parts), BF16),
            jax.ShapeDtypeStruct((BATCH * AHEAD, 2, *parts[1:]), BF16),
        ],
        scratch_shapes=[
            pltpu.VMEM(w_in.shape, BF16),
            pltpu.VMEM(w_out.shape, BF16),
            pltpu.VMEM(xs.shape, BF16),
            pltpu.VMEM(gates.shape, F32),
            pltpu.VMEM(gates.shape, F32),
            pltpu.VMEM(xs.shape, BF16),
            pltpu.VMEM(xs.shape, BF16),
            pltpu.VMEM((GROUPS, rows, hidden), BF16),
            pltpu.VMEM((GROUPS, rows, hidden), BF16),
            pltpu.VMEM((GROUPS, rows, hidden), BF16),
            pltpu.VMEM(xs.shape, BF16),
            pltpu.VMEM(xs.shape, BF16),
            pltpu.VMEM((2, 3, rows, TILE), F32),
            pltpu.VMEM((BATCH, *parts), BF16),
            pltpu.SemaphoreType.DMA((5,)),
            pltpu.SemaphoreType.DMA((3,)),
        ]
        + [peers] * 8
        + [pltpu.SemaphoreType.DMA((GROUPS,))]
        + [pltpu.SemaphoreType.DMA((BATCH * AHEAD, 2))] * 2,
        compiler_params=pltpu.CompilerParams(
            collective_id=1, has_side_effects=True, vmem_limit_bytes=61 * 1024 * 1024
        ),
        name="experts",
    )(xs, gates, g, w_in, w_out)


def column(values, k):
    return values[:, k : k + 1]


def route_column(routes_ref, k):
    row = routes_ref[k : k + 1, :].astype(F32)
    return jnp.broadcast_to(row, (128, row.shape[1])).T


def attend_pair(j, a, qkv_v, table_ref, p_ref):
    def lanes(part):
        return pl.ds(pl.multiple_of(256 * part + 128 * a, 128), 128)

    query = qkv_v[j, :, lanes(0)] * jnp.asarray(0.125, BF16)
    values_t = qkv_v[j, :, lanes(2)].T
    half = iota((512, 128), 1) // 64
    halves = []
    for t in range(2):
        shifted = spread_bias(table_ref[pl.ds(4 * j + 2 * a + t, 1), :])
        query_t = jnp.where(half == t, query, jnp.zeros_like(query))
        scores = [
            dot_nt(qkv_v[j, 128 * c : 128 * c + 128, lanes(1)], query_t)
            + shifted[:, 384 - 128 * c : 896 - 128 * c]
            for c in range(4)
        ]
        top = functools.reduce(jnp.maximum, [jnp.max(s, axis=0, keepdims=True) for s in scores])
        exps = [jnp.exp(s - top) for s in scores]
        total = functools.reduce(jnp.add, [jnp.sum(e, axis=0, keepdims=True) for e in exps])
        inverse = 1.0 / total
        for c in range(4):
            p_ref[t, 128 * c : 128 * c + 128, :] = (exps[c] * inverse).astype(BF16)
        halves.append(dot_nn(values_t, p_ref[t]))
    return jnp.where(iota((128, 512), 0) < 64, halves[0], halves[1])


def front_kernel(
    tokens_ref,
    gain1_ref,
    gain2_ref,
    table_ref,
    routes_ref,
    grad_ref,
    router_ref,
    ws_ref,
    wo_ref,
    wq_out,
    wo_out,
    qkv_out,
    p_out,
    g_back,
    mixed_t_ref,
    normed_t_ref,
    resid_ref,
    normed2_ref,
    xs_ref,
    gates_ref,
    cols_ref,
    wq_v,
    wo_v,
    qkv_v,
    p_v,
    mixed_v,
    normed_v,
    hot_v,
    g_v,
    own_sem,
    z_send,
    z_recv,
    xy_send,
    xy_recv,
    core_send,
    core_recv,
    g_send,
    g_recv,
    out_sem,
    p_sem,
):
    expert_count, capacity, width = xs_ref.shape
    lane_count = gates_ref.shape[2]
    slots = expert_count * capacity
    size = expert_count // GROUPS
    chips = expert_count // 2
    me, dp = lax.axis_index("expert"), lax.axis_index("dp")
    core, chip = me % 2, me // 2
    x, y = dp % 2, dp // 2
    core_peer = me + 1 - 2 * core
    x_peer, y_peer = dp + 1 - 2 * x, dp + 2 - 4 * y
    my_group, my_place = me // size, me % size
    chip_peers = [(chip + d) % chips for d in range(1, chips)]
    greet(
        [{"expert": (me + d) % expert_count} for d in range(1, expert_count)]
        + [{"dp": x_peer}, {"dp": y_peer}]
    )

    groups = ws_ref.shape[0]
    count = groups + 1
    srcs = [ws_ref.at[j] for j in range(groups)] + [wo_ref]
    bufs = [wq_v.at[j] for j in range(groups)] + [wo_v]
    widths = [ws_ref.shape[2]] * groups + [wo_ref.shape[1]]
    places = ((y, x), (y, 1 - x), (1 - y, x), (1 - y, 1 - x))

    def z_copy(j, peer, at):
        return remote(
            srcs[j], bufs[j].at[y, x, at, core], z_send.at[j, peer], z_recv.at[j, at], expert=peer * 2 + core
        )

    def own_copy(j):
        return pltpu.make_async_copy(srcs[j], bufs[j].at[y, x, chip, core], own_sem.at[j])

    def xy_copy(j, k):
        half = widths[j] // 2
        src = (
            bufs[j].at[y, x, :, core],
            bufs[j].at[y, x, :, core],
            bufs[j].at[1 - y, x, :, core, :, half : 2 * half],
            bufs[j].at[y, 1 - x, :, core, :, 0:half],
        )[k]
        return remote(src, src, xy_send.at[j, k], xy_recv.at[j, k], dp=(x_peer, y_peer)[k % 2])

    def core_copy(j, k):
        src = bufs[j].at[places[k][0], places[k][1], :, core]
        return remote(src, src, core_send.at[j, k], core_recv.at[j, k], expert=core_peer)

    def spread(j):
        own_copy(j).wait()
        for peer in chip_peers:
            z_copy(j, peer, peer).wait_recv()
        for k in range(2):
            xy_copy(j, k).start()
        core_copy(j, 0).start()

    def forward(j):
        for k in range(2):
            xy_copy(j, k).wait_recv()
            xy_copy(j, 3 - k).start()
            core_copy(j, 1 + k).start()

    def complete(j):
        for k in (2, 3):
            xy_copy(j, k).wait_recv()
        core_copy(j, 3).start()

    def out_copy(j):
        src, dst = (wq_v.at[j], wq_out.at[j]) if j < groups else (wo_v, wo_out)
        return pltpu.make_async_copy(src, dst, out_sem.at[j])

    def gathered(j):
        for k in range(4):
            core_copy(j, k).wait_recv()
        out_copy(j).start()

    for j in range(count):
        own_copy(j).start()
        for peer in chip_peers:
            z_copy(j, peer, chip).start()

    inputs = tokens_ref[...].astype(F32)
    inv_rms = lax.rsqrt(jnp.mean(inputs * inputs, axis=1, keepdims=True) + EPS)
    normed = (inputs * inv_rms * gain1_ref[...]).astype(BF16)
    normed_v[...] = normed
    normed_t_ref[...] = normed.T
    spread(0)
    spread(1)

    rows = routes_ref.shape[1]
    lane = iota((rows, 128), 1)
    routes = [route_column(routes_ref, k) for k in range(2)]
    hots = [lane == routes[k].astype(jnp.int32) for k in range(2)]
    earlier = (iota((rows, rows), 0) > iota((rows, rows), 1)).astype(BF16)
    ones = [jnp.where(h, 1.0, 0.0) for h in hots]
    counts = [dot_nn(earlier, o.astype(BF16)) for o in ones]
    counts[1] = counts[1] + jnp.sum(ones[0], axis=0, keepdims=True)
    slot = []
    for k in range(2):
        place = jnp.sum(counts[k] * ones[k], axis=1, keepdims=True)
        at = column(routes[k], 0) * capacity + place
        slot.append(jnp.where(place < capacity, at, float(slots)))
    slot_rows = jnp.where(lane == 0, slot[0], slot[1]).T
    slot_ids = iota((slots, rows), 0).astype(F32)
    hot = (slot_ids == slot_rows[0:1]) | (slot_ids == slot_rows[1:2])
    hot_v[...] = jnp.where(hot, 1.0, 0.0).astype(BF16)
    g_v[...] = dot_nn(hot_v[...], grad_ref[...]).astype(BF16).reshape(g_v.shape)

    def g_copy(peer, at):
        return remote(g_v.at[peer], g_back.at[at], g_send.at[peer], g_recv.at[at], expert=peer)

    def others(c):
        group = flip(my_group, c)
        return [group * size + (my_place + s) % size for s in range(1 if c == 0 else 0, size)]

    peers = [peer for c in (2, 3, 1, 0) for peer in others(c)]
    g_own = pltpu.make_async_copy(g_v.at[me], g_back.at[me], own_sem.at[count])
    g_own.start()

    def p_copy(j, a):
        return pltpu.make_async_copy(p_v.at[a], p_out.at[pl.ds(4 * j + 2 * a, 2)], p_sem.at[a])

    def group(j):
        gathered(j)
        qkv_v[j] = dot_nn(normed_v[...], wq_v[j].reshape(width, widths[j])).astype(BF16)

        def pair(a, carry):
            if j > 0:
                p_copy(j - 1, a).wait()
            mixed = attend_pair(j, a, qkv_v, table_ref, p_v.at[a])
            p_copy(j, a).start()
            span = pl.ds(pl.multiple_of(256 * j + 128 * a, 128), 128)
            mixed_t_ref[span, :] = mixed.astype(BF16)
            mixed_v[:, span] = mixed.T.astype(BF16)
            return carry

        lax.fori_loop(0, 2, pair, 0)

    forward(0)
    spread(2)
    spread(3)
    forward(1)
    complete(0)
    spread(4)
    for peer in peers:
        g_copy(peer, me).start()
    forward(2)
    complete(1)
    group(0)
    forward(3)
    complete(2)
    group(1)
    forward(4)
    complete(3)
    group(2)
    complete(4)
    group(3)
    qkv_copy = pltpu.make_async_copy(qkv_v, qkv_out, own_sem.at[count + 1])
    qkv_copy.start()
    gathered(groups)

    resid = tokens_ref[...].astype(F32) + dot_nn(mixed_v[...], wo_v[...].reshape(width, width))
    resid_ref[...] = resid
    inv_rms2 = lax.rsqrt(jnp.mean(resid * resid, axis=1, keepdims=True) + EPS)
    normed2 = (resid * inv_rms2 * gain2_ref[...]).astype(BF16)
    normed2_ref[...] = normed2
    xs_ref[...] = dot_nn(hot_v[...], normed2).astype(BF16).reshape(xs_ref.shape)
    rest = router_ref[...]
    logits = jnp.zeros((rows, expert_count), F32)
    for _ in range(3):
        piece = rest.astype(BF16)
        rest = rest - piece.astype(F32)
        logits = logits + dot_nt(normed2, piece)
    ids = iota((rows, expert_count), 1)
    chosen = [
        jnp.sum(
            jnp.where(ids == column(routes[k], 0).astype(jnp.int32), logits, 0.0),
            axis=1,
            keepdims=True,
        )
        for k in range(2)
    ]
    top = jnp.maximum(chosen[0], chosen[1])
    exps = [jnp.exp(c - top) for c in chosen]
    gates = [e / (exps[0] + exps[1]) for e in exps]
    cols = jnp.where(lane == 2, gates[0], jnp.where(lane == 3, gates[1], 0.0))
    cols_ref[...] = jnp.where(lane == 0, slot[0], jnp.where(lane == 1, slot[1], cols))
    wide = iota((rows, lane_count), 1)

    def gate_row(e, carry):
        base = (e * capacity).astype(F32)
        total = jnp.zeros((rows, lane_count), F32)
        for k in range(2):
            here = (wide.astype(F32) == slot[k] - base) & (wide < capacity)
            total = total + jnp.where(here, gates[k], 0.0)
        row = jnp.sum(total, axis=0, keepdims=True)
        gates_ref[pl.ds(e, 1)] = jnp.broadcast_to(row, (8, lane_count))[None]
        return carry

    lax.fori_loop(0, expert_count, gate_row, 0)

    for a in range(2):
        p_copy(groups - 1, a).wait()
    qkv_copy.wait()
    g_own.wait()
    for j in range(count):
        out_copy(j).wait()
        for peer in chip_peers:
            z_copy(j, peer, chip).wait_send()
        for k in range(4):
            xy_copy(j, k).wait_send()
            core_copy(j, k).wait_send()
    for peer in peers:
        g_copy(peer, me).wait_send()
        g_copy(peer, peer).wait_recv()


def front(tokens, gain1, gain2, table, routes, grad_out, router, ws, wo, dp_count, capacity):
    rows, width = tokens.shape
    expert_count = router.shape[0]
    chips = expert_count // 2
    groups, own, part = ws.shape
    heads = table.shape[0]
    lane_count = -(-capacity // 128) * 128
    vmem = pl.BlockSpec(memory_space=pltpu.VMEM)
    sem = pltpu.SemaphoreType.DMA
    shape = jax.ShapeDtypeStruct
    slots = (expert_count, capacity, width)
    spread = (2, 2, chips, 2, own)
    return pl.pallas_call(
        front_kernel,
        in_specs=[vmem] * 9,
        out_specs=[ANY] * 5 + [vmem] * 7,
        out_shape=[
            shape((groups, *spread, part), BF16),
            shape((*spread, width), BF16),
            shape((groups, rows, part), BF16),
            shape((heads, rows, rows), BF16),
            shape(slots, BF16),
            shape((width, rows), BF16),
            shape((width, rows), BF16),
            shape((rows, width), F32),
            shape((rows, width), BF16),
            shape(slots, BF16),
            shape((expert_count, 8, lane_count), F32),
            shape((rows, 128), F32),
        ],
        scratch_shapes=[
            pltpu.VMEM((groups, *spread, part), BF16),
            pltpu.VMEM((*spread, width), BF16),
            pltpu.VMEM((groups, rows, part), BF16),
            pltpu.VMEM((2, 2, rows, rows), BF16),
            pltpu.VMEM((rows, width), BF16),
            pltpu.VMEM((rows, width), BF16),
            pltpu.VMEM((expert_count * capacity, rows), BF16),
            pltpu.VMEM(slots, BF16),
            sem((groups + 3,)),
            sem((groups + 1, chips)),
            sem((groups + 1, chips)),
            sem((groups + 1, 4)),
            sem((groups + 1, 4)),
            sem((groups + 1, 4)),
            sem((groups + 1, 4)),
            sem((expert_count,)),
            sem((expert_count,)),
            sem((groups + 1,)),
            sem((2,)),
        ],
        compiler_params=pltpu.CompilerParams(
            collective_id=3, has_side_effects=True, vmem_limit_bytes=60 * 1024 * 1024
        ),
        name="front",
    )(tokens, gain1, gain2, table, routes, grad_out, router, ws, wo)


def attend_back_pair(j, a, qkv_v, p_ref, grads_v, dqkv_v, fold_ref):
    def lanes(part):
        return pl.ds(pl.multiple_of(256 * part + 128 * a, 128), 128)

    query = qkv_v[j, :, lanes(0)] * jnp.asarray(0.125, BF16)
    keys_t = qkv_v[j, :, lanes(1)].T
    values = qkv_v[j, :, lanes(2)]
    grads = grads_v[:, pl.ds(pl.multiple_of(256 * j + 128 * a, 128), 128)]
    half = iota((512, 128), 1) // 64
    dq_halves, dk_halves, dv_halves = [], [], []
    for t in range(2):
        values_t = jnp.where(half == t, values, jnp.zeros_like(values))
        probs = [p_ref[t, 128 * c : 128 * c + 128, :].astype(F32) for c in range(4)]
        grad_probs = [dot_nt(values_t[128 * c : 128 * c + 128], grads) for c in range(4)]
        delta = functools.reduce(
            jnp.add,
            [jnp.sum(p * g, axis=0, keepdims=True) for p, g in zip(probs, grad_probs)],
        )
        scores = [(p * (g - delta)).astype(BF16) for p, g in zip(probs, grad_probs)]
        padded = [
            jnp.concatenate(
                ([jnp.zeros((128, 384 - 128 * c), F32)] if c < 3 else [])
                + [scores[c].astype(F32), jnp.zeros((128, 128 + 128 * c), F32)],
                axis=1,
            )
            for c in range(4)
        ]
        fold_ref[pl.ds(4 * j + 2 * a + t, 1), :] = fold_bias(functools.reduce(jnp.add, padded))
        grad_scores = jnp.concatenate(scores, axis=0)
        dv_halves.append(dot_nn(p_ref[t], grads))
        dk_halves.append(dot_nn(grad_scores, query))
        dq_halves.append(dot_nn(keys_t, grad_scores))
    dq = jnp.where(iota((128, 512), 0) < 64, dq_halves[0], dq_halves[1]) * 0.125
    dqkv_v[:, lanes(0)] = dq.T.astype(BF16)
    dqkv_v[:, lanes(1)] = jnp.where(half == 0, dk_halves[0], dk_halves[1]).astype(BF16)
    dqkv_v[:, lanes(2)] = jnp.where(half == 0, dv_halves[0], dv_halves[1]).astype(BF16)


def dot_exact(a, b, dot=dot_nn):
    total = None
    for _ in range(3):
        piece = a.astype(BF16)
        a = a - piece.astype(F32)
        term = dot(piece, b)
        total = term if total is None else total + term
    return total


def dot_f32(a, b):
    total = None
    for _ in range(3):
        piece = b.astype(BF16)
        b = b - piece.astype(F32)
        term = dot_exact(a, piece)
        total = term if total is None else total + term
    return total


def back_kernel(
    dw_ref,
    head_ref,
    ys_ref,
    dx_ref,
    dgates_ref,
    cols_ref,
    routes_ref,
    tokens_ref,
    grad_ref,
    resid_ref,
    normed2_ref,
    normed_t_ref,
    mixed_t_ref,
    gain1_ref,
    gain2_ref,
    router_t_ref,
    bucket_hot_ref,
    wq_ref,
    wo_ref,
    qkv_ref,
    p_ref,
    first_ref,
    second_ref,
    small_out_ref,
    gq_out_ref,
    go_out_ref,
    block_ref,
    grad_tokens_ref,
    y_v,
    grads_q,
    grads_o,
    core_q,
    core_o,
    step1_q,
    step1_o,
    step2_q,
    step2_o,
    last_q,
    last_o,
    qkv_v,
    p_v,
    wq_v,
    dqkv_v,
    dmix_v,
    dn1_v,
    fold_v,
    small_v,
    own_v,
    first_v,
    pass_v,
    y_send,
    y_recv,
    first_send,
    first_recv,
    second_send,
    second_recv,
    ring_sem,
    small_send,
    small_recv,
    core_send,
    core_recv,
    step1_send,
    step1_recv,
    step2_send,
    step2_recv,
    last_send,
    last_recv,
    local_sem,
    p_sem,
    wq_sem,
):
    expert_count, capacity, width = ys_ref.shape
    slots = expert_count * capacity
    rows = tokens_ref.shape[0]
    chips = expert_count // 2
    size = expert_count // GROUPS
    me, dp = lax.axis_index("expert"), lax.axis_index("dp")
    core, chip = me % 2, me // 2
    x, y = dp % 2, dp // 2
    core_peer = me + 1 - 2 * core
    x_peer, y_peer = dp + 1 - 2 * x, dp + 2 - 4 * y
    my_group, my_place = me // size, me % size
    chip_peers = [(chip + d) % chips for d in range(1, chips)]
    greet(
        [{"expert": (me + d) % expert_count} for d in range(1, expert_count)]
        + [{"dp": x_peer}, {"dp": y_peer}]
    )

    tile_count = dw_ref.shape[0]
    batches = tile_count // BATCH

    def first_copy(t, i):
        sent, _, peer, _, _ = ways(dp, t)
        return remote(
            dw_ref.at[t, sent[i]],
            first_ref.at[t - BATCH * AHEAD, i],
            first_send.at[t - BATCH * AHEAD, i],
            first_recv.at[t - BATCH * AHEAD, i],
            dp=peer,
        )

    def second_copy(t, n):
        peer = ways(dp, t)[3]
        return remote(
            pass_v.at[n % 2, t % BATCH], second_ref.at[t], second_send.at[t], second_recv.at[t], dp=peer
        )

    def relay_loads(t, b):
        _, held, _, _, keep = ways(dp, t)
        q = t % BATCH
        came = head_ref.at[t, 1 - keep] if b < AHEAD else first_ref.at[t - BATCH * AHEAD, 1 - keep]
        return [
            pltpu.make_async_copy(dw_ref.at[t, held[1]], own_v.at[b % 2, q], ring_sem.at[b % 2, q, 0]),
            pltpu.make_async_copy(came, first_v.at[b % 2, q], ring_sem.at[b % 2, q, 1]),
        ]

    def over(b, body):
        def step(t, carry):
            body(t)
            return carry

        lax.fori_loop(BATCH * b, BATCH * b + BATCH, step, 0)

    def issue(b):
        def body(t):
            for i in range(2):
                first_copy(t, i).start()

        over(b, body)

    def relay_begin(b):
        def body(t):
            if b >= AHEAD:
                for i in range(2):
                    first_copy(t, i).wait_recv()
            for load in relay_loads(t, b):
                load.start()

        over(b, body)

    def relay_end(b):
        def body(t):
            for load in relay_loads(t, b):
                load.wait()
            if b >= 2:
                second_copy(t - 2 * BATCH, b).wait_send()
            q = t % BATCH
            pass_v[b % 2, q] = (
                own_v[b % 2, q].astype(F32) + first_v[b % 2, q].astype(F32)
            ).astype(BF16)
            second_copy(t, b).start()

        over(b, body)

    groups = grads_q.shape[0]
    count = groups + 1

    def pick(many, one, p):
        return many.at[p] if p < groups else one

    grads = [pick(grads_q, grads_o, p) for p in range(count)]
    cores = [pick(core_q, core_o, p) for p in range(count)]
    step1 = [pick(step1_q, step1_o, p) for p in range(count)]
    step2 = [pick(step2_q, step2_o, p) for p in range(count)]
    lasts = [pick(last_q, last_o, p) for p in range(count)]
    outs = [pick(gq_out_ref, go_out_ref, p) for p in range(count)]
    widths = [grads_q.shape[-1]] * groups + [grads_o.shape[-1]]

    def part_core(p):
        return remote(
            grads[p].at[:, :, :, 1 - core], cores[p], core_send.at[p], core_recv.at[p], expert=core_peer
        )

    def part_step1(p, b):
        half = widths[p] // 2
        src = (
            grads[p].at[:, 1 - x, :, core, :, 0:half]
            if b == 0
            else grads[p].at[1 - y, :, :, core, :, half : 2 * half]
        )
        return remote(
            src, step1[p].at[b], step1_send.at[p, b], step1_recv.at[p, b], dp=(x_peer, y_peer)[b]
        )

    def part_step2(p, b):
        src = step1[p].at[b, (1 - y, 1 - x)[b]]
        return remote(
            src, step2[p].at[b], step2_send.at[p, b], step2_recv.at[p, b], dp=(y_peer, x_peer)[b]
        )

    def part_last(p, peer, at):
        return remote(
            cores[p].at[0, 0, peer], lasts[p].at[at], last_send.at[p, peer], last_recv.at[p, at],
            expert=peer * 2 + core,
        )

    def part_a(p):
        part_core(p).start()

    def part_b(p):
        part_core(p).wait()
        total = grads[p][:, :, :, core].astype(F32) + cores[p][...].astype(F32)
        grads[p][:, :, :, core] = total.astype(BF16)
        for b in range(2):
            part_step1(p, b).start()

    def part_c(p):
        half = widths[p] // 2
        for b in range(2):
            part_step1(p, b).wait()
            for i in range(2):
                held = (
                    grads[p][i, x, :, core, :, 0:half]
                    if b == 0
                    else grads[p][y, i, :, core, :, half : 2 * half]
                )
                total = held.astype(F32) + step1[p][b, i].astype(F32)
                step1[p][b, i] = total.astype(BF16)
            part_step2(p, b).start()

    def part_d(p):
        half = widths[p] // 2
        for b in range(2):
            part_step2(p, b).wait()
            total = step1[p][b, (y, x)[b]].astype(F32) + step2[p][b].astype(F32)
            cores[p][0, 0, :, :, b * half : b * half + half] = total.astype(BF16)
        for peer in chip_peers:
            part_last(p, peer, chip).start()

    def part_e(p):
        total = cores[p][0, 0, chip].astype(F32)
        for peer in chip_peers:
            part_last(p, peer, peer).wait_recv()
            total = total + lasts[p][peer].astype(F32)
        outs[p][...] = total
        for peer in chip_peers:
            part_last(p, peer, chip).wait_send()

    partners = []
    bit = 1
    while bit < expert_count:
        partners.append({"expert": flip(me, bit)})
        bit *= 2
    partners += [{"dp": x_peer}, {"dp": y_peer}]
    stages = len(partners)

    def small_copy(s):
        return remote(
            small_v.at[0], small_v.at[1 + s], small_send.at[s], small_recv.at[s], **partners[s]
        )

    def small_next(s):
        small_copy(s).wait()
        small_v[0] = small_v[0] + small_v[1 + s]
        if s + 1 < stages:
            small_copy(s + 1).start()

    def y_copy(peer, at):
        return remote(ys_ref.at[peer], y_v.at[at], y_send.at[peer], y_recv.at[at], expert=peer)

    def others(c):
        group = flip(my_group, c)
        return [group * size + (my_place + s) % size for s in range(1 if c == 0 else 0, size)]

    peers = [peer for c in (2, 3, 1, 0) for peer in others(c)]

    def p_copy(j, a):
        return pltpu.make_async_copy(p_ref.at[pl.ds(4 * j + 2 * a, 2)], p_v.at[a], p_sem.at[a])

    def wq_copy(j):
        return pltpu.make_async_copy(wq_ref.at[j], wq_v.at[j % 2], wq_sem.at[j % 2])

    lane = iota((rows, 128), 1)
    slot = [column(cols_ref[...], k) for k in range(2)]
    gates = [column(cols_ref[...], 2 + k) for k in range(2)]

    def hots():
        at = iota((rows, slots), 1).astype(F32)
        return [at == s for s in slot]

    def dense():
        lanes = dgates_ref.shape[2]
        wide = iota((rows, lanes), 1)

        def step(e, totals):
            base = (e * capacity).astype(F32)
            row = dgates_ref[pl.ds(e, 1)][0][0:1]
            return tuple(
                totals[k]
                + jnp.where((wide.astype(F32) == slot[k] - base) & (wide < capacity), row, 0.0)
                for k in range(2)
            )

        zero = jnp.zeros((rows, lanes), F32)
        sums = lax.fori_loop(0, expert_count, step, (zero, zero))
        dgates = [jnp.sum(s, axis=1, keepdims=True) for s in sums]
        mean = gates[0] * dgates[0] + gates[1] * dgates[1]
        dchosen = [gates[k] * (dgates[k] - mean) for k in range(2)]
        dlogits = jnp.zeros((rows, 128), F32)
        for k in range(2):
            here = lane == route_column(routes_ref, k).astype(jnp.int32)
            dlogits = dlogits + jnp.where(here, dchosen[k], 0.0)
        small_rows = dot_exact(dlogits.T[0:expert_count], normed2_ref[...])
        small_v[0, 0:expert_count] = small_rows
        blank = jnp.zeros((128 - expert_count, width), F32)
        router = jnp.concatenate([router_t_ref[...], blank], axis=0)
        hot0, hot1 = hots()
        hot = jnp.where(hot0 | hot1, 1.0, 0.0).astype(BF16)
        dnormed = dot_f32(dlogits, router)
        dnormed = dnormed + dot_nn(hot, dx_ref[...].reshape(slots, width))
        resid = resid_ref[...]
        inv_rms = lax.rsqrt(jnp.mean(resid * resid, axis=1, keepdims=True) + EPS)
        normed = resid * inv_rms
        scaled = dnormed * gain2_ref[...]
        small_v[0, expert_count + 1 : expert_count + 2] = jnp.sum(
            dnormed * normed, axis=0, keepdims=True
        )
        inner = jnp.mean(scaled * normed, axis=1, keepdims=True)
        dresid = grad_ref[...].astype(F32) + inv_rms * (scaled - normed * inner)
        grad_tokens_ref[...] = dresid
        dresid_r = dresid.astype(BF16)
        grads_o[...] = dot_nn(mixed_t_ref[...], dresid_r).astype(BF16).reshape(grads_o.shape)
        part_a(groups)
        dmix_v[...] = dot_nt(dresid_r, wo_ref[...]).astype(BF16)

    def group(j):
        if j + 1 < groups:
            wq_copy(j + 1).start()

        def pair(a, carry):
            p_copy(j, a).wait()
            attend_back_pair(j, a, qkv_v, p_v.at[a], dmix_v, dqkv_v, fold_v)
            if j + 1 < groups:
                p_copy(j + 1, a).start()
            return carry

        lax.fori_loop(0, 2, pair, 0)
        block = dot_nn(normed_t_ref[...], dqkv_v[...])
        grads_q[j] = block.astype(BF16).reshape(grads_q.shape[1:])
        part_a(j)
        wq_copy(j).wait()
        term = dot_nt(dqkv_v[...], wq_v[j % 2])
        dn1_v[...] = term if j == 0 else dn1_v[...] + term

    def norm_back():
        inputs = tokens_ref[...].astype(F32)
        inv_rms = lax.rsqrt(jnp.mean(inputs * inputs, axis=1, keepdims=True) + EPS)
        normed = inputs * inv_rms
        dnormed = dn1_v[...]
        scaled = dnormed * gain1_ref[...]
        small_v[0, expert_count : expert_count + 1] = jnp.sum(
            dnormed * normed, axis=0, keepdims=True
        )
        inner = jnp.mean(scaled * normed, axis=1, keepdims=True)
        grad_tokens_ref[...] += inv_rms * (scaled - normed * inner)
        buckets = dot_exact(fold_v[...], bucket_hot_ref[...], dot_nt)
        base = expert_count + 2
        heads = fold_v.shape[0]
        small_v[0, base : base + heads, 0 : buckets.shape[1]] = buckets
        small_copy(0).start()

    def outputs():
        for peer in peers:
            y_copy(peer, peer).wait_recv()
        y_own.wait()
        values = y_v[...].reshape(slots, width)
        total = resid_ref[...]
        for k, hot in enumerate(hots()):
            total = total + gates[k] * dot_nn(jnp.where(hot, 1.0, 0.0).astype(BF16), values)
        block_ref[...] = total.astype(BF16)

    small_v[0] = jnp.zeros(small_v.shape[1:], F32)
    for peer in peers:
        y_copy(peer, me).start()
    y_own = pltpu.make_async_copy(ys_ref.at[me], y_v.at[me], local_sem.at[0])
    y_own.start()
    qkv_copy = pltpu.make_async_copy(qkv_ref, qkv_v, local_sem.at[1])
    qkv_copy.start()
    wq_copy(0).start()
    for a in range(2):
        p_copy(0, a).start()
    late = [b for b in range(AHEAD, batches)]

    def send_more(number):
        for _ in range(min(number, len(late))):
            issue(late.pop(0))

    def relay(b):
        relay_begin(b)
        relay_end(b)

    send_more(2)
    for b in range(AHEAD):
        relay_begin(b)
        if b > 0:
            relay_end(b - 1)
    relay_end(AHEAD - 1)
    send_more(1)
    dense()
    qkv_copy.wait()
    group(0)
    part_b(groups)
    relay(4)
    send_more(1)
    group(1)
    part_b(0)
    relay(5)
    send_more(1)
    group(2)
    part_b(1)
    part_c(groups)
    relay(6)
    send_more(1)
    group(3)
    part_b(2)
    part_c(0)
    send_more(1)
    norm_back()
    part_b(3)
    relay_begin(7)
    small_next(0)
    part_d(groups)
    relay_end(7)
    part_c(1)
    small_next(1)
    outputs()
    part_c(2)
    part_d(0)
    small_next(2)
    relay_begin(8)
    part_c(3)
    part_d(1)
    relay_end(8)
    small_next(3)
    relay_begin(9)
    part_d(2)
    part_e(groups)
    relay_end(9)
    for s in range(4, stages):
        small_next(s)
    small_out_ref[...] = small_v[0]
    relay_begin(10)
    part_d(3)
    relay_end(10)
    for p in range(groups):
        part_e(p)
    for b in (batches - 2, batches - 1):
        over(b, lambda t, b=b: second_copy(t, b).wait_send())

    def drain_first(t, carry):
        for i in range(2):
            first_copy(t, i).wait_send()
        return carry

    def drain_second(t, carry):
        second_copy(t, 0).wait_recv()
        return carry

    lax.fori_loop(BATCH * AHEAD, tile_count, drain_first, 0)
    lax.fori_loop(0, tile_count, drain_second, 0)
    for peer in peers:
        y_copy(peer, me).wait_send()


def back(
    dw, head, ys, dx, dgates, cols, routes, tokens, grad_out, resid, normed2, normed_t, mixed_t,
    gain1, gain2, router_t, bucket_hot, wq, wo, qkv, probs,
):
    tile_count, dp_count, deep, _ = dw.shape
    expert_count, capacity, width = ys.shape
    chips = expert_count // 2
    rows = tokens.shape[0]
    groups, _, part = qkv.shape
    own = width // (dp_count * expert_count)
    heads = probs.shape[0]
    small_rows = -(-(expert_count + 2 + heads) // 8) * 8
    stages = expert_count.bit_length() + 1
    vmem = pl.BlockSpec(memory_space=pltpu.VMEM)
    sem = pltpu.SemaphoreType.DMA
    shape = jax.ShapeDtypeStruct
    ring = (2, BATCH, deep, TILE)
    late = tile_count - BATCH * AHEAD

    def pairs(make):
        return [pltpu.VMEM((groups, *make(part)), BF16), pltpu.VMEM(make(width), BF16)]

    return pl.pallas_call(
        back_kernel,
        in_specs=[ANY] * 3 + [vmem] * 14 + [ANY, vmem, ANY, ANY],
        out_specs=[ANY] * 2 + [vmem] * 5,
        out_shape=[
            shape((late, 2, deep, TILE), BF16),
            shape((tile_count, deep, TILE), BF16),
            shape((small_rows, width), F32),
            shape((groups, own, part), F32),
            shape((own, width), F32),
            shape((rows, width), BF16),
            shape((rows, width), F32),
        ],
        scratch_shapes=[pltpu.VMEM(ys.shape, BF16)]
        + pairs(lambda w: (2, 2, chips, 2, own, w))
        + pairs(lambda w: (2, 2, chips, own, w))
        + pairs(lambda w: (2, 2, chips, own, w // 2))
        + pairs(lambda w: (2, chips, own, w // 2))
        + pairs(lambda w: (chips, own, w))
        + [
            pltpu.VMEM(qkv.shape, BF16),
            pltpu.VMEM((2, 2, rows, rows), BF16),
            pltpu.VMEM((2, *wq.shape[1:]), BF16),
            pltpu.VMEM((rows, part), BF16),
            pltpu.VMEM((rows, width), BF16),
            pltpu.VMEM((rows, width), F32),
            pltpu.VMEM((heads, bucket_hot.shape[1]), F32),
            pltpu.VMEM((stages + 1, small_rows, width), F32),
            pltpu.VMEM(ring, BF16),
            pltpu.VMEM(ring, BF16),
            pltpu.VMEM(ring, BF16),
            sem((expert_count,)),
            sem((expert_count,)),
            sem((late, 2)),
            sem((late, 2)),
            sem((tile_count,)),
            sem((tile_count,)),
            sem((2, BATCH, 2)),
            sem((stages,)),
            sem((stages,)),
            sem((groups + 1,)),
            sem((groups + 1,)),
            sem((groups + 1, 2)),
            sem((groups + 1, 2)),
            sem((groups + 1, 2)),
            sem((groups + 1, 2)),
            sem((groups + 1, chips)),
            sem((groups + 1, chips)),
            sem((2,)),
            sem((2,)),
            sem((2,)),
        ],
        compiler_params=pltpu.CompilerParams(
            collective_id=2, has_side_effects=True, vmem_limit_bytes=61 * 1024 * 1024
        ),
        name="back",
    )(
        dw, head, ys, dx, dgates, cols, routes, tokens, grad_out, resid, normed2, normed_t, mixed_t,
        gain1, gain2, router_t, bucket_hot, wq, wo, qkv, probs,
    )


def tail_kernel(expert_count, heads, buckets, where_ref, *refs):
    dw, head, first, second = (refs[BATCH * n : BATCH * n + BATCH] for n in range(4))
    small_ref, gq_ref, go_ref, block_ref, tokens_ref = refs[4 * BATCH : 4 * BATCH + 5]
    (
        in_ref,
        out_ref,
        router_ref,
        norm1_ref,
        norm2_ref,
        bias_ref,
        qkv_ref,
        proj_ref,
        block_out_ref,
        tokens_out_ref,
    ) = refs[4 * BATCH + 5 :]
    f = pl.program_id(0)
    for m in range(BATCH):
        came = jnp.where(f < AHEAD, head[m][0, 0].astype(F32), first[m][0, 0].astype(F32))
        total = dw[m][0, 0].astype(F32) + came + second[m][0].astype(F32)
        if m < 2:
            in_ref[m] = total
        else:
            out_ref[...] = total.T

    @pl.when(f == 0)
    def _():
        router_ref[...] = small_ref[0:expert_count]
        norm1_ref[...] = small_ref[expert_count : expert_count + 1]
        norm2_ref[...] = small_ref[expert_count + 1 : expert_count + 2]
        bias_ref[...] = small_ref[expert_count + 2 : expert_count + 2 + heads, 0:buckets]
        groups, _, part = gq_ref.shape
        third = part // 3
        for j in range(groups):
            for k in range(3):
                at = (k * groups + j) * third
                qkv_ref[:, at : at + third] = gq_ref[j, :, k * third : (k + 1) * third]
        proj_ref[...] = go_ref[...]
        block_out_ref[...] = block_ref[...]
        tokens_out_ref[...] = tokens_ref[...]


def tail(dw, head, first, second, small, gq, go, block, tokens, expert_count, heads, buckets):
    tile_count, _, deep, _ = dw.shape
    tiles = tile_count // BATCH
    groups, own, part = gq.shape
    rows, width = tokens.shape
    dp = lax.axis_index("dp")
    x, y = dp % 2, dp // 2
    where = jnp.stack([dp, dp, y, x]).astype(jnp.int32)
    shape = jax.ShapeDtypeStruct
    block_shape = (1, 1, deep, TILE)

    def whole(a):
        return pl.BlockSpec(a.shape, lambda f, w: (0,) * len(a.shape))

    late = BATCH * AHEAD
    in_specs = [
        pl.BlockSpec(block_shape, lambda f, w, m=m: (BATCH * f + m, w[(f + m) % 2], 0, 0))
        for m in range(BATCH)
    ]
    in_specs += [
        pl.BlockSpec(
            block_shape,
            lambda f, w, m=m: (
                jnp.minimum(BATCH * f + m, late - BATCH + m),
                w[2 + (f + m) % 2],
                0,
                0,
            ),
        )
        for m in range(BATCH)
    ]
    in_specs += [
        pl.BlockSpec(
            block_shape,
            lambda f, w, m=m: (jnp.maximum(BATCH * f + m - late, m), w[2 + (f + m) % 2], 0, 0),
        )
        for m in range(BATCH)
    ]
    in_specs += [
        pl.BlockSpec((1, deep, TILE), lambda f, w, m=m: (BATCH * f + m, 0, 0)) for m in range(BATCH)
    ]
    flat = [small, gq, go, block, tokens]
    outs = [
        shape((2, deep, tiles * TILE), F32),
        shape((tiles * TILE, deep), F32),
        shape((expert_count, width), F32),
        shape((1, width), F32),
        shape((1, width), F32),
        shape((heads, buckets), F32),
        shape((own, groups * part), F32),
        shape((own, width), F32),
        shape(block.shape, BF16),
        shape(tokens.shape, F32),
    ]
    return pl.pallas_call(
        functools.partial(tail_kernel, expert_count, heads, buckets),
        grid_spec=pltpu.PrefetchScalarGridSpec(
            num_scalar_prefetch=1,
            grid=(tiles,),
            in_specs=in_specs + [whole(a) for a in flat],
            out_specs=[
                pl.BlockSpec((2, deep, TILE), lambda f, w: (0, 0, f)),
                pl.BlockSpec((TILE, deep), lambda f, w: (f, 0)),
            ]
            + [whole(a) for a in outs[2:]],
        ),
        out_shape=outs,
        compiler_params=pltpu.CompilerParams(vmem_limit_bytes=48 * 1024 * 1024),
        name="tail",
    )(where, *[dw] * BATCH, *[head] * BATCH, *[first] * BATCH, *[second] * BATCH, *flat)


def shards(
    tokens,
    routes,
    rel_bucket,
    norm_gain1,
    w_qkv,
    w_out_proj,
    bias_table,
    norm_gain2,
    w_router,
    w_expert_in,
    w_expert_out,
    grad_out,
):
    row_count, model_width = tokens.shape
    bucket_count, head_count = bias_table.shape
    expert_count = lax.axis_size("expert")
    capacity = 10 * row_count // (4 * expert_count)
    slot_total = expert_count * capacity
    hidden_groups = 4
    shard_rows = w_qkv.shape[0]
    ws = w_qkv.reshape(shard_rows, 3, hidden_groups, -1).transpose(2, 0, 1, 3)
    ws = ws.reshape(hidden_groups, shard_rows, -1)

    bucket_ids = jnp.arange(bucket_count, dtype=jnp.int32)
    bucket_hot = jnp.concatenate(
        [bucket_ids[:, None] == rel_bucket[None, :], jnp.zeros((bucket_count, 1), bool)], axis=1
    ).astype(F32)
    table = jnp.dot(bias_table.T, bucket_hot, precision=HIGHEST)

    wq_full, out_full, qkv, probs, g_rows, mixed_t, normed1_t, residual, normed2_r, xs, gates, cols = front(
        tokens,
        norm_gain1[None],
        norm_gain2[None],
        table,
        routes.T,
        grad_out,
        w_router.T,
        ws,
        w_out_proj,
        lax.axis_size("dp"),
        capacity,
    )
    produced, grad_rows, grad_gates, grad_w, head = experts(
        xs, gates, g_rows, w_expert_in[0], w_expert_out[0], lax.axis_size("dp")
    )
    first, second, *rest = back(
        grad_w,
        head,
        produced,
        grad_rows,
        grad_gates,
        cols,
        routes.T,
        tokens,
        grad_out,
        residual,
        normed2_r,
        normed1_t,
        mixed_t,
        norm_gain1[None],
        norm_gain2[None],
        w_router.T,
        bucket_hot.astype(BF16),
        wq_full.reshape(hidden_groups, model_width, -1),
        out_full.reshape(model_width, model_width),
        qkv,
        probs,
    )
    (
        grad_in,
        grad_out_t,
        grad_router,
        grad_norm1,
        grad_norm2,
        grad_bias,
        grad_qkv,
        grad_out_proj,
        block_out,
        grad_tokens,
    ) = tail(grad_w, head, first, second, *rest, expert_count, head_count, bucket_count)
    grad_expert_in, grad_expert_out = grad_in[None], grad_out_t[None]
    grad_router_all, grad_bias = grad_router.T, grad_bias.T
    grad_norm1, grad_norm2 = grad_norm1[0], grad_norm2[0]
    return (
        block_out,
        grad_tokens,
        grad_norm1,
        grad_qkv,
        grad_out_proj,
        grad_bias,
        grad_norm2,
        grad_router_all,
        grad_expert_in,
        grad_expert_out,
    )


def solution(mesh):
    split = P(("dp", "expert"), None)
    in_specs = (
        split,
        split,
        P(),
        P(),
        split,
        split,
        P(),
        P(),
        P(),
        P("expert", None, None, None),
        P("expert", None, None),
        split,
    )
    out_specs = (
        split,
        split,
        P(),
        split,
        split,
        P(),
        P(),
        P(),
        P("expert", None, "dp", None),
        P("expert", None, "dp"),
    )
    return jax.shard_map(shards, mesh=mesh, in_specs=in_specs, out_specs=out_specs, check_vma=False)
```

```python
import functools

import jax
import jax.numpy as jnp
from jax import lax
from jax.experimental import pallas as pl
from jax.experimental.pallas import tpu as pltpu
from jax.sharding import PartitionSpec as P

LENGTH = 512
EPS = 1e-06
HIGHEST = lax.Precision.HIGHEST
F32 = jnp.float32
BF16 = jnp.bfloat16


def dot_nt(a, b):
    return lax.dot_general(a, b, (((1,), (1,)), ((), ())), preferred_element_type=F32)


def dot_nn(a, b):
    return jnp.dot(a, b, preferred_element_type=F32)


def iota(shape, axis):
    return lax.broadcasted_iota(jnp.int32, shape, axis)


def spread_bias(row):
    values = jnp.broadcast_to(row, (8, 1024))
    lift = 7 - iota((8, 1024), 0)
    for bit in (1, 2, 4):
        values = jnp.where((lift // bit) % 2 == 1, pltpu.roll(values, 1024 - bit, 1), values)
    return jnp.concatenate(
        [pltpu.roll(values, (904 + 8 * block) % 1024, 1) for block in range(16)], axis=0
    )


def fold_bias(parts):
    total = parts[0:8]
    total = pltpu.roll(total, 120, 1)
    for block in range(1, 16):
        piece = parts[8 * block : 8 * block + 8]
        total = total + (pltpu.roll(piece, 120 - 8 * block, 1) if block < 15 else piece)
    lift = 7 - iota((8, 1024), 0)
    for bit in (1, 2, 4):
        total = jnp.where((lift // bit) % 2 == 1, pltpu.roll(total, bit, 1), total)
    return jnp.sum(total, axis=0, keepdims=True)


MESH = pl.DeviceIdType.MESH
ANY = pl.BlockSpec(memory_space=pl.ANY)
GROUPS = 4
TILE = 256
WIDE = 512


def flip(index, mask):
    bit = 1
    while bit <= mask:
        if mask & bit:
            index = index + bit - 2 * bit * ((index // bit) % 2)
        bit *= 2
    return index


def remote(src, dst, send_sem, recv_sem, **axes):
    return pltpu.make_async_remote_copy(
        src_ref=src,
        dst_ref=dst,
        send_sem=send_sem,
        recv_sem=recv_sem,
        device_id=axes,
        device_id_type=MESH,
    )


def greet(partners):
    barrier = pltpu.get_barrier_semaphore()
    for axes in partners:
        pl.semaphore_signal(barrier, inc=1, device_id=axes, device_id_type=MESH)
    pl.semaphore_wait(barrier, len(partners))


def gelu_parts(x):
    root = 0.7978845608028654
    square = x * x
    t = jnp.tanh(root * x * (1.0 + 0.044715 * square))
    half = 0.5 * (1.0 + t)
    slope = half + 0.5 * x * (1.0 - t * t) * (root * (1.0 + 3 * 0.044715 * square))
    return x * half, slope


BATCH = 3
AHEAD = 4
CHIPS_FIRST_GROUPS = 1
CHIPS_FIRST = (*range(CHIPS_FIRST_GROUPS), 4)


def ways(dp, t):
    x, y = dp % 2, dp // 2
    x_peer, y_peer = dp + 1 - 2 * x, dp + 2 - 4 * y
    q = t % 2
    sent = [(1 - q) * (2 * i + 1 - x) + q * (2 * (1 - y) + i) for i in range(2)]
    keep = (1 - q) * y + q * x
    held = [(1 - q) * (2 * k + x) + q * (2 * y + k) for k in (keep, 1 - keep)]
    return sent, held, (1 - q) * x_peer + q * y_peer, (1 - q) * y_peer + q * x_peer, keep


def experts_kernel(
    xs_ref,
    gates_ref,
    g_ref,
    w_in_ref,
    w_out_ref,
    y_ref,
    dx_back_ref,
    dgates_back_ref,
    dw_ref,
    head_ref,
    w_in_v,
    w_out_v,
    x_v,
    gates_v,
    dgates_v,
    g_v,
    dy_v,
    hid_v,
    dgate_v,
    dup_v,
    y_v,
    dx_v,
    pre_v,
    stage,
    local_sem,
    stage_sem,
    x_send,
    x_recv,
    gates_send,
    gates_recv,
    dgates_send,
    dgates_recv,
    dx_send,
    dx_recv,
    y_sem,
    head_send,
    head_recv,
):
    expert_count, capacity, width = xs_ref.shape
    hidden = w_out_ref.shape[0]
    tiles = hidden // TILE
    size = expert_count // GROUPS
    rows = size * capacity
    me = lax.axis_index("expert")
    my_group, my_place = me // size, me % size

    def others(c):
        group = flip(my_group, c)
        return [group * size + (my_place + s) % size for s in range(1 if c == 0 else 0, size)]

    dp = lax.axis_index("dp")
    greet(
        [{"expert": (me + d) % expert_count} for d in range(1, expert_count)]
        + [{"dp": flip(dp, 1)}, {"dp": flip(dp, 2)}]
    )

    def send_rows(c):
        for peer in others(c):
            remote(
                xs_ref.at[peer], x_v.at[me], x_send.at[peer], x_recv.at[me], expert=peer
            ).start()
            remote(
                gates_ref.at[peer], gates_v.at[me], gates_send.at[peer], gates_recv.at[me], expert=peer
            ).start()

    for c in (2, 1, 0):
        send_rows(c)
    own = [
        pltpu.make_async_copy(xs_ref.at[me], x_v.at[me], local_sem.at[0]),
        pltpu.make_async_copy(gates_ref.at[me], gates_v.at[me], local_sem.at[1]),
        pltpu.make_async_copy(g_ref, g_v, local_sem.at[4]),
        pltpu.make_async_copy(w_in_ref, w_in_v, local_sem.at[2]),
        pltpu.make_async_copy(w_out_ref, w_out_v, local_sem.at[3]),
    ]
    for copy in own:
        copy.start()
    for copy in own:
        copy.wait()

    def y_copy(c):
        span = pl.ds(flip(my_group, c) * size, size)
        return pltpu.make_async_copy(y_v.at[span], y_ref.at[span], y_sem.at[c])

    def back_copies(peer, at):
        return [
            remote(
                dx_v.at[peer], dx_back_ref.at[at], dx_send.at[peer], dx_recv.at[at], expert=peer
            ),
            remote(
                dgates_v.at[peer],
                dgates_back_ref.at[at],
                dgates_send.at[peer],
                dgates_recv.at[at],
                expert=peer,
            ),
        ]

    dgates_v[...] = jnp.zeros_like(dgates_v)
    for c in range(GROUPS):
        group = flip(my_group, c)
        span = pl.ds(group * size, size)
        for peer in others(c):
            remote(
                xs_ref.at[peer], x_v.at[peer], x_send.at[peer], x_recv.at[peer], expert=peer
            ).wait_recv()
            remote(
                gates_ref.at[peer], gates_v.at[peer], gates_send.at[peer], gates_recv.at[peer], expert=peer
            ).wait_recv()
        for s in range(size):
            src = group * size + s
            gate_col = gates_v[src].T[0:capacity, 0:1]
            dy_v[src] = (g_v[src].astype(F32) * gate_col).astype(BF16)

        def before(f, slot, span=span):
            cols = pl.ds(pl.multiple_of(f * TILE, TILE), TILE)
            x = x_v[span].reshape(rows, width)
            pre_v[slot, 0] = dot_nn(x, w_in_v[0, :, cols])
            pre_v[slot, 1] = dot_nn(x, w_in_v[1, :, cols])
            pre_v[slot, 2] = dot_nt(dy_v[span].reshape(rows, width), w_out_v[cols, :])

        def after(f, slot, group=group):
            cols = pl.ds(pl.multiple_of(f * TILE, TILE), TILE)
            gate, up, dhid = pre_v[slot, 0], pre_v[slot, 1], pre_v[slot, 2]
            gelu, slope = gelu_parts(gate)
            hid_v[group, :, cols] = (gelu * up).astype(BF16)
            dgate_v[group, :, cols] = (dhid * up * slope).astype(BF16)
            dup_v[group, :, cols] = (dhid * gelu).astype(BF16)

        def two(h, carry):
            before(2 * h + 1, 1)
            after(2 * h, 0)
            before(jnp.minimum(2 * h + 2, tiles - 1), 0)
            after(2 * h + 1, 1)
            return carry

        def backs(n, carry, group=group, span=span):
            cols = pl.ds(pl.multiple_of(n * WIDE, WIDE), WIDE)
            out = dot_nn(hid_v[group], w_out_v[:, cols])
            y_v[span, :, cols] = out.astype(BF16).reshape(size, capacity, WIDE)
            back = dot_nt(dgate_v[group], w_in_v[0, cols, :])
            back = back + dot_nt(dup_v[group], w_in_v[1, cols, :])
            dx_v[span, :, cols] = back.astype(BF16).reshape(size, capacity, WIDE)
            return carry

        before(0, 0)
        lax.fori_loop(0, tiles // 2, two, 0)
        if tiles % 2:
            after(tiles - 1, 0)
        lax.fori_loop(0, width // WIDE, backs, 0)
        if c == 0:
            send_rows(3)
        y_copy(c).start()
        for s in range(size):
            src = group * size + s
            product = g_v[src].astype(F32) * y_v[src].astype(F32)
            dgate = jnp.sum(product, axis=1, keepdims=True)
            dgates_v[src, :, 0:capacity] = jnp.broadcast_to(dgate, (capacity, 128)).T[0:8]
        for peer in others(c):
            for copy in back_copies(peer, me):
                copy.start()
    own = [
        pltpu.make_async_copy(dx_v.at[me], dx_back_ref.at[me], local_sem.at[0]),
        pltpu.make_async_copy(dgates_v.at[me], dgates_back_ref.at[me], local_sem.at[1]),
    ]
    for copy in own:
        copy.start()

    slots = expert_count * capacity
    w_in_v[0, :, 0:slots] = x_v[...].reshape(slots, width).T
    w_in_v[1, :, 0:slots] = dy_v[...].reshape(slots, width).T

    def put(f, m):
        return pltpu.make_async_copy(stage.at[m], dw_ref.at[BATCH * f + m], stage_sem.at[m])

    def head_copy(f, m, i):
        t = BATCH * f + m
        sent, _, peer, _, _ = ways(dp, t)
        return remote(
            dw_ref.at[t, sent[i]], head_ref.at[t, i], head_send.at[t, i], head_recv.at[t, i], dp=peer
        )

    parts, deep = stage.shape[1:3]

    def grads(f, carry):
        cols = pl.ds(pl.multiple_of(f * TILE, TILE), TILE)
        for m, (side, right) in enumerate(((0, dgate_v), (0, dup_v), (1, hid_v))):

            @pl.when(f > 0)
            def _():
                put(f - 1, m).wait()

            @pl.when((f > 0) & (f <= AHEAD))
            def _():
                for i in range(2):
                    head_copy(f - 1, m, i).start()

            across = right[:, :, cols].reshape(slots, TILE)
            for r in range(0, parts, 2):
                span = slice(r * deep, (r + 2) * deep)
                block = dot_nn(w_in_v[side, span, 0:slots], across)
                stage[m, r : r + 2] = block.astype(BF16).reshape(2, deep, TILE)
            put(f, m).start()
        return carry

    lax.fori_loop(0, tiles, grads, 0)
    for m in range(BATCH):
        put(tiles - 1, m).wait()

    def heads(t, carry):
        for i in range(2):
            head_copy(t // BATCH, t % BATCH, i).wait()
        return carry

    lax.fori_loop(0, BATCH * AHEAD, heads, 0)
    for copy in own:
        copy.wait()
    for c in range(GROUPS):
        for peer in others(c):
            for src, dst, send_sem, recv_sem in (
                (xs_ref, x_v, x_send, x_recv),
                (gates_ref, gates_v, gates_send, gates_recv),
            ):
                remote(
                    src.at[peer], dst.at[me], send_sem.at[peer], recv_sem.at[me], expert=peer
                ).wait_send()
            for copy in back_copies(peer, me):
                copy.wait_send()
            for copy in back_copies(peer, peer):
                copy.wait_recv()
        y_copy(c).wait()


def experts(xs, gates, g, w_in, w_out, dp_count):
    expert_count, capacity, width = xs.shape
    hidden = w_out.shape[0]
    size = expert_count // GROUPS
    tiles = hidden // TILE
    rows = size * capacity
    slots = jax.ShapeDtypeStruct(xs.shape, BF16)
    parts = (dp_count, width // dp_count, TILE)
    peers = pltpu.SemaphoreType.DMA((expert_count,))
    return pl.pallas_call(
        experts_kernel,
        in_specs=[ANY] * 5,
        out_specs=[ANY] * 5,
        out_shape=[slots, slots, jax.ShapeDtypeStruct(gates.shape, F32), jax.ShapeDtypeStruct((BATCH * tiles, *parts), BF16),
            jax.ShapeDtypeStruct((BATCH * AHEAD, 2, *parts[1:]), BF16),
        ],
        scratch_shapes=[
            pltpu.VMEM(w_in.shape, BF16),
            pltpu.VMEM(w_out.shape, BF16),
            pltpu.VMEM(xs.shape, BF16),
            pltpu.VMEM(gates.shape, F32),
            pltpu.VMEM(gates.shape, F32),
            pltpu.VMEM(xs.shape, BF16),
            pltpu.VMEM(xs.shape, BF16),
            pltpu.VMEM((GROUPS, rows, hidden), BF16),
            pltpu.VMEM((GROUPS, rows, hidden), BF16),
            pltpu.VMEM((GROUPS, rows, hidden), BF16),
            pltpu.VMEM(xs.shape, BF16),
            pltpu.VMEM(xs.shape, BF16),
            pltpu.VMEM((2, 3, rows, TILE), F32),
            pltpu.VMEM((BATCH, *parts), BF16),
            pltpu.SemaphoreType.DMA((5,)),
            pltpu.SemaphoreType.DMA((3,)),
        ]
        + [peers] * 8
        + [pltpu.SemaphoreType.DMA((GROUPS,))]
        + [pltpu.SemaphoreType.DMA((BATCH * AHEAD, 2))] * 2,
        compiler_params=pltpu.CompilerParams(
            collective_id=1, has_side_effects=True, vmem_limit_bytes=61 * 1024 * 1024
        ),
        name="experts",
    )(xs, gates, g, w_in, w_out)


def column(values, k):
    return values[:, k : k + 1]


def route_column(routes_ref, k):
    row = routes_ref[k : k + 1, :].astype(F32)
    return jnp.broadcast_to(row, (128, row.shape[1])).T


def attend_pair(j, a, qkv_v, table_ref, p_ref):
    def lanes(part):
        return pl.ds(pl.multiple_of(256 * part + 128 * a, 128), 128)

    query = qkv_v[j, :, lanes(0)] * jnp.asarray(0.125, BF16)
    values_t = qkv_v[j, :, lanes(2)].T
    half = iota((512, 128), 1) // 64
    halves = []
    for t in range(2):
        shifted = spread_bias(table_ref[pl.ds(4 * j + 2 * a + t, 1), :])
        query_t = jnp.where(half == t, query, jnp.zeros_like(query))
        scores = [
            dot_nt(qkv_v[j, 128 * c : 128 * c + 128, lanes(1)], query_t)
            + shifted[:, 384 - 128 * c : 896 - 128 * c]
            for c in range(4)
        ]
        top = functools.reduce(jnp.maximum, [jnp.max(s, axis=0, keepdims=True) for s in scores])
        exps = [jnp.exp(s - top) for s in scores]
        total = functools.reduce(jnp.add, [jnp.sum(e, axis=0, keepdims=True) for e in exps])
        inverse = 1.0 / total
        for c in range(4):
            p_ref[t, 128 * c : 128 * c + 128, :] = (exps[c] * inverse).astype(BF16)
        halves.append(dot_nn(values_t, p_ref[t]))
    return jnp.where(iota((128, 512), 0) < 64, halves[0], halves[1])


def front_kernel(
    tokens_ref,
    gain1_ref,
    gain2_ref,
    table_ref,
    routes_ref,
    grad_ref,
    router_ref,
    w_qkv_ref,
    wo_ref,
    wq_out,
    wo_out,
    qkv_out,
    p_out,
    g_back,
    mixed_t_hbm,
    normed_t_hbm,
    resid_hbm,
    normed2_hbm,
    xs_hbm,
    gates_ref,
    cols_ref,
    ws_ref,
    wq_v,
    wo_v,
    qkv_v,
    p_v,
    mixed_v,
    normed_v,
    hot_v,
    g_v,
    own_sem,
    z_send,
    z_recv,
    xy_send,
    xy_recv,
    core_send,
    core_recv,
    g_send,
    g_recv,
    out_sem,
    p_sem,
    mixed_t_ref,
    normed_t_ref,
    resid_ref,
    normed2_ref,
    xs_ref,
    stores_sem,
):
    stores = {
        name: pltpu.make_async_copy(src, dst, stores_sem.at[n])
        for n, (name, src, dst) in enumerate(
            (
                ("mixed_t", mixed_t_ref, mixed_t_hbm),
                ("normed_t", normed_t_ref, normed_t_hbm),
                ("resid", resid_ref, resid_hbm),
                ("normed2", normed2_ref, normed2_hbm),
                ("xs", xs_ref, xs_hbm),
            )
        )
    }
    expert_count, capacity, width = xs_ref.shape
    lane_count = gates_ref.shape[2]
    slots = expert_count * capacity
    size = expert_count // GROUPS
    chips = expert_count // 2
    me, dp = lax.axis_index("expert"), lax.axis_index("dp")
    core, chip = me % 2, me // 2
    x, y = dp % 2, dp // 2
    core_peer = me + 1 - 2 * core
    x_peer, y_peer = dp + 1 - 2 * x, dp + 2 - 4 * y
    my_group, my_place = me // size, me % size
    chip_peers = [(chip + d) % chips for d in range(1, chips)]
    greet(
        [{"expert": (me + d) % expert_count} for d in range(1, expert_count)]
        + [{"dp": x_peer}, {"dp": y_peer}]
    )

    groups = ws_ref.shape[0]
    count = groups + 1
    srcs = [ws_ref.at[j] for j in range(groups)] + [wo_ref]
    bufs = [wq_v.at[j] for j in range(groups)] + [wo_v]
    widths = [ws_ref.shape[2]] * groups + [wo_ref.shape[1]]
    places = ((y, x), (y, 1 - x), (1 - y, x), (1 - y, 1 - x))

    def z_copy(j, peer, at):
        return remote(
            srcs[j], bufs[j].at[y, x, at, core], z_send.at[j, peer], z_recv.at[j, at], expert=peer * 2 + core
        )

    def own_copy(j):
        return pltpu.make_async_copy(srcs[j], bufs[j].at[y, x, chip, core], own_sem.at[j])

    def xy_copy(j, k):
        half = widths[j] // 2
        src = (
            bufs[j].at[y, x, :, core],
            bufs[j].at[y, x, :, core],
            bufs[j].at[1 - y, x, :, core, :, half : 2 * half],
            bufs[j].at[y, 1 - x, :, core, :, 0:half],
        )[k]
        return remote(src, src, xy_send.at[j, k], xy_recv.at[j, k], dp=(x_peer, y_peer)[k % 2])

    def core_copy(j, k):
        src = bufs[j].at[places[k][0], places[k][1], :, core]
        return remote(src, src, core_send.at[j, k], core_recv.at[j, k], expert=core_peer)

    def spread(j):
        own_copy(j).wait()
        for peer in chip_peers:
            z_copy(j, peer, peer).wait_recv()
        for k in range(2):
            xy_copy(j, k).start()
        core_copy(j, 0).start()

    def forward(j):
        for k in range(2):
            xy_copy(j, k).wait_recv()
            xy_copy(j, 3 - k).start()
            core_copy(j, 1 + k).start()

    def complete(j):
        for k in (2, 3):
            xy_copy(j, k).wait_recv()
        core_copy(j, 3).start()

    def out_copy(j):
        src, dst = (wq_v.at[j], wq_out.at[j]) if j < groups else (wo_v, wo_out)
        return pltpu.make_async_copy(src, dst, out_sem.at[j])

    def gathered(j):
        for k in range(4):
            core_copy(j, k).wait_recv()
        out_copy(j).start()

    third = ws_ref.shape[2] // 3
    for j in range(count):
        if j < groups:
            for k in range(3):
                at = (k * groups + j) * third
                ws_ref[j, :, k * third : (k + 1) * third] = w_qkv_ref[:, at : at + third]
        own_copy(j).start()
        for peer in chip_peers:
            z_copy(j, peer, chip).start()

    inputs = tokens_ref[...].astype(F32)
    inv_rms = lax.rsqrt(jnp.mean(inputs * inputs, axis=1, keepdims=True) + EPS)
    normed = (inputs * inv_rms * gain1_ref[...]).astype(BF16)
    normed_v[...] = normed
    normed_t_ref[...] = normed.T
    stores["normed_t"].start()
    spread(0)
    spread(1)

    rows = routes_ref.shape[1]
    lane = iota((rows, 128), 1)
    routes = [route_column(routes_ref, k) for k in range(2)]
    hots = [lane == routes[k].astype(jnp.int32) for k in range(2)]
    earlier = (iota((rows, rows), 0) > iota((rows, rows), 1)).astype(BF16)
    ones = [jnp.where(h, 1.0, 0.0) for h in hots]
    counts = [dot_nn(earlier, o.astype(BF16)) for o in ones]
    counts[1] = counts[1] + jnp.sum(ones[0], axis=0, keepdims=True)
    slot = []
    for k in range(2):
        place = jnp.sum(counts[k] * ones[k], axis=1, keepdims=True)
        at = column(routes[k], 0) * capacity + place
        slot.append(jnp.where(place < capacity, at, float(slots)))
    slot_rows = jnp.where(lane == 0, slot[0], slot[1]).T
    slot_ids = iota((slots, rows), 0).astype(F32)
    hot = (slot_ids == slot_rows[0:1]) | (slot_ids == slot_rows[1:2])
    hot_v[...] = jnp.where(hot, 1.0, 0.0).astype(BF16)
    g_v[...] = dot_nn(hot_v[...], grad_ref[...]).astype(BF16).reshape(g_v.shape)

    def g_copy(peer, at):
        return remote(g_v.at[peer], g_back.at[at], g_send.at[peer], g_recv.at[at], expert=peer)

    def others(c):
        group = flip(my_group, c)
        return [group * size + (my_place + s) % size for s in range(1 if c == 0 else 0, size)]

    peers = [peer for c in (2, 3, 1, 0) for peer in others(c)]
    g_own = pltpu.make_async_copy(g_v.at[me], g_back.at[me], own_sem.at[count])
    g_own.start()

    def p_copy(j, a):
        return pltpu.make_async_copy(p_v.at[a], p_out.at[pl.ds(4 * j + 2 * a, 2)], p_sem.at[a])

    def group(j):
        gathered(j)
        qkv_v[j] = dot_nn(normed_v[...], wq_v[j].reshape(width, widths[j])).astype(BF16)

        def pair(a, carry):
            if j > 0:
                p_copy(j - 1, a).wait()
            mixed = attend_pair(j, a, qkv_v, table_ref, p_v.at[a])
            p_copy(j, a).start()
            span = pl.ds(pl.multiple_of(256 * j + 128 * a, 128), 128)
            mixed_t_ref[span, :] = mixed.astype(BF16)
            mixed_v[:, span] = mixed.T.astype(BF16)
            return carry

        lax.fori_loop(0, 2, pair, 0)

    forward(0)
    spread(2)
    spread(3)
    forward(1)
    complete(0)
    spread(4)
    for peer in peers:
        g_copy(peer, me).start()
    forward(2)
    complete(1)
    group(0)
    forward(3)
    complete(2)
    group(1)
    forward(4)
    complete(3)
    group(2)
    complete(4)
    group(3)
    qkv_copy = pltpu.make_async_copy(qkv_v, qkv_out, own_sem.at[count + 1])
    qkv_copy.start()
    stores["mixed_t"].start()
    gathered(groups)

    resid = tokens_ref[...].astype(F32) + dot_nn(mixed_v[...], wo_v[...].reshape(width, width))
    resid_ref[...] = resid
    stores["resid"].start()
    inv_rms2 = lax.rsqrt(jnp.mean(resid * resid, axis=1, keepdims=True) + EPS)
    normed2 = (resid * inv_rms2 * gain2_ref[...]).astype(BF16)
    normed2_ref[...] = normed2
    stores["normed2"].start()
    xs_ref[...] = dot_nn(hot_v[...], normed2).astype(BF16).reshape(xs_ref.shape)
    stores["xs"].start()
    rest = router_ref[...]
    logits = jnp.zeros((rows, expert_count), F32)
    for _ in range(3):
        piece = rest.astype(BF16)
        rest = rest - piece.astype(F32)
        logits = logits + dot_nt(normed2, piece)
    ids = iota((rows, expert_count), 1)
    chosen = [
        jnp.sum(
            jnp.where(ids == column(routes[k], 0).astype(jnp.int32), logits, 0.0),
            axis=1,
            keepdims=True,
        )
        for k in range(2)
    ]
    top = jnp.maximum(chosen[0], chosen[1])
    exps = [jnp.exp(c - top) for c in chosen]
    gates = [e / (exps[0] + exps[1]) for e in exps]
    cols = jnp.where(lane == 2, gates[0], jnp.where(lane == 3, gates[1], 0.0))
    cols_ref[...] = jnp.where(lane == 0, slot[0], jnp.where(lane == 1, slot[1], cols))
    wide = iota((rows, lane_count), 1)

    def gate_row(e, carry):
        base = (e * capacity).astype(F32)
        total = jnp.zeros((rows, lane_count), F32)
        for k in range(2):
            here = (wide.astype(F32) == slot[k] - base) & (wide < capacity)
            total = total + jnp.where(here, gates[k], 0.0)
        row = jnp.sum(total, axis=0, keepdims=True)
        gates_ref[pl.ds(e, 1)] = jnp.broadcast_to(row, (8, lane_count))[None]
        return carry

    lax.fori_loop(0, expert_count, gate_row, 0)

    for a in range(2):
        p_copy(groups - 1, a).wait()
    qkv_copy.wait()
    for copy in stores.values():
        copy.wait()
    g_own.wait()
    for j in range(count):
        out_copy(j).wait()
        for peer in chip_peers:
            z_copy(j, peer, chip).wait_send()
        for k in range(4):
            xy_copy(j, k).wait_send()
            core_copy(j, k).wait_send()
    for peer in peers:
        g_copy(peer, me).wait_send()
        g_copy(peer, peer).wait_recv()


def front(tokens, gain1, gain2, table, routes, grad_out, router, w_qkv, wo, groups, capacity):
    rows, width = tokens.shape
    expert_count = router.shape[0]
    chips = expert_count // 2
    own, part = w_qkv.shape[0], w_qkv.shape[1] // groups
    heads = table.shape[0]
    lane_count = -(-capacity // 128) * 128
    vmem = pl.BlockSpec(memory_space=pltpu.VMEM)
    sem = pltpu.SemaphoreType.DMA
    shape = jax.ShapeDtypeStruct
    slots = (expert_count, capacity, width)
    spread = (2, 2, chips, 2, own)
    return pl.pallas_call(
        front_kernel,
        in_specs=[vmem] * 9,
        out_specs=[ANY] * 10 + [vmem] * 2,
        out_shape=[
            shape((groups, *spread, part), BF16),
            shape((*spread, width), BF16),
            shape((groups, rows, part), BF16),
            shape((heads, rows, rows), BF16),
            shape(slots, BF16),
            shape((width, rows), BF16),
            shape((width, rows), BF16),
            shape((rows, width), F32),
            shape((rows, width), BF16),
            shape(slots, BF16),
            shape((expert_count, 8, lane_count), F32),
            shape((rows, 128), F32),
        ],
        scratch_shapes=[
            pltpu.VMEM((groups, own, part), BF16),
            pltpu.VMEM((groups, *spread, part), BF16),
            pltpu.VMEM((*spread, width), BF16),
            pltpu.VMEM((groups, rows, part), BF16),
            pltpu.VMEM((2, 2, rows, rows), BF16),
            pltpu.VMEM((rows, width), BF16),
            pltpu.VMEM((rows, width), BF16),
            pltpu.VMEM((expert_count * capacity, rows), BF16),
            pltpu.VMEM(slots, BF16),
            sem((groups + 3,)),
            sem((groups + 1, chips)),
            sem((groups + 1, chips)),
            sem((groups + 1, 4)),
            sem((groups + 1, 4)),
            sem((groups + 1, 4)),
            sem((groups + 1, 4)),
            sem((expert_count,)),
            sem((expert_count,)),
            sem((groups + 1,)),
            sem((2,)),
            pltpu.VMEM((width, rows), BF16),
            pltpu.VMEM((width, rows), BF16),
            pltpu.VMEM((rows, width), F32),
            pltpu.VMEM((rows, width), BF16),
            pltpu.VMEM(slots, BF16),
            sem((5,)),
        ],
        compiler_params=pltpu.CompilerParams(
            collective_id=3, has_side_effects=True, vmem_limit_bytes=60 * 1024 * 1024
        ),
        name="front",
    )(tokens, gain1, gain2, table, routes, grad_out, router, w_qkv, wo)


def attend_back_pair(j, a, qkv_v, p_ref, grads_v, dqkv_v, fold_ref):
    def lanes(part):
        return pl.ds(pl.multiple_of(256 * part + 128 * a, 128), 128)

    query = qkv_v[j, :, lanes(0)] * jnp.asarray(0.125, BF16)
    keys_t = qkv_v[j, :, lanes(1)].T
    values = qkv_v[j, :, lanes(2)]
    grads = grads_v[:, pl.ds(pl.multiple_of(256 * j + 128 * a, 128), 128)]
    half = iota((512, 128), 1) // 64
    dq_halves, dk_halves, dv_halves = [], [], []
    for t in range(2):
        values_t = jnp.where(half == t, values, jnp.zeros_like(values))
        probs = [p_ref[t, 128 * c : 128 * c + 128, :].astype(F32) for c in range(4)]
        grad_probs = [dot_nt(values_t[128 * c : 128 * c + 128], grads) for c in range(4)]
        delta = functools.reduce(
            jnp.add,
            [jnp.sum(p * g, axis=0, keepdims=True) for p, g in zip(probs, grad_probs)],
        )
        scores = [(p * (g - delta)).astype(BF16) for p, g in zip(probs, grad_probs)]
        padded = [
            jnp.concatenate(
                ([jnp.zeros((128, 384 - 128 * c), F32)] if c < 3 else [])
                + [scores[c].astype(F32), jnp.zeros((128, 128 + 128 * c), F32)],
                axis=1,
            )
            for c in range(4)
        ]
        fold_ref[pl.ds(4 * j + 2 * a + t, 1), :] = fold_bias(functools.reduce(jnp.add, padded))
        grad_scores = jnp.concatenate(scores, axis=0)
        dv_halves.append(dot_nn(p_ref[t], grads))
        dk_halves.append(dot_nn(grad_scores, query))
        dq_halves.append(dot_nn(keys_t, grad_scores))
    dq = jnp.where(iota((128, 512), 0) < 64, dq_halves[0], dq_halves[1]) * 0.125
    dqkv_v[:, lanes(0)] = dq.T.astype(BF16)
    dqkv_v[:, lanes(1)] = jnp.where(half == 0, dk_halves[0], dk_halves[1]).astype(BF16)
    dqkv_v[:, lanes(2)] = jnp.where(half == 0, dv_halves[0], dv_halves[1]).astype(BF16)


def dot_exact(a, b, dot=dot_nn):
    total = None
    for _ in range(3):
        piece = a.astype(BF16)
        a = a - piece.astype(F32)
        term = dot(piece, b)
        total = term if total is None else total + term
    return total


def dot_f32(a, b):
    total = None
    for _ in range(3):
        piece = b.astype(BF16)
        b = b - piece.astype(F32)
        term = dot_exact(a, piece)
        total = term if total is None else total + term
    return total


def back_kernel(
    dw_ref,
    head_ref,
    ys_ref,
    dx_hbm,
    dgates_hbm,
    cols_ref,
    routes_ref,
    tokens_hbm,
    grad_hbm,
    resid_hbm,
    normed2_hbm,
    normed_t_hbm,
    mixed_t_hbm,
    gain1_ref,
    gain2_ref,
    router_t_ref,
    bucket_hot_ref,
    wq_ref,
    wo_hbm,
    qkv_ref,
    p_ref,
    first_ref,
    second_ref,
    small_out_ref,
    gq_out_ref,
    go_out_ref,
    block_hbm,
    grad_tokens_hbm,
    y_v,
    grads_q,
    grads_o,
    core_q,
    core_o,
    step1_q,
    step1_o,
    step2_q,
    step2_o,
    last_q,
    last_o,
    rows_q,
    rows_o,
    sum_q,
    sum_o,
    qkv_v,
    p_v,
    wq_v,
    dqkv_v,
    dmix_v,
    dn1_v,
    fold_v,
    small_v,
    own_v,
    first_v,
    pass_v,
    y_send,
    y_recv,
    first_send,
    first_recv,
    second_send,
    second_recv,
    ring_sem,
    small_send,
    small_recv,
    core_send,
    core_recv,
    step1_send,
    step1_recv,
    step2_send,
    step2_recv,
    last_send,
    last_recv,
    local_sem,
    p_sem,
    wq_sem,
    dx_ref,
    dgates_ref,
    tokens_ref,
    resid_ref,
    normed2_ref,
    normed_t_ref,
    mixed_t_ref,
    wo_ref,
    grad_ref,
    input_sem,
    block_sem,
    block_ref,
    grad_tokens_ref,
):
    loads = {
        name: pltpu.make_async_copy(src, dst, input_sem.at[n])
        for n, (name, src, dst) in enumerate(
            (
                ("dx", dx_hbm, dx_ref),
                ("dgates", dgates_hbm, dgates_ref),
                ("tokens", tokens_hbm, tokens_ref),
                ("resid", resid_hbm, resid_ref),
                ("normed2", normed2_hbm, normed2_ref),
                ("normed_t", normed_t_hbm, normed_t_ref),
                ("mixed_t", mixed_t_hbm, mixed_t_ref),
                ("wo", wo_hbm, wo_ref),
                ("grad", grad_hbm, grad_ref),
            )
        )
    }
    for copy in loads.values():
        copy.start()
    expert_count, capacity, width = ys_ref.shape
    slots = expert_count * capacity
    rows = tokens_ref.shape[0]
    chips = expert_count // 2
    size = expert_count // GROUPS
    me, dp = lax.axis_index("expert"), lax.axis_index("dp")
    core, chip = me % 2, me // 2
    x, y = dp % 2, dp // 2
    core_peer = me + 1 - 2 * core
    x_peer, y_peer = dp + 1 - 2 * x, dp + 2 - 4 * y
    my_group, my_place = me // size, me % size
    chip_peers = [(chip + d) % chips for d in range(1, chips)]
    greet(
        [{"expert": (me + d) % expert_count} for d in range(1, expert_count)]
        + [{"dp": x_peer}, {"dp": y_peer}]
    )

    tile_count = dw_ref.shape[0]
    batches = tile_count // BATCH

    def first_copy(t, i):
        sent, _, peer, _, _ = ways(dp, t)
        return remote(
            dw_ref.at[t, sent[i]],
            first_ref.at[t - BATCH * AHEAD, i],
            first_send.at[t - BATCH * AHEAD, i],
            first_recv.at[t - BATCH * AHEAD, i],
            dp=peer,
        )

    def second_copy(t, n):
        peer = ways(dp, t)[3]
        return remote(
            pass_v.at[n % 2, t % BATCH], second_ref.at[t], second_send.at[t], second_recv.at[t], dp=peer
        )

    def relay_loads(t, b):
        _, held, _, _, keep = ways(dp, t)
        q = t % BATCH
        came = head_ref.at[t, 1 - keep] if b < AHEAD else first_ref.at[t - BATCH * AHEAD, 1 - keep]
        return [
            pltpu.make_async_copy(dw_ref.at[t, held[1]], own_v.at[b % 2, q], ring_sem.at[b % 2, q, 0]),
            pltpu.make_async_copy(came, first_v.at[b % 2, q], ring_sem.at[b % 2, q, 1]),
        ]

    def over(b, body):
        def step(t, carry):
            body(t)
            return carry

        lax.fori_loop(BATCH * b, BATCH * b + BATCH, step, 0)

    def issue(b):
        def body(t):
            for i in range(2):
                first_copy(t, i).start()

        over(b, body)

    def relay_begin(b):
        def body(t):
            if b >= AHEAD:
                for i in range(2):
                    first_copy(t, i).wait_recv()
            for load in relay_loads(t, b):
                load.start()

        over(b, body)

    def relay_end(b):
        def body(t):
            for load in relay_loads(t, b):
                load.wait()
            if b >= 2:
                second_copy(t - 2 * BATCH, b).wait_send()
            q = t % BATCH
            pass_v[b % 2, q] = (
                own_v[b % 2, q].astype(F32) + first_v[b % 2, q].astype(F32)
            ).astype(BF16)
            second_copy(t, b).start()

        over(b, body)

    groups = grads_q.shape[0]
    count = groups + 1

    def pick(many, one, p):
        return many.at[p] if p < groups else one

    grads = [pick(grads_q, grads_o, p) for p in range(count)]
    cores = [pick(core_q, core_o, p) for p in range(count)]
    step1 = [pick(step1_q, step1_o, p) for p in range(count)]
    step2 = [pick(step2_q, step2_o, p) for p in range(count)]
    lasts = [pick(last_q, last_o, p) for p in range(count)]
    outs = [pick(gq_out_ref, go_out_ref, p) for p in range(count)]
    widths = [grads_q.shape[-1]] * groups + [grads_o.shape[-1]]

    def part_core(p):
        return remote(
            grads[p].at[:, :, :, 1 - core], cores[p], core_send.at[p], core_recv.at[p], expert=core_peer
        )

    def part_step1(p, b):
        half = widths[p] // 2
        src = (
            grads[p].at[:, 1 - x, :, core, :, 0:half]
            if b == 0
            else grads[p].at[1 - y, :, :, core, :, half : 2 * half]
        )
        return remote(
            src, step1[p].at[b], step1_send.at[p, b], step1_recv.at[p, b], dp=(x_peer, y_peer)[b]
        )

    def part_step2(p, b):
        src = step1[p].at[b, (1 - y, 1 - x)[b]]
        return remote(
            src, step2[p].at[b], step2_send.at[p, b], step2_recv.at[p, b], dp=(y_peer, x_peer)[b]
        )

    def part_last(p, peer, at):
        return remote(
            cores[p].at[0, 0, peer], lasts[p].at[at], last_send.at[p, peer], last_recv.at[p, at],
            expert=peer * 2 + core,
        )

    arrivals = {p: rows_o if p == groups else rows_q.at[p] for p in CHIPS_FIRST}
    sums = {p: sum_o if p == groups else sum_q.at[p] for p in CHIPS_FIRST}

    def chip_rows(p, peer, at):
        return remote(
            grads[p].at[:, :, peer, core], arrivals[p].at[at], last_send.at[p, peer], last_recv.at[p, at],
            expert=peer * 2 + core,
        )

    def chip_step1(p, b):
        half = widths[p] // 2
        src = (
            sums[p].at[:, 1 - x, :, 0:half] if b == 0 else sums[p].at[1 - y, :, :, half : 2 * half]
        )
        return remote(
            src, step1[p].at[b, :, 0], step1_send.at[p, b], step1_recv.at[p, b], dp=(x_peer, y_peer)[b]
        )

    def chip_step2(p, b):
        src = step1[p].at[b, (1 - y, 1 - x)[b], 0]
        return remote(
            src, step2[p].at[b, 0], step2_send.at[p, b], step2_recv.at[p, b], dp=(y_peer, x_peer)[b]
        )

    def chip_held(p, b, i):
        half = widths[p] // 2
        held = sums[p][i, x, :, 0:half] if b == 0 else sums[p][y, i, :, half : 2 * half]
        return held.astype(F32) + step1[p][b, i, 0].astype(F32)

    def part_a(p):
        part_core(p).start()

    def part_b(p):
        part_core(p).wait()
        total = grads[p][:, :, :, core].astype(F32) + cores[p][...].astype(F32)
        grads[p][:, :, :, core] = total.astype(BF16)
        if p in CHIPS_FIRST:
            for peer in chip_peers:
                chip_rows(p, peer, chip).start()
            return
        for b in range(2):
            part_step1(p, b).start()

    def part_c(p):
        half = widths[p] // 2
        if p in CHIPS_FIRST:
            total = grads[p][:, :, chip, core].astype(F32)
            for peer in chip_peers:
                chip_rows(p, peer, peer).wait_recv()
                total = total + arrivals[p][peer].astype(F32)
            sums[p][...] = total.astype(BF16)
            for b in range(2):
                chip_step1(p, b).start()
            return
        for b in range(2):
            part_step1(p, b).wait()
            for i in range(2):
                held = (
                    grads[p][i, x, :, core, :, 0:half]
                    if b == 0
                    else grads[p][y, i, :, core, :, half : 2 * half]
                )
                total = held.astype(F32) + step1[p][b, i].astype(F32)
                step1[p][b, i] = total.astype(BF16)
            part_step2(p, b).start()

    def part_d(p):
        half = widths[p] // 2
        if p in CHIPS_FIRST:
            for b in range(2):
                chip_step1(p, b).wait()
                give = (1 - y, 1 - x)[b]
                step1[p][b, give, 0] = chip_held(p, b, give).astype(BF16)
                chip_step2(p, b).start()
            return
        for b in range(2):
            part_step2(p, b).wait()
            total = step1[p][b, (y, x)[b]].astype(F32) + step2[p][b].astype(F32)
            cores[p][0, 0, :, :, b * half : b * half + half] = total.astype(BF16)
        for peer in chip_peers:
            part_last(p, peer, chip).start()

    def part_e(p):
        half = widths[p] // 2
        if p in CHIPS_FIRST:
            for b in range(2):
                chip_step2(p, b).wait()
                total = chip_held(p, b, (y, x)[b]) + step2[p][b, 0].astype(F32)
                outs[p][:, b * half : b * half + half] = total
            for peer in chip_peers:
                chip_rows(p, peer, chip).wait_send()
            return
        total = cores[p][0, 0, chip].astype(F32)
        for peer in chip_peers:
            part_last(p, peer, peer).wait_recv()
            total = total + lasts[p][peer].astype(F32)
        outs[p][...] = total
        for peer in chip_peers:
            part_last(p, peer, chip).wait_send()

    partners = []
    bit = 1
    while bit < expert_count:
        partners.append({"expert": flip(me, bit)})
        bit *= 2
    partners += [{"dp": x_peer}, {"dp": y_peer}]
    stages = len(partners)

    def small_copy(s):
        return remote(
            small_v.at[0], small_v.at[1 + s], small_send.at[s], small_recv.at[s], **partners[s]
        )

    def small_next(s):
        small_copy(s).wait()
        small_v[0] = small_v[0] + small_v[1 + s]
        if s + 1 < stages:
            small_copy(s + 1).start()

    def y_copy(peer, at):
        return remote(ys_ref.at[peer], y_v.at[at], y_send.at[peer], y_recv.at[at], expert=peer)

    def others(c):
        group = flip(my_group, c)
        return [group * size + (my_place + s) % size for s in range(1 if c == 0 else 0, size)]

    peers = [peer for c in (2, 3, 1, 0) for peer in others(c)]

    def p_copy(j, a):
        return pltpu.make_async_copy(p_ref.at[pl.ds(4 * j + 2 * a, 2)], p_v.at[a], p_sem.at[a])

    def wq_copy(j):
        return pltpu.make_async_copy(wq_ref.at[j], wq_v.at[j % 2], wq_sem.at[j % 2])

    lane = iota((rows, 128), 1)
    slot = [column(cols_ref[...], k) for k in range(2)]
    gates = [column(cols_ref[...], 2 + k) for k in range(2)]

    def hots():
        at = iota((rows, slots), 1).astype(F32)
        return [at == s for s in slot]

    def dense():
        lanes = dgates_ref.shape[2]
        wide = iota((rows, lanes), 1)

        def step(e, totals):
            base = (e * capacity).astype(F32)
            row = dgates_ref[pl.ds(e, 1)][0][0:1]
            return tuple(
                totals[k]
                + jnp.where((wide.astype(F32) == slot[k] - base) & (wide < capacity), row, 0.0)
                for k in range(2)
            )

        zero = jnp.zeros((rows, lanes), F32)
        sums = lax.fori_loop(0, expert_count, step, (zero, zero))
        dgates = [jnp.sum(s, axis=1, keepdims=True) for s in sums]
        mean = gates[0] * dgates[0] + gates[1] * dgates[1]
        dchosen = [gates[k] * (dgates[k] - mean) for k in range(2)]
        dlogits = jnp.zeros((rows, 128), F32)
        for k in range(2):
            here = lane == route_column(routes_ref, k).astype(jnp.int32)
            dlogits = dlogits + jnp.where(here, dchosen[k], 0.0)
        small_rows = dot_exact(dlogits.T[0:expert_count], normed2_ref[...])
        small_v[0, 0:expert_count] = small_rows
        blank = jnp.zeros((128 - expert_count, width), F32)
        router = jnp.concatenate([router_t_ref[...], blank], axis=0)
        hot0, hot1 = hots()
        hot = jnp.where(hot0 | hot1, 1.0, 0.0).astype(BF16)
        dnormed = dot_f32(dlogits, router)
        dnormed = dnormed + dot_nn(hot, dx_ref[...].reshape(slots, width))
        resid = resid_ref[...]
        inv_rms = lax.rsqrt(jnp.mean(resid * resid, axis=1, keepdims=True) + EPS)
        normed = resid * inv_rms
        scaled = dnormed * gain2_ref[...]
        small_v[0, expert_count + 1 : expert_count + 2] = jnp.sum(
            dnormed * normed, axis=0, keepdims=True
        )
        inner = jnp.mean(scaled * normed, axis=1, keepdims=True)
        dresid = grad_ref[...].astype(F32) + inv_rms * (scaled - normed * inner)
        grad_tokens_ref[...] = dresid
        dresid_r = dresid.astype(BF16)
        grads_o[...] = dot_nn(mixed_t_ref[...], dresid_r).astype(BF16).reshape(grads_o.shape)
        part_a(groups)
        dmix_v[...] = dot_nt(dresid_r, wo_ref[...]).astype(BF16)

    def group(j):
        if j + 1 < groups:
            wq_copy(j + 1).start()

        def pair(a, carry):
            p_copy(j, a).wait()
            attend_back_pair(j, a, qkv_v, p_v.at[a], dmix_v, dqkv_v, fold_v)
            if j + 1 < groups:
                p_copy(j + 1, a).start()
            return carry

        lax.fori_loop(0, 2, pair, 0)
        block = dot_nn(normed_t_ref[...], dqkv_v[...])
        grads_q[j] = block.astype(BF16).reshape(grads_q.shape[1:])
        part_a(j)
        wq_copy(j).wait()
        term = dot_nt(dqkv_v[...], wq_v[j % 2])
        dn1_v[...] = term if j == 0 else dn1_v[...] + term

    def norm_back():
        inputs = tokens_ref[...].astype(F32)
        inv_rms = lax.rsqrt(jnp.mean(inputs * inputs, axis=1, keepdims=True) + EPS)
        normed = inputs * inv_rms
        dnormed = dn1_v[...]
        scaled = dnormed * gain1_ref[...]
        small_v[0, expert_count : expert_count + 1] = jnp.sum(
            dnormed * normed, axis=0, keepdims=True
        )
        inner = jnp.mean(scaled * normed, axis=1, keepdims=True)
        grad_tokens_ref[...] += inv_rms * (scaled - normed * inner)
        buckets = dot_exact(fold_v[...], bucket_hot_ref[...], dot_nt)
        tokens_copy.start()
        base = expert_count + 2
        heads = fold_v.shape[0]
        small_v[0, base : base + heads, 0 : buckets.shape[1]] = buckets
        small_copy(0).start()

    def outputs():
        for peer in peers:
            y_copy(peer, peer).wait_recv()
        y_own.wait()
        values = y_v[...].reshape(slots, width)
        total = resid_ref[...]
        for k, hot in enumerate(hots()):
            total = total + gates[k] * dot_nn(jnp.where(hot, 1.0, 0.0).astype(BF16), values)
        block_ref[...] = total.astype(BF16)
        block_copy.start()

    block_copy = pltpu.make_async_copy(block_ref, block_hbm, block_sem.at[0])
    tokens_copy = pltpu.make_async_copy(grad_tokens_ref, grad_tokens_hbm, block_sem.at[1])
    small_v[0] = jnp.zeros(small_v.shape[1:], F32)
    for peer in peers:
        y_copy(peer, me).start()
    y_own = pltpu.make_async_copy(ys_ref.at[me], y_v.at[me], local_sem.at[0])
    y_own.start()
    qkv_copy = pltpu.make_async_copy(qkv_ref, qkv_v, local_sem.at[1])
    qkv_copy.start()
    wq_copy(0).start()
    for a in range(2):
        p_copy(0, a).start()
    late = [b for b in range(AHEAD, batches)]
    turn = [b for b in range(AHEAD, batches)]
    open_relays = []

    def send_more(number):
        for _ in range(min(number, len(late))):
            issue(late.pop(0))

    def relay_in():
        if turn:
            b = turn.pop(0)
            relay_begin(b)
            open_relays.append(b)

    def relay_out():
        if open_relays:
            relay_end(open_relays.pop(0))

    send_more(2)
    for b in range(AHEAD):
        relay_begin(b)
        if b > 0:
            relay_end(b - 1)
    relay_end(AHEAD - 1)
    send_more(1)
    for copy in loads.values():
        copy.wait()
    dense()
    qkv_copy.wait()
    group(0)
    part_b(groups)
    relay_in()
    relay_out()
    send_more(1)
    group(1)
    part_b(0)
    relay_in()
    relay_out()
    send_more(1)
    group(2)
    part_b(1)
    relay_in()
    relay_out()
    send_more(1)
    group(3)
    part_b(2)
    send_more(1)
    norm_back()
    part_b(3)
    send_more(len(late))
    relay_in()
    small_next(0)
    relay_out()
    direct = [p for p in (groups, *range(groups)) if p not in CHIPS_FIRST]
    first_on = [p for p in (groups, *range(groups)) if p in CHIPS_FIRST]
    for p in direct:
        part_c(p)
    small_next(1)
    outputs()
    small_next(2)
    relay_in()
    for p in direct[:-1]:
        part_d(p)
    relay_out()
    for p in first_on[:1]:
        part_c(p)
    small_next(3)
    relay_in()
    for p in direct[-1:]:
        part_d(p)
    for p in first_on[1:2]:
        part_c(p)
    relay_out()
    for s in range(4, stages):
        small_next(s)
    small_out_ref[...] = small_v[0]
    for p in first_on[:1]:
        part_d(p)
    relay_in()
    for p in first_on[2:]:
        part_c(p)
    for p in first_on[1:2]:
        part_d(p)
    relay_out()
    while turn:
        relay_in()
        relay_out()
    for p in first_on[2:]:
        part_d(p)
    for p in direct:
        part_e(p)
    for p in first_on:
        part_e(p)
    for b in (batches - 2, batches - 1):
        over(b, lambda t, b=b: second_copy(t, b).wait_send())

    def drain_first(t, carry):
        for i in range(2):
            first_copy(t, i).wait_send()
        return carry

    def drain_second(t, carry):
        second_copy(t, 0).wait_recv()
        return carry

    block_copy.wait()
    tokens_copy.wait()
    lax.fori_loop(BATCH * AHEAD, tile_count, drain_first, 0)
    lax.fori_loop(0, tile_count, drain_second, 0)
    for peer in peers:
        y_copy(peer, me).wait_send()


def back(
    dw, head, ys, dx, dgates, cols, routes, tokens, grad_out, resid, normed2, normed_t, mixed_t,
    gain1, gain2, router_t, bucket_hot, wq, wo, qkv, probs,
):
    tile_count, dp_count, deep, _ = dw.shape
    expert_count, capacity, width = ys.shape
    chips = expert_count // 2
    rows = tokens.shape[0]
    groups, _, part = qkv.shape
    own = width // (dp_count * expert_count)
    heads = probs.shape[0]
    small_rows = -(-(expert_count + 2 + heads) // 8) * 8
    stages = expert_count.bit_length() + 1
    vmem = pl.BlockSpec(memory_space=pltpu.VMEM)
    sem = pltpu.SemaphoreType.DMA
    shape = jax.ShapeDtypeStruct
    ring = (2, BATCH, deep, TILE)
    late = tile_count - BATCH * AHEAD

    def pairs(make, number=groups):
        return [pltpu.VMEM((number, *make(part)), BF16), pltpu.VMEM(make(width), BF16)]

    return pl.pallas_call(
        back_kernel,
        in_specs=[ANY] * 5 + [vmem] * 2 + [ANY] * 6 + [vmem] * 4 + [ANY] * 4,
        out_specs=[ANY] * 2 + [vmem] * 3 + [ANY] * 2,
        out_shape=[
            shape((late, 2, deep, TILE), BF16),
            shape((tile_count, deep, TILE), BF16),
            shape((small_rows, width), F32),
            shape((groups, own, part), F32),
            shape((own, width), F32),
            shape((rows, width), BF16),
            shape((rows, width), F32),
        ],
        scratch_shapes=[pltpu.VMEM(ys.shape, BF16)]
        + pairs(lambda w: (2, 2, chips, 2, own, w))
        + pairs(lambda w: (2, 2, chips, own, w))
        + pairs(lambda w: (2, 2, chips, own, w // 2))
        + pairs(lambda w: (2, chips, own, w // 2))
        + pairs(lambda w: (chips, own, w))
        + pairs(lambda w: (chips, 2, 2, own, w), CHIPS_FIRST_GROUPS)
        + pairs(lambda w: (2, 2, own, w), CHIPS_FIRST_GROUPS)
        + [
            pltpu.VMEM(qkv.shape, BF16),
            pltpu.VMEM((2, 2, rows, rows), BF16),
            pltpu.VMEM((2, *wq.shape[1:]), BF16),
            pltpu.VMEM((rows, part), BF16),
            pltpu.VMEM((rows, width), BF16),
            pltpu.VMEM((rows, width), F32),
            pltpu.VMEM((heads, bucket_hot.shape[1]), F32),
            pltpu.VMEM((stages + 1, small_rows, width), F32),
            pltpu.VMEM(ring, BF16),
            pltpu.VMEM(ring, BF16),
            pltpu.VMEM(ring, BF16),
            sem((expert_count,)),
            sem((expert_count,)),
            sem((late, 2)),
            sem((late, 2)),
            sem((tile_count,)),
            sem((tile_count,)),
            sem((2, BATCH, 2)),
            sem((stages,)),
            sem((stages,)),
            sem((groups + 1,)),
            sem((groups + 1,)),
            sem((groups + 1, 2)),
            sem((groups + 1, 2)),
            sem((groups + 1, 2)),
            sem((groups + 1, 2)),
            sem((groups + 1, chips)),
            sem((groups + 1, chips)),
            sem((2,)),
            sem((2,)),
            sem((2,)),
        ]
        + [
            pltpu.VMEM(a.shape, a.dtype)
            for a in (dx, dgates, tokens, resid, normed2, normed_t, mixed_t, wo, grad_out)
        ]
        + [
            sem((9,)),
            sem((2,)),
            pltpu.VMEM((rows, width), BF16),
            pltpu.VMEM((rows, width), F32),
        ],
        compiler_params=pltpu.CompilerParams(
            collective_id=2, has_side_effects=True, vmem_limit_bytes=61 * 1024 * 1024
        ),
        name="back",
    )(
        dw, head, ys, dx, dgates, cols, routes, tokens, grad_out, resid, normed2, normed_t, mixed_t,
        gain1, gain2, router_t, bucket_hot, wq, wo, qkv, probs,
    )


def tail_kernel(expert_count, heads, buckets, where_ref, *refs):
    dw, head, first, second = (refs[BATCH * n : BATCH * n + BATCH] for n in range(4))
    small_ref, gq_ref, go_ref, block_ref, tokens_ref = refs[4 * BATCH : 4 * BATCH + 5]
    (
        in_ref,
        out_ref,
        router_ref,
        norm1_ref,
        norm2_ref,
        bias_ref,
        qkv_ref,
        proj_ref,
        block_out_ref,
        tokens_out_ref,
    ) = refs[4 * BATCH + 5 :]
    f = pl.program_id(0)
    for m in range(BATCH):
        came = jnp.where(f < AHEAD, head[m][0, 0].astype(F32), first[m][0, 0].astype(F32))
        total = dw[m][0, 0].astype(F32) + came + second[m][0].astype(F32)
        if m < 2:
            in_ref[m] = total
        else:
            out_ref[...] = total.T

    @pl.when(f == 0)
    def _():
        router_ref[...] = small_ref[0:expert_count]
        norm1_ref[...] = small_ref[expert_count : expert_count + 1]
        norm2_ref[...] = small_ref[expert_count + 1 : expert_count + 2]
        bias_ref[...] = small_ref[expert_count + 2 : expert_count + 2 + heads, 0:buckets]
        groups, _, part = gq_ref.shape
        third = part // 3
        for j in range(groups):
            for k in range(3):
                at = (k * groups + j) * third
                qkv_ref[:, at : at + third] = gq_ref[j, :, k * third : (k + 1) * third]
        proj_ref[...] = go_ref[...]
        block_out_ref[...] = block_ref[...]
        tokens_out_ref[...] = tokens_ref[...]


def tail(dw, head, first, second, small, gq, go, block, tokens, expert_count, heads, buckets):
    tile_count, _, deep, _ = dw.shape
    tiles = tile_count // BATCH
    groups, own, part = gq.shape
    rows, width = tokens.shape
    dp = lax.axis_index("dp")
    x, y = dp % 2, dp // 2
    where = jnp.stack([dp, dp, y, x]).astype(jnp.int32)
    shape = jax.ShapeDtypeStruct
    block_shape = (1, 1, deep, TILE)

    def whole(a):
        return pl.BlockSpec(a.shape, lambda f, w: (0,) * len(a.shape))

    late = BATCH * AHEAD
    in_specs = [
        pl.BlockSpec(block_shape, lambda f, w, m=m: (BATCH * f + m, w[(f + m) % 2], 0, 0))
        for m in range(BATCH)
    ]
    in_specs += [
        pl.BlockSpec(
            block_shape,
            lambda f, w, m=m: (
                jnp.minimum(BATCH * f + m, late - BATCH + m),
                w[2 + (f + m) % 2],
                0,
                0,
            ),
        )
        for m in range(BATCH)
    ]
    in_specs += [
        pl.BlockSpec(
            block_shape,
            lambda f, w, m=m: (jnp.maximum(BATCH * f + m - late, m), w[2 + (f + m) % 2], 0, 0),
        )
        for m in range(BATCH)
    ]
    in_specs += [
        pl.BlockSpec((1, deep, TILE), lambda f, w, m=m: (BATCH * f + m, 0, 0)) for m in range(BATCH)
    ]
    flat = [small, gq, go, block, tokens]
    outs = [
        shape((2, deep, tiles * TILE), F32),
        shape((tiles * TILE, deep), F32),
        shape((expert_count, width), F32),
        shape((1, width), F32),
        shape((1, width), F32),
        shape((heads, buckets), F32),
        shape((own, groups * part), F32),
        shape((own, width), F32),
        shape(block.shape, BF16),
        shape(tokens.shape, F32),
    ]
    return pl.pallas_call(
        functools.partial(tail_kernel, expert_count, heads, buckets),
        grid_spec=pltpu.PrefetchScalarGridSpec(
            num_scalar_prefetch=1,
            grid=(tiles,),
            in_specs=in_specs + [whole(a) for a in flat],
            out_specs=[
                pl.BlockSpec((2, deep, TILE), lambda f, w: (0, 0, f)),
                pl.BlockSpec((TILE, deep), lambda f, w: (f, 0)),
            ]
            + [whole(a) for a in outs[2:]],
        ),
        out_shape=outs,
        compiler_params=pltpu.CompilerParams(vmem_limit_bytes=62 * 1024 * 1024),
        name="tail",
    )(where, *[dw] * BATCH, *[head] * BATCH, *[first] * BATCH, *[second] * BATCH, *flat)


def shards(
    tokens,
    routes,
    rel_bucket,
    norm_gain1,
    w_qkv,
    w_out_proj,
    bias_table,
    norm_gain2,
    w_router,
    w_expert_in,
    w_expert_out,
    grad_out,
):
    row_count, model_width = tokens.shape
    bucket_count, head_count = bias_table.shape
    expert_count = lax.axis_size("expert")
    capacity = 10 * row_count // (4 * expert_count)
    slot_total = expert_count * capacity
    hidden_groups = 4

    bucket_ids = jnp.arange(bucket_count, dtype=jnp.int32)
    bucket_hot = jnp.concatenate(
        [bucket_ids[:, None] == rel_bucket[None, :], jnp.zeros((bucket_count, 1), bool)], axis=1
    ).astype(F32)
    table = jnp.dot(bias_table.T, bucket_hot, precision=HIGHEST)

    wq_full, out_full, qkv, probs, g_rows, mixed_t, normed1_t, residual, normed2_r, xs, gates, cols = front(
        tokens,
        norm_gain1[None],
        norm_gain2[None],
        table,
        routes.T,
        grad_out,
        w_router.T,
        w_qkv,
        w_out_proj,
        hidden_groups,
        capacity,
    )
    produced, grad_rows, grad_gates, grad_w, head = experts(
        xs, gates, g_rows, w_expert_in[0], w_expert_out[0], lax.axis_size("dp")
    )
    first, second, *rest = back(
        grad_w,
        head,
        produced,
        grad_rows,
        grad_gates,
        cols,
        routes.T,
        tokens,
        grad_out,
        residual,
        normed2_r,
        normed1_t,
        mixed_t,
        norm_gain1[None],
        norm_gain2[None],
        w_router.T,
        bucket_hot.astype(BF16),
        wq_full.reshape(hidden_groups, model_width, -1),
        out_full.reshape(model_width, model_width),
        qkv,
        probs,
    )
    (
        grad_in,
        grad_out_t,
        grad_router,
        grad_norm1,
        grad_norm2,
        grad_bias,
        grad_qkv,
        grad_out_proj,
        block_out,
        grad_tokens,
    ) = tail(grad_w, head, first, second, *rest, expert_count, head_count, bucket_count)
    grad_expert_in, grad_expert_out = grad_in[None], grad_out_t[None]
    grad_router_all, grad_bias = grad_router.T, grad_bias.T
    grad_norm1, grad_norm2 = grad_norm1[0], grad_norm2[0]
    return (
        block_out,
        grad_tokens,
        grad_norm1,
        grad_qkv,
        grad_out_proj,
        grad_bias,
        grad_norm2,
        grad_router_all,
        grad_expert_in,
        grad_expert_out,
    )


def solution(mesh):
    split = P(("dp", "expert"), None)
    in_specs = (
        split,
        split,
        P(),
        P(),
        split,
        split,
        P(),
        P(),
        P(),
        P("expert", None, None, None),
        P("expert", None, None),
        split,
    )
    out_specs = (
        split,
        split,
        P(),
        split,
        split,
        P(),
        P(),
        P(),
        P("expert", None, "dp", None),
        P("expert", None, "dp"),
    )
    return jax.shard_map(shards, mesh=mesh, in_specs=in_specs, out_specs=out_specs, check_vma=False)
```

```python
import functools

import jax
import jax.numpy as jnp
from jax import lax
from jax.experimental import pallas as pl
from jax.experimental.pallas import tpu as pltpu
from jax.sharding import PartitionSpec as P

LENGTH = 512
EPS = 1e-06
HIGHEST = lax.Precision.HIGHEST
F32 = jnp.float32
BF16 = jnp.bfloat16


def dot_nt(a, b):
    return lax.dot_general(a, b, (((1,), (1,)), ((), ())), preferred_element_type=F32)


def dot_nn(a, b):
    return jnp.dot(a, b, preferred_element_type=F32)


def iota(shape, axis):
    return lax.broadcasted_iota(jnp.int32, shape, axis)


def spread_bias(row):
    values = jnp.broadcast_to(row, (8, 1024))
    lift = 7 - iota((8, 1024), 0)
    for bit in (1, 2, 4):
        values = jnp.where((lift // bit) % 2 == 1, pltpu.roll(values, 1024 - bit, 1), values)
    return jnp.concatenate(
        [pltpu.roll(values, (904 + 8 * block) % 1024, 1) for block in range(16)], axis=0
    )


def fold_bias(parts):
    total = parts[0:8]
    total = pltpu.roll(total, 120, 1)
    for block in range(1, 16):
        piece = parts[8 * block : 8 * block + 8]
        total = total + (pltpu.roll(piece, 120 - 8 * block, 1) if block < 15 else piece)
    lift = 7 - iota((8, 1024), 0)
    for bit in (1, 2, 4):
        total = jnp.where((lift // bit) % 2 == 1, pltpu.roll(total, bit, 1), total)
    return jnp.sum(total, axis=0, keepdims=True)


MESH = pl.DeviceIdType.MESH
ANY = pl.BlockSpec(memory_space=pl.ANY)
GROUPS = 4
TILE = 256
WIDE = 512


def flip(index, mask):
    bit = 1
    while bit <= mask:
        if mask & bit:
            index = index + bit - 2 * bit * ((index // bit) % 2)
        bit *= 2
    return index


def remote(src, dst, send_sem, recv_sem, **axes):
    return pltpu.make_async_remote_copy(
        src_ref=src,
        dst_ref=dst,
        send_sem=send_sem,
        recv_sem=recv_sem,
        device_id=axes,
        device_id_type=MESH,
    )


def greet(partners):
    barrier = pltpu.get_barrier_semaphore()
    for axes in partners:
        pl.semaphore_signal(barrier, inc=1, device_id=axes, device_id_type=MESH)
    pl.semaphore_wait(barrier, len(partners))


def gelu_parts(x):
    root = 0.7978845608028654
    square = x * x
    t = jnp.tanh(root * x * (1.0 + 0.044715 * square))
    half = 0.5 * (1.0 + t)
    slope = half + 0.5 * x * (1.0 - t * t) * (root * (1.0 + 3 * 0.044715 * square))
    return x * half, slope


BATCH = 3
AHEAD = 4
CHIPS_FIRST_GROUPS = 1
CHIPS_FIRST = (*range(CHIPS_FIRST_GROUPS), 4)


def ways(dp, t):
    x, y = dp % 2, dp // 2
    x_peer, y_peer = dp + 1 - 2 * x, dp + 2 - 4 * y
    q = t % 2
    sent = [(1 - q) * (2 * i + 1 - x) + q * (2 * (1 - y) + i) for i in range(2)]
    keep = (1 - q) * y + q * x
    held = [(1 - q) * (2 * k + x) + q * (2 * y + k) for k in (keep, 1 - keep)]
    return sent, held, (1 - q) * x_peer + q * y_peer, (1 - q) * y_peer + q * x_peer, keep


def experts_kernel(
    xs_ref,
    gates_ref,
    g_ref,
    w_in_ref,
    w_out_ref,
    y_ref,
    dx_back_ref,
    dgates_back_ref,
    dw_ref,
    head_ref,
    w_in_v,
    w_out_v,
    x_v,
    gates_v,
    dgates_v,
    g_v,
    dy_v,
    hid_v,
    dgate_v,
    dup_v,
    y_v,
    dx_v,
    pre_v,
    stage,
    local_sem,
    stage_sem,
    x_send,
    x_recv,
    gates_send,
    gates_recv,
    dgates_send,
    dgates_recv,
    dx_send,
    dx_recv,
    y_sem,
    head_send,
    head_recv,
    weight_sem,
):
    expert_count, capacity, width = xs_ref.shape
    hidden = w_out_ref.shape[0]
    tiles = hidden // TILE
    size = expert_count // GROUPS
    rows = size * capacity
    me = lax.axis_index("expert")
    my_group, my_place = me // size, me % size

    def others(c):
        group = flip(my_group, c)
        return [group * size + (my_place + s) % size for s in range(1 if c == 0 else 0, size)]

    dp = lax.axis_index("dp")
    greet(
        [{"expert": (me + d) % expert_count} for d in range(1, expert_count)]
        + [{"dp": flip(dp, 1)}, {"dp": flip(dp, 2)}]
    )

    def send_rows(c):
        for peer in others(c):
            remote(
                xs_ref.at[peer], x_v.at[me], x_send.at[peer], x_recv.at[me], expert=peer
            ).start()
            remote(
                gates_ref.at[peer], gates_v.at[me], gates_send.at[peer], gates_recv.at[me], expert=peer
            ).start()

    for c in (2, 1, 0):
        send_rows(c)
    def weights(f):
        cols = pl.ds(pl.multiple_of(f * TILE, TILE), TILE)
        return [
            pltpu.make_async_copy(
                w_in_ref.at[:, :, cols], w_in_v.at[:, :, cols], weight_sem.at[f, 0]
            ),
            pltpu.make_async_copy(w_out_ref.at[cols], w_out_v.at[cols], weight_sem.at[f, 1]),
        ]

    own = [
        pltpu.make_async_copy(xs_ref.at[me], x_v.at[me], local_sem.at[0]),
        pltpu.make_async_copy(gates_ref.at[me], gates_v.at[me], local_sem.at[1]),
        pltpu.make_async_copy(g_ref, g_v, local_sem.at[4]),
    ]
    for copy in own:
        copy.start()

    def fetch(f, carry):
        for copy in weights(f):
            copy.start()
        return carry

    lax.fori_loop(0, tiles, fetch, 0)
    for copy in own:
        copy.wait()

    def y_copy(c):
        span = pl.ds(flip(my_group, c) * size, size)
        return pltpu.make_async_copy(y_v.at[span], y_ref.at[span], y_sem.at[c])

    def back_copies(peer, at):
        return [
            remote(
                dx_v.at[peer], dx_back_ref.at[at], dx_send.at[peer], dx_recv.at[at], expert=peer
            ),
            remote(
                dgates_v.at[peer],
                dgates_back_ref.at[at],
                dgates_send.at[peer],
                dgates_recv.at[at],
                expert=peer,
            ),
        ]

    dgates_v[...] = jnp.zeros_like(dgates_v)
    for c in range(GROUPS):
        group = flip(my_group, c)
        span = pl.ds(group * size, size)
        for peer in others(c):
            remote(
                xs_ref.at[peer], x_v.at[peer], x_send.at[peer], x_recv.at[peer], expert=peer
            ).wait_recv()
            remote(
                gates_ref.at[peer], gates_v.at[peer], gates_send.at[peer], gates_recv.at[peer], expert=peer
            ).wait_recv()
        for s in range(size):
            src = group * size + s
            gate_col = gates_v[src].T[0:capacity, 0:1]
            dy_v[src] = (g_v[src].astype(F32) * gate_col).astype(BF16)

        def before(f, slot, span=span, c=c):
            if c == 0:
                for copy in weights(f):
                    copy.wait()
            cols = pl.ds(pl.multiple_of(f * TILE, TILE), TILE)
            x = x_v[span].reshape(rows, width)
            pre_v[slot, 0] = dot_nn(x, w_in_v[0, :, cols])
            pre_v[slot, 1] = dot_nn(x, w_in_v[1, :, cols])
            pre_v[slot, 2] = dot_nt(dy_v[span].reshape(rows, width), w_out_v[cols, :])

        def after(f, slot, group=group):
            cols = pl.ds(pl.multiple_of(f * TILE, TILE), TILE)
            gate, up, dhid = pre_v[slot, 0], pre_v[slot, 1], pre_v[slot, 2]
            gelu, slope = gelu_parts(gate)
            hid_v[group, :, cols] = (gelu * up).astype(BF16)
            dgate_v[group, :, cols] = (dhid * up * slope).astype(BF16)
            dup_v[group, :, cols] = (dhid * gelu).astype(BF16)

        def two(h, carry):
            before(2 * h + 1, 1)
            after(2 * h, 0)
            before(2 * h + 2, 0)
            after(2 * h + 1, 1)
            return carry

        def backs(n, carry, group=group, span=span):
            cols = pl.ds(pl.multiple_of(n * WIDE, WIDE), WIDE)
            out = dot_nn(hid_v[group], w_out_v[:, cols])
            y_v[span, :, cols] = out.astype(BF16).reshape(size, capacity, WIDE)
            back = dot_nt(dgate_v[group], w_in_v[0, cols, :])
            back = back + dot_nt(dup_v[group], w_in_v[1, cols, :])
            dx_v[span, :, cols] = back.astype(BF16).reshape(size, capacity, WIDE)
            return carry

        assert tiles % 2 == 1
        before(0, 0)
        lax.fori_loop(0, tiles // 2, two, 0)
        after(tiles - 1, 0)
        lax.fori_loop(0, width // WIDE, backs, 0)
        if c == 0:
            send_rows(3)
        y_copy(c).start()
        for s in range(size):
            src = group * size + s
            product = g_v[src].astype(F32) * y_v[src].astype(F32)
            dgate = jnp.sum(product, axis=1, keepdims=True)
            dgates_v[src, :, 0:capacity] = jnp.broadcast_to(dgate, (capacity, 128)).T[0:8]
        for peer in others(c):
            for copy in back_copies(peer, me):
                copy.start()
    own = [
        pltpu.make_async_copy(dx_v.at[me], dx_back_ref.at[me], local_sem.at[0]),
        pltpu.make_async_copy(dgates_v.at[me], dgates_back_ref.at[me], local_sem.at[1]),
    ]
    for copy in own:
        copy.start()

    slots = expert_count * capacity
    w_in_v[0, :, 0:slots] = x_v[...].reshape(slots, width).T
    w_in_v[1, :, 0:slots] = dy_v[...].reshape(slots, width).T

    def put(f, m):
        return pltpu.make_async_copy(stage.at[m], dw_ref.at[BATCH * f + m], stage_sem.at[m])

    def head_copy(f, m, i):
        t = BATCH * f + m
        sent, _, peer, _, keep = ways(dp, t)
        return remote(
            dw_ref.at[t, sent[i]], head_ref.at[t, (i + keep) % 2], head_send.at[t, i], head_recv.at[t, i], dp=peer
        )

    parts, deep = stage.shape[1:3]

    def grads(f, carry):
        cols = pl.ds(pl.multiple_of(f * TILE, TILE), TILE)
        for m, (side, right) in enumerate(((0, dgate_v), (0, dup_v), (1, hid_v))):

            @pl.when(f > 0)
            def _():
                put(f - 1, m).wait()

            @pl.when((f > 0) & (f <= AHEAD))
            def _():
                for i in range(2):
                    head_copy(f - 1, m, i).start()

            across = right[:, :, cols].reshape(slots, TILE)
            for r in range(0, parts, 2):
                span = slice(r * deep, (r + 2) * deep)
                block = dot_nn(w_in_v[side, span, 0:slots], across)
                stage[m, r : r + 2] = block.astype(BF16).reshape(2, deep, TILE)
            put(f, m).start()
        return carry

    lax.fori_loop(0, tiles, grads, 0)
    for m in range(BATCH):
        put(tiles - 1, m).wait()

    def heads(t, carry):
        for i in range(2):
            head_copy(t // BATCH, t % BATCH, i).wait()
        return carry

    lax.fori_loop(0, BATCH * AHEAD, heads, 0)
    for copy in own:
        copy.wait()
    for c in range(GROUPS):
        for peer in others(c):
            for src, dst, send_sem, recv_sem in (
                (xs_ref, x_v, x_send, x_recv),
                (gates_ref, gates_v, gates_send, gates_recv),
            ):
                remote(
                    src.at[peer], dst.at[me], send_sem.at[peer], recv_sem.at[me], expert=peer
                ).wait_send()
            for copy in back_copies(peer, me):
                copy.wait_send()
            for copy in back_copies(peer, peer):
                copy.wait_recv()
        y_copy(c).wait()


def experts(xs, gates, g, w_in, w_out, dp_count):
    expert_count, capacity, width = xs.shape
    hidden = w_out.shape[0]
    size = expert_count // GROUPS
    tiles = hidden // TILE
    rows = size * capacity
    slots = jax.ShapeDtypeStruct(xs.shape, BF16)
    parts = (dp_count, width // dp_count, TILE)
    peers = pltpu.SemaphoreType.DMA((expert_count,))
    return pl.pallas_call(
        experts_kernel,
        in_specs=[ANY] * 5,
        out_specs=[ANY] * 5,
        out_shape=[slots, slots, jax.ShapeDtypeStruct(gates.shape, F32), jax.ShapeDtypeStruct((BATCH * tiles, *parts), BF16),
            jax.ShapeDtypeStruct((BATCH * AHEAD, 2, *parts[1:]), BF16),
        ],
        scratch_shapes=[
            pltpu.VMEM(w_in.shape, BF16),
            pltpu.VMEM(w_out.shape, BF16),
            pltpu.VMEM(xs.shape, BF16),
            pltpu.VMEM(gates.shape, F32),
            pltpu.VMEM(gates.shape, F32),
            pltpu.VMEM(xs.shape, BF16),
            pltpu.VMEM(xs.shape, BF16),
            pltpu.VMEM((GROUPS, rows, hidden), BF16),
            pltpu.VMEM((GROUPS, rows, hidden), BF16),
            pltpu.VMEM((GROUPS, rows, hidden), BF16),
            pltpu.VMEM(xs.shape, BF16),
            pltpu.VMEM(xs.shape, BF16),
            pltpu.VMEM((2, 3, rows, TILE), F32),
            pltpu.VMEM((BATCH, *parts), BF16),
            pltpu.SemaphoreType.DMA((5,)),
            pltpu.SemaphoreType.DMA((3,)),
        ]
        + [peers] * 8
        + [pltpu.SemaphoreType.DMA((GROUPS,))]
        + [pltpu.SemaphoreType.DMA((BATCH * AHEAD, 2))] * 2
        + [pltpu.SemaphoreType.DMA((tiles, 2))],
        compiler_params=pltpu.CompilerParams(
            collective_id=1, has_side_effects=True, vmem_limit_bytes=61 * 1024 * 1024
        ),
        name="experts",
    )(xs, gates, g, w_in, w_out)


def column(values, k):
    return values[:, k : k + 1]


def route_column(routes_ref, k):
    row = routes_ref[k : k + 1, :].astype(F32)
    return jnp.broadcast_to(row, (128, row.shape[1])).T


def attend_pair(j, a, qkv_v, table_ref, p_ref):
    def lanes(part):
        return pl.ds(pl.multiple_of(256 * part + 128 * a, 128), 128)

    query = qkv_v[j, :, lanes(0)] * jnp.asarray(0.125, BF16)
    values_t = qkv_v[j, :, lanes(2)].T
    half = iota((512, 128), 1) // 64
    halves = []
    for t in range(2):
        shifted = spread_bias(table_ref[pl.ds(4 * j + 2 * a + t, 1), :])
        query_t = jnp.where(half == t, query, jnp.zeros_like(query))
        scores = [
            dot_nt(qkv_v[j, 128 * c : 128 * c + 128, lanes(1)], query_t)
            + shifted[:, 384 - 128 * c : 896 - 128 * c]
            for c in range(4)
        ]
        top = functools.reduce(jnp.maximum, [jnp.max(s, axis=0, keepdims=True) for s in scores])
        exps = [jnp.exp(s - top) for s in scores]
        total = functools.reduce(jnp.add, [jnp.sum(e, axis=0, keepdims=True) for e in exps])
        inverse = 1.0 / total
        for c in range(4):
            p_ref[t, 128 * c : 128 * c + 128, :] = (exps[c] * inverse).astype(BF16)
        halves.append(dot_nn(values_t, p_ref[t]))
    return jnp.where(iota((128, 512), 0) < 64, halves[0], halves[1])


def front_kernel(
    tokens_ref,
    gain1_ref,
    gain2_ref,
    table_ref,
    routes_ref,
    grad_ref,
    router_ref,
    w_qkv_ref,
    wo_ref,
    wq_out,
    wo_out,
    qkv_out,
    p_out,
    g_back,
    mixed_t_hbm,
    normed_t_hbm,
    resid_hbm,
    normed2_hbm,
    xs_hbm,
    gates_ref,
    cols_ref,
    ws_ref,
    wq_v,
    wo_v,
    qkv_v,
    p_v,
    mixed_v,
    normed_v,
    hot_v,
    g_v,
    own_sem,
    z_send,
    z_recv,
    xy_send,
    xy_recv,
    core_send,
    core_recv,
    g_send,
    g_recv,
    out_sem,
    p_sem,
    mixed_t_ref,
    normed_t_ref,
    resid_ref,
    normed2_ref,
    xs_ref,
    stores_sem,
):
    stores = {
        name: pltpu.make_async_copy(src, dst, stores_sem.at[n])
        for n, (name, src, dst) in enumerate(
            (
                ("mixed_t", mixed_t_ref, mixed_t_hbm),
                ("normed_t", normed_t_ref, normed_t_hbm),
                ("resid", resid_ref, resid_hbm),
                ("normed2", normed2_ref, normed2_hbm),
                ("xs", xs_ref, xs_hbm),
            )
        )
    }
    expert_count, capacity, width = xs_ref.shape
    lane_count = gates_ref.shape[2]
    slots = expert_count * capacity
    size = expert_count // GROUPS
    chips = expert_count // 2
    me, dp = lax.axis_index("expert"), lax.axis_index("dp")
    core, chip = me % 2, me // 2
    x, y = dp % 2, dp // 2
    core_peer = me + 1 - 2 * core
    x_peer, y_peer = dp + 1 - 2 * x, dp + 2 - 4 * y
    my_group, my_place = me // size, me % size
    chip_peers = [(chip + d) % chips for d in range(1, chips)]
    greet(
        [{"expert": (me + d) % expert_count} for d in range(1, expert_count)]
        + [{"dp": x_peer}, {"dp": y_peer}]
    )

    groups = ws_ref.shape[0]
    count = groups + 1
    srcs = [ws_ref.at[j] for j in range(groups)] + [wo_ref]
    bufs = [wq_v.at[j] for j in range(groups)] + [wo_v]
    widths = [ws_ref.shape[2]] * groups + [wo_ref.shape[1]]
    places = ((y, x), (y, 1 - x), (1 - y, x), (1 - y, 1 - x))

    def z_copy(j, peer, at):
        return remote(
            srcs[j], bufs[j].at[y, x, at, core], z_send.at[j, peer], z_recv.at[j, at], expert=peer * 2 + core
        )

    def own_copy(j):
        return pltpu.make_async_copy(srcs[j], bufs[j].at[y, x, chip, core], own_sem.at[j])

    def xy_copy(j, k):
        half = widths[j] // 2
        src = (
            bufs[j].at[y, x, :, core],
            bufs[j].at[y, x, :, core],
            bufs[j].at[1 - y, x, :, core, :, half : 2 * half],
            bufs[j].at[y, 1 - x, :, core, :, 0:half],
        )[k]
        return remote(src, src, xy_send.at[j, k], xy_recv.at[j, k], dp=(x_peer, y_peer)[k % 2])

    def core_copy(j, k):
        src = bufs[j].at[places[k][0], places[k][1], :, core]
        return remote(src, src, core_send.at[j, k], core_recv.at[j, k], expert=core_peer)

    line = chips == 4
    pair = chip // 2
    mate = chip + 1 - 2 * (chip % 2)
    middle = (chip % 4) * (3 - chip % 4) // 2

    def pair_copy(j, k, at, peer):
        span = bufs[j].at[y, x, pl.ds(2 * at, 2), core]
        return remote(span, span, z_send.at[j, k], z_recv.at[j, k], expert=peer * 2 + core)

    def spread_first(j):
        own_copy(j).wait()
        if line:
            z_copy(j, mate, mate).wait_recv()

            @pl.when(middle == 1)
            def _():
                pair_copy(j, 4, pair, 3 - chip).start()

    def spread_second(j):
        if line:

            @pl.when(middle == 1)
            def _():
                pair_copy(j, 4, 1 - pair, 3 - chip).wait_recv()
                pair_copy(j, 5, 1 - pair, mate).start()

    def spread(j):
        if line:

            @pl.when(middle == 0)
            def _():
                pair_copy(j, 5, 1 - pair, mate).wait_recv()
        else:
            for peer in chip_peers:
                z_copy(j, peer, peer).wait_recv()
        for k in range(2):
            xy_copy(j, k).start()
        core_copy(j, 0).start()

    def forward(j):
        for k in range(2):
            xy_copy(j, k).wait_recv()
            xy_copy(j, 3 - k).start()
            core_copy(j, 1 + k).start()

    def complete(j):
        for k in (2, 3):
            xy_copy(j, k).wait_recv()
        core_copy(j, 3).start()

    def out_copy(j):
        src, dst = (wq_v.at[j], wq_out.at[j]) if j < groups else (wo_v, wo_out)
        return pltpu.make_async_copy(src, dst, out_sem.at[j])

    def gathered(j):
        for k in range(4):
            core_copy(j, k).wait_recv()
        out_copy(j).start()

    third = ws_ref.shape[2] // 3
    for j in range(count):
        if j < groups:
            for k in range(3):
                at = (k * groups + j) * third
                ws_ref[j, :, k * third : (k + 1) * third] = w_qkv_ref[:, at : at + third]
        own_copy(j).start()
        for peer in [mate] if line else chip_peers:
            z_copy(j, peer, chip).start()

    inputs = tokens_ref[...].astype(F32)
    inv_rms = lax.rsqrt(jnp.mean(inputs * inputs, axis=1, keepdims=True) + EPS)
    normed = (inputs * inv_rms * gain1_ref[...]).astype(BF16)
    normed_v[...] = normed
    normed_t_ref[...] = normed.T
    stores["normed_t"].start()
    spread_first(0)
    spread_first(1)
    spread_second(0)
    spread_first(2)
    spread_second(1)
    spread(0)
    spread_first(3)
    spread_second(2)
    spread(1)
    spread_first(4)
    spread_second(3)

    rows = routes_ref.shape[1]
    lane = iota((rows, 128), 1)
    routes = [route_column(routes_ref, k) for k in range(2)]
    hots = [lane == routes[k].astype(jnp.int32) for k in range(2)]
    earlier = (iota((rows, rows), 0) > iota((rows, rows), 1)).astype(BF16)
    ones = [jnp.where(h, 1.0, 0.0) for h in hots]
    counts = [dot_nn(earlier, o.astype(BF16)) for o in ones]
    counts[1] = counts[1] + jnp.sum(ones[0], axis=0, keepdims=True)
    slot = []
    for k in range(2):
        place = jnp.sum(counts[k] * ones[k], axis=1, keepdims=True)
        at = column(routes[k], 0) * capacity + place
        slot.append(jnp.where(place < capacity, at, float(slots)))
    slot_rows = jnp.where(lane == 0, slot[0], slot[1]).T
    slot_ids = iota((slots, rows), 0).astype(F32)
    hot = (slot_ids == slot_rows[0:1]) | (slot_ids == slot_rows[1:2])
    hot_v[...] = jnp.where(hot, 1.0, 0.0).astype(BF16)
    g_v[...] = dot_nn(hot_v[...], grad_ref[...]).astype(BF16).reshape(g_v.shape)

    def g_copy(peer, at):
        return remote(g_v.at[peer], g_back.at[at], g_send.at[peer], g_recv.at[at], expert=peer)

    def others(c):
        group = flip(my_group, c)
        return [group * size + (my_place + s) % size for s in range(1 if c == 0 else 0, size)]

    peers = [peer for c in (2, 3, 1, 0) for peer in others(c)]
    g_own = pltpu.make_async_copy(g_v.at[me], g_back.at[me], own_sem.at[count])
    g_own.start()

    def p_copy(j, a):
        return pltpu.make_async_copy(p_v.at[a], p_out.at[pl.ds(4 * j + 2 * a, 2)], p_sem.at[a])

    def group(j):
        gathered(j)
        qkv_v[j] = dot_nn(normed_v[...], wq_v[j].reshape(width, widths[j])).astype(BF16)

        def pair(a, carry):
            if j > 0:
                p_copy(j - 1, a).wait()
            mixed = attend_pair(j, a, qkv_v, table_ref, p_v.at[a])
            p_copy(j, a).start()
            span = pl.ds(pl.multiple_of(256 * j + 128 * a, 128), 128)
            mixed_t_ref[span, :] = mixed.astype(BF16)
            mixed_v[:, span] = mixed.T.astype(BF16)
            return carry

        lax.fori_loop(0, 2, pair, 0)

    spread(2)
    spread_second(4)
    forward(0)
    spread(3)
    spread(4)
    for peer in peers:
        g_copy(peer, me).start()
    forward(1)
    complete(0)
    forward(2)
    complete(1)
    group(0)
    forward(3)
    complete(2)
    group(1)
    forward(4)
    complete(3)
    group(2)
    complete(4)
    group(3)
    qkv_copy = pltpu.make_async_copy(qkv_v, qkv_out, own_sem.at[count + 1])
    qkv_copy.start()
    stores["mixed_t"].start()
    gathered(groups)

    resid = tokens_ref[...].astype(F32) + dot_nn(mixed_v[...], wo_v[...].reshape(width, width))
    resid_ref[...] = resid
    stores["resid"].start()
    inv_rms2 = lax.rsqrt(jnp.mean(resid * resid, axis=1, keepdims=True) + EPS)
    normed2 = (resid * inv_rms2 * gain2_ref[...]).astype(BF16)
    normed2_ref[...] = normed2
    stores["normed2"].start()
    xs_ref[...] = dot_nn(hot_v[...], normed2).astype(BF16).reshape(xs_ref.shape)
    stores["xs"].start()
    rest = router_ref[...]
    logits = jnp.zeros((rows, expert_count), F32)
    for _ in range(3):
        piece = rest.astype(BF16)
        rest = rest - piece.astype(F32)
        logits = logits + dot_nt(normed2, piece)
    ids = iota((rows, expert_count), 1)
    chosen = [
        jnp.sum(
            jnp.where(ids == column(routes[k], 0).astype(jnp.int32), logits, 0.0),
            axis=1,
            keepdims=True,
        )
        for k in range(2)
    ]
    top = jnp.maximum(chosen[0], chosen[1])
    exps = [jnp.exp(c - top) for c in chosen]
    gates = [e / (exps[0] + exps[1]) for e in exps]
    cols = jnp.where(lane == 2, gates[0], jnp.where(lane == 3, gates[1], 0.0))
    cols_ref[...] = jnp.where(lane == 0, slot[0], jnp.where(lane == 1, slot[1], cols))
    wide = iota((rows, lane_count), 1)

    def gate_row(e, carry):
        base = (e * capacity).astype(F32)
        total = jnp.zeros((rows, lane_count), F32)
        for k in range(2):
            here = (wide.astype(F32) == slot[k] - base) & (wide < capacity)
            total = total + jnp.where(here, gates[k], 0.0)
        row = jnp.sum(total, axis=0, keepdims=True)
        gates_ref[pl.ds(e, 1)] = jnp.broadcast_to(row, (8, lane_count))[None]
        return carry

    lax.fori_loop(0, expert_count, gate_row, 0)

    for a in range(2):
        p_copy(groups - 1, a).wait()
    qkv_copy.wait()
    for copy in stores.values():
        copy.wait()
    g_own.wait()
    for j in range(count):
        out_copy(j).wait()
        for peer in [mate] if line else chip_peers:
            z_copy(j, peer, chip).wait_send()
        if line:

            @pl.when(middle == 1)
            def _():
                pair_copy(j, 4, pair, 3 - chip).wait_send()
                pair_copy(j, 5, 1 - pair, mate).wait_send()

        for k in range(4):
            xy_copy(j, k).wait_send()
            core_copy(j, k).wait_send()
    for peer in peers:
        g_copy(peer, me).wait_send()
        g_copy(peer, peer).wait_recv()


def front(tokens, gain1, gain2, table, routes, grad_out, router, w_qkv, wo, groups, capacity):
    rows, width = tokens.shape
    expert_count = router.shape[0]
    chips = expert_count // 2
    own, part = w_qkv.shape[0], w_qkv.shape[1] // groups
    heads = table.shape[0]
    lane_count = -(-capacity // 128) * 128
    vmem = pl.BlockSpec(memory_space=pltpu.VMEM)
    sem = pltpu.SemaphoreType.DMA
    shape = jax.ShapeDtypeStruct
    slots = (expert_count, capacity, width)
    spread = (2, 2, chips, 2, own)
    return pl.pallas_call(
        front_kernel,
        in_specs=[vmem] * 9,
        out_specs=[ANY] * 10 + [vmem] * 2,
        out_shape=[
            shape((groups, *spread, part), BF16),
            shape((*spread, width), BF16),
            shape((groups, rows, part), BF16),
            shape((heads, rows, rows), BF16),
            shape(slots, BF16),
            shape((width, rows), BF16),
            shape((width, rows), BF16),
            shape((rows, width), F32),
            shape((rows, width), BF16),
            shape(slots, BF16),
            shape((expert_count, 8, lane_count), F32),
            shape((rows, 128), F32),
        ],
        scratch_shapes=[
            pltpu.VMEM((groups, own, part), BF16),
            pltpu.VMEM((groups, *spread, part), BF16),
            pltpu.VMEM((*spread, width), BF16),
            pltpu.VMEM((groups, rows, part), BF16),
            pltpu.VMEM((2, 2, rows, rows), BF16),
            pltpu.VMEM((rows, width), BF16),
            pltpu.VMEM((rows, width), BF16),
            pltpu.VMEM((expert_count * capacity, rows), BF16),
            pltpu.VMEM(slots, BF16),
            sem((groups + 3,)),
            sem((groups + 1, max(chips, 6))),
            sem((groups + 1, max(chips, 6))),
            sem((groups + 1, 4)),
            sem((groups + 1, 4)),
            sem((groups + 1, 4)),
            sem((groups + 1, 4)),
            sem((expert_count,)),
            sem((expert_count,)),
            sem((groups + 1,)),
            sem((2,)),
            pltpu.VMEM((width, rows), BF16),
            pltpu.VMEM((width, rows), BF16),
            pltpu.VMEM((rows, width), F32),
            pltpu.VMEM((rows, width), BF16),
            pltpu.VMEM(slots, BF16),
            sem((5,)),
        ],
        compiler_params=pltpu.CompilerParams(
            collective_id=3, has_side_effects=True, vmem_limit_bytes=60 * 1024 * 1024
        ),
        name="front",
    )(tokens, gain1, gain2, table, routes, grad_out, router, w_qkv, wo)


def attend_back_pair(j, a, qkv_v, p_ref, grads_v, dqkv_v, fold_ref):
    def lanes(part):
        return pl.ds(pl.multiple_of(256 * part + 128 * a, 128), 128)

    query = qkv_v[j, :, lanes(0)] * jnp.asarray(0.125, BF16)
    keys_t = qkv_v[j, :, lanes(1)].T
    values = qkv_v[j, :, lanes(2)]
    grads = grads_v[:, pl.ds(pl.multiple_of(256 * j + 128 * a, 128), 128)]
    half = iota((512, 128), 1) // 64
    dq_halves, dk_halves, dv_halves = [], [], []
    for t in range(2):
        values_t = jnp.where(half == t, values, jnp.zeros_like(values))
        probs = [p_ref[t, 128 * c : 128 * c + 128, :].astype(F32) for c in range(4)]
        grad_probs = [dot_nt(values_t[128 * c : 128 * c + 128], grads) for c in range(4)]
        delta = functools.reduce(
            jnp.add,
            [jnp.sum(p * g, axis=0, keepdims=True) for p, g in zip(probs, grad_probs)],
        )
        scores = [(p * (g - delta)).astype(BF16) for p, g in zip(probs, grad_probs)]
        padded = [
            jnp.concatenate(
                ([jnp.zeros((128, 384 - 128 * c), F32)] if c < 3 else [])
                + [scores[c].astype(F32), jnp.zeros((128, 128 + 128 * c), F32)],
                axis=1,
            )
            for c in range(4)
        ]
        fold_ref[pl.ds(4 * j + 2 * a + t, 1), :] = fold_bias(functools.reduce(jnp.add, padded))
        grad_scores = jnp.concatenate(scores, axis=0)
        dv_halves.append(dot_nn(p_ref[t], grads))
        dk_halves.append(dot_nn(grad_scores, query))
        dq_halves.append(dot_nn(keys_t, grad_scores))
    dq = jnp.where(iota((128, 512), 0) < 64, dq_halves[0], dq_halves[1]) * 0.125
    dqkv_v[:, lanes(0)] = dq.T.astype(BF16)
    dqkv_v[:, lanes(1)] = jnp.where(half == 0, dk_halves[0], dk_halves[1]).astype(BF16)
    dqkv_v[:, lanes(2)] = jnp.where(half == 0, dv_halves[0], dv_halves[1]).astype(BF16)


def dot_exact(a, b, dot=dot_nn):
    total = None
    for _ in range(3):
        piece = a.astype(BF16)
        a = a - piece.astype(F32)
        term = dot(piece, b)
        total = term if total is None else total + term
    return total


def dot_f32(a, b):
    total = None
    for _ in range(3):
        piece = b.astype(BF16)
        b = b - piece.astype(F32)
        term = dot_exact(a, piece)
        total = term if total is None else total + term
    return total


def back_kernel(
    dw_ref,
    head_ref,
    ys_ref,
    dx_hbm,
    dgates_hbm,
    cols_ref,
    routes_ref,
    tokens_hbm,
    grad_hbm,
    resid_hbm,
    normed2_hbm,
    normed_t_hbm,
    mixed_t_hbm,
    gain1_ref,
    gain2_ref,
    router_t_ref,
    bucket_hot_ref,
    wq_ref,
    wo_hbm,
    qkv_ref,
    p_ref,
    first_ref,
    second_ref,
    small_out_ref,
    gq_out_ref,
    go_out_ref,
    block_hbm,
    grad_tokens_hbm,
    y_v,
    grads_q,
    grads_o,
    core_q,
    core_o,
    step1_q,
    step1_o,
    step2_q,
    step2_o,
    last_q,
    last_o,
    rows_q,
    rows_o,
    sum_q,
    sum_o,
    qkv_v,
    p_v,
    wq_v,
    dqkv_v,
    dmix_v,
    dn1_v,
    fold_v,
    small_v,
    own_v,
    first_v,
    pass_v,
    y_send,
    y_recv,
    first_send,
    first_recv,
    second_send,
    second_recv,
    ring_sem,
    small_send,
    small_recv,
    core_send,
    core_recv,
    step1_send,
    step1_recv,
    step2_send,
    step2_recv,
    last_send,
    last_recv,
    local_sem,
    p_sem,
    wq_sem,
    dx_ref,
    dgates_ref,
    tokens_ref,
    resid_ref,
    normed2_ref,
    normed_t_ref,
    mixed_t_ref,
    wo_ref,
    grad_ref,
    input_sem,
    block_sem,
    block_ref,
    grad_tokens_ref,
):
    loads = {
        name: pltpu.make_async_copy(src, dst, input_sem.at[n])
        for n, (name, src, dst) in enumerate(
            (
                ("dx", dx_hbm, dx_ref),
                ("dgates", dgates_hbm, dgates_ref),
                ("tokens", tokens_hbm, tokens_ref),
                ("resid", resid_hbm, resid_ref),
                ("normed2", normed2_hbm, normed2_ref),
                ("normed_t", normed_t_hbm, normed_t_ref),
                ("mixed_t", mixed_t_hbm, mixed_t_ref),
                ("wo", wo_hbm, wo_ref),
                ("grad", grad_hbm, grad_ref),
            )
        )
    }
    for copy in loads.values():
        copy.start()
    expert_count, capacity, width = ys_ref.shape
    slots = expert_count * capacity
    rows = tokens_ref.shape[0]
    chips = expert_count // 2
    size = expert_count // GROUPS
    me, dp = lax.axis_index("expert"), lax.axis_index("dp")
    core, chip = me % 2, me // 2
    x, y = dp % 2, dp // 2
    core_peer = me + 1 - 2 * core
    x_peer, y_peer = dp + 1 - 2 * x, dp + 2 - 4 * y
    my_group, my_place = me // size, me % size
    chip_peers = [(chip + d) % chips for d in range(1, chips)]
    greet(
        [{"expert": (me + d) % expert_count} for d in range(1, expert_count)]
        + [{"dp": x_peer}, {"dp": y_peer}]
    )

    tile_count = dw_ref.shape[0]
    batches = tile_count // BATCH

    def first_copy(t, i):
        sent, _, peer, _, keep = ways(dp, t)
        return remote(
            dw_ref.at[t, sent[i]],
            first_ref.at[t - BATCH * AHEAD, (i + keep) % 2],
            first_send.at[t - BATCH * AHEAD, i],
            first_recv.at[t - BATCH * AHEAD, i],
            dp=peer,
        )

    def second_copy(t, n):
        peer = ways(dp, t)[3]
        return remote(
            pass_v.at[n % 2, t % BATCH], second_ref.at[t], second_send.at[t], second_recv.at[t], dp=peer
        )

    def relay_loads(t, b):
        held = ways(dp, t)[1]
        q = t % BATCH
        came = head_ref.at[t, 1] if b < AHEAD else first_ref.at[t - BATCH * AHEAD, 1]
        return [
            pltpu.make_async_copy(dw_ref.at[t, held[1]], own_v.at[b % 2, q], ring_sem.at[b % 2, q, 0]),
            pltpu.make_async_copy(came, first_v.at[b % 2, q], ring_sem.at[b % 2, q, 1]),
        ]

    def over(b, body):
        def step(t, carry):
            body(t)
            return carry

        lax.fori_loop(BATCH * b, BATCH * b + BATCH, step, 0)

    def issue(b):
        def body(t):
            for i in range(2):
                first_copy(t, i).start()

        over(b, body)

    def relay_begin(b):
        def body(t):
            if b >= AHEAD:
                for i in range(2):
                    first_copy(t, i).wait_recv()
            for load in relay_loads(t, b):
                load.start()

        over(b, body)

    def relay_end(b):
        def body(t):
            for load in relay_loads(t, b):
                load.wait()
            if b >= 2:
                second_copy(t - 2 * BATCH, b).wait_send()
            q = t % BATCH
            pass_v[b % 2, q] = (
                own_v[b % 2, q].astype(F32) + first_v[b % 2, q].astype(F32)
            ).astype(BF16)
            second_copy(t, b).start()

        over(b, body)

    groups = grads_q.shape[0]
    count = groups + 1

    def pick(many, one, p):
        return many.at[p] if p < groups else one

    grads = [pick(grads_q, grads_o, p) for p in range(count)]
    cores = [pick(core_q, core_o, p) for p in range(count)]
    step1 = [pick(step1_q, step1_o, p) for p in range(count)]
    step2 = [pick(step2_q, step2_o, p) for p in range(count)]
    lasts = [pick(last_q, last_o, p) for p in range(count)]
    outs = [pick(gq_out_ref, go_out_ref, p) for p in range(count)]
    widths = [grads_q.shape[-1]] * groups + [grads_o.shape[-1]]

    def part_core(p):
        return remote(
            grads[p].at[:, :, :, 1 - core], cores[p], core_send.at[p], core_recv.at[p], expert=core_peer
        )

    def part_step1(p, b):
        half = widths[p] // 2
        src = (
            grads[p].at[:, 1 - x, :, core, :, 0:half]
            if b == 0
            else grads[p].at[1 - y, :, :, core, :, half : 2 * half]
        )
        return remote(
            src, step1[p].at[b], step1_send.at[p, b], step1_recv.at[p, b], dp=(x_peer, y_peer)[b]
        )

    def part_step2(p, b):
        src = step1[p].at[b, (1 - y, 1 - x)[b]]
        return remote(
            src, step2[p].at[b], step2_send.at[p, b], step2_recv.at[p, b], dp=(y_peer, x_peer)[b]
        )

    def part_last(p, peer, at):
        return remote(
            cores[p].at[0, 0, peer], lasts[p].at[at], last_send.at[p, peer], last_recv.at[p, at],
            expert=peer * 2 + core,
        )

    arrivals = {p: rows_o if p == groups else rows_q.at[p] for p in CHIPS_FIRST}
    sums = {p: sum_o if p == groups else sum_q.at[p] for p in CHIPS_FIRST}

    def chip_rows(p, peer, at):
        return remote(
            grads[p].at[:, :, peer, core], arrivals[p].at[at], last_send.at[p, peer], last_recv.at[p, at],
            expert=peer * 2 + core,
        )

    def chip_step1(p, b):
        half = widths[p] // 2
        src = (
            sums[p].at[:, 1 - x, :, 0:half] if b == 0 else sums[p].at[1 - y, :, :, half : 2 * half]
        )
        return remote(
            src, step1[p].at[b, :, 0], step1_send.at[p, b], step1_recv.at[p, b], dp=(x_peer, y_peer)[b]
        )

    def chip_step2(p, b):
        src = step1[p].at[b, (1 - y, 1 - x)[b], 0]
        return remote(
            src, step2[p].at[b, 0], step2_send.at[p, b], step2_recv.at[p, b], dp=(y_peer, x_peer)[b]
        )

    def chip_held(p, b, i):
        half = widths[p] // 2
        held = sums[p][i, x, :, 0:half] if b == 0 else sums[p][y, i, :, half : 2 * half]
        return held.astype(F32) + step1[p][b, i, 0].astype(F32)

    def part_a(p):
        part_core(p).start()

    def part_b(p):
        part_core(p).wait()
        total = grads[p][:, :, :, core].astype(F32) + cores[p][...].astype(F32)
        grads[p][:, :, :, core] = total.astype(BF16)
        if p in CHIPS_FIRST:
            for peer in chip_peers:
                chip_rows(p, peer, chip).start()
            return
        for b in range(2):
            part_step1(p, b).start()

    def part_c(p):
        half = widths[p] // 2
        if p in CHIPS_FIRST:
            total = grads[p][:, :, chip, core].astype(F32)
            for peer in chip_peers:
                chip_rows(p, peer, peer).wait_recv()
                total = total + arrivals[p][peer].astype(F32)
            sums[p][...] = total.astype(BF16)
            for b in range(2):
                chip_step1(p, b).start()
            return
        for b in range(2):
            part_step1(p, b).wait()
            for i in range(2):
                held = (
                    grads[p][i, x, :, core, :, 0:half]
                    if b == 0
                    else grads[p][y, i, :, core, :, half : 2 * half]
                )
                total = held.astype(F32) + step1[p][b, i].astype(F32)
                step1[p][b, i] = total.astype(BF16)
            part_step2(p, b).start()

    def part_d(p):
        half = widths[p] // 2
        if p in CHIPS_FIRST:
            for b in range(2):
                chip_step1(p, b).wait()
                give = (1 - y, 1 - x)[b]
                step1[p][b, give, 0] = chip_held(p, b, give).astype(BF16)
                chip_step2(p, b).start()
            return
        for b in range(2):
            part_step2(p, b).wait()
            total = step1[p][b, (y, x)[b]].astype(F32) + step2[p][b].astype(F32)
            cores[p][0, 0, :, :, b * half : b * half + half] = total.astype(BF16)
        for peer in chip_peers:
            part_last(p, peer, chip).start()

    def part_e(p):
        half = widths[p] // 2
        if p in CHIPS_FIRST:
            for b in range(2):
                chip_step2(p, b).wait()
                total = chip_held(p, b, (y, x)[b]) + step2[p][b, 0].astype(F32)
                outs[p][:, b * half : b * half + half] = total
            for peer in chip_peers:
                chip_rows(p, peer, chip).wait_send()
            return
        total = cores[p][0, 0, chip].astype(F32)
        for peer in chip_peers:
            part_last(p, peer, peer).wait_recv()
            total = total + lasts[p][peer].astype(F32)
        outs[p][...] = total
        for peer in chip_peers:
            part_last(p, peer, chip).wait_send()

    partners = []
    bit = 1
    while bit < expert_count:
        partners.append({"expert": flip(me, bit)})
        bit *= 2
    partners += [{"dp": x_peer}, {"dp": y_peer}]
    stages = len(partners)

    def small_copy(s):
        return remote(
            small_v.at[0], small_v.at[1 + s], small_send.at[s], small_recv.at[s], **partners[s]
        )

    def small_next(s):
        small_copy(s).wait()
        small_v[0] = small_v[0] + small_v[1 + s]
        if s + 1 < stages:
            small_copy(s + 1).start()

    def y_copy(peer, at):
        return remote(ys_ref.at[peer], y_v.at[at], y_send.at[peer], y_recv.at[at], expert=peer)

    def others(c):
        group = flip(my_group, c)
        return [group * size + (my_place + s) % size for s in range(1 if c == 0 else 0, size)]

    peers = [peer for c in (2, 3, 1, 0) for peer in others(c)]

    def p_copy(j, a):
        return pltpu.make_async_copy(p_ref.at[pl.ds(4 * j + 2 * a, 2)], p_v.at[a], p_sem.at[a])

    def wq_copy(j):
        return pltpu.make_async_copy(wq_ref.at[j], wq_v.at[j % 2], wq_sem.at[j % 2])

    lane = iota((rows, 128), 1)
    slot = [column(cols_ref[...], k) for k in range(2)]
    gates = [column(cols_ref[...], 2 + k) for k in range(2)]

    def hots():
        at = iota((rows, slots), 1).astype(F32)
        return [at == s for s in slot]

    def dense():
        lanes = dgates_ref.shape[2]
        wide = iota((rows, lanes), 1)

        def step(e, totals):
            base = (e * capacity).astype(F32)
            row = dgates_ref[pl.ds(e, 1)][0][0:1]
            return tuple(
                totals[k]
                + jnp.where((wide.astype(F32) == slot[k] - base) & (wide < capacity), row, 0.0)
                for k in range(2)
            )

        zero = jnp.zeros((rows, lanes), F32)
        sums = lax.fori_loop(0, expert_count, step, (zero, zero))
        dgates = [jnp.sum(s, axis=1, keepdims=True) for s in sums]
        mean = gates[0] * dgates[0] + gates[1] * dgates[1]
        dchosen = [gates[k] * (dgates[k] - mean) for k in range(2)]
        dlogits = jnp.zeros((rows, 128), F32)
        for k in range(2):
            here = lane == route_column(routes_ref, k).astype(jnp.int32)
            dlogits = dlogits + jnp.where(here, dchosen[k], 0.0)
        small_rows = dot_exact(dlogits.T[0:expert_count], normed2_ref[...])
        small_v[0, 0:expert_count] = small_rows
        blank = jnp.zeros((128 - expert_count, width), F32)
        router = jnp.concatenate([router_t_ref[...], blank], axis=0)
        hot0, hot1 = hots()
        hot = jnp.where(hot0 | hot1, 1.0, 0.0).astype(BF16)
        dnormed = dot_f32(dlogits, router)
        dnormed = dnormed + dot_nn(hot, dx_ref[...].reshape(slots, width))
        resid = resid_ref[...]
        inv_rms = lax.rsqrt(jnp.mean(resid * resid, axis=1, keepdims=True) + EPS)
        normed = resid * inv_rms
        scaled = dnormed * gain2_ref[...]
        small_v[0, expert_count + 1 : expert_count + 2] = jnp.sum(
            dnormed * normed, axis=0, keepdims=True
        )
        inner = jnp.mean(scaled * normed, axis=1, keepdims=True)
        dresid = grad_ref[...].astype(F32) + inv_rms * (scaled - normed * inner)
        grad_tokens_ref[...] = dresid
        dresid_r = dresid.astype(BF16)
        grads_o[...] = dot_nn(mixed_t_ref[...], dresid_r).astype(BF16).reshape(grads_o.shape)
        part_a(groups)
        dmix_v[...] = dot_nt(dresid_r, wo_ref[...]).astype(BF16)

    def group(j):
        if j + 1 < groups:
            wq_copy(j + 1).start()

        def pair(a, carry):
            p_copy(j, a).wait()
            attend_back_pair(j, a, qkv_v, p_v.at[a], dmix_v, dqkv_v, fold_v)
            if j + 1 < groups:
                p_copy(j + 1, a).start()
            return carry

        lax.fori_loop(0, 2, pair, 0)
        block = dot_nn(normed_t_ref[...], dqkv_v[...])
        grads_q[j] = block.astype(BF16).reshape(grads_q.shape[1:])
        part_a(j)
        wq_copy(j).wait()
        term = dot_nt(dqkv_v[...], wq_v[j % 2])
        dn1_v[...] = term if j == 0 else dn1_v[...] + term

    def norm_back():
        inputs = tokens_ref[...].astype(F32)
        inv_rms = lax.rsqrt(jnp.mean(inputs * inputs, axis=1, keepdims=True) + EPS)
        normed = inputs * inv_rms
        dnormed = dn1_v[...]
        scaled = dnormed * gain1_ref[...]
        small_v[0, expert_count : expert_count + 1] = jnp.sum(
            dnormed * normed, axis=0, keepdims=True
        )
        inner = jnp.mean(scaled * normed, axis=1, keepdims=True)
        grad_tokens_ref[...] += inv_rms * (scaled - normed * inner)
        buckets = dot_exact(fold_v[...], bucket_hot_ref[...], dot_nt)
        tokens_copy.start()
        base = expert_count + 2
        heads = fold_v.shape[0]
        small_v[0, base : base + heads, 0 : buckets.shape[1]] = buckets
        small_copy(0).start()

    def outputs():
        for peer in peers:
            y_copy(peer, peer).wait_recv()
        y_own.wait()
        values = y_v[...].reshape(slots, width)
        total = resid_ref[...]
        for k, hot in enumerate(hots()):
            total = total + gates[k] * dot_nn(jnp.where(hot, 1.0, 0.0).astype(BF16), values)
        block_ref[...] = total.astype(BF16)
        block_copy.start()

    block_copy = pltpu.make_async_copy(block_ref, block_hbm, block_sem.at[0])
    tokens_copy = pltpu.make_async_copy(grad_tokens_ref, grad_tokens_hbm, block_sem.at[1])
    small_v[0] = jnp.zeros(small_v.shape[1:], F32)
    for peer in peers:
        y_copy(peer, me).start()
    y_own = pltpu.make_async_copy(ys_ref.at[me], y_v.at[me], local_sem.at[0])
    y_own.start()
    qkv_copy = pltpu.make_async_copy(qkv_ref, qkv_v, local_sem.at[1])
    qkv_copy.start()
    wq_copy(0).start()
    for a in range(2):
        p_copy(0, a).start()
    late = [b for b in range(AHEAD, batches)]
    turn = [b for b in range(AHEAD, batches)]
    open_relays = []

    def send_more(number):
        for _ in range(min(number, len(late))):
            issue(late.pop(0))

    def relay_in():
        if turn:
            b = turn.pop(0)
            relay_begin(b)
            open_relays.append(b)

    def relay_out():
        if open_relays:
            relay_end(open_relays.pop(0))

    send_more(4)
    for b in range(AHEAD):
        relay_begin(b)
        if b > 0:
            relay_end(b - 1)
    relay_end(AHEAD - 1)
    send_more(1)
    for copy in loads.values():
        copy.wait()
    dense()
    qkv_copy.wait()
    group(0)
    part_b(groups)
    relay_in()
    relay_out()
    send_more(1)
    group(1)
    part_b(0)
    relay_in()
    relay_out()
    send_more(1)
    group(2)
    part_b(1)
    relay_in()
    relay_out()
    send_more(1)
    group(3)
    part_b(2)
    send_more(1)
    norm_back()
    part_b(3)
    send_more(len(late))
    relay_in()
    small_next(0)
    relay_out()
    direct = [p for p in (groups, *range(groups)) if p not in CHIPS_FIRST]
    first_on = [p for p in (groups, *range(groups)) if p in CHIPS_FIRST]
    for p in direct:
        part_c(p)
    small_next(1)
    outputs()
    small_next(2)
    relay_in()
    for p in direct[:-1]:
        part_d(p)
    relay_out()
    for p in first_on[:1]:
        part_c(p)
    small_next(3)
    relay_in()
    for p in direct[-1:]:
        part_d(p)
    for p in first_on[1:2]:
        part_c(p)
    relay_out()
    for s in range(4, stages):
        small_next(s)
    small_out_ref[...] = small_v[0]
    for p in first_on[:1]:
        part_d(p)
    relay_in()
    for p in first_on[2:]:
        part_c(p)
    for p in first_on[1:2]:
        part_d(p)
    relay_out()
    while turn:
        relay_in()
        relay_out()
    for p in first_on[2:]:
        part_d(p)
    for p in direct:
        part_e(p)
    for p in first_on:
        part_e(p)
    for b in (batches - 2, batches - 1):
        over(b, lambda t, b=b: second_copy(t, b).wait_send())

    def drain_first(t, carry):
        for i in range(2):
            first_copy(t, i).wait_send()
        return carry

    def drain_second(t, carry):
        second_copy(t, 0).wait_recv()
        return carry

    block_copy.wait()
    tokens_copy.wait()
    lax.fori_loop(BATCH * AHEAD, tile_count, drain_first, 0)
    lax.fori_loop(0, tile_count, drain_second, 0)
    for peer in peers:
        y_copy(peer, me).wait_send()


def back(
    dw, head, ys, dx, dgates, cols, routes, tokens, grad_out, resid, normed2, normed_t, mixed_t,
    gain1, gain2, router_t, bucket_hot, wq, wo, qkv, probs,
):
    tile_count, dp_count, deep, _ = dw.shape
    expert_count, capacity, width = ys.shape
    chips = expert_count // 2
    rows = tokens.shape[0]
    groups, _, part = qkv.shape
    own = width // (dp_count * expert_count)
    heads = probs.shape[0]
    small_rows = -(-(expert_count + 2 + heads) // 8) * 8
    stages = expert_count.bit_length() + 1
    vmem = pl.BlockSpec(memory_space=pltpu.VMEM)
    sem = pltpu.SemaphoreType.DMA
    shape = jax.ShapeDtypeStruct
    ring = (2, BATCH, deep, TILE)
    late = tile_count - BATCH * AHEAD

    def pairs(make, number=groups):
        return [pltpu.VMEM((number, *make(part)), BF16), pltpu.VMEM(make(width), BF16)]

    return pl.pallas_call(
        back_kernel,
        in_specs=[ANY] * 5 + [vmem] * 2 + [ANY] * 6 + [vmem] * 4 + [ANY] * 4,
        out_specs=[ANY] * 2 + [vmem] * 3 + [ANY] * 2,
        out_shape=[
            shape((late, 2, deep, TILE), BF16),
            shape((tile_count, deep, TILE), BF16),
            shape((small_rows, width), F32),
            shape((groups, own, part), F32),
            shape((own, width), F32),
            shape((rows, width), BF16),
            shape((rows, width), F32),
        ],
        scratch_shapes=[pltpu.VMEM(ys.shape, BF16)]
        + pairs(lambda w: (2, 2, chips, 2, own, w))
        + pairs(lambda w: (2, 2, chips, own, w))
        + pairs(lambda w: (2, 2, chips, own, w // 2))
        + pairs(lambda w: (2, chips, own, w // 2))
        + pairs(lambda w: (chips, own, w))
        + pairs(lambda w: (chips, 2, 2, own, w), CHIPS_FIRST_GROUPS)
        + pairs(lambda w: (2, 2, own, w), CHIPS_FIRST_GROUPS)
        + [
            pltpu.VMEM(qkv.shape, BF16),
            pltpu.VMEM((2, 2, rows, rows), BF16),
            pltpu.VMEM((2, *wq.shape[1:]), BF16),
            pltpu.VMEM((rows, part), BF16),
            pltpu.VMEM((rows, width), BF16),
            pltpu.VMEM((rows, width), F32),
            pltpu.VMEM((heads, bucket_hot.shape[1]), F32),
            pltpu.VMEM((stages + 1, small_rows, width), F32),
            pltpu.VMEM(ring, BF16),
            pltpu.VMEM(ring, BF16),
            pltpu.VMEM(ring, BF16),
            sem((expert_count,)),
            sem((expert_count,)),
            sem((late, 2)),
            sem((late, 2)),
            sem((tile_count,)),
            sem((tile_count,)),
            sem((2, BATCH, 2)),
            sem((stages,)),
            sem((stages,)),
            sem((groups + 1,)),
            sem((groups + 1,)),
            sem((groups + 1, 2)),
            sem((groups + 1, 2)),
            sem((groups + 1, 2)),
            sem((groups + 1, 2)),
            sem((groups + 1, chips)),
            sem((groups + 1, chips)),
            sem((2,)),
            sem((2,)),
            sem((2,)),
        ]
        + [
            pltpu.VMEM(a.shape, a.dtype)
            for a in (dx, dgates, tokens, resid, normed2, normed_t, mixed_t, wo, grad_out)
        ]
        + [
            sem((9,)),
            sem((2,)),
            pltpu.VMEM((rows, width), BF16),
            pltpu.VMEM((rows, width), F32),
        ],
        compiler_params=pltpu.CompilerParams(
            collective_id=2, has_side_effects=True, vmem_limit_bytes=61 * 1024 * 1024
        ),
        name="back",
    )(
        dw, head, ys, dx, dgates, cols, routes, tokens, grad_out, resid, normed2, normed_t, mixed_t,
        gain1, gain2, router_t, bucket_hot, wq, wo, qkv, probs,
    )


def tail_kernel(
    heads,
    buckets,
    dw_ref,
    head_ref,
    first_ref,
    second_ref,
    block_ref,
    tokens_ref,
    small_ref,
    gq_ref,
    go_ref,
    in_ref,
    out_ref,
    block_out_ref,
    tokens_out_ref,
    router_ref,
    norm1_ref,
    norm2_ref,
    bias_ref,
    qkv_ref,
    proj_ref,
    own_v,
    came_v,
    second_v,
    in_v,
    out_v,
    block_v,
    tokens_v,
    load_sem,
    store_sem,
    pass_sem,
):
    dp = lax.axis_index("dp")
    tiles = own_v.shape[0]
    expert_count = router_ref.shape[0]

    def loads(f):
        span = pl.ds(BATCH * f, BATCH)
        late = pl.ds(BATCH * (f - AHEAD), BATCH)
        came = head_ref.at[span, 0] if f < AHEAD else first_ref.at[late, 0]
        return [
            pltpu.make_async_copy(src, dst.at[f], load_sem.at[f, k])
            for k, (src, dst) in enumerate(
                ((dw_ref.at[span, dp], own_v), (came, came_v), (second_ref.at[span], second_v))
            )
        ]

    def stores(f):
        cols = pl.ds(TILE * f, TILE)
        return [
            pltpu.make_async_copy(in_v.at[f], in_ref.at[:, :, cols], store_sem.at[f, 0]),
            pltpu.make_async_copy(out_v.at[f], out_ref.at[cols], store_sem.at[f, 1]),
        ]

    for f in range(tiles):
        for copy in loads(f):
            copy.start()
    taken = [
        pltpu.make_async_copy(block_ref, block_v, pass_sem.at[0]),
        pltpu.make_async_copy(tokens_ref, tokens_v, pass_sem.at[1]),
    ]
    given = [
        pltpu.make_async_copy(block_v, block_out_ref, pass_sem.at[2]),
        pltpu.make_async_copy(tokens_v, tokens_out_ref, pass_sem.at[3]),
    ]
    for copy in taken:
        copy.start()
    router_ref[...] = small_ref[0:expert_count]
    norm1_ref[...] = small_ref[expert_count : expert_count + 1]
    norm2_ref[...] = small_ref[expert_count + 1 : expert_count + 2]
    bias_ref[...] = small_ref[expert_count + 2 : expert_count + 2 + heads, 0:buckets]
    groups, _, part = gq_ref.shape
    third = part // 3
    for j in range(groups):
        for k in range(3):
            at = (k * groups + j) * third
            qkv_ref[:, at : at + third] = gq_ref[j, :, k * third : (k + 1) * third]
    proj_ref[...] = go_ref[...]
    for f in range(tiles):
        for copy in loads(f):
            copy.wait()
        for m in range(BATCH):
            total = own_v[f, m].astype(F32) + came_v[f, m].astype(F32) + second_v[f, m].astype(F32)
            if m < 2:
                in_v[f, m] = total
            else:
                out_v[f] = total.T
        for copy in stores(f):
            copy.start()
    for came, copy in zip(taken, given):
        came.wait()
        copy.start()
    for f in range(tiles):
        for copy in stores(f):
            copy.wait()
    for copy in given:
        copy.wait()


def tail(dw, head, first, second, small, gq, go, block, tokens, expert_count, heads, buckets):
    tile_count, _, deep, _ = dw.shape
    tiles = tile_count // BATCH
    groups, own, part = gq.shape
    width = tokens.shape[1]
    shape = jax.ShapeDtypeStruct
    vmem = pl.BlockSpec(memory_space=pltpu.VMEM)
    terms = pltpu.VMEM((tiles, BATCH, deep, TILE), BF16)
    sem = pltpu.SemaphoreType.DMA
    return pl.pallas_call(
        functools.partial(tail_kernel, heads, buckets),
        in_specs=[ANY] * 6 + [vmem] * 3,
        out_specs=[ANY] * 4 + [vmem] * 6,
        out_shape=[
            shape((2, deep, tiles * TILE), F32),
            shape((tiles * TILE, deep), F32),
            shape(block.shape, BF16),
            shape(tokens.shape, F32),
            shape((expert_count, width), F32),
            shape((1, width), F32),
            shape((1, width), F32),
            shape((heads, buckets), F32),
            shape((own, groups * part), F32),
            shape((own, width), F32),
        ],
        scratch_shapes=[
            terms,
            terms,
            terms,
            pltpu.VMEM((tiles, 2, deep, TILE), F32),
            pltpu.VMEM((tiles, TILE, deep), F32),
            pltpu.VMEM(block.shape, BF16),
            pltpu.VMEM(tokens.shape, F32),
            sem((tiles, 3)),
            sem((tiles, 2)),
            sem((4,)),
        ],
        compiler_params=pltpu.CompilerParams(vmem_limit_bytes=62 * 1024 * 1024),
        name="tail",
    )(dw, head, first, second, block, tokens, small, gq, go)


def shards(
    tokens,
    routes,
    rel_bucket,
    norm_gain1,
    w_qkv,
    w_out_proj,
    bias_table,
    norm_gain2,
    w_router,
    w_expert_in,
    w_expert_out,
    grad_out,
):
    row_count, model_width = tokens.shape
    bucket_count, head_count = bias_table.shape
    expert_count = lax.axis_size("expert")
    capacity = 10 * row_count // (4 * expert_count)
    slot_total = expert_count * capacity
    hidden_groups = 4

    bucket_ids = jnp.arange(bucket_count, dtype=jnp.int32)
    bucket_hot = jnp.concatenate(
        [bucket_ids[:, None] == rel_bucket[None, :], jnp.zeros((bucket_count, 1), bool)], axis=1
    ).astype(F32)
    table = jnp.dot(bias_table.T, bucket_hot, precision=HIGHEST)

    wq_full, out_full, qkv, probs, g_rows, mixed_t, normed1_t, residual, normed2_r, xs, gates, cols = front(
        tokens,
        norm_gain1[None],
        norm_gain2[None],
        table,
        routes.T,
        grad_out,
        w_router.T,
        w_qkv,
        w_out_proj,
        hidden_groups,
        capacity,
    )
    produced, grad_rows, grad_gates, grad_w, head = experts(
        xs, gates, g_rows, w_expert_in[0], w_expert_out[0], lax.axis_size("dp")
    )
    first, second, *rest = back(
        grad_w,
        head,
        produced,
        grad_rows,
        grad_gates,
        cols,
        routes.T,
        tokens,
        grad_out,
        residual,
        normed2_r,
        normed1_t,
        mixed_t,
        norm_gain1[None],
        norm_gain2[None],
        w_router.T,
        bucket_hot.astype(BF16),
        wq_full.reshape(hidden_groups, model_width, -1),
        out_full.reshape(model_width, model_width),
        qkv,
        probs,
    )
    (
        grad_in,
        grad_out_t,
        block_out,
        grad_tokens,
        grad_router,
        grad_norm1,
        grad_norm2,
        grad_bias,
        grad_qkv,
        grad_out_proj,
    ) = tail(grad_w, head, first, second, *rest, expert_count, head_count, bucket_count)
    grad_expert_in, grad_expert_out = grad_in[None], grad_out_t[None]
    grad_router_all, grad_bias = grad_router.T, grad_bias.T
    grad_norm1, grad_norm2 = grad_norm1[0], grad_norm2[0]
    return (
        block_out,
        grad_tokens,
        grad_norm1,
        grad_qkv,
        grad_out_proj,
        grad_bias,
        grad_norm2,
        grad_router_all,
        grad_expert_in,
        grad_expert_out,
    )


def solution(mesh):
    split = P(("dp", "expert"), None)
    in_specs = (
        split,
        split,
        P(),
        P(),
        split,
        split,
        P(),
        P(),
        P(),
        P("expert", None, None, None),
        P("expert", None, None),
        split,
    )
    out_specs = (
        split,
        split,
        P(),
        split,
        split,
        P(),
        P(),
        P(),
        P("expert", None, "dp", None),
        P("expert", None, "dp"),
    )
    return jax.shard_map(shards, mesh=mesh, in_specs=in_specs, out_specs=out_specs, check_vma=False)
```

```python
import functools

import jax
import jax.numpy as jnp
from jax import lax
from jax.experimental import pallas as pl
from jax.experimental.pallas import tpu as pltpu
from jax.sharding import PartitionSpec as P

LENGTH = 512
EPS = 1e-06
HIGHEST = lax.Precision.HIGHEST
F32 = jnp.float32
BF16 = jnp.bfloat16


def dot_nt(a, b):
    return lax.dot_general(a, b, (((1,), (1,)), ((), ())), preferred_element_type=F32)


def dot_nn(a, b):
    return jnp.dot(a, b, preferred_element_type=F32)


def iota(shape, axis):
    return lax.broadcasted_iota(jnp.int32, shape, axis)


def spread_bias(row):
    values = jnp.broadcast_to(row, (8, 1024))
    lift = 7 - iota((8, 1024), 0)
    for bit in (1, 2, 4):
        values = jnp.where((lift // bit) % 2 == 1, pltpu.roll(values, 1024 - bit, 1), values)
    return jnp.concatenate(
        [pltpu.roll(values, (904 + 8 * block) % 1024, 1) for block in range(16)], axis=0
    )


def fold_bias(parts):
    total = parts[0:8]
    total = pltpu.roll(total, 120, 1)
    for block in range(1, 16):
        piece = parts[8 * block : 8 * block + 8]
        total = total + (pltpu.roll(piece, 120 - 8 * block, 1) if block < 15 else piece)
    lift = 7 - iota((8, 1024), 0)
    for bit in (1, 2, 4):
        total = jnp.where((lift // bit) % 2 == 1, pltpu.roll(total, bit, 1), total)
    return jnp.sum(total, axis=0, keepdims=True)


MESH = pl.DeviceIdType.MESH
ANY = pl.BlockSpec(memory_space=pl.ANY)
GROUPS = 4
TILE = 256
WIDE = 512


def flip(index, mask):
    bit = 1
    while bit <= mask:
        if mask & bit:
            index = index + bit - 2 * bit * ((index // bit) % 2)
        bit *= 2
    return index


def remote(src, dst, send_sem, recv_sem, **axes):
    return pltpu.make_async_remote_copy(
        src_ref=src,
        dst_ref=dst,
        send_sem=send_sem,
        recv_sem=recv_sem,
        device_id=axes,
        device_id_type=MESH,
    )


def greet(partners):
    barrier = pltpu.get_barrier_semaphore()
    for axes in partners:
        pl.semaphore_signal(barrier, inc=1, device_id=axes, device_id_type=MESH)
    pl.semaphore_wait(barrier, len(partners))


def gelu_parts(x):
    root = 0.7978845608028654
    square = x * x
    t = jnp.tanh(root * x * (1.0 + 0.044715 * square))
    half = 0.5 * (1.0 + t)
    slope = half + 0.5 * x * (1.0 - t * t) * (root * (1.0 + 3 * 0.044715 * square))
    return x * half, slope


BATCH = 3
AHEAD = 4
CHIPS_FIRST_GROUPS = 1
CHIPS_FIRST = (*range(CHIPS_FIRST_GROUPS), 4)


def ways(dp, t):
    x, y = dp % 2, dp // 2
    x_peer, y_peer = dp + 1 - 2 * x, dp + 2 - 4 * y
    q = t % 2
    sent = [(1 - q) * (2 * i + 1 - x) + q * (2 * (1 - y) + i) for i in range(2)]
    keep = (1 - q) * y + q * x
    held = [(1 - q) * (2 * k + x) + q * (2 * y + k) for k in (keep, 1 - keep)]
    return sent, held, (1 - q) * x_peer + q * y_peer, (1 - q) * y_peer + q * x_peer, keep


def experts_kernel(
    xs_ref,
    gates_ref,
    g_ref,
    w_in_ref,
    w_out_ref,
    y_ref,
    dx_back_ref,
    dgates_back_ref,
    dw_ref,
    head_ref,
    w_in_v,
    w_out_v,
    x_v,
    gates_v,
    dgates_v,
    g_v,
    dy_v,
    hid_v,
    dgate_v,
    dup_v,
    y_v,
    dx_v,
    pre_v,
    stage,
    local_sem,
    stage_sem,
    x_send,
    x_recv,
    gates_send,
    gates_recv,
    dgates_send,
    dgates_recv,
    dx_send,
    dx_recv,
    y_sem,
    head_send,
    head_recv,
    weight_sem,
):
    expert_count, capacity, width = xs_ref.shape
    hidden = w_out_ref.shape[0]
    tiles = hidden // TILE
    size = expert_count // GROUPS
    rows = size * capacity
    me = lax.axis_index("expert")
    my_group, my_place = me // size, me % size

    def others(c):
        group = flip(my_group, c)
        return [group * size + (my_place + s) % size for s in range(1 if c == 0 else 0, size)]

    dp = lax.axis_index("dp")
    greet(
        [{"expert": (me + d) % expert_count} for d in range(1, expert_count)]
        + [{"dp": flip(dp, 1)}, {"dp": flip(dp, 2)}]
    )

    def send_rows(c):
        for peer in others(c):
            remote(
                xs_ref.at[peer], x_v.at[me], x_send.at[peer], x_recv.at[me], expert=peer
            ).start()
            remote(
                gates_ref.at[peer, 0:1],
                gates_v.at[me, 0:1],
                gates_send.at[peer],
                gates_recv.at[me],
                expert=peer,
            ).start()

    for c in (2, 1, 0):
        send_rows(c)
    def weights(f):
        cols = pl.ds(pl.multiple_of(f * TILE, TILE), TILE)
        return [
            pltpu.make_async_copy(
                w_in_ref.at[:, :, cols], w_in_v.at[:, :, cols], weight_sem.at[f, 0]
            ),
            pltpu.make_async_copy(w_out_ref.at[cols], w_out_v.at[cols], weight_sem.at[f, 1]),
        ]

    own = [
        pltpu.make_async_copy(xs_ref.at[me], x_v.at[me], local_sem.at[0]),
        pltpu.make_async_copy(gates_ref.at[me], gates_v.at[me], local_sem.at[1]),
        pltpu.make_async_copy(g_ref, g_v, local_sem.at[4]),
    ]
    for copy in own:
        copy.start()

    def fetch(f, carry):
        for copy in weights(f):
            copy.start()
        return carry

    lax.fori_loop(0, tiles, fetch, 0)
    for copy in own:
        copy.wait()

    def y_copy(c):
        span = pl.ds(flip(my_group, c) * size, size)
        return pltpu.make_async_copy(y_v.at[span], y_ref.at[span], y_sem.at[c])

    def back_copies(peer, at):
        return [
            remote(
                dx_v.at[peer], dx_back_ref.at[at], dx_send.at[peer], dx_recv.at[at], expert=peer
            ),
            remote(
                dgates_v.at[peer, 0:1],
                dgates_back_ref.at[at, 0:1],
                dgates_send.at[peer],
                dgates_recv.at[at],
                expert=peer,
            ),
        ]

    dgates_v[...] = jnp.zeros_like(dgates_v)
    for c in range(GROUPS):
        group = flip(my_group, c)
        span = pl.ds(group * size, size)
        for peer in others(c):
            remote(
                xs_ref.at[peer], x_v.at[peer], x_send.at[peer], x_recv.at[peer], expert=peer
            ).wait_recv()
            remote(
                gates_ref.at[peer, 0:1],
                gates_v.at[peer, 0:1],
                gates_send.at[peer],
                gates_recv.at[peer],
                expert=peer,
            ).wait_recv()
        for s in range(size):
            src = group * size + s
            gate_col = gates_v[src].T[0:capacity, 0:1]
            dy_v[src] = (g_v[src].astype(F32) * gate_col).astype(BF16)

        def before(f, slot, span=span, c=c):
            if c == 0:
                for copy in weights(f):
                    copy.wait()
            cols = pl.ds(pl.multiple_of(f * TILE, TILE), TILE)
            x = x_v[span].reshape(rows, width)
            pre_v[slot, 0] = dot_nn(x, w_in_v[0, :, cols])
            pre_v[slot, 1] = dot_nn(x, w_in_v[1, :, cols])
            pre_v[slot, 2] = dot_nt(dy_v[span].reshape(rows, width), w_out_v[cols, :])

        def after(f, slot, group=group):
            cols = pl.ds(pl.multiple_of(f * TILE, TILE), TILE)
            gate, up, dhid = pre_v[slot, 0], pre_v[slot, 1], pre_v[slot, 2]
            gelu, slope = gelu_parts(gate)
            hid_v[group, :, cols] = (gelu * up).astype(BF16)
            dgate_v[group, :, cols] = (dhid * up * slope).astype(BF16)
            dup_v[group, :, cols] = (dhid * gelu).astype(BF16)

        def two(h, carry):
            before(2 * h + 1, 1)
            after(2 * h, 0)
            before(2 * h + 2, 0)
            after(2 * h + 1, 1)
            return carry

        def backs(n, carry, group=group, span=span):
            cols = pl.ds(pl.multiple_of(n * WIDE, WIDE), WIDE)
            out = dot_nn(hid_v[group], w_out_v[:, cols])
            y_v[span, :, cols] = out.astype(BF16).reshape(size, capacity, WIDE)
            back = dot_nt(dgate_v[group], w_in_v[0, cols, :])
            back = back + dot_nt(dup_v[group], w_in_v[1, cols, :])
            dx_v[span, :, cols] = back.astype(BF16).reshape(size, capacity, WIDE)
            return carry

        assert tiles % 2 == 1
        before(0, 0)
        lax.fori_loop(0, tiles // 2, two, 0)
        after(tiles - 1, 0)
        lax.fori_loop(0, width // WIDE, backs, 0)
        if c == 0:
            send_rows(3)
        y_copy(c).start()
        for s in range(size):
            src = group * size + s
            product = g_v[src].astype(F32) * y_v[src].astype(F32)
            dgate = jnp.sum(product, axis=1, keepdims=True)
            dgates_v[src, :, 0:capacity] = jnp.broadcast_to(dgate, (capacity, 128)).T[0:8]
        for peer in others(c):
            for copy in back_copies(peer, me):
                copy.start()
    own = [
        pltpu.make_async_copy(dx_v.at[me], dx_back_ref.at[me], local_sem.at[0]),
        pltpu.make_async_copy(dgates_v.at[me], dgates_back_ref.at[me], local_sem.at[1]),
    ]
    for copy in own:
        copy.start()

    slots = expert_count * capacity
    w_in_v[0, :, 0:slots] = x_v[...].reshape(slots, width).T
    w_in_v[1, :, 0:slots] = dy_v[...].reshape(slots, width).T

    def put(f, m):
        return pltpu.make_async_copy(stage.at[m], dw_ref.at[BATCH * f + m], stage_sem.at[m])

    def head_copy(f, m, i):
        t = BATCH * f + m
        sent, _, peer, _, keep = ways(dp, t)
        return remote(
            dw_ref.at[t, sent[i]], head_ref.at[t, (i + keep) % 2], head_send.at[t, i], head_recv.at[t, i], dp=peer
        )

    parts, deep = stage.shape[1:3]

    def grads(f, carry):
        cols = pl.ds(pl.multiple_of(f * TILE, TILE), TILE)
        for m, (side, right) in enumerate(((0, dgate_v), (0, dup_v), (1, hid_v))):

            @pl.when(f > 0)
            def _():
                put(f - 1, m).wait()

            @pl.when((f > 0) & (f <= AHEAD))
            def _():
                for i in range(2):
                    head_copy(f - 1, m, i).start()

            across = right[:, :, cols].reshape(slots, TILE)
            for r in range(0, parts, 2):
                span = slice(r * deep, (r + 2) * deep)
                block = dot_nn(w_in_v[side, span, 0:slots], across)
                stage[m, r : r + 2] = block.astype(BF16).reshape(2, deep, TILE)
            put(f, m).start()
        return carry

    lax.fori_loop(0, tiles, grads, 0)
    for m in range(BATCH):
        put(tiles - 1, m).wait()

    def heads(t, carry):
        for i in range(2):
            head_copy(t // BATCH, t % BATCH, i).wait()
        return carry

    lax.fori_loop(0, BATCH * AHEAD, heads, 0)
    for copy in own:
        copy.wait()
    for c in range(GROUPS):
        for peer in others(c):
            remote(
                xs_ref.at[peer], x_v.at[me], x_send.at[peer], x_recv.at[me], expert=peer
            ).wait_send()
            remote(
                gates_ref.at[peer, 0:1],
                gates_v.at[me, 0:1],
                gates_send.at[peer],
                gates_recv.at[me],
                expert=peer,
            ).wait_send()
            for copy in back_copies(peer, me):
                copy.wait_send()
            for copy in back_copies(peer, peer):
                copy.wait_recv()
        y_copy(c).wait()


def experts(xs, gates, g, w_in, w_out, dp_count):
    expert_count, capacity, width = xs.shape
    hidden = w_out.shape[0]
    size = expert_count // GROUPS
    tiles = hidden // TILE
    rows = size * capacity
    slots = jax.ShapeDtypeStruct(xs.shape, BF16)
    parts = (dp_count, width // dp_count, TILE)
    peers = pltpu.SemaphoreType.DMA((expert_count,))
    return pl.pallas_call(
        experts_kernel,
        in_specs=[ANY] * 5,
        out_specs=[ANY] * 5,
        out_shape=[slots, slots, jax.ShapeDtypeStruct(gates.shape, F32), jax.ShapeDtypeStruct((BATCH * tiles, *parts), BF16),
            jax.ShapeDtypeStruct((BATCH * AHEAD, 2, *parts[1:]), BF16),
        ],
        scratch_shapes=[
            pltpu.VMEM(w_in.shape, BF16),
            pltpu.VMEM(w_out.shape, BF16),
            pltpu.VMEM(xs.shape, BF16),
            pltpu.VMEM(gates.shape, F32),
            pltpu.VMEM(gates.shape, F32),
            pltpu.VMEM(xs.shape, BF16),
            pltpu.VMEM(xs.shape, BF16),
            pltpu.VMEM((GROUPS, rows, hidden), BF16),
            pltpu.VMEM((GROUPS, rows, hidden), BF16),
            pltpu.VMEM((GROUPS, rows, hidden), BF16),
            pltpu.VMEM(xs.shape, BF16),
            pltpu.VMEM(xs.shape, BF16),
            pltpu.VMEM((2, 3, rows, TILE), F32),
            pltpu.VMEM((BATCH, *parts), BF16),
            pltpu.SemaphoreType.DMA((5,)),
            pltpu.SemaphoreType.DMA((3,)),
        ]
        + [peers] * 8
        + [pltpu.SemaphoreType.DMA((GROUPS,))]
        + [pltpu.SemaphoreType.DMA((BATCH * AHEAD, 2))] * 2
        + [pltpu.SemaphoreType.DMA((tiles, 2))],
        compiler_params=pltpu.CompilerParams(
            collective_id=1, has_side_effects=True, vmem_limit_bytes=61 * 1024 * 1024
        ),
        name="experts",
    )(xs, gates, g, w_in, w_out)


def column(values, k):
    return values[:, k : k + 1]


def route_column(routes_ref, k):
    row = routes_ref[k : k + 1, :].astype(F32)
    return jnp.broadcast_to(row, (128, row.shape[1])).T


def attend_pair(j, a, qkv_v, table_ref, p_ref):
    def lanes(part):
        return pl.ds(pl.multiple_of(256 * part + 128 * a, 128), 128)

    query = qkv_v[j, :, lanes(0)] * jnp.asarray(0.125, BF16)
    values_t = qkv_v[j, :, lanes(2)].T
    half = iota((512, 128), 1) // 64
    halves = []
    for t in range(2):
        shifted = spread_bias(table_ref[pl.ds(4 * j + 2 * a + t, 1), :])
        query_t = jnp.where(half == t, query, jnp.zeros_like(query))
        scores = [
            dot_nt(qkv_v[j, 128 * c : 128 * c + 128, lanes(1)], query_t)
            + shifted[:, 384 - 128 * c : 896 - 128 * c]
            for c in range(4)
        ]
        top = functools.reduce(jnp.maximum, [jnp.max(s, axis=0, keepdims=True) for s in scores])
        exps = [jnp.exp(s - top) for s in scores]
        total = functools.reduce(jnp.add, [jnp.sum(e, axis=0, keepdims=True) for e in exps])
        inverse = 1.0 / total
        for c in range(4):
            p_ref[t, 128 * c : 128 * c + 128, :] = (exps[c] * inverse).astype(BF16)
        halves.append(dot_nn(values_t, p_ref[t]))
    return jnp.where(iota((128, 512), 0) < 64, halves[0], halves[1])


def front_kernel(
    tokens_ref,
    gain1_ref,
    gain2_ref,
    table_ref,
    routes_ref,
    grad_ref,
    router_ref,
    w_qkv_ref,
    wo_ref,
    wq_out,
    wo_out,
    qkv_out,
    p_out,
    g_back,
    mixed_t_hbm,
    normed_t_hbm,
    resid_hbm,
    normed2_hbm,
    xs_hbm,
    gates_ref,
    cols_ref,
    ws_ref,
    wq_v,
    wo_v,
    qkv_v,
    p_v,
    mixed_v,
    normed_v,
    hot_v,
    g_v,
    own_sem,
    z_send,
    z_recv,
    xy_send,
    xy_recv,
    core_send,
    core_recv,
    g_send,
    g_recv,
    out_sem,
    p_sem,
    mixed_t_ref,
    normed_t_ref,
    resid_ref,
    normed2_ref,
    xs_ref,
    stores_sem,
):
    stores = {
        name: pltpu.make_async_copy(src, dst, stores_sem.at[n])
        for n, (name, src, dst) in enumerate(
            (
                ("mixed_t", mixed_t_ref, mixed_t_hbm),
                ("normed_t", normed_t_ref, normed_t_hbm),
                ("resid", resid_ref, resid_hbm),
                ("normed2", normed2_ref, normed2_hbm),
                ("xs", xs_ref, xs_hbm),
            )
        )
    }
    expert_count, capacity, width = xs_ref.shape
    lane_count = gates_ref.shape[2]
    slots = expert_count * capacity
    size = expert_count // GROUPS
    chips = expert_count // 2
    me, dp = lax.axis_index("expert"), lax.axis_index("dp")
    core, chip = me % 2, me // 2
    x, y = dp % 2, dp // 2
    core_peer = me + 1 - 2 * core
    x_peer, y_peer = dp + 1 - 2 * x, dp + 2 - 4 * y
    my_group, my_place = me // size, me % size
    chip_peers = [(chip + d) % chips for d in range(1, chips)]
    greet(
        [{"expert": (me + d) % expert_count} for d in range(1, expert_count)]
        + [{"dp": x_peer}, {"dp": y_peer}]
    )

    groups = ws_ref.shape[0]
    count = groups + 1
    srcs = [ws_ref.at[j] for j in range(groups)] + [wo_ref]
    bufs = [wq_v.at[j] for j in range(groups)] + [wo_v]
    widths = [ws_ref.shape[2]] * groups + [wo_ref.shape[1]]
    places = ((y, x), (y, 1 - x), (1 - y, x), (1 - y, 1 - x))

    def z_copy(j, peer, at):
        return remote(
            srcs[j], bufs[j].at[y, x, at, core], z_send.at[j, peer], z_recv.at[j, at], expert=peer * 2 + core
        )

    def own_copy(j):
        return pltpu.make_async_copy(srcs[j], bufs[j].at[y, x, chip, core], own_sem.at[j])

    def xy_copy(j, k):
        half = widths[j] // 2
        src = (
            bufs[j].at[y, x, :, core],
            bufs[j].at[y, x, :, core],
            bufs[j].at[1 - y, x, :, core, :, half : 2 * half],
            bufs[j].at[y, 1 - x, :, core, :, 0:half],
        )[k]
        return remote(src, src, xy_send.at[j, k], xy_recv.at[j, k], dp=(x_peer, y_peer)[k % 2])

    def core_copy(j, k):
        src = bufs[j].at[places[k][0], places[k][1], :, core]
        return remote(src, src, core_send.at[j, k], core_recv.at[j, k], expert=core_peer)

    line = chips == 4
    pair = chip // 2
    mate = chip + 1 - 2 * (chip % 2)
    middle = (chip % 4) * (3 - chip % 4) // 2

    def pair_copy(j, k, at, peer):
        span = bufs[j].at[y, x, pl.ds(2 * at, 2), core]
        return remote(span, span, z_send.at[j, k], z_recv.at[j, k], expert=peer * 2 + core)

    def spread_first(j):
        own_copy(j).wait()
        if line:
            z_copy(j, mate, mate).wait_recv()

            @pl.when(middle == 1)
            def _():
                pair_copy(j, 4, pair, 3 - chip).start()

    def spread_second(j):
        if line:

            @pl.when(middle == 1)
            def _():
                pair_copy(j, 4, 1 - pair, 3 - chip).wait_recv()
                pair_copy(j, 5, 1 - pair, mate).start()

    def spread(j):
        if line:

            @pl.when(middle == 0)
            def _():
                pair_copy(j, 5, 1 - pair, mate).wait_recv()
        else:
            for peer in chip_peers:
                z_copy(j, peer, peer).wait_recv()
        for k in range(2):
            xy_copy(j, k).start()
        core_copy(j, 0).start()

    def forward(j):
        for k in range(2):
            xy_copy(j, k).wait_recv()
            xy_copy(j, 3 - k).start()
            core_copy(j, 1 + k).start()

    def complete(j):
        for k in (2, 3):
            xy_copy(j, k).wait_recv()
        core_copy(j, 3).start()

    def out_copy(j):
        src, dst = (wq_v.at[j], wq_out.at[j]) if j < groups else (wo_v, wo_out)
        return pltpu.make_async_copy(src, dst, out_sem.at[j])

    def gathered(j):
        for k in range(4):
            core_copy(j, k).wait_recv()
        out_copy(j).start()

    third = ws_ref.shape[2] // 3
    for j in range(count):
        if j < groups:
            for k in range(3):
                at = (k * groups + j) * third
                ws_ref[j, :, k * third : (k + 1) * third] = w_qkv_ref[:, at : at + third]
        own_copy(j).start()
        for peer in [mate] if line else chip_peers:
            z_copy(j, peer, chip).start()

    inputs = tokens_ref[...].astype(F32)
    inv_rms = lax.rsqrt(jnp.mean(inputs * inputs, axis=1, keepdims=True) + EPS)
    normed = (inputs * inv_rms * gain1_ref[...]).astype(BF16)
    normed_v[...] = normed
    normed_t_ref[...] = normed.T
    stores["normed_t"].start()
    spread_first(0)
    spread_first(1)
    spread_second(0)
    spread_first(2)
    spread_second(1)
    spread(0)
    spread_first(3)
    spread_second(2)
    spread(1)
    spread_first(4)
    spread_second(3)

    rows = routes_ref.shape[1]
    lane = iota((rows, 128), 1)
    routes = [route_column(routes_ref, k) for k in range(2)]
    hots = [lane == routes[k].astype(jnp.int32) for k in range(2)]
    earlier = (iota((rows, rows), 0) > iota((rows, rows), 1)).astype(BF16)
    ones = [jnp.where(h, 1.0, 0.0) for h in hots]
    counts = [dot_nn(earlier, o.astype(BF16)) for o in ones]
    counts[1] = counts[1] + jnp.sum(ones[0], axis=0, keepdims=True)
    slot = []
    for k in range(2):
        place = jnp.sum(counts[k] * ones[k], axis=1, keepdims=True)
        at = column(routes[k], 0) * capacity + place
        slot.append(jnp.where(place < capacity, at, float(slots)))
    slot_rows = jnp.where(lane == 0, slot[0], slot[1]).T
    slot_ids = iota((slots, rows), 0).astype(F32)
    hot = (slot_ids == slot_rows[0:1]) | (slot_ids == slot_rows[1:2])
    hot_v[...] = jnp.where(hot, 1.0, 0.0).astype(BF16)
    g_v[...] = dot_nn(hot_v[...], grad_ref[...]).astype(BF16).reshape(g_v.shape)

    def g_copy(peer, at):
        return remote(g_v.at[peer], g_back.at[at], g_send.at[peer], g_recv.at[at], expert=peer)

    def others(c):
        group = flip(my_group, c)
        return [group * size + (my_place + s) % size for s in range(1 if c == 0 else 0, size)]

    peers = [peer for c in (2, 3, 1, 0) for peer in others(c)]
    g_own = pltpu.make_async_copy(g_v.at[me], g_back.at[me], own_sem.at[count])
    g_own.start()

    def p_copy(j, a):
        return pltpu.make_async_copy(p_v.at[a], p_out.at[pl.ds(4 * j + 2 * a, 2)], p_sem.at[a])

    def group(j):
        gathered(j)
        qkv_v[j] = dot_nn(normed_v[...], wq_v[j].reshape(width, widths[j])).astype(BF16)

        def pair(a, carry):
            if j > 0:
                p_copy(j - 1, a).wait()
            mixed = attend_pair(j, a, qkv_v, table_ref, p_v.at[a])
            p_copy(j, a).start()
            span = pl.ds(pl.multiple_of(256 * j + 128 * a, 128), 128)
            mixed_t_ref[span, :] = mixed.astype(BF16)
            mixed_v[:, span] = mixed.T.astype(BF16)
            return carry

        lax.fori_loop(0, 2, pair, 0)

    spread(2)
    spread_second(4)
    forward(0)
    spread(3)
    spread(4)
    for peer in peers:
        g_copy(peer, me).start()
    forward(1)
    complete(0)
    forward(2)
    complete(1)
    group(0)
    forward(3)
    complete(2)
    group(1)
    forward(4)
    complete(3)
    group(2)
    complete(4)
    group(3)
    qkv_copy = pltpu.make_async_copy(qkv_v, qkv_out, own_sem.at[count + 1])
    qkv_copy.start()
    stores["mixed_t"].start()
    gathered(groups)

    resid = tokens_ref[...].astype(F32) + dot_nn(mixed_v[...], wo_v[...].reshape(width, width))
    resid_ref[...] = resid
    stores["resid"].start()
    inv_rms2 = lax.rsqrt(jnp.mean(resid * resid, axis=1, keepdims=True) + EPS)
    normed2 = (resid * inv_rms2 * gain2_ref[...]).astype(BF16)
    normed2_ref[...] = normed2
    stores["normed2"].start()
    xs_ref[...] = dot_nn(hot_v[...], normed2).astype(BF16).reshape(xs_ref.shape)
    stores["xs"].start()
    rest = router_ref[...]
    logits = jnp.zeros((rows, expert_count), F32)
    for _ in range(3):
        piece = rest.astype(BF16)
        rest = rest - piece.astype(F32)
        logits = logits + dot_nt(normed2, piece)
    ids = iota((rows, expert_count), 1)
    chosen = [
        jnp.sum(
            jnp.where(ids == column(routes[k], 0).astype(jnp.int32), logits, 0.0),
            axis=1,
            keepdims=True,
        )
        for k in range(2)
    ]
    top = jnp.maximum(chosen[0], chosen[1])
    exps = [jnp.exp(c - top) for c in chosen]
    gates = [e / (exps[0] + exps[1]) for e in exps]
    cols = jnp.where(lane == 2, gates[0], jnp.where(lane == 3, gates[1], 0.0))
    cols_ref[...] = jnp.where(lane == 0, slot[0], jnp.where(lane == 1, slot[1], cols))
    wide = iota((rows, lane_count), 1)

    def gate_row(e, carry):
        base = (e * capacity).astype(F32)
        total = jnp.zeros((rows, lane_count), F32)
        for k in range(2):
            here = (wide.astype(F32) == slot[k] - base) & (wide < capacity)
            total = total + jnp.where(here, gates[k], 0.0)
        row = jnp.sum(total, axis=0, keepdims=True)
        gates_ref[pl.ds(e, 1)] = jnp.broadcast_to(row, (8, lane_count))[None]
        return carry

    lax.fori_loop(0, expert_count, gate_row, 0)

    for a in range(2):
        p_copy(groups - 1, a).wait()
    qkv_copy.wait()
    for copy in stores.values():
        copy.wait()
    g_own.wait()
    for j in range(count):
        out_copy(j).wait()
        for peer in [mate] if line else chip_peers:
            z_copy(j, peer, chip).wait_send()
        if line:

            @pl.when(middle == 1)
            def _():
                pair_copy(j, 4, pair, 3 - chip).wait_send()
                pair_copy(j, 5, 1 - pair, mate).wait_send()

        for k in range(4):
            xy_copy(j, k).wait_send()
            core_copy(j, k).wait_send()
    for peer in peers:
        g_copy(peer, me).wait_send()
        g_copy(peer, peer).wait_recv()


def front(tokens, gain1, gain2, table, routes, grad_out, router, w_qkv, wo, groups, capacity):
    rows, width = tokens.shape
    expert_count = router.shape[0]
    chips = expert_count // 2
    own, part = w_qkv.shape[0], w_qkv.shape[1] // groups
    heads = table.shape[0]
    lane_count = -(-capacity // 128) * 128
    vmem = pl.BlockSpec(memory_space=pltpu.VMEM)
    sem = pltpu.SemaphoreType.DMA
    shape = jax.ShapeDtypeStruct
    slots = (expert_count, capacity, width)
    spread = (2, 2, chips, 2, own)
    return pl.pallas_call(
        front_kernel,
        in_specs=[vmem] * 9,
        out_specs=[ANY] * 10 + [vmem] * 2,
        out_shape=[
            shape((groups, *spread, part), BF16),
            shape((*spread, width), BF16),
            shape((groups, rows, part), BF16),
            shape((heads, rows, rows), BF16),
            shape(slots, BF16),
            shape((width, rows), BF16),
            shape((width, rows), BF16),
            shape((rows, width), F32),
            shape((rows, width), BF16),
            shape(slots, BF16),
            shape((expert_count, 8, lane_count), F32),
            shape((rows, 128), F32),
        ],
        scratch_shapes=[
            pltpu.VMEM((groups, own, part), BF16),
            pltpu.VMEM((groups, *spread, part), BF16),
            pltpu.VMEM((*spread, width), BF16),
            pltpu.VMEM((groups, rows, part), BF16),
            pltpu.VMEM((2, 2, rows, rows), BF16),
            pltpu.VMEM((rows, width), BF16),
            pltpu.VMEM((rows, width), BF16),
            pltpu.VMEM((expert_count * capacity, rows), BF16),
            pltpu.VMEM(slots, BF16),
            sem((groups + 3,)),
            sem((groups + 1, max(chips, 6))),
            sem((groups + 1, max(chips, 6))),
            sem((groups + 1, 4)),
            sem((groups + 1, 4)),
            sem((groups + 1, 4)),
            sem((groups + 1, 4)),
            sem((expert_count,)),
            sem((expert_count,)),
            sem((groups + 1,)),
            sem((2,)),
            pltpu.VMEM((width, rows), BF16),
            pltpu.VMEM((width, rows), BF16),
            pltpu.VMEM((rows, width), F32),
            pltpu.VMEM((rows, width), BF16),
            pltpu.VMEM(slots, BF16),
            sem((5,)),
        ],
        compiler_params=pltpu.CompilerParams(
            collective_id=3, has_side_effects=True, vmem_limit_bytes=60 * 1024 * 1024
        ),
        name="front",
    )(tokens, gain1, gain2, table, routes, grad_out, router, w_qkv, wo)


def attend_back_pair(j, a, qkv_v, p_ref, grads_v, dqkv_v, fold_ref):
    def lanes(part):
        return pl.ds(pl.multiple_of(256 * part + 128 * a, 128), 128)

    query = qkv_v[j, :, lanes(0)] * jnp.asarray(0.125, BF16)
    keys_t = qkv_v[j, :, lanes(1)].T
    values = qkv_v[j, :, lanes(2)]
    grads = grads_v[:, pl.ds(pl.multiple_of(256 * j + 128 * a, 128), 128)]
    half = iota((512, 128), 1) // 64
    dq_halves, dk_halves, dv_halves = [], [], []
    for t in range(2):
        values_t = jnp.where(half == t, values, jnp.zeros_like(values))
        probs = [p_ref[t, 128 * c : 128 * c + 128, :].astype(F32) for c in range(4)]
        grad_probs = [dot_nt(values_t[128 * c : 128 * c + 128], grads) for c in range(4)]
        delta = functools.reduce(
            jnp.add,
            [jnp.sum(p * g, axis=0, keepdims=True) for p, g in zip(probs, grad_probs)],
        )
        scores = [(p * (g - delta)).astype(BF16) for p, g in zip(probs, grad_probs)]
        padded = [
            jnp.concatenate(
                ([jnp.zeros((128, 384 - 128 * c), F32)] if c < 3 else [])
                + [scores[c].astype(F32), jnp.zeros((128, 128 + 128 * c), F32)],
                axis=1,
            )
            for c in range(4)
        ]
        fold_ref[pl.ds(4 * j + 2 * a + t, 1), :] = fold_bias(functools.reduce(jnp.add, padded))
        grad_scores = jnp.concatenate(scores, axis=0)
        dv_halves.append(dot_nn(p_ref[t], grads))
        dk_halves.append(dot_nn(grad_scores, query))
        dq_halves.append(dot_nn(keys_t, grad_scores))
    dq = jnp.where(iota((128, 512), 0) < 64, dq_halves[0], dq_halves[1]) * 0.125
    dqkv_v[:, lanes(0)] = dq.T.astype(BF16)
    dqkv_v[:, lanes(1)] = jnp.where(half == 0, dk_halves[0], dk_halves[1]).astype(BF16)
    dqkv_v[:, lanes(2)] = jnp.where(half == 0, dv_halves[0], dv_halves[1]).astype(BF16)


def dot_exact(a, b, dot=dot_nn):
    total = None
    for _ in range(3):
        piece = a.astype(BF16)
        a = a - piece.astype(F32)
        term = dot(piece, b)
        total = term if total is None else total + term
    return total


def dot_f32(a, b):
    total = None
    for _ in range(3):
        piece = b.astype(BF16)
        b = b - piece.astype(F32)
        term = dot_exact(a, piece)
        total = term if total is None else total + term
    return total


def back_kernel(
    dw_ref,
    head_ref,
    ys_ref,
    dx_hbm,
    dgates_hbm,
    cols_ref,
    routes_ref,
    tokens_hbm,
    grad_hbm,
    resid_hbm,
    normed2_hbm,
    normed_t_hbm,
    mixed_t_hbm,
    gain1_ref,
    gain2_ref,
    router_t_ref,
    bucket_hot_ref,
    wq_ref,
    wo_hbm,
    qkv_ref,
    p_ref,
    first_ref,
    second_ref,
    small_out_ref,
    gq_out_ref,
    go_out_ref,
    block_hbm,
    grad_tokens_hbm,
    y_v,
    grads_q,
    grads_o,
    core_q,
    core_o,
    step1_q,
    step1_o,
    step2_q,
    step2_o,
    last_q,
    last_o,
    rows_q,
    rows_o,
    sum_q,
    sum_o,
    qkv_v,
    p_v,
    wq_v,
    dqkv_v,
    dmix_v,
    dn1_v,
    fold_v,
    small_v,
    own_v,
    first_v,
    pass_v,
    y_send,
    y_recv,
    first_send,
    first_recv,
    second_send,
    second_recv,
    ring_sem,
    small_send,
    small_recv,
    core_send,
    core_recv,
    step1_send,
    step1_recv,
    step2_send,
    step2_recv,
    last_send,
    last_recv,
    local_sem,
    p_sem,
    wq_sem,
    dx_ref,
    dgates_ref,
    tokens_ref,
    resid_ref,
    normed2_ref,
    normed_t_ref,
    mixed_t_ref,
    wo_ref,
    grad_ref,
    input_sem,
    block_sem,
    block_ref,
    grad_tokens_ref,
):
    loads = {
        name: pltpu.make_async_copy(src, dst, input_sem.at[n])
        for n, (name, src, dst) in enumerate(
            (
                ("dx", dx_hbm, dx_ref),
                ("dgates", dgates_hbm, dgates_ref),
                ("tokens", tokens_hbm, tokens_ref),
                ("resid", resid_hbm, resid_ref),
                ("normed2", normed2_hbm, normed2_ref),
                ("normed_t", normed_t_hbm, normed_t_ref),
                ("mixed_t", mixed_t_hbm, mixed_t_ref),
                ("wo", wo_hbm, wo_ref),
                ("grad", grad_hbm, grad_ref),
            )
        )
    }
    for copy in loads.values():
        copy.start()
    expert_count, capacity, width = ys_ref.shape
    slots = expert_count * capacity
    rows = tokens_ref.shape[0]
    chips = expert_count // 2
    size = expert_count // GROUPS
    me, dp = lax.axis_index("expert"), lax.axis_index("dp")
    core, chip = me % 2, me // 2
    x, y = dp % 2, dp // 2
    core_peer = me + 1 - 2 * core
    x_peer, y_peer = dp + 1 - 2 * x, dp + 2 - 4 * y
    my_group, my_place = me // size, me % size
    chip_peers = [(chip + d) % chips for d in range(1, chips)]
    greet(
        [{"expert": (me + d) % expert_count} for d in range(1, expert_count)]
        + [{"dp": x_peer}, {"dp": y_peer}]
    )

    tile_count = dw_ref.shape[0]
    batches = tile_count // BATCH

    def first_copy(t, i):
        sent, _, peer, _, keep = ways(dp, t)
        return remote(
            dw_ref.at[t, sent[i]],
            first_ref.at[t - BATCH * AHEAD, (i + keep) % 2],
            first_send.at[t - BATCH * AHEAD, i],
            first_recv.at[t - BATCH * AHEAD, i],
            dp=peer,
        )

    def second_copy(t, n):
        peer = ways(dp, t)[3]
        return remote(
            pass_v.at[n % 2, t % BATCH], second_ref.at[t], second_send.at[t], second_recv.at[t], dp=peer
        )

    def relay_loads(t, b):
        held = ways(dp, t)[1]
        q = t % BATCH
        came = head_ref.at[t, 1] if b < AHEAD else first_ref.at[t - BATCH * AHEAD, 1]
        return [
            pltpu.make_async_copy(dw_ref.at[t, held[1]], own_v.at[b % 2, q], ring_sem.at[b % 2, q, 0]),
            pltpu.make_async_copy(came, first_v.at[b % 2, q], ring_sem.at[b % 2, q, 1]),
        ]

    def over(b, body):
        def step(t, carry):
            body(t)
            return carry

        lax.fori_loop(BATCH * b, BATCH * b + BATCH, step, 0)

    def issue(b):
        def body(t):
            for i in range(2):
                first_copy(t, i).start()

        over(b, body)

    def relay_begin(b):
        def body(t):
            if b >= AHEAD:
                for i in range(2):
                    first_copy(t, i).wait_recv()
            for load in relay_loads(t, b):
                load.start()

        over(b, body)

    def relay_end(b):
        def body(t):
            for load in relay_loads(t, b):
                load.wait()
            if b >= 2:
                second_copy(t - 2 * BATCH, b).wait_send()
            q = t % BATCH
            pass_v[b % 2, q] = (
                own_v[b % 2, q].astype(F32) + first_v[b % 2, q].astype(F32)
            ).astype(BF16)
            second_copy(t, b).start()

        over(b, body)

    groups = grads_q.shape[0]
    count = groups + 1

    def pick(many, one, p):
        return many.at[p] if p < groups else one

    grads = [pick(grads_q, grads_o, p) for p in range(count)]
    cores = [pick(core_q, core_o, p) for p in range(count)]
    step1 = [pick(step1_q, step1_o, p) for p in range(count)]
    step2 = [pick(step2_q, step2_o, p) for p in range(count)]
    lasts = [pick(last_q, last_o, p) for p in range(count)]
    outs = [pick(gq_out_ref, go_out_ref, p) for p in range(count)]
    widths = [grads_q.shape[-1]] * groups + [grads_o.shape[-1]]

    def part_core(p):
        return remote(
            grads[p].at[:, :, :, 1 - core], cores[p], core_send.at[p], core_recv.at[p], expert=core_peer
        )

    def part_step1(p, b):
        half = widths[p] // 2
        src = (
            grads[p].at[:, 1 - x, :, core, :, 0:half]
            if b == 0
            else grads[p].at[1 - y, :, :, core, :, half : 2 * half]
        )
        return remote(
            src, step1[p].at[b], step1_send.at[p, b], step1_recv.at[p, b], dp=(x_peer, y_peer)[b]
        )

    def part_step2(p, b):
        src = step1[p].at[b, (1 - y, 1 - x)[b]]
        return remote(
            src, step2[p].at[b], step2_send.at[p, b], step2_recv.at[p, b], dp=(y_peer, x_peer)[b]
        )

    def part_last(p, peer, at):
        return remote(
            cores[p].at[0, 0, peer], lasts[p].at[at], last_send.at[p, peer], last_recv.at[p, at],
            expert=peer * 2 + core,
        )

    arrivals = {p: rows_o if p == groups else rows_q.at[p] for p in CHIPS_FIRST}
    sums = {p: sum_o if p == groups else sum_q.at[p] for p in CHIPS_FIRST}

    def chip_rows(p, peer, at):
        return remote(
            grads[p].at[:, :, peer, core], arrivals[p].at[at], last_send.at[p, peer], last_recv.at[p, at],
            expert=peer * 2 + core,
        )

    def chip_step1(p, b):
        half = widths[p] // 2
        src = (
            sums[p].at[:, 1 - x, :, 0:half] if b == 0 else sums[p].at[1 - y, :, :, half : 2 * half]
        )
        return remote(
            src, step1[p].at[b, :, 0], step1_send.at[p, b], step1_recv.at[p, b], dp=(x_peer, y_peer)[b]
        )

    def chip_step2(p, b):
        src = step1[p].at[b, (1 - y, 1 - x)[b], 0]
        return remote(
            src, step2[p].at[b, 0], step2_send.at[p, b], step2_recv.at[p, b], dp=(y_peer, x_peer)[b]
        )

    def chip_held(p, b, i):
        half = widths[p] // 2
        held = sums[p][i, x, :, 0:half] if b == 0 else sums[p][y, i, :, half : 2 * half]
        return held.astype(F32) + step1[p][b, i, 0].astype(F32)

    def part_a(p):
        part_core(p).start()

    def part_b(p):
        part_core(p).wait()
        total = grads[p][:, :, :, core].astype(F32) + cores[p][...].astype(F32)
        grads[p][:, :, :, core] = total.astype(BF16)
        if p in CHIPS_FIRST:
            for peer in chip_peers:
                chip_rows(p, peer, chip).start()
            return
        for b in range(2):
            part_step1(p, b).start()

    def part_c(p):
        half = widths[p] // 2
        if p in CHIPS_FIRST:
            total = grads[p][:, :, chip, core].astype(F32)
            for peer in chip_peers:
                chip_rows(p, peer, peer).wait_recv()
                total = total + arrivals[p][peer].astype(F32)
            sums[p][...] = total.astype(BF16)
            for b in range(2):
                chip_step1(p, b).start()
            return
        for b in range(2):
            part_step1(p, b).wait()
            for i in range(2):
                held = (
                    grads[p][i, x, :, core, :, 0:half]
                    if b == 0
                    else grads[p][y, i, :, core, :, half : 2 * half]
                )
                total = held.astype(F32) + step1[p][b, i].astype(F32)
                step1[p][b, i] = total.astype(BF16)
            part_step2(p, b).start()

    def part_d(p):
        half = widths[p] // 2
        if p in CHIPS_FIRST:
            for b in range(2):
                chip_step1(p, b).wait()
                give = (1 - y, 1 - x)[b]
                step1[p][b, give, 0] = chip_held(p, b, give).astype(BF16)
                chip_step2(p, b).start()
            return
        for b in range(2):
            part_step2(p, b).wait()
            total = step1[p][b, (y, x)[b]].astype(F32) + step2[p][b].astype(F32)
            cores[p][0, 0, :, :, b * half : b * half + half] = total.astype(BF16)
        for peer in chip_peers:
            part_last(p, peer, chip).start()

    def part_e(p):
        half = widths[p] // 2
        if p in CHIPS_FIRST:
            for b in range(2):
                chip_step2(p, b).wait()
                total = chip_held(p, b, (y, x)[b]) + step2[p][b, 0].astype(F32)
                outs[p][:, b * half : b * half + half] = total
            for peer in chip_peers:
                chip_rows(p, peer, chip).wait_send()
            return
        total = cores[p][0, 0, chip].astype(F32)
        for peer in chip_peers:
            part_last(p, peer, peer).wait_recv()
            total = total + lasts[p][peer].astype(F32)
        outs[p][...] = total
        for peer in chip_peers:
            part_last(p, peer, chip).wait_send()

    partners = []
    bit = 1
    while bit < expert_count:
        partners.append({"expert": flip(me, bit)})
        bit *= 2
    partners += [{"dp": x_peer}, {"dp": y_peer}]
    stages = len(partners)

    def small_copy(s):
        return remote(
            small_v.at[0], small_v.at[1 + s], small_send.at[s], small_recv.at[s], **partners[s]
        )

    def small_next(s):
        small_copy(s).wait()
        small_v[0] = small_v[0] + small_v[1 + s]
        if s + 1 < stages:
            small_copy(s + 1).start()

    def y_copy(peer, at):
        return remote(ys_ref.at[peer], y_v.at[at], y_send.at[peer], y_recv.at[at], expert=peer)

    def others(c):
        group = flip(my_group, c)
        return [group * size + (my_place + s) % size for s in range(1 if c == 0 else 0, size)]

    peers = [peer for c in (2, 3, 1, 0) for peer in others(c)]

    def p_copy(j, a):
        return pltpu.make_async_copy(p_ref.at[pl.ds(4 * j + 2 * a, 2)], p_v.at[a], p_sem.at[a])

    def wq_copy(j):
        return pltpu.make_async_copy(wq_ref.at[j], wq_v.at[j % 2], wq_sem.at[j % 2])

    lane = iota((rows, 128), 1)
    slot = [column(cols_ref[...], k) for k in range(2)]
    gates = [column(cols_ref[...], 2 + k) for k in range(2)]

    def hots():
        at = iota((rows, slots), 1).astype(F32)
        return [at == s for s in slot]

    def dense():
        lanes = dgates_ref.shape[2]
        wide = iota((rows, lanes), 1)

        def step(e, totals):
            base = (e * capacity).astype(F32)
            row = dgates_ref[pl.ds(e, 1)][0][0:1]
            return tuple(
                totals[k]
                + jnp.where((wide.astype(F32) == slot[k] - base) & (wide < capacity), row, 0.0)
                for k in range(2)
            )

        zero = jnp.zeros((rows, lanes), F32)
        sums = lax.fori_loop(0, expert_count, step, (zero, zero))
        dgates = [jnp.sum(s, axis=1, keepdims=True) for s in sums]
        mean = gates[0] * dgates[0] + gates[1] * dgates[1]
        dchosen = [gates[k] * (dgates[k] - mean) for k in range(2)]
        dlogits = jnp.zeros((rows, 128), F32)
        for k in range(2):
            here = lane == route_column(routes_ref, k).astype(jnp.int32)
            dlogits = dlogits + jnp.where(here, dchosen[k], 0.0)
        small_rows = dot_exact(dlogits.T[0:expert_count], normed2_ref[...])
        small_v[0, 0:expert_count] = small_rows
        blank = jnp.zeros((128 - expert_count, width), F32)
        router = jnp.concatenate([router_t_ref[...], blank], axis=0)
        hot0, hot1 = hots()
        hot = jnp.where(hot0 | hot1, 1.0, 0.0).astype(BF16)
        dnormed = dot_f32(dlogits, router)
        dnormed = dnormed + dot_nn(hot, dx_ref[...].reshape(slots, width))
        resid = resid_ref[...]
        inv_rms = lax.rsqrt(jnp.mean(resid * resid, axis=1, keepdims=True) + EPS)
        normed = resid * inv_rms
        scaled = dnormed * gain2_ref[...]
        small_v[0, expert_count + 1 : expert_count + 2] = jnp.sum(
            dnormed * normed, axis=0, keepdims=True
        )
        inner = jnp.mean(scaled * normed, axis=1, keepdims=True)
        dresid = grad_ref[...].astype(F32) + inv_rms * (scaled - normed * inner)
        grad_tokens_ref[...] = dresid
        dresid_r = dresid.astype(BF16)
        grads_o[...] = dot_nn(mixed_t_ref[...], dresid_r).astype(BF16).reshape(grads_o.shape)
        part_a(groups)
        dmix_v[...] = dot_nt(dresid_r, wo_ref[...]).astype(BF16)

    def group(j):
        if j + 1 < groups:
            wq_copy(j + 1).start()

        def pair(a, carry):
            p_copy(j, a).wait()
            attend_back_pair(j, a, qkv_v, p_v.at[a], dmix_v, dqkv_v, fold_v)
            if j + 1 < groups:
                p_copy(j + 1, a).start()
            return carry

        lax.fori_loop(0, 2, pair, 0)
        block = dot_nn(normed_t_ref[...], dqkv_v[...])
        grads_q[j] = block.astype(BF16).reshape(grads_q.shape[1:])
        part_a(j)
        wq_copy(j).wait()
        term = dot_nt(dqkv_v[...], wq_v[j % 2])
        dn1_v[...] = term if j == 0 else dn1_v[...] + term

    def norm_back():
        inputs = tokens_ref[...].astype(F32)
        inv_rms = lax.rsqrt(jnp.mean(inputs * inputs, axis=1, keepdims=True) + EPS)
        normed = inputs * inv_rms
        dnormed = dn1_v[...]
        scaled = dnormed * gain1_ref[...]
        small_v[0, expert_count : expert_count + 1] = jnp.sum(
            dnormed * normed, axis=0, keepdims=True
        )
        inner = jnp.mean(scaled * normed, axis=1, keepdims=True)
        grad_tokens_ref[...] += inv_rms * (scaled - normed * inner)
        heads, buckets = fold_v.shape[0], bucket_hot_ref.shape[0]
        spread = jnp.concatenate([bucket_hot_ref[...]] * heads, axis=0)
        table = dot_exact(fold_v[...], spread, dot_nt)
        own = iota(table.shape, 1) // buckets == iota(table.shape, 0)
        base = expert_count + 2
        small_v[0, base : base + 1, 0 : heads * buckets] = jnp.sum(
            jnp.where(own, table, 0.0), axis=0, keepdims=True
        )
        tokens_copy.start()
        small_copy(0).start()

    def outputs():
        for peer in peers:
            y_copy(peer, peer).wait_recv()
        y_own.wait()
        values = y_v[...].reshape(slots, width)
        total = resid_ref[...]
        for k, hot in enumerate(hots()):
            total = total + gates[k] * dot_nn(jnp.where(hot, 1.0, 0.0).astype(BF16), values)
        block_ref[...] = total.astype(BF16)
        block_copy.start()

    block_copy = pltpu.make_async_copy(block_ref, block_hbm, block_sem.at[0])
    tokens_copy = pltpu.make_async_copy(grad_tokens_ref, grad_tokens_hbm, block_sem.at[1])
    small_v[0] = jnp.zeros(small_v.shape[1:], F32)
    for peer in peers:
        y_copy(peer, me).start()
    y_own = pltpu.make_async_copy(ys_ref.at[me], y_v.at[me], local_sem.at[0])
    y_own.start()
    qkv_copy = pltpu.make_async_copy(qkv_ref, qkv_v, local_sem.at[1])
    qkv_copy.start()
    wq_copy(0).start()
    for a in range(2):
        p_copy(0, a).start()
    late = [b for b in range(AHEAD, batches)]
    turn = [b for b in range(AHEAD, batches)]
    open_relays = []

    def send_more(number):
        for _ in range(min(number, len(late))):
            issue(late.pop(0))

    def relay_in():
        if turn:
            b = turn.pop(0)
            relay_begin(b)
            open_relays.append(b)

    def relay_out():
        if open_relays:
            relay_end(open_relays.pop(0))

    send_more(4)
    for b in range(AHEAD):
        relay_begin(b)
        if b > 0:
            relay_end(b - 1)
    relay_end(AHEAD - 1)
    send_more(1)
    for copy in loads.values():
        copy.wait()
    dense()
    qkv_copy.wait()
    group(0)
    part_b(groups)
    relay_in()
    relay_out()
    send_more(1)
    group(1)
    part_b(0)
    relay_in()
    relay_out()
    send_more(1)
    group(2)
    part_b(1)
    relay_in()
    relay_out()
    send_more(1)
    group(3)
    part_b(2)
    send_more(1)
    norm_back()
    part_b(3)
    send_more(len(late))
    relay_in()
    small_next(0)
    relay_out()
    direct = [p for p in (groups, *range(groups)) if p not in CHIPS_FIRST]
    first_on = [p for p in (groups, *range(groups)) if p in CHIPS_FIRST]
    for p in direct:
        part_c(p)
    small_next(1)
    outputs()
    small_next(2)
    relay_in()
    for p in direct[:-1]:
        part_d(p)
    relay_out()
    for p in first_on[:1]:
        part_c(p)
    small_next(3)
    relay_in()
    for p in direct[-1:]:
        part_d(p)
    for p in first_on[1:2]:
        part_c(p)
    relay_out()
    for s in range(4, stages):
        small_next(s)
    small_out_ref[...] = small_v[0]
    for p in first_on[:1]:
        part_d(p)
    relay_in()
    for p in first_on[2:]:
        part_c(p)
    for p in first_on[1:2]:
        part_d(p)
    relay_out()
    while turn:
        relay_in()
        relay_out()
    for p in first_on[2:]:
        part_d(p)
    for p in direct:
        part_e(p)
    for p in first_on:
        part_e(p)
    for b in (batches - 2, batches - 1):
        over(b, lambda t, b=b: second_copy(t, b).wait_send())

    def drain_first(t, carry):
        for i in range(2):
            first_copy(t, i).wait_send()
        return carry

    def drain_second(t, carry):
        second_copy(t, 0).wait_recv()
        return carry

    block_copy.wait()
    tokens_copy.wait()
    lax.fori_loop(BATCH * AHEAD, tile_count, drain_first, 0)
    lax.fori_loop(0, tile_count, drain_second, 0)
    for peer in peers:
        y_copy(peer, me).wait_send()


def back(
    dw, head, ys, dx, dgates, cols, routes, tokens, grad_out, resid, normed2, normed_t, mixed_t,
    gain1, gain2, router_t, bucket_hot, wq, wo, qkv, probs,
):
    tile_count, dp_count, deep, _ = dw.shape
    expert_count, capacity, width = ys.shape
    chips = expert_count // 2
    rows = tokens.shape[0]
    groups, _, part = qkv.shape
    own = width // (dp_count * expert_count)
    heads = probs.shape[0]
    small_rows = -(-(expert_count + 3) // 8) * 8
    stages = expert_count.bit_length() + 1
    vmem = pl.BlockSpec(memory_space=pltpu.VMEM)
    sem = pltpu.SemaphoreType.DMA
    shape = jax.ShapeDtypeStruct
    ring = (2, BATCH, deep, TILE)
    late = tile_count - BATCH * AHEAD

    def pairs(make, number=groups):
        return [pltpu.VMEM((number, *make(part)), BF16), pltpu.VMEM(make(width), BF16)]

    return pl.pallas_call(
        back_kernel,
        in_specs=[ANY] * 5 + [vmem] * 2 + [ANY] * 6 + [vmem] * 4 + [ANY] * 4,
        out_specs=[ANY] * 2 + [vmem] * 3 + [ANY] * 2,
        out_shape=[
            shape((late, 2, deep, TILE), BF16),
            shape((tile_count, deep, TILE), BF16),
            shape((small_rows, width), F32),
            shape((groups, own, part), F32),
            shape((own, width), F32),
            shape((rows, width), BF16),
            shape((rows, width), F32),
        ],
        scratch_shapes=[pltpu.VMEM(ys.shape, BF16)]
        + pairs(lambda w: (2, 2, chips, 2, own, w))
        + pairs(lambda w: (2, 2, chips, own, w))
        + pairs(lambda w: (2, 2, chips, own, w // 2))
        + pairs(lambda w: (2, chips, own, w // 2))
        + pairs(lambda w: (chips, own, w))
        + pairs(lambda w: (chips, 2, 2, own, w), CHIPS_FIRST_GROUPS)
        + pairs(lambda w: (2, 2, own, w), CHIPS_FIRST_GROUPS)
        + [
            pltpu.VMEM(qkv.shape, BF16),
            pltpu.VMEM((2, 2, rows, rows), BF16),
            pltpu.VMEM((2, *wq.shape[1:]), BF16),
            pltpu.VMEM((rows, part), BF16),
            pltpu.VMEM((rows, width), BF16),
            pltpu.VMEM((rows, width), F32),
            pltpu.VMEM((heads, bucket_hot.shape[1]), F32),
            pltpu.VMEM((stages + 1, small_rows, width), F32),
            pltpu.VMEM(ring, BF16),
            pltpu.VMEM(ring, BF16),
            pltpu.VMEM(ring, BF16),
            sem((expert_count,)),
            sem((expert_count,)),
            sem((late, 2)),
            sem((late, 2)),
            sem((tile_count,)),
            sem((tile_count,)),
            sem((2, BATCH, 2)),
            sem((stages,)),
            sem((stages,)),
            sem((groups + 1,)),
            sem((groups + 1,)),
            sem((groups + 1, 2)),
            sem((groups + 1, 2)),
            sem((groups + 1, 2)),
            sem((groups + 1, 2)),
            sem((groups + 1, chips)),
            sem((groups + 1, chips)),
            sem((2,)),
            sem((2,)),
            sem((2,)),
        ]
        + [
            pltpu.VMEM(a.shape, a.dtype)
            for a in (dx, dgates, tokens, resid, normed2, normed_t, mixed_t, wo, grad_out)
        ]
        + [
            sem((9,)),
            sem((2,)),
            pltpu.VMEM((rows, width), BF16),
            pltpu.VMEM((rows, width), F32),
        ],
        compiler_params=pltpu.CompilerParams(
            collective_id=2, has_side_effects=True, vmem_limit_bytes=61 * 1024 * 1024
        ),
        name="back",
    )(
        dw, head, ys, dx, dgates, cols, routes, tokens, grad_out, resid, normed2, normed_t, mixed_t,
        gain1, gain2, router_t, bucket_hot, wq, wo, qkv, probs,
    )


def tail_kernel(
    heads,
    buckets,
    dw_ref,
    head_ref,
    first_ref,
    second_ref,
    block_ref,
    tokens_ref,
    small_ref,
    gq_ref,
    go_ref,
    in_ref,
    out_ref,
    block_out_ref,
    tokens_out_ref,
    router_ref,
    norm1_ref,
    norm2_ref,
    bias_ref,
    qkv_ref,
    proj_ref,
    own_v,
    came_v,
    second_v,
    in_v,
    out_v,
    block_v,
    tokens_v,
    load_sem,
    store_sem,
    pass_sem,
):
    dp = lax.axis_index("dp")
    tiles = own_v.shape[0]
    expert_count = router_ref.shape[0]

    def loads(f):
        span = pl.ds(BATCH * f, BATCH)
        late = pl.ds(BATCH * (f - AHEAD), BATCH)
        came = head_ref.at[span, 0] if f < AHEAD else first_ref.at[late, 0]
        return [
            pltpu.make_async_copy(src, dst.at[f], load_sem.at[f, k])
            for k, (src, dst) in enumerate(
                ((dw_ref.at[span, dp], own_v), (came, came_v), (second_ref.at[span], second_v))
            )
        ]

    def stores(f):
        cols = pl.ds(TILE * f, TILE)
        return [
            pltpu.make_async_copy(in_v.at[f], in_ref.at[:, :, cols], store_sem.at[f, 0]),
            pltpu.make_async_copy(out_v.at[f], out_ref.at[cols], store_sem.at[f, 1]),
        ]

    for f in range(tiles):
        for copy in loads(f):
            copy.start()
    taken = [
        pltpu.make_async_copy(block_ref, block_v, pass_sem.at[0]),
        pltpu.make_async_copy(tokens_ref, tokens_v, pass_sem.at[1]),
    ]
    given = [
        pltpu.make_async_copy(block_v, block_out_ref, pass_sem.at[2]),
        pltpu.make_async_copy(tokens_v, tokens_out_ref, pass_sem.at[3]),
    ]
    for copy in taken:
        copy.start()
    router_ref[...] = small_ref[0:expert_count]
    norm1_ref[...] = small_ref[expert_count : expert_count + 1]
    norm2_ref[...] = small_ref[expert_count + 1 : expert_count + 2]
    base = expert_count + 2
    row = jnp.broadcast_to(small_ref[base : base + 1, 0 : heads * buckets], (8, heads * buckets))
    for h in range(heads):
        turned = pltpu.roll(row, (heads - h) % heads * buckets, 1) if h else row
        bias_ref[h : h + 1] = turned[0:1, 0:buckets]
    groups, _, part = gq_ref.shape
    third = part // 3
    for j in range(groups):
        for k in range(3):
            at = (k * groups + j) * third
            qkv_ref[:, at : at + third] = gq_ref[j, :, k * third : (k + 1) * third]
    proj_ref[...] = go_ref[...]
    for f in range(tiles):
        for copy in loads(f):
            copy.wait()
        for m in range(BATCH):
            total = own_v[f, m].astype(F32) + came_v[f, m].astype(F32) + second_v[f, m].astype(F32)
            if m < 2:
                in_v[f, m] = total
            else:
                out_v[f] = total.T
        for copy in stores(f):
            copy.start()
    for came, copy in zip(taken, given):
        came.wait()
        copy.start()
    for f in range(tiles):
        for copy in stores(f):
            copy.wait()
    for copy in given:
        copy.wait()


def tail(dw, head, first, second, small, gq, go, block, tokens, expert_count, heads, buckets):
    tile_count, _, deep, _ = dw.shape
    tiles = tile_count // BATCH
    groups, own, part = gq.shape
    width = tokens.shape[1]
    shape = jax.ShapeDtypeStruct
    vmem = pl.BlockSpec(memory_space=pltpu.VMEM)
    terms = pltpu.VMEM((tiles, BATCH, deep, TILE), BF16)
    sem = pltpu.SemaphoreType.DMA
    return pl.pallas_call(
        functools.partial(tail_kernel, heads, buckets),
        in_specs=[ANY] * 6 + [vmem] * 3,
        out_specs=[ANY] * 4 + [vmem] * 6,
        out_shape=[
            shape((2, deep, tiles * TILE), F32),
            shape((tiles * TILE, deep), F32),
            shape(block.shape, BF16),
            shape(tokens.shape, F32),
            shape((expert_count, width), F32),
            shape((1, width), F32),
            shape((1, width), F32),
            shape((heads, buckets), F32),
            shape((own, groups * part), F32),
            shape((own, width), F32),
        ],
        scratch_shapes=[
            terms,
            terms,
            terms,
            pltpu.VMEM((tiles, 2, deep, TILE), F32),
            pltpu.VMEM((tiles, TILE, deep), F32),
            pltpu.VMEM(block.shape, BF16),
            pltpu.VMEM(tokens.shape, F32),
            sem((tiles, 3)),
            sem((tiles, 2)),
            sem((4,)),
        ],
        compiler_params=pltpu.CompilerParams(vmem_limit_bytes=62 * 1024 * 1024),
        name="tail",
    )(dw, head, first, second, block, tokens, small, gq, go)


def shards(
    tokens,
    routes,
    rel_bucket,
    norm_gain1,
    w_qkv,
    w_out_proj,
    bias_table,
    norm_gain2,
    w_router,
    w_expert_in,
    w_expert_out,
    grad_out,
):
    row_count, model_width = tokens.shape
    bucket_count, head_count = bias_table.shape
    expert_count = lax.axis_size("expert")
    capacity = 10 * row_count // (4 * expert_count)
    slot_total = expert_count * capacity
    hidden_groups = 4

    bucket_ids = jnp.arange(bucket_count, dtype=jnp.int32)
    bucket_hot = jnp.concatenate(
        [bucket_ids[:, None] == rel_bucket[None, :], jnp.zeros((bucket_count, 1), bool)], axis=1
    ).astype(F32)
    table = jnp.dot(bias_table.T, bucket_hot, precision=HIGHEST)

    wq_full, out_full, qkv, probs, g_rows, mixed_t, normed1_t, residual, normed2_r, xs, gates, cols = front(
        tokens,
        norm_gain1[None],
        norm_gain2[None],
        table,
        routes.T,
        grad_out,
        w_router.T,
        w_qkv,
        w_out_proj,
        hidden_groups,
        capacity,
    )
    produced, grad_rows, grad_gates, grad_w, head = experts(
        xs, gates, g_rows, w_expert_in[0], w_expert_out[0], lax.axis_size("dp")
    )
    first, second, *rest = back(
        grad_w,
        head,
        produced,
        grad_rows,
        grad_gates,
        cols,
        routes.T,
        tokens,
        grad_out,
        residual,
        normed2_r,
        normed1_t,
        mixed_t,
        norm_gain1[None],
        norm_gain2[None],
        w_router.T,
        bucket_hot.astype(BF16),
        wq_full.reshape(hidden_groups, model_width, -1),
        out_full.reshape(model_width, model_width),
        qkv,
        probs,
    )
    (
        grad_in,
        grad_out_t,
        block_out,
        grad_tokens,
        grad_router,
        grad_norm1,
        grad_norm2,
        grad_bias,
        grad_qkv,
        grad_out_proj,
    ) = tail(grad_w, head, first, second, *rest, expert_count, head_count, bucket_count)
    grad_expert_in, grad_expert_out = grad_in[None], grad_out_t[None]
    grad_router_all, grad_bias = grad_router.T, grad_bias.T
    grad_norm1, grad_norm2 = grad_norm1[0], grad_norm2[0]
    return (
        block_out,
        grad_tokens,
        grad_norm1,
        grad_qkv,
        grad_out_proj,
        grad_bias,
        grad_norm2,
        grad_router_all,
        grad_expert_in,
        grad_expert_out,
    )


def solution(mesh):
    split = P(("dp", "expert"), None)
    in_specs = (
        split,
        split,
        P(),
        P(),
        split,
        split,
        P(),
        P(),
        P(),
        P("expert", None, None, None),
        P("expert", None, None),
        split,
    )
    out_specs = (
        split,
        split,
        P(),
        split,
        split,
        P(),
        P(),
        P(),
        P("expert", None, "dp", None),
        P("expert", None, "dp"),
    )
    return jax.shard_map(shards, mesh=mesh, in_specs=in_specs, out_specs=out_specs, check_vma=False)
```

```python
import functools

import jax
import jax.numpy as jnp
from jax import lax
from jax.experimental import pallas as pl
from jax.experimental.pallas import tpu as pltpu
from jax.sharding import PartitionSpec as P

LENGTH = 512
EPS = 1e-06
HIGHEST = lax.Precision.HIGHEST
F32 = jnp.float32
BF16 = jnp.bfloat16


def dot_nt(a, b):
    return lax.dot_general(a, b, (((1,), (1,)), ((), ())), preferred_element_type=F32)


def dot_nn(a, b):
    return jnp.dot(a, b, preferred_element_type=F32)


def iota(shape, axis):
    return lax.broadcasted_iota(jnp.int32, shape, axis)


def spread_bias(row):
    values = jnp.broadcast_to(row, (8, 1024))
    lift = 7 - iota((8, 1024), 0)
    for bit in (1, 2, 4):
        values = jnp.where((lift // bit) % 2 == 1, pltpu.roll(values, 1024 - bit, 1), values)
    return jnp.concatenate(
        [pltpu.roll(values, (904 + 8 * block) % 1024, 1) for block in range(16)], axis=0
    )


def fold_bias(parts):
    total = parts[0:8]
    total = pltpu.roll(total, 120, 1)
    for block in range(1, 16):
        piece = parts[8 * block : 8 * block + 8]
        total = total + (pltpu.roll(piece, 120 - 8 * block, 1) if block < 15 else piece)
    lift = 7 - iota((8, 1024), 0)
    for bit in (1, 2, 4):
        total = jnp.where((lift // bit) % 2 == 1, pltpu.roll(total, bit, 1), total)
    return jnp.sum(total, axis=0, keepdims=True)


MESH = pl.DeviceIdType.MESH
ANY = pl.BlockSpec(memory_space=pl.ANY)
GROUPS = 4
TILE = 256
WIDE = 512


def flip(index, mask):
    bit = 1
    while bit <= mask:
        if mask & bit:
            index = index + bit - 2 * bit * ((index // bit) % 2)
        bit *= 2
    return index


def remote(src, dst, send_sem, recv_sem, **axes):
    return pltpu.make_async_remote_copy(
        src_ref=src,
        dst_ref=dst,
        send_sem=send_sem,
        recv_sem=recv_sem,
        device_id=axes,
        device_id_type=MESH,
    )


def greet(partners):
    barrier = pltpu.get_barrier_semaphore()
    for axes in partners:
        pl.semaphore_signal(barrier, inc=1, device_id=axes, device_id_type=MESH)
    pl.semaphore_wait(barrier, len(partners))


def gelu_parts(x):
    root = 0.7978845608028654
    square = x * x
    t = jnp.tanh(root * x * (1.0 + 0.044715 * square))
    half = 0.5 * (1.0 + t)
    slope = half + 0.5 * x * (1.0 - t * t) * (root * (1.0 + 3 * 0.044715 * square))
    return x * half, slope


BATCH = 3
AHEAD = 4
CHIPS_FIRST_GROUPS = 1
CHIPS_FIRST = (*range(CHIPS_FIRST_GROUPS), 4)


def ways(dp, t):
    x, y = dp % 2, dp // 2
    x_peer, y_peer = dp + 1 - 2 * x, dp + 2 - 4 * y
    q = t % 2
    sent = [(1 - q) * (2 * i + 1 - x) + q * (2 * (1 - y) + i) for i in range(2)]
    keep = (1 - q) * y + q * x
    held = [(1 - q) * (2 * k + x) + q * (2 * y + k) for k in (keep, 1 - keep)]
    return sent, held, (1 - q) * x_peer + q * y_peer, (1 - q) * y_peer + q * x_peer, keep


def experts_kernel(
    xs_ref,
    gates_ref,
    g_ref,
    w_in_ref,
    w_out_ref,
    y_ref,
    dx_back_ref,
    dgates_back_ref,
    dw_ref,
    head_ref,
    w_in_v,
    w_out_v,
    x_v,
    gates_v,
    dgates_v,
    g_v,
    dy_v,
    hid_v,
    dgate_v,
    dup_v,
    y_v,
    dx_v,
    pre_v,
    stage,
    local_sem,
    stage_sem,
    x_send,
    x_recv,
    gates_send,
    gates_recv,
    dgates_send,
    dgates_recv,
    dx_send,
    dx_recv,
    y_sem,
    head_send,
    head_recv,
    weight_sem,
):
    expert_count, capacity, width = xs_ref.shape
    hidden = w_out_ref.shape[0]
    tiles = hidden // TILE
    size = expert_count // GROUPS
    rows = size * capacity
    me = lax.axis_index("expert")
    my_group, my_place = me // size, me % size

    def others(c):
        group = flip(my_group, c)
        return [group * size + (my_place + s) % size for s in range(1 if c == 0 else 0, size)]

    dp = lax.axis_index("dp")
    greet(
        [{"expert": (me + d) % expert_count} for d in range(1, expert_count)]
        + [{"dp": flip(dp, 1)}, {"dp": flip(dp, 2)}]
    )

    def send_rows(c):
        for peer in others(c):
            remote(
                xs_ref.at[peer], x_v.at[me], x_send.at[peer], x_recv.at[me], expert=peer
            ).start()
            remote(
                gates_ref.at[peer, 0:1],
                gates_v.at[me, 0:1],
                gates_send.at[peer],
                gates_recv.at[me],
                expert=peer,
            ).start()

    for c in (2, 1, 0):
        send_rows(c)
    def weights(f):
        cols = pl.ds(pl.multiple_of(f * TILE, TILE), TILE)
        return [
            pltpu.make_async_copy(
                w_in_ref.at[:, :, cols], w_in_v.at[:, :, cols], weight_sem.at[f, 0]
            ),
            pltpu.make_async_copy(w_out_ref.at[cols], w_out_v.at[cols], weight_sem.at[f, 1]),
        ]

    own = [
        pltpu.make_async_copy(xs_ref.at[me], x_v.at[me], local_sem.at[0]),
        pltpu.make_async_copy(gates_ref.at[me], gates_v.at[me], local_sem.at[1]),
        pltpu.make_async_copy(g_ref, g_v, local_sem.at[4]),
    ]
    for copy in own:
        copy.start()

    def fetch(f, carry):
        for copy in weights(f):
            copy.start()
        return carry

    lax.fori_loop(0, tiles, fetch, 0)
    for copy in own:
        copy.wait()

    def y_copy(c):
        span = pl.ds(flip(my_group, c) * size, size)
        return pltpu.make_async_copy(y_v.at[span], y_ref.at[span], y_sem.at[c])

    def back_copies(peer, at):
        return [
            remote(
                dx_v.at[peer], dx_back_ref.at[at], dx_send.at[peer], dx_recv.at[at], expert=peer
            ),
            remote(
                dgates_v.at[peer, 0:1],
                dgates_back_ref.at[at, 0:1],
                dgates_send.at[peer],
                dgates_recv.at[at],
                expert=peer,
            ),
        ]

    dgates_v[...] = jnp.zeros_like(dgates_v)
    for c in range(GROUPS):
        group = flip(my_group, c)
        span = pl.ds(group * size, size)
        for peer in others(c):
            remote(
                xs_ref.at[peer], x_v.at[peer], x_send.at[peer], x_recv.at[peer], expert=peer
            ).wait_recv()
            remote(
                gates_ref.at[peer, 0:1],
                gates_v.at[peer, 0:1],
                gates_send.at[peer],
                gates_recv.at[peer],
                expert=peer,
            ).wait_recv()
        for s in range(size):
            src = group * size + s
            gate_col = gates_v[src].T[0:capacity, 0:1]
            dy_v[src] = (g_v[src].astype(F32) * gate_col).astype(BF16)

        def before(f, slot, span=span, c=c):
            if c == 0:
                for copy in weights(f):
                    copy.wait()
            cols = pl.ds(pl.multiple_of(f * TILE, TILE), TILE)
            x = x_v[span].reshape(rows, width)
            pre_v[slot, 0] = dot_nn(x, w_in_v[0, :, cols])
            pre_v[slot, 1] = dot_nn(x, w_in_v[1, :, cols])
            pre_v[slot, 2] = dot_nt(dy_v[span].reshape(rows, width), w_out_v[cols, :])

        def after(f, slot, group=group):
            cols = pl.ds(pl.multiple_of(f * TILE, TILE), TILE)
            gate, up, dhid = pre_v[slot, 0], pre_v[slot, 1], pre_v[slot, 2]
            gelu, slope = gelu_parts(gate)
            hid_v[group, :, cols] = (gelu * up).astype(BF16)
            dgate_v[group, :, cols] = (dhid * up * slope).astype(BF16)
            dup_v[group, :, cols] = (dhid * gelu).astype(BF16)

        def two(h, carry):
            before(2 * h + 1, 1)
            after(2 * h, 0)
            before(2 * h + 2, 0)
            after(2 * h + 1, 1)
            return carry

        def backs(n, carry, group=group, span=span):
            cols = pl.ds(pl.multiple_of(n * WIDE, WIDE), WIDE)
            out = dot_nn(hid_v[group], w_out_v[:, cols])
            y_v[span, :, cols] = out.astype(BF16).reshape(size, capacity, WIDE)
            back = dot_nt(dgate_v[group], w_in_v[0, cols, :])
            back = back + dot_nt(dup_v[group], w_in_v[1, cols, :])
            dx_v[span, :, cols] = back.astype(BF16).reshape(size, capacity, WIDE)
            return carry

        assert tiles % 2 == 1
        before(0, 0)
        lax.fori_loop(0, tiles // 2, two, 0)
        after(tiles - 1, 0)
        lax.fori_loop(0, width // WIDE, backs, 0)
        if c == 0:
            send_rows(3)
        y_copy(c).start()
        for s in range(size):
            src = group * size + s
            product = g_v[src].astype(F32) * y_v[src].astype(F32)
            dgate = jnp.sum(product, axis=1, keepdims=True)
            dgates_v[src, :, 0:capacity] = jnp.broadcast_to(dgate, (capacity, 128)).T[0:8]
        for peer in others(c):
            for copy in back_copies(peer, me):
                copy.start()
    own = [
        pltpu.make_async_copy(dx_v.at[me], dx_back_ref.at[me], local_sem.at[0]),
        pltpu.make_async_copy(dgates_v.at[me], dgates_back_ref.at[me], local_sem.at[1]),
    ]
    for copy in own:
        copy.start()

    slots = expert_count * capacity
    w_in_v[0, :, 0:slots] = x_v[...].reshape(slots, width).T
    w_in_v[1, :, 0:slots] = dy_v[...].reshape(slots, width).T

    def put(f, m):
        return pltpu.make_async_copy(stage.at[m], dw_ref.at[BATCH * f + m], stage_sem.at[m])

    def head_copy(f, m, i):
        t = BATCH * f + m
        sent, _, peer, _, keep = ways(dp, t)
        return remote(
            dw_ref.at[t, sent[i]], head_ref.at[t, (i + keep) % 2], head_send.at[t, i], head_recv.at[t, i], dp=peer
        )

    parts, deep = stage.shape[1:3]

    def grads(f, carry):
        cols = pl.ds(pl.multiple_of(f * TILE, TILE), TILE)
        for m, (side, right) in enumerate(((0, dgate_v), (0, dup_v), (1, hid_v))):

            @pl.when(f > 1)
            def _():
                put(f - 1, m).wait()

            @pl.when((f > 1) & (f <= AHEAD))
            def _():
                for i in range(2):
                    head_copy(f - 1, m, i).start()

            across = right[:, :, cols].reshape(slots, TILE)
            for r in range(0, parts, 2):
                span = slice(r * deep, (r + 2) * deep)
                block = dot_nn(w_in_v[side, span, 0:slots], across)
                stage[m, r : r + 2] = block.astype(BF16).reshape(2, deep, TILE)
            put(f, m).start()
            for done in [m - 1] * (m > 0) + [m] * (m == BATCH - 1):

                @pl.when(f == 0)
                def _(done=done):
                    put(0, done).wait()
                    for i in range(2):
                        head_copy(0, done, i).start()

        return carry

    lax.fori_loop(0, tiles, grads, 0)
    for m in range(BATCH):
        put(tiles - 1, m).wait()

    def heads(t, carry):
        for i in range(2):
            head_copy(t // BATCH, t % BATCH, i).wait()
        return carry

    lax.fori_loop(0, BATCH * AHEAD, heads, 0)
    for copy in own:
        copy.wait()
    for c in range(GROUPS):
        for peer in others(c):
            remote(
                xs_ref.at[peer], x_v.at[me], x_send.at[peer], x_recv.at[me], expert=peer
            ).wait_send()
            remote(
                gates_ref.at[peer, 0:1],
                gates_v.at[me, 0:1],
                gates_send.at[peer],
                gates_recv.at[me],
                expert=peer,
            ).wait_send()
            for copy in back_copies(peer, me):
                copy.wait_send()
            for copy in back_copies(peer, peer):
                copy.wait_recv()
        y_copy(c).wait()


def experts(xs, gates, g, w_in, w_out, dp_count):
    expert_count, capacity, width = xs.shape
    hidden = w_out.shape[0]
    size = expert_count // GROUPS
    tiles = hidden // TILE
    rows = size * capacity
    slots = jax.ShapeDtypeStruct(xs.shape, BF16)
    parts = (dp_count, width // dp_count, TILE)
    peers = pltpu.SemaphoreType.DMA((expert_count,))
    return pl.pallas_call(
        experts_kernel,
        in_specs=[ANY] * 5,
        out_specs=[ANY] * 5,
        out_shape=[slots, slots, jax.ShapeDtypeStruct(gates.shape, F32), jax.ShapeDtypeStruct((BATCH * tiles, *parts), BF16),
            jax.ShapeDtypeStruct((BATCH * AHEAD, 2, *parts[1:]), BF16),
        ],
        scratch_shapes=[
            pltpu.VMEM(w_in.shape, BF16),
            pltpu.VMEM(w_out.shape, BF16),
            pltpu.VMEM(xs.shape, BF16),
            pltpu.VMEM(gates.shape, F32),
            pltpu.VMEM(gates.shape, F32),
            pltpu.VMEM(xs.shape, BF16),
            pltpu.VMEM(xs.shape, BF16),
            pltpu.VMEM((GROUPS, rows, hidden), BF16),
            pltpu.VMEM((GROUPS, rows, hidden), BF16),
            pltpu.VMEM((GROUPS, rows, hidden), BF16),
            pltpu.VMEM(xs.shape, BF16),
            pltpu.VMEM(xs.shape, BF16),
            pltpu.VMEM((2, 3, rows, TILE), F32),
            pltpu.VMEM((BATCH, *parts), BF16),
            pltpu.SemaphoreType.DMA((5,)),
            pltpu.SemaphoreType.DMA((3,)),
        ]
        + [peers] * 8
        + [pltpu.SemaphoreType.DMA((GROUPS,))]
        + [pltpu.SemaphoreType.DMA((BATCH * AHEAD, 2))] * 2
        + [pltpu.SemaphoreType.DMA((tiles, 2))],
        compiler_params=pltpu.CompilerParams(
            collective_id=1, has_side_effects=True, vmem_limit_bytes=61 * 1024 * 1024
        ),
        name="experts",
    )(xs, gates, g, w_in, w_out)


def column(values, k):
    return values[:, k : k + 1]


def bucket_rows(rel_ref, rel_v, buckets):
    rel_v[...] = jnp.full(rel_v.shape, -1, jnp.int32)
    rel_v[0:1, 0 : rel_ref.shape[1]] = rel_ref[...]
    here = iota((buckets, rel_v.shape[1]), 0) == rel_v[0:1]
    return jnp.where(here, 1.0, 0.0).astype(BF16)


def route_column(routes_ref, k):
    row = routes_ref[k : k + 1, :].astype(F32)
    return jnp.broadcast_to(row, (128, row.shape[1])).T


def attend_pair(j, a, qkv_v, table_ref, p_ref):
    def lanes(part):
        return pl.ds(pl.multiple_of(256 * part + 128 * a, 128), 128)

    query = qkv_v[j, :, lanes(0)] * jnp.asarray(0.125, BF16)
    values_t = qkv_v[j, :, lanes(2)].T
    half = iota((512, 128), 1) // 64
    halves = []
    for t in range(2):
        shifted = spread_bias(table_ref[pl.ds(4 * j + 2 * a + t, 1), :])
        query_t = jnp.where(half == t, query, jnp.zeros_like(query))
        scores = [
            dot_nt(qkv_v[j, 128 * c : 128 * c + 128, lanes(1)], query_t)
            + shifted[:, 384 - 128 * c : 896 - 128 * c]
            for c in range(4)
        ]
        top = functools.reduce(jnp.maximum, [jnp.max(s, axis=0, keepdims=True) for s in scores])
        exps = [jnp.exp(s - top) for s in scores]
        total = functools.reduce(jnp.add, [jnp.sum(e, axis=0, keepdims=True) for e in exps])
        inverse = 1.0 / total
        for c in range(4):
            p_ref[t, 128 * c : 128 * c + 128, :] = (exps[c] * inverse).astype(BF16)
        halves.append(dot_nn(values_t, p_ref[t]))
    return jnp.where(iota((128, 512), 0) < 64, halves[0], halves[1])


def front_kernel(
    tokens_ref,
    gain1_ref,
    gain2_ref,
    bias_ref,
    rel_ref,
    routes_ref,
    grad_ref,
    router_ref,
    w_qkv_ref,
    wo_ref,
    wq_out,
    wo_out,
    qkv_out,
    p_out,
    g_back,
    mixed_t_hbm,
    normed_t_hbm,
    resid_hbm,
    normed2_hbm,
    xs_hbm,
    gates_ref,
    cols_ref,
    ws_ref,
    wq_v,
    wo_v,
    qkv_v,
    p_v,
    mixed_v,
    normed_v,
    hot_v,
    g_v,
    own_sem,
    z_send,
    z_recv,
    xy_send,
    xy_recv,
    core_send,
    core_recv,
    g_send,
    g_recv,
    out_sem,
    p_sem,
    mixed_t_ref,
    normed_t_ref,
    resid_ref,
    normed2_ref,
    xs_ref,
    stores_sem,
    table_ref,
    rel_v,
):
    stores = {
        name: pltpu.make_async_copy(src, dst, stores_sem.at[n])
        for n, (name, src, dst) in enumerate(
            (
                ("mixed_t", mixed_t_ref, mixed_t_hbm),
                ("normed_t", normed_t_ref, normed_t_hbm),
                ("resid", resid_ref, resid_hbm),
                ("normed2", normed2_ref, normed2_hbm),
                ("xs", xs_ref, xs_hbm),
            )
        )
    }
    expert_count, capacity, width = xs_ref.shape
    lane_count = gates_ref.shape[2]
    slots = expert_count * capacity
    size = expert_count // GROUPS
    chips = expert_count // 2
    me, dp = lax.axis_index("expert"), lax.axis_index("dp")
    core, chip = me % 2, me // 2
    x, y = dp % 2, dp // 2
    core_peer = me + 1 - 2 * core
    x_peer, y_peer = dp + 1 - 2 * x, dp + 2 - 4 * y
    my_group, my_place = me // size, me % size
    chip_peers = [(chip + d) % chips for d in range(1, chips)]
    greet(
        [{"expert": (me + d) % expert_count} for d in range(1, expert_count)]
        + [{"dp": x_peer}, {"dp": y_peer}]
    )

    groups = ws_ref.shape[0]
    count = groups + 1
    srcs = [ws_ref.at[j] for j in range(groups)] + [wo_ref]
    bufs = [wq_v.at[j] for j in range(groups)] + [wo_v]
    widths = [ws_ref.shape[2]] * groups + [wo_ref.shape[1]]
    places = ((y, x), (y, 1 - x), (1 - y, x), (1 - y, 1 - x))

    def z_copy(j, peer, at):
        return remote(
            srcs[j], bufs[j].at[y, x, at, core], z_send.at[j, peer], z_recv.at[j, at], expert=peer * 2 + core
        )

    def own_copy(j):
        return pltpu.make_async_copy(srcs[j], bufs[j].at[y, x, chip, core], own_sem.at[j])

    def xy_copy(j, k):
        half = widths[j] // 2
        src = (
            bufs[j].at[y, x, :, core],
            bufs[j].at[y, x, :, core],
            bufs[j].at[1 - y, x, :, core, :, half : 2 * half],
            bufs[j].at[y, 1 - x, :, core, :, 0:half],
        )[k]
        return remote(src, src, xy_send.at[j, k], xy_recv.at[j, k], dp=(x_peer, y_peer)[k % 2])

    def core_copy(j, k):
        src = bufs[j].at[places[k][0], places[k][1], :, core]
        return remote(src, src, core_send.at[j, k], core_recv.at[j, k], expert=core_peer)

    line = chips == 4
    pair = chip // 2
    mate = chip + 1 - 2 * (chip % 2)
    middle = (chip % 4) * (3 - chip % 4) // 2

    def pair_copy(j, k, at, peer):
        span = bufs[j].at[y, x, pl.ds(2 * at, 2), core]
        return remote(span, span, z_send.at[j, k], z_recv.at[j, k], expert=peer * 2 + core)

    def spread_first(j):
        own_copy(j).wait()
        if line:
            z_copy(j, mate, mate).wait_recv()

            @pl.when(middle == 1)
            def _():
                pair_copy(j, 4, pair, 3 - chip).start()

    def spread_second(j):
        if line:

            @pl.when(middle == 1)
            def _():
                pair_copy(j, 4, 1 - pair, 3 - chip).wait_recv()
                pair_copy(j, 5, 1 - pair, mate).start()

    def spread(j):
        if line:

            @pl.when(middle == 0)
            def _():
                pair_copy(j, 5, 1 - pair, mate).wait_recv()
        else:
            for peer in chip_peers:
                z_copy(j, peer, peer).wait_recv()
        for k in range(2):
            xy_copy(j, k).start()
        core_copy(j, 0).start()

    def forward(j):
        for k in range(2):
            xy_copy(j, k).wait_recv()
            xy_copy(j, 3 - k).start()
            core_copy(j, 1 + k).start()

    def complete(j):
        for k in (2, 3):
            xy_copy(j, k).wait_recv()
        core_copy(j, 3).start()

    def out_copy(j):
        src, dst = (wq_v.at[j], wq_out.at[j]) if j < groups else (wo_v, wo_out)
        return pltpu.make_async_copy(src, dst, out_sem.at[j])

    def gathered(j):
        for k in range(4):
            core_copy(j, k).wait_recv()
        out_copy(j).start()

    third = ws_ref.shape[2] // 3
    for j in range(count):
        if j < groups:
            for k in range(3):
                at = (k * groups + j) * third
                ws_ref[j, :, k * third : (k + 1) * third] = w_qkv_ref[:, at : at + third]
        own_copy(j).start()
        for peer in [mate] if line else chip_peers:
            z_copy(j, peer, chip).start()

    inputs = tokens_ref[...].astype(F32)
    inv_rms = lax.rsqrt(jnp.mean(inputs * inputs, axis=1, keepdims=True) + EPS)
    normed = (inputs * inv_rms * gain1_ref[...]).astype(BF16)
    normed_v[...] = normed
    normed_t_ref[...] = normed.T
    stores["normed_t"].start()
    spread_first(0)
    spread_first(1)
    spread_second(0)
    spread_first(2)
    spread_second(1)
    spread(0)
    spread_first(3)
    spread_second(2)
    spread(1)
    spread_first(4)
    spread_second(3)

    table_ref[...] = dot_exact(bias_ref[...], bucket_rows(rel_ref, rel_v, bias_ref.shape[1]))

    rows = routes_ref.shape[1]
    lane = iota((rows, 128), 1)
    routes = [route_column(routes_ref, k) for k in range(2)]
    hots = [lane == routes[k].astype(jnp.int32) for k in range(2)]
    earlier = (iota((rows, rows), 0) > iota((rows, rows), 1)).astype(BF16)
    ones = [jnp.where(h, 1.0, 0.0) for h in hots]
    counts = [dot_nn(earlier, o.astype(BF16)) for o in ones]
    counts[1] = counts[1] + jnp.sum(ones[0], axis=0, keepdims=True)
    slot = []
    for k in range(2):
        place = jnp.sum(counts[k] * ones[k], axis=1, keepdims=True)
        at = column(routes[k], 0) * capacity + place
        slot.append(jnp.where(place < capacity, at, float(slots)))
    slot_rows = jnp.where(lane == 0, slot[0], slot[1]).T
    slot_ids = iota((slots, rows), 0).astype(F32)
    hot = (slot_ids == slot_rows[0:1]) | (slot_ids == slot_rows[1:2])
    hot_v[...] = jnp.where(hot, 1.0, 0.0).astype(BF16)
    g_v[...] = dot_nn(hot_v[...], grad_ref[...]).astype(BF16).reshape(g_v.shape)

    def g_copy(peer, at):
        return remote(g_v.at[peer], g_back.at[at], g_send.at[peer], g_recv.at[at], expert=peer)

    def others(c):
        group = flip(my_group, c)
        return [group * size + (my_place + s) % size for s in range(1 if c == 0 else 0, size)]

    peers = [peer for c in (2, 3, 1, 0) for peer in others(c)]
    g_own = pltpu.make_async_copy(g_v.at[me], g_back.at[me], own_sem.at[count])
    g_own.start()

    def p_copy(j, a):
        return pltpu.make_async_copy(p_v.at[a], p_out.at[pl.ds(4 * j + 2 * a, 2)], p_sem.at[a])

    def group(j):
        gathered(j)
        qkv_v[j] = dot_nn(normed_v[...], wq_v[j].reshape(width, widths[j])).astype(BF16)

        def pair(a, carry):
            if j > 0:
                p_copy(j - 1, a).wait()
            mixed = attend_pair(j, a, qkv_v, table_ref, p_v.at[a])
            p_copy(j, a).start()
            span = pl.ds(pl.multiple_of(256 * j + 128 * a, 128), 128)
            mixed_t_ref[span, :] = mixed.astype(BF16)
            mixed_v[:, span] = mixed.T.astype(BF16)
            return carry

        lax.fori_loop(0, 2, pair, 0)

    spread(2)
    spread_second(4)
    forward(0)
    spread(3)
    spread(4)
    for peer in peers:
        g_copy(peer, me).start()
    forward(1)
    complete(0)
    forward(2)
    complete(1)
    group(0)
    forward(3)
    complete(2)
    group(1)
    forward(4)
    complete(3)
    group(2)
    complete(4)
    group(3)
    qkv_copy = pltpu.make_async_copy(qkv_v, qkv_out, own_sem.at[count + 1])
    qkv_copy.start()
    stores["mixed_t"].start()
    gathered(groups)

    resid = tokens_ref[...].astype(F32) + dot_nn(mixed_v[...], wo_v[...].reshape(width, width))
    resid_ref[...] = resid
    stores["resid"].start()
    inv_rms2 = lax.rsqrt(jnp.mean(resid * resid, axis=1, keepdims=True) + EPS)
    normed2 = (resid * inv_rms2 * gain2_ref[...]).astype(BF16)
    normed2_ref[...] = normed2
    stores["normed2"].start()
    xs_ref[...] = dot_nn(hot_v[...], normed2).astype(BF16).reshape(xs_ref.shape)
    stores["xs"].start()
    rest = router_ref[...]
    logits = jnp.zeros((rows, expert_count), F32)
    for _ in range(3):
        piece = rest.astype(BF16)
        rest = rest - piece.astype(F32)
        logits = logits + dot_nt(normed2, piece)
    ids = iota((rows, expert_count), 1)
    chosen = [
        jnp.sum(
            jnp.where(ids == column(routes[k], 0).astype(jnp.int32), logits, 0.0),
            axis=1,
            keepdims=True,
        )
        for k in range(2)
    ]
    top = jnp.maximum(chosen[0], chosen[1])
    exps = [jnp.exp(c - top) for c in chosen]
    gates = [e / (exps[0] + exps[1]) for e in exps]
    cols = jnp.where(lane == 2, gates[0], jnp.where(lane == 3, gates[1], 0.0))
    cols_ref[...] = jnp.where(lane == 0, slot[0], jnp.where(lane == 1, slot[1], cols))
    wide = iota((rows, lane_count), 1)

    def gate_row(e, carry):
        base = (e * capacity).astype(F32)
        total = jnp.zeros((rows, lane_count), F32)
        for k in range(2):
            here = (wide.astype(F32) == slot[k] - base) & (wide < capacity)
            total = total + jnp.where(here, gates[k], 0.0)
        row = jnp.sum(total, axis=0, keepdims=True)
        gates_ref[pl.ds(e, 1)] = jnp.broadcast_to(row, (8, lane_count))[None]
        return carry

    lax.fori_loop(0, expert_count, gate_row, 0)

    for a in range(2):
        p_copy(groups - 1, a).wait()
    qkv_copy.wait()
    for copy in stores.values():
        copy.wait()
    g_own.wait()
    for j in range(count):
        out_copy(j).wait()
        for peer in [mate] if line else chip_peers:
            z_copy(j, peer, chip).wait_send()
        if line:

            @pl.when(middle == 1)
            def _():
                pair_copy(j, 4, pair, 3 - chip).wait_send()
                pair_copy(j, 5, 1 - pair, mate).wait_send()

        for k in range(4):
            xy_copy(j, k).wait_send()
            core_copy(j, k).wait_send()
    for peer in peers:
        g_copy(peer, me).wait_send()
        g_copy(peer, peer).wait_recv()


def front(tokens, gain1, gain2, bias, rel, routes, grad_out, router, w_qkv, wo, groups, capacity):
    rows, width = tokens.shape
    expert_count = router.shape[0]
    chips = expert_count // 2
    own, part = w_qkv.shape[0], w_qkv.shape[1] // groups
    heads = bias.shape[0]
    lane_count = -(-capacity // 128) * 128
    vmem = pl.BlockSpec(memory_space=pltpu.VMEM)
    sem = pltpu.SemaphoreType.DMA
    shape = jax.ShapeDtypeStruct
    slots = (expert_count, capacity, width)
    spread = (2, 2, chips, 2, own)
    return pl.pallas_call(
        front_kernel,
        in_specs=[vmem] * 10,
        out_specs=[ANY] * 10 + [vmem] * 2,
        out_shape=[
            shape((groups, *spread, part), BF16),
            shape((*spread, width), BF16),
            shape((groups, rows, part), BF16),
            shape((heads, rows, rows), BF16),
            shape(slots, BF16),
            shape((width, rows), BF16),
            shape((width, rows), BF16),
            shape((rows, width), F32),
            shape((rows, width), BF16),
            shape(slots, BF16),
            shape((expert_count, 8, lane_count), F32),
            shape((rows, 128), F32),
        ],
        scratch_shapes=[
            pltpu.VMEM((groups, own, part), BF16),
            pltpu.VMEM((groups, *spread, part), BF16),
            pltpu.VMEM((*spread, width), BF16),
            pltpu.VMEM((groups, rows, part), BF16),
            pltpu.VMEM((2, 2, rows, rows), BF16),
            pltpu.VMEM((rows, width), BF16),
            pltpu.VMEM((rows, width), BF16),
            pltpu.VMEM((expert_count * capacity, rows), BF16),
            pltpu.VMEM(slots, BF16),
            sem((groups + 3,)),
            sem((groups + 1, max(chips, 6))),
            sem((groups + 1, max(chips, 6))),
            sem((groups + 1, 4)),
            sem((groups + 1, 4)),
            sem((groups + 1, 4)),
            sem((groups + 1, 4)),
            sem((expert_count,)),
            sem((expert_count,)),
            sem((groups + 1,)),
            sem((2,)),
            pltpu.VMEM((width, rows), BF16),
            pltpu.VMEM((width, rows), BF16),
            pltpu.VMEM((rows, width), F32),
            pltpu.VMEM((rows, width), BF16),
            pltpu.VMEM(slots, BF16),
            sem((5,)),
            pltpu.VMEM((heads, rel.shape[1] + 1), F32),
            pltpu.VMEM((8, rel.shape[1] + 1), jnp.int32),
        ],
        compiler_params=pltpu.CompilerParams(
            collective_id=3, has_side_effects=True, vmem_limit_bytes=60 * 1024 * 1024
        ),
        name="front",
    )(tokens, gain1, gain2, bias, rel, routes, grad_out, router, w_qkv, wo)


def attend_back_pair(j, a, qkv_v, p_ref, grads_v, dqkv_v, fold_ref):
    def lanes(part):
        return pl.ds(pl.multiple_of(256 * part + 128 * a, 128), 128)

    query = qkv_v[j, :, lanes(0)] * jnp.asarray(0.125, BF16)
    keys_t = qkv_v[j, :, lanes(1)].T
    values = qkv_v[j, :, lanes(2)]
    grads = grads_v[:, pl.ds(pl.multiple_of(256 * j + 128 * a, 128), 128)]
    half = iota((512, 128), 1) // 64
    dq_halves, dk_halves, dv_halves = [], [], []
    for t in range(2):
        values_t = jnp.where(half == t, values, jnp.zeros_like(values))
        probs = [p_ref[t, 128 * c : 128 * c + 128, :].astype(F32) for c in range(4)]
        grad_probs = [dot_nt(values_t[128 * c : 128 * c + 128], grads) for c in range(4)]
        delta = functools.reduce(
            jnp.add,
            [jnp.sum(p * g, axis=0, keepdims=True) for p, g in zip(probs, grad_probs)],
        )
        scores = [(p * (g - delta)).astype(BF16) for p, g in zip(probs, grad_probs)]
        padded = [
            jnp.concatenate(
                ([jnp.zeros((128, 384 - 128 * c), F32)] if c < 3 else [])
                + [scores[c].astype(F32), jnp.zeros((128, 128 + 128 * c), F32)],
                axis=1,
            )
            for c in range(4)
        ]
        fold_ref[pl.ds(4 * j + 2 * a + t, 1), :] = fold_bias(functools.reduce(jnp.add, padded))
        grad_scores = jnp.concatenate(scores, axis=0)
        dv_halves.append(dot_nn(p_ref[t], grads))
        dk_halves.append(dot_nn(grad_scores, query))
        dq_halves.append(dot_nn(keys_t, grad_scores))
    dq = jnp.where(iota((128, 512), 0) < 64, dq_halves[0], dq_halves[1]) * 0.125
    dqkv_v[:, lanes(0)] = dq.T.astype(BF16)
    dqkv_v[:, lanes(1)] = jnp.where(half == 0, dk_halves[0], dk_halves[1]).astype(BF16)
    dqkv_v[:, lanes(2)] = jnp.where(half == 0, dv_halves[0], dv_halves[1]).astype(BF16)


def dot_exact(a, b, dot=dot_nn):
    total = None
    for _ in range(3):
        piece = a.astype(BF16)
        a = a - piece.astype(F32)
        term = dot(piece, b)
        total = term if total is None else total + term
    return total


def dot_f32(a, b):
    total = None
    for _ in range(3):
        piece = b.astype(BF16)
        b = b - piece.astype(F32)
        term = dot_exact(a, piece)
        total = term if total is None else total + term
    return total


def back_kernel(
    buckets,
    dw_ref,
    head_ref,
    ys_ref,
    dx_hbm,
    dgates_hbm,
    cols_ref,
    routes_ref,
    tokens_hbm,
    grad_hbm,
    resid_hbm,
    normed2_hbm,
    normed_t_hbm,
    mixed_t_hbm,
    gain1_ref,
    gain2_ref,
    router_t_ref,
    rel_ref,
    wq_ref,
    wo_hbm,
    qkv_ref,
    p_ref,
    first_ref,
    second_ref,
    small_out_ref,
    gq_out_ref,
    go_out_ref,
    block_hbm,
    grad_tokens_hbm,
    y_v,
    grads_q,
    grads_o,
    core_q,
    core_o,
    step1_q,
    step1_o,
    step2_q,
    step2_o,
    last_q,
    last_o,
    rows_q,
    rows_o,
    sum_q,
    sum_o,
    qkv_v,
    p_v,
    wq_v,
    dqkv_v,
    dmix_v,
    dn1_v,
    fold_v,
    small_v,
    own_v,
    first_v,
    pass_v,
    y_send,
    y_recv,
    first_send,
    first_recv,
    second_send,
    second_recv,
    ring_sem,
    small_send,
    small_recv,
    core_send,
    core_recv,
    step1_send,
    step1_recv,
    step2_send,
    step2_recv,
    last_send,
    last_recv,
    local_sem,
    p_sem,
    wq_sem,
    dx_ref,
    dgates_ref,
    tokens_ref,
    resid_ref,
    normed2_ref,
    normed_t_ref,
    mixed_t_ref,
    wo_ref,
    grad_ref,
    input_sem,
    block_sem,
    block_ref,
    grad_tokens_ref,
    rel_v,
):
    loads = {
        name: pltpu.make_async_copy(src, dst, input_sem.at[n])
        for n, (name, src, dst) in enumerate(
            (
                ("dx", dx_hbm, dx_ref),
                ("dgates", dgates_hbm, dgates_ref),
                ("tokens", tokens_hbm, tokens_ref),
                ("resid", resid_hbm, resid_ref),
                ("normed2", normed2_hbm, normed2_ref),
                ("normed_t", normed_t_hbm, normed_t_ref),
                ("mixed_t", mixed_t_hbm, mixed_t_ref),
                ("wo", wo_hbm, wo_ref),
                ("grad", grad_hbm, grad_ref),
            )
        )
    }
    for copy in loads.values():
        copy.start()
    expert_count, capacity, width = ys_ref.shape
    slots = expert_count * capacity
    rows = tokens_ref.shape[0]
    chips = expert_count // 2
    size = expert_count // GROUPS
    me, dp = lax.axis_index("expert"), lax.axis_index("dp")
    core, chip = me % 2, me // 2
    x, y = dp % 2, dp // 2
    core_peer = me + 1 - 2 * core
    x_peer, y_peer = dp + 1 - 2 * x, dp + 2 - 4 * y
    my_group, my_place = me // size, me % size
    chip_peers = [(chip + d) % chips for d in range(1, chips)]
    greet(
        [{"expert": (me + d) % expert_count} for d in range(1, expert_count)]
        + [{"dp": x_peer}, {"dp": y_peer}]
    )

    tile_count = dw_ref.shape[0]
    batches = tile_count // BATCH

    def first_copy(t, i):
        sent, _, peer, _, keep = ways(dp, t)
        return remote(
            dw_ref.at[t, sent[i]],
            first_ref.at[t - BATCH * AHEAD, (i + keep) % 2],
            first_send.at[t - BATCH * AHEAD, i],
            first_recv.at[t - BATCH * AHEAD, i],
            dp=peer,
        )

    def second_copy(t, n):
        peer = ways(dp, t)[3]
        return remote(
            pass_v.at[n % 2, t % BATCH], second_ref.at[t], second_send.at[t], second_recv.at[t], dp=peer
        )

    def relay_loads(t, b):
        held = ways(dp, t)[1]
        q = t % BATCH
        came = head_ref.at[t, 1] if b < AHEAD else first_ref.at[t - BATCH * AHEAD, 1]
        return [
            pltpu.make_async_copy(dw_ref.at[t, held[1]], own_v.at[b % 2, q], ring_sem.at[b % 2, q, 0]),
            pltpu.make_async_copy(came, first_v.at[b % 2, q], ring_sem.at[b % 2, q, 1]),
        ]

    def over(b, body):
        def step(t, carry):
            body(t)
            return carry

        lax.fori_loop(BATCH * b, BATCH * b + BATCH, step, 0)

    def issue(b):
        def body(t):
            for i in range(2):
                first_copy(t, i).start()

        over(b, body)

    def relay_begin(b):
        def body(t):
            if b >= AHEAD:
                for i in range(2):
                    first_copy(t, i).wait_recv()
            for load in relay_loads(t, b):
                load.start()

        over(b, body)

    def relay_end(b):
        def body(t):
            for load in relay_loads(t, b):
                load.wait()
            if b >= 2:
                second_copy(t - 2 * BATCH, b).wait_send()
            q = t % BATCH
            pass_v[b % 2, q] = (
                own_v[b % 2, q].astype(F32) + first_v[b % 2, q].astype(F32)
            ).astype(BF16)
            second_copy(t, b).start()

        over(b, body)

    groups = grads_q.shape[0]
    count = groups + 1

    def pick(many, one, p):
        return many.at[p] if p < groups else one

    grads = [pick(grads_q, grads_o, p) for p in range(count)]
    cores = [pick(core_q, core_o, p) for p in range(count)]
    step1 = [pick(step1_q, step1_o, p) for p in range(count)]
    step2 = [pick(step2_q, step2_o, p) for p in range(count)]
    lasts = [pick(last_q, last_o, p) for p in range(count)]
    outs = [pick(gq_out_ref, go_out_ref, p) for p in range(count)]
    widths = [grads_q.shape[-1]] * groups + [grads_o.shape[-1]]

    def part_core(p):
        return remote(
            grads[p].at[:, :, :, 1 - core], cores[p], core_send.at[p], core_recv.at[p], expert=core_peer
        )

    def part_step1(p, b):
        half = widths[p] // 2
        src = (
            grads[p].at[:, 1 - x, :, core, :, 0:half]
            if b == 0
            else grads[p].at[1 - y, :, :, core, :, half : 2 * half]
        )
        return remote(
            src, step1[p].at[b], step1_send.at[p, b], step1_recv.at[p, b], dp=(x_peer, y_peer)[b]
        )

    def part_step2(p, b):
        src = step1[p].at[b, (1 - y, 1 - x)[b]]
        return remote(
            src, step2[p].at[b], step2_send.at[p, b], step2_recv.at[p, b], dp=(y_peer, x_peer)[b]
        )

    def part_last(p, peer, at):
        return remote(
            cores[p].at[0, 0, peer], lasts[p].at[at], last_send.at[p, peer], last_recv.at[p, at],
            expert=peer * 2 + core,
        )

    arrivals = {p: rows_o if p == groups else rows_q.at[p] for p in CHIPS_FIRST}
    sums = {p: sum_o if p == groups else sum_q.at[p] for p in CHIPS_FIRST}

    def chip_rows(p, peer, at):
        return remote(
            grads[p].at[:, :, peer, core], arrivals[p].at[at], last_send.at[p, peer], last_recv.at[p, at],
            expert=peer * 2 + core,
        )

    def chip_step1(p, b):
        half = widths[p] // 2
        src = (
            sums[p].at[:, 1 - x, :, 0:half] if b == 0 else sums[p].at[1 - y, :, :, half : 2 * half]
        )
        return remote(
            src, step1[p].at[b, :, 0], step1_send.at[p, b], step1_recv.at[p, b], dp=(x_peer, y_peer)[b]
        )

    def chip_step2(p, b):
        src = step1[p].at[b, (1 - y, 1 - x)[b], 0]
        return remote(
            src, step2[p].at[b, 0], step2_send.at[p, b], step2_recv.at[p, b], dp=(y_peer, x_peer)[b]
        )

    def chip_held(p, b, i):
        half = widths[p] // 2
        held = sums[p][i, x, :, 0:half] if b == 0 else sums[p][y, i, :, half : 2 * half]
        return held.astype(F32) + step1[p][b, i, 0].astype(F32)

    def part_a(p):
        part_core(p).start()

    def part_b(p):
        part_core(p).wait()
        total = grads[p][:, :, :, core].astype(F32) + cores[p][...].astype(F32)
        grads[p][:, :, :, core] = total.astype(BF16)
        if p in CHIPS_FIRST:
            for peer in chip_peers:
                chip_rows(p, peer, chip).start()
            return
        for b in range(2):
            part_step1(p, b).start()

    def part_c(p):
        half = widths[p] // 2
        if p in CHIPS_FIRST:
            total = grads[p][:, :, chip, core].astype(F32)
            for peer in chip_peers:
                chip_rows(p, peer, peer).wait_recv()
                total = total + arrivals[p][peer].astype(F32)
            sums[p][...] = total.astype(BF16)
            for b in range(2):
                chip_step1(p, b).start()
            return
        for b in range(2):
            part_step1(p, b).wait()
            for i in range(2):
                held = (
                    grads[p][i, x, :, core, :, 0:half]
                    if b == 0
                    else grads[p][y, i, :, core, :, half : 2 * half]
                )
                total = held.astype(F32) + step1[p][b, i].astype(F32)
                step1[p][b, i] = total.astype(BF16)
            part_step2(p, b).start()

    def part_d(p):
        half = widths[p] // 2
        if p in CHIPS_FIRST:
            for b in range(2):
                chip_step1(p, b).wait()
                give = (1 - y, 1 - x)[b]
                step1[p][b, give, 0] = chip_held(p, b, give).astype(BF16)
                chip_step2(p, b).start()
            return
        for b in range(2):
            part_step2(p, b).wait()
            total = step1[p][b, (y, x)[b]].astype(F32) + step2[p][b].astype(F32)
            cores[p][0, 0, :, :, b * half : b * half + half] = total.astype(BF16)
        for peer in chip_peers:
            part_last(p, peer, chip).start()

    def part_e(p):
        half = widths[p] // 2
        if p in CHIPS_FIRST:
            for b in range(2):
                chip_step2(p, b).wait()
                total = chip_held(p, b, (y, x)[b]) + step2[p][b, 0].astype(F32)
                outs[p][:, b * half : b * half + half] = total
            for peer in chip_peers:
                chip_rows(p, peer, chip).wait_send()
            return
        total = cores[p][0, 0, chip].astype(F32)
        for peer in chip_peers:
            part_last(p, peer, peer).wait_recv()
            total = total + lasts[p][peer].astype(F32)
        outs[p][...] = total
        for peer in chip_peers:
            part_last(p, peer, chip).wait_send()

    partners = []
    bit = 1
    while bit < expert_count:
        partners.append({"expert": flip(me, bit)})
        bit *= 2
    partners += [{"dp": x_peer}, {"dp": y_peer}]
    stages = len(partners)

    def small_copy(s):
        return remote(
            small_v.at[0], small_v.at[1 + s], small_send.at[s], small_recv.at[s], **partners[s]
        )

    def small_next(s):
        small_copy(s).wait()
        small_v[0] = small_v[0] + small_v[1 + s]
        if s + 1 < stages:
            small_copy(s + 1).start()

    def y_copy(peer, at):
        return remote(ys_ref.at[peer], y_v.at[at], y_send.at[peer], y_recv.at[at], expert=peer)

    def others(c):
        group = flip(my_group, c)
        return [group * size + (my_place + s) % size for s in range(1 if c == 0 else 0, size)]

    peers = [peer for c in (2, 3, 1, 0) for peer in others(c)]

    def p_copy(j, a):
        return pltpu.make_async_copy(p_ref.at[pl.ds(4 * j + 2 * a, 2)], p_v.at[a], p_sem.at[a])

    def wq_copy(j):
        return pltpu.make_async_copy(wq_ref.at[j], wq_v.at[j % 2], wq_sem.at[j % 2])

    lane = iota((rows, 128), 1)
    slot = [column(cols_ref[...], k) for k in range(2)]
    gates = [column(cols_ref[...], 2 + k) for k in range(2)]

    def hots():
        at = iota((rows, slots), 1).astype(F32)
        return [at == s for s in slot]

    def dense():
        lanes = dgates_ref.shape[2]
        wide = iota((rows, lanes), 1)

        def step(e, totals):
            base = (e * capacity).astype(F32)
            row = dgates_ref[pl.ds(e, 1)][0][0:1]
            return tuple(
                totals[k]
                + jnp.where((wide.astype(F32) == slot[k] - base) & (wide < capacity), row, 0.0)
                for k in range(2)
            )

        zero = jnp.zeros((rows, lanes), F32)
        sums = lax.fori_loop(0, expert_count, step, (zero, zero))
        dgates = [jnp.sum(s, axis=1, keepdims=True) for s in sums]
        mean = gates[0] * dgates[0] + gates[1] * dgates[1]
        dchosen = [gates[k] * (dgates[k] - mean) for k in range(2)]
        dlogits = jnp.zeros((rows, 128), F32)
        for k in range(2):
            here = lane == route_column(routes_ref, k).astype(jnp.int32)
            dlogits = dlogits + jnp.where(here, dchosen[k], 0.0)
        small_rows = dot_exact(dlogits.T[0:expert_count], normed2_ref[...])
        small_v[0, 0:expert_count] = small_rows
        blank = jnp.zeros((128 - expert_count, width), F32)
        router = jnp.concatenate([router_t_ref[...], blank], axis=0)
        hot0, hot1 = hots()
        hot = jnp.where(hot0 | hot1, 1.0, 0.0).astype(BF16)
        dnormed = dot_f32(dlogits, router)
        dnormed = dnormed + dot_nn(hot, dx_ref[...].reshape(slots, width))
        resid = resid_ref[...]
        inv_rms = lax.rsqrt(jnp.mean(resid * resid, axis=1, keepdims=True) + EPS)
        normed = resid * inv_rms
        scaled = dnormed * gain2_ref[...]
        small_v[0, expert_count + 1 : expert_count + 2] = jnp.sum(
            dnormed * normed, axis=0, keepdims=True
        )
        inner = jnp.mean(scaled * normed, axis=1, keepdims=True)
        dresid = grad_ref[...].astype(F32) + inv_rms * (scaled - normed * inner)
        grad_tokens_ref[...] = dresid
        dresid_r = dresid.astype(BF16)
        grads_o[...] = dot_nn(mixed_t_ref[...], dresid_r).astype(BF16).reshape(grads_o.shape)
        part_a(groups)
        dmix_v[...] = dot_nt(dresid_r, wo_ref[...]).astype(BF16)

    def group(j):
        if j + 1 < groups:
            wq_copy(j + 1).start()

        def pair(a, carry):
            p_copy(j, a).wait()
            attend_back_pair(j, a, qkv_v, p_v.at[a], dmix_v, dqkv_v, fold_v)
            if j + 1 < groups:
                p_copy(j + 1, a).start()
            return carry

        lax.fori_loop(0, 2, pair, 0)
        block = dot_nn(normed_t_ref[...], dqkv_v[...])
        grads_q[j] = block.astype(BF16).reshape(grads_q.shape[1:])
        part_a(j)
        wq_copy(j).wait()
        term = dot_nt(dqkv_v[...], wq_v[j % 2])
        dn1_v[...] = term if j == 0 else dn1_v[...] + term

    def norm_back():
        inputs = tokens_ref[...].astype(F32)
        inv_rms = lax.rsqrt(jnp.mean(inputs * inputs, axis=1, keepdims=True) + EPS)
        normed = inputs * inv_rms
        dnormed = dn1_v[...]
        scaled = dnormed * gain1_ref[...]
        small_v[0, expert_count : expert_count + 1] = jnp.sum(
            dnormed * normed, axis=0, keepdims=True
        )
        inner = jnp.mean(scaled * normed, axis=1, keepdims=True)
        grad_tokens_ref[...] += inv_rms * (scaled - normed * inner)
        heads = fold_v.shape[0]
        spread = jnp.concatenate([bucket_rows(rel_ref, rel_v, buckets)] * heads, axis=0)
        table = dot_exact(fold_v[...], spread, dot_nt)
        own = iota(table.shape, 1) // buckets == iota(table.shape, 0)
        base = expert_count + 2
        small_v[0, base : base + 1, 0 : heads * buckets] = jnp.sum(
            jnp.where(own, table, 0.0), axis=0, keepdims=True
        )
        tokens_copy.start()
        small_copy(0).start()

    def outputs():
        for peer in peers:
            y_copy(peer, peer).wait_recv()
        y_own.wait()
        values = y_v[...].reshape(slots, width)
        total = resid_ref[...]
        for k, hot in enumerate(hots()):
            total = total + gates[k] * dot_nn(jnp.where(hot, 1.0, 0.0).astype(BF16), values)
        block_ref[...] = total.astype(BF16)
        block_copy.start()

    block_copy = pltpu.make_async_copy(block_ref, block_hbm, block_sem.at[0])
    tokens_copy = pltpu.make_async_copy(grad_tokens_ref, grad_tokens_hbm, block_sem.at[1])
    small_v[0] = jnp.zeros(small_v.shape[1:], F32)
    for peer in peers:
        y_copy(peer, me).start()
    y_own = pltpu.make_async_copy(ys_ref.at[me], y_v.at[me], local_sem.at[0])
    y_own.start()
    qkv_copy = pltpu.make_async_copy(qkv_ref, qkv_v, local_sem.at[1])
    qkv_copy.start()
    wq_copy(0).start()
    for a in range(2):
        p_copy(0, a).start()
    late = [b for b in range(AHEAD, batches)]
    turn = [b for b in range(AHEAD, batches)]
    open_relays = []

    def send_more(number):
        for _ in range(min(number, len(late))):
            issue(late.pop(0))

    def relay_in():
        if turn:
            b = turn.pop(0)
            relay_begin(b)
            open_relays.append(b)

    def relay_out():
        if open_relays:
            relay_end(open_relays.pop(0))

    send_more(4)
    for b in range(AHEAD):
        relay_begin(b)
        if b > 0:
            relay_end(b - 1)
    relay_end(AHEAD - 1)
    send_more(1)
    for copy in loads.values():
        copy.wait()
    dense()
    qkv_copy.wait()
    group(0)
    part_b(groups)
    relay_in()
    relay_out()
    send_more(1)
    group(1)
    part_b(0)
    relay_in()
    relay_out()
    send_more(1)
    group(2)
    part_b(1)
    relay_in()
    relay_out()
    send_more(1)
    group(3)
    part_b(2)
    send_more(1)
    norm_back()
    part_b(3)
    send_more(len(late))
    relay_in()
    small_next(0)
    relay_out()
    direct = [p for p in (groups, *range(groups)) if p not in CHIPS_FIRST]
    first_on = [p for p in (groups, *range(groups)) if p in CHIPS_FIRST]
    for p in direct:
        part_c(p)
    small_next(1)
    outputs()
    small_next(2)
    relay_in()
    for p in direct[:-1]:
        part_d(p)
    relay_out()
    for p in first_on[:1]:
        part_c(p)
    small_next(3)
    relay_in()
    for p in direct[-1:]:
        part_d(p)
    for p in first_on[1:2]:
        part_c(p)
    relay_out()
    for s in range(4, stages):
        small_next(s)
    small_out_ref[...] = small_v[0]
    for p in first_on[:1]:
        part_d(p)
    relay_in()
    for p in first_on[2:]:
        part_c(p)
    for p in first_on[1:2]:
        part_d(p)
    relay_out()
    while turn:
        relay_in()
        relay_out()
    for p in first_on[2:]:
        part_d(p)
    for p in direct:
        part_e(p)
    for p in first_on:
        part_e(p)
    for b in (batches - 2, batches - 1):
        over(b, lambda t, b=b: second_copy(t, b).wait_send())

    def drain_first(t, carry):
        for i in range(2):
            first_copy(t, i).wait_send()
        return carry

    def drain_second(t, carry):
        second_copy(t, 0).wait_recv()
        return carry

    block_copy.wait()
    tokens_copy.wait()
    lax.fori_loop(BATCH * AHEAD, tile_count, drain_first, 0)
    lax.fori_loop(0, tile_count, drain_second, 0)
    for peer in peers:
        y_copy(peer, me).wait_send()


def back(
    dw, head, ys, dx, dgates, cols, routes, tokens, grad_out, resid, normed2, normed_t, mixed_t,
    gain1, gain2, router_t, rel, wq, wo, qkv, probs, buckets,
):
    tile_count, dp_count, deep, _ = dw.shape
    expert_count, capacity, width = ys.shape
    chips = expert_count // 2
    rows = tokens.shape[0]
    groups, _, part = qkv.shape
    own = width // (dp_count * expert_count)
    heads = probs.shape[0]
    small_rows = -(-(expert_count + 3) // 8) * 8
    stages = expert_count.bit_length() + 1
    vmem = pl.BlockSpec(memory_space=pltpu.VMEM)
    sem = pltpu.SemaphoreType.DMA
    shape = jax.ShapeDtypeStruct
    ring = (2, BATCH, deep, TILE)
    late = tile_count - BATCH * AHEAD

    def pairs(make, number=groups):
        return [pltpu.VMEM((number, *make(part)), BF16), pltpu.VMEM(make(width), BF16)]

    return pl.pallas_call(
        functools.partial(back_kernel, buckets),
        in_specs=[ANY] * 5 + [vmem] * 2 + [ANY] * 6 + [vmem] * 4 + [ANY] * 4,
        out_specs=[ANY] * 2 + [vmem] * 3 + [ANY] * 2,
        out_shape=[
            shape((late, 2, deep, TILE), BF16),
            shape((tile_count, deep, TILE), BF16),
            shape((small_rows, width), F32),
            shape((groups, own, part), F32),
            shape((own, width), F32),
            shape((rows, width), BF16),
            shape((rows, width), F32),
        ],
        scratch_shapes=[pltpu.VMEM(ys.shape, BF16)]
        + pairs(lambda w: (2, 2, chips, 2, own, w))
        + pairs(lambda w: (2, 2, chips, own, w))
        + pairs(lambda w: (2, 2, chips, own, w // 2))
        + pairs(lambda w: (2, chips, own, w // 2))
        + pairs(lambda w: (chips, own, w))
        + pairs(lambda w: (chips, 2, 2, own, w), CHIPS_FIRST_GROUPS)
        + pairs(lambda w: (2, 2, own, w), CHIPS_FIRST_GROUPS)
        + [
            pltpu.VMEM(qkv.shape, BF16),
            pltpu.VMEM((2, 2, rows, rows), BF16),
            pltpu.VMEM((2, *wq.shape[1:]), BF16),
            pltpu.VMEM((rows, part), BF16),
            pltpu.VMEM((rows, width), BF16),
            pltpu.VMEM((rows, width), F32),
            pltpu.VMEM((heads, rel.shape[1] + 1), F32),
            pltpu.VMEM((stages + 1, small_rows, width), F32),
            pltpu.VMEM(ring, BF16),
            pltpu.VMEM(ring, BF16),
            pltpu.VMEM(ring, BF16),
            sem((expert_count,)),
            sem((expert_count,)),
            sem((late, 2)),
            sem((late, 2)),
            sem((tile_count,)),
            sem((tile_count,)),
            sem((2, BATCH, 2)),
            sem((stages,)),
            sem((stages,)),
            sem((groups + 1,)),
            sem((groups + 1,)),
            sem((groups + 1, 2)),
            sem((groups + 1, 2)),
            sem((groups + 1, 2)),
            sem((groups + 1, 2)),
            sem((groups + 1, chips)),
            sem((groups + 1, chips)),
            sem((2,)),
            sem((2,)),
            sem((2,)),
        ]
        + [
            pltpu.VMEM(a.shape, a.dtype)
            for a in (dx, dgates, tokens, resid, normed2, normed_t, mixed_t, wo, grad_out)
        ]
        + [
            sem((9,)),
            sem((2,)),
            pltpu.VMEM((rows, width), BF16),
            pltpu.VMEM((rows, width), F32),
            pltpu.VMEM((8, rel.shape[1] + 1), jnp.int32),
        ],
        compiler_params=pltpu.CompilerParams(
            collective_id=2, has_side_effects=True, vmem_limit_bytes=61 * 1024 * 1024
        ),
        name="back",
    )(
        dw, head, ys, dx, dgates, cols, routes, tokens, grad_out, resid, normed2, normed_t, mixed_t,
        gain1, gain2, router_t, rel, wq, wo, qkv, probs,
    )


def tail_kernel(
    heads,
    buckets,
    dw_ref,
    head_ref,
    first_ref,
    second_ref,
    block_ref,
    tokens_ref,
    small_ref,
    gq_ref,
    go_ref,
    in_ref,
    out_ref,
    block_out_ref,
    tokens_out_ref,
    router_ref,
    norm1_ref,
    norm2_ref,
    bias_ref,
    qkv_ref,
    proj_ref,
    own_v,
    came_v,
    second_v,
    in_v,
    out_v,
    block_v,
    tokens_v,
    load_sem,
    store_sem,
    pass_sem,
):
    dp = lax.axis_index("dp")
    tiles = own_v.shape[0]
    expert_count = router_ref.shape[0]

    def loads(f):
        span = pl.ds(BATCH * f, BATCH)
        late = pl.ds(BATCH * (f - AHEAD), BATCH)
        came = head_ref.at[span, 0] if f < AHEAD else first_ref.at[late, 0]
        return [
            pltpu.make_async_copy(src, dst.at[f], load_sem.at[f, k])
            for k, (src, dst) in enumerate(
                ((dw_ref.at[span, dp], own_v), (came, came_v), (second_ref.at[span], second_v))
            )
        ]

    def stores(f):
        cols = pl.ds(TILE * f, TILE)
        return [
            pltpu.make_async_copy(in_v.at[f], in_ref.at[:, :, cols], store_sem.at[f, 0]),
            pltpu.make_async_copy(out_v.at[f], out_ref.at[cols], store_sem.at[f, 1]),
        ]

    for f in range(tiles):
        for copy in loads(f):
            copy.start()
    taken = [
        pltpu.make_async_copy(block_ref, block_v, pass_sem.at[0]),
        pltpu.make_async_copy(tokens_ref, tokens_v, pass_sem.at[1]),
    ]
    given = [
        pltpu.make_async_copy(block_v, block_out_ref, pass_sem.at[2]),
        pltpu.make_async_copy(tokens_v, tokens_out_ref, pass_sem.at[3]),
    ]
    for copy in taken:
        copy.start()
    router_ref[...] = small_ref[0:expert_count]
    norm1_ref[...] = small_ref[expert_count : expert_count + 1]
    norm2_ref[...] = small_ref[expert_count + 1 : expert_count + 2]
    base = expert_count + 2
    row = jnp.broadcast_to(small_ref[base : base + 1, 0 : heads * buckets], (8, heads * buckets))
    for h in range(heads):
        turned = pltpu.roll(row, (heads - h) % heads * buckets, 1) if h else row
        bias_ref[h : h + 1] = turned[0:1, 0:buckets]
    groups, _, part = gq_ref.shape
    third = part // 3
    for j in range(groups):
        for k in range(3):
            at = (k * groups + j) * third
            qkv_ref[:, at : at + third] = gq_ref[j, :, k * third : (k + 1) * third]
    proj_ref[...] = go_ref[...]
    for f in range(tiles):
        for copy in loads(f):
            copy.wait()
        for m in range(BATCH):
            total = own_v[f, m].astype(F32) + came_v[f, m].astype(F32) + second_v[f, m].astype(F32)
            if m < 2:
                in_v[f, m] = total
            else:
                out_v[f] = total.T
        for copy in stores(f):
            copy.start()
    for came, copy in zip(taken, given):
        came.wait()
        copy.start()
    for f in range(tiles):
        for copy in stores(f):
            copy.wait()
    for copy in given:
        copy.wait()


def tail(dw, head, first, second, small, gq, go, block, tokens, expert_count, heads, buckets):
    tile_count, _, deep, _ = dw.shape
    tiles = tile_count // BATCH
    groups, own, part = gq.shape
    width = tokens.shape[1]
    shape = jax.ShapeDtypeStruct
    vmem = pl.BlockSpec(memory_space=pltpu.VMEM)
    terms = pltpu.VMEM((tiles, BATCH, deep, TILE), BF16)
    sem = pltpu.SemaphoreType.DMA
    return pl.pallas_call(
        functools.partial(tail_kernel, heads, buckets),
        in_specs=[ANY] * 6 + [vmem] * 3,
        out_specs=[ANY] * 4 + [vmem] * 6,
        out_shape=[
            shape((2, deep, tiles * TILE), F32),
            shape((tiles * TILE, deep), F32),
            shape(block.shape, BF16),
            shape(tokens.shape, F32),
            shape((expert_count, width), F32),
            shape((1, width), F32),
            shape((1, width), F32),
            shape((heads, buckets), F32),
            shape((own, groups * part), F32),
            shape((own, width), F32),
        ],
        scratch_shapes=[
            terms,
            terms,
            terms,
            pltpu.VMEM((tiles, 2, deep, TILE), F32),
            pltpu.VMEM((tiles, TILE, deep), F32),
            pltpu.VMEM(block.shape, BF16),
            pltpu.VMEM(tokens.shape, F32),
            sem((tiles, 3)),
            sem((tiles, 2)),
            sem((4,)),
        ],
        compiler_params=pltpu.CompilerParams(vmem_limit_bytes=62 * 1024 * 1024),
        name="tail",
    )(dw, head, first, second, block, tokens, small, gq, go)


def shards(
    tokens,
    routes,
    rel_bucket,
    norm_gain1,
    w_qkv,
    w_out_proj,
    bias_table,
    norm_gain2,
    w_router,
    w_expert_in,
    w_expert_out,
    grad_out,
):
    row_count, model_width = tokens.shape
    bucket_count, head_count = bias_table.shape
    expert_count = lax.axis_size("expert")
    capacity = 10 * row_count // (4 * expert_count)
    slot_total = expert_count * capacity
    hidden_groups = 4

    wq_full, out_full, qkv, probs, g_rows, mixed_t, normed1_t, residual, normed2_r, xs, gates, cols = front(
        tokens,
        norm_gain1[None],
        norm_gain2[None],
        bias_table.T,
        rel_bucket[None],
        routes.T,
        grad_out,
        w_router.T,
        w_qkv,
        w_out_proj,
        hidden_groups,
        capacity,
    )
    produced, grad_rows, grad_gates, grad_w, head = experts(
        xs, gates, g_rows, w_expert_in[0], w_expert_out[0], lax.axis_size("dp")
    )
    first, second, *rest = back(
        grad_w,
        head,
        produced,
        grad_rows,
        grad_gates,
        cols,
        routes.T,
        tokens,
        grad_out,
        residual,
        normed2_r,
        normed1_t,
        mixed_t,
        norm_gain1[None],
        norm_gain2[None],
        w_router.T,
        rel_bucket[None],
        wq_full.reshape(hidden_groups, model_width, -1),
        out_full.reshape(model_width, model_width),
        qkv,
        probs,
        bucket_count,
    )
    (
        grad_in,
        grad_out_t,
        block_out,
        grad_tokens,
        grad_router,
        grad_norm1,
        grad_norm2,
        grad_bias,
        grad_qkv,
        grad_out_proj,
    ) = tail(grad_w, head, first, second, *rest, expert_count, head_count, bucket_count)
    grad_expert_in, grad_expert_out = grad_in[None], grad_out_t[None]
    grad_router_all, grad_bias = grad_router.T, grad_bias.T
    grad_norm1, grad_norm2 = grad_norm1[0], grad_norm2[0]
    return (
        block_out,
        grad_tokens,
        grad_norm1,
        grad_qkv,
        grad_out_proj,
        grad_bias,
        grad_norm2,
        grad_router_all,
        grad_expert_in,
        grad_expert_out,
    )


def solution(mesh):
    split = P(("dp", "expert"), None)
    in_specs = (
        split,
        split,
        P(),
        P(),
        split,
        split,
        P(),
        P(),
        P(),
        P("expert", None, None, None),
        P("expert", None, None),
        split,
    )
    out_specs = (
        split,
        split,
        P(),
        split,
        split,
        P(),
        P(),
        P(),
        P("expert", None, "dp", None),
        P("expert", None, "dp"),
    )
    return jax.shard_map(shards, mesh=mesh, in_specs=in_specs, out_specs=out_specs, check_vma=False)
```
